32 devices in a mesh: node: 8 (over z, y), head: 4 (over x, core).
Axes of the slice: x: 2, y: 2, z: 4, core: 2. Of those that a mesh axis runs over, the one named last changes fastest.
Arguments:
- features: bfloat16 [16384, 256], P(('node', 'head')), may hold values from -40 to 40
- in_weight: bfloat16 [256, 768], replicated, may hold values from -0.6 to 0.6
- out_weight: bfloat16 [256, 256], replicated, may hold values from -0.375 to 0.375
- cotangent: bfloat16 [16384, 256], P(('node', 'head')), may hold values from -6 to 6
- key_slots: int32 [128, 12], P('node'), may hold values from 0 to 31, as said below
- block_count: int32 [128], P('node'), may hold values from 1 to 12
- wanted: int32 [8, 8, 2], P('node'), may hold values from 0 to 15
Outputs:
- output: bfloat16 [16384, 256], P(('node', 'head'))
- feature_grad: bfloat16 [16384, 256], P(('node', 'head'))
- in_weight_grad: float32 [256, 768], P(None, 'head')
- out_weight_grad: float32 [256, 256], P('head')
The draws below stay inside these ranges and needn't reach their ends.
Inputs may be any that keep to these rules, and one draw needn't show every extreme that they name: `key_slots`: slot 0 of a query block names the block itself; the slots of one query block are distinct.
All inputs are finite; a program needn't handle non-finite values.
Results may differ from the reference program's by a relative error of at most 0.02.
The reference program's roundings to bfloat16 on the way count: a program that leaves them out, or rounds other values in their place, can miss the bound.
Values may be sent and summed in bfloat16 or wider, within the bound.
No kernel may reach another device: no remote copies, remote signals or barrier semaphores. Data moves between devices by JAX's collectives and lax.ppermute only.
A program may use at most 128 MiB of HBM per device.

```python
import jax
import jax.numpy as jnp
from jax import lax

D = 256
HEADS = 4
HD = 64
BLOCK = 128
BLK = 16
PER = 12
CAP = 2
NODES = 16384
N_NODE = 8


def draw_features(key, part):
    key = jax.random.fold_in(key, 11)
    first = jax.random.fold_in(key, 0)
    base = jax.random.truncated_normal(first, -4.0, 4.0, (NODES, D), jnp.float32)
    return base.astype(jnp.bfloat16)


def draw_in_weight(key, part):
    key = jax.random.fold_in(key, 12)
    first = jax.random.fold_in(key, 0)
    deviation = D ** (-0.5)
    weights = jax.random.truncated_normal(first, -4.0, 4.0, (D, HEADS, 3, HD), jnp.float32) * deviation
    return weights.reshape(D, 3 * D).astype(jnp.bfloat16)


def draw_key_slots(key, part):
    key = jax.random.fold_in(key, 22)
    table_size = BLK + N_NODE * CAP
    row_total = N_NODE * BLK
    subkeys = jax.random.split(key, row_total)
    picks = jax.vmap(lambda subkey: jax.random.permutation(subkey, table_size - 1)[:PER - 1])(subkeys)
    leading = table_size - 2 - jnp.arange(PER - 1, dtype=jnp.int32)
    picks = picks.astype(jnp.int32).at[0].set(leading)
    own_block = (jnp.arange(row_total, dtype=jnp.int32) % BLK)[:, None]
    picks = picks + (picks >= own_block).astype(jnp.int32)
    return jnp.concatenate([own_block, picks], axis=1).astype(jnp.int32)


def draw_block_count(key, part):
    key = jax.random.fold_in(key, 23)
    first, second, third = jax.random.split(key, 3)
    loaded = jax.random.randint(first, (N_NODE, 1), 0, 4) == 0
    level = jnp.where(loaded, PER, jax.random.randint(second, (N_NODE, 1), 1, PER // 3 + 1))
    counts = jnp.clip(level - jax.random.randint(third, (N_NODE, BLK), 0, 2), 1, PER)
    counts = counts.reshape(-1).at[0].set(PER).at[1].set(1)
    return counts.astype(jnp.int32)


def plant(values, rng, low, largest):
    dims = values.shape
    place = [jax.random.randint(jax.random.fold_in(rng, axis), (), 0, dims[axis]) for axis in range(len(dims))]
    values = values.at[tuple(place)].set(low)
    longest = dims.index(max(dims))
    place[longest] = (place[longest] + 1) % dims[longest]
    return values.at[tuple(place)].set(largest)


def shard_levels(own_key, extent, pieces, smallest, top_value):
    level, own = 1.0, jax.random.fold_in(own_key, 6)
    for axis_at, parts in pieces:
        steps = jnp.exp(jax.random.uniform(jax.random.fold_in(own, axis_at), (parts,), jnp.float32, smallest / len(pieces), top_value / len(pieces)))
        level = level * jnp.repeat(steps, extent[axis_at] // parts).reshape([-1 if axis == axis_at else 1 for axis in range(len(extent))])
    return level


def noise(key, extent, scale, reach, shards=(), kind=jnp.bfloat16):
    array = scale * jax.random.normal(key, extent, jnp.float32)
    if shards:
        array = array * shard_levels(key, extent, shards, -0.22, 0.18)
    return jnp.clip(array, -reach, reach).astype(kind)


def setup_inputs(seed: int = 0) -> dict:
    seeds = jax.random.split(jax.random.key(seed), 8)
    return {
        "features": draw_features(jax.random.fold_in(seeds[7], 71), 0),
        "in_weight": draw_in_weight(jax.random.fold_in(seeds[7], 71), 0),
        "out_weight": noise(seeds[2], (D, D), D ** -0.5, 0.375),
        "cotangent": noise(seeds[3], (NODES, D), 1.0, 6.0, ((0, 32),)),
        "key_slots": draw_key_slots(jax.random.fold_in(seeds[7], 71), 0),
        "block_count": draw_block_count(jax.random.fold_in(seeds[7], 71), 0),
        "wanted": plant(jax.random.randint(seeds[6], (N_NODE, N_NODE, CAP), 0, BLK), jax.random.fold_in(seeds[6], 1), 0, BLK - 1).astype(jnp.int32),
    }


def block_attention(query_block, key_block, live_mask):
    score_scale = HD ** (-0.5)
    scores = jnp.einsum('qhd,pkhd->hqpk', query_block.astype(jnp.float32), key_block.astype(jnp.float32)) * score_scale
    scores = jnp.where(live_mask[None, None, :, None], scores, -1e+30)
    scores = scores.reshape(HEADS, BLOCK, PER * BLOCK)
    highest = lax.optimization_barrier(jnp.max(scores, axis=-1, keepdims=True))
    raised = jnp.exp(scores - highest)
    return raised / lax.optimization_barrier(jnp.sum(raised, axis=-1, keepdims=True))

def reference(features, in_weight, out_weight, cotangent, key_slots, block_count, wanted):
    block_total = N_NODE * BLK
    table_size = BLK + N_NODE * CAP
    score_scale = HD ** (-0.5)
    projected = jnp.dot(features, in_weight, preferred_element_type=jnp.float32).astype(jnp.bfloat16)
    projected = projected.reshape(block_total, BLOCK, HEADS, 3, HD)
    queries = projected[:, :, :, 0]
    keys_all = projected[:, :, :, 1]
    values_all = projected[:, :, :, 2]
    partition = (jnp.arange(block_total, dtype=jnp.int32) // BLK)[:, None]
    remote = jnp.maximum(key_slots - BLK, 0)
    owner = remote // CAP
    within = remote % CAP
    remote_block = owner * BLK + wanted[partition, owner, within]
    key_index = jnp.where(key_slots < BLK, partition * BLK + key_slots, remote_block).astype(jnp.int32)
    live = jnp.arange(PER, dtype=jnp.int32)[None, :] < block_count[:, None]

    def forward(index):
        chosen = key_index[index]
        attention = block_attention(queries[index], keys_all[chosen], live[index])
        attention_low = attention.astype(jnp.bfloat16).reshape(HEADS, BLOCK, PER, BLOCK)
        result = jnp.einsum('hqpk,pkhd->qhd', attention_low.astype(jnp.float32), values_all[chosen].astype(jnp.float32))
        return result.astype(jnp.bfloat16)
    attended = lax.map(forward, jnp.arange(block_total, dtype=jnp.int32)).reshape(NODES, D)
    summed = features.astype(jnp.float32) + jnp.dot(attended, out_weight, preferred_element_type=jnp.float32)
    root_mean = jnp.sqrt(lax.optimization_barrier(jnp.mean(summed * summed, axis=-1, keepdims=True)) + 1e-06)
    normed = summed / root_mean
    output = normed.astype(jnp.bfloat16)
    upstream = cotangent.astype(jnp.float32)
    norm_grad = (upstream - normed * lax.optimization_barrier(jnp.mean(upstream * normed, axis=-1, keepdims=True))) / root_mean
    norm_grad_low = norm_grad.astype(jnp.bfloat16)
    out_weight_grad = jnp.dot(attended.T, norm_grad_low, preferred_element_type=jnp.float32) * NODES ** (-0.5)
    attended_grad = jnp.dot(norm_grad_low, out_weight.T, preferred_element_type=jnp.float32).astype(jnp.bfloat16)
    grad_blocks = attended_grad.reshape(block_total, BLOCK, HEADS, HD)
    attended_blocks = attended.reshape(block_total, BLOCK, HEADS, HD)
    row_dots = lax.optimization_barrier(jnp.sum(grad_blocks.astype(jnp.float32) * attended_blocks.astype(jnp.float32), axis=-1))

    def block_backward(tables, index):
        key_table, value_table = tables
        chosen = key_index[index]
        slots = key_slots[index]
        key_block = keys_all[chosen]
        value_block = values_all[chosen]
        attention = block_attention(queries[index], key_block, live[index])
        attention_low = attention.astype(jnp.bfloat16).reshape(HEADS, BLOCK, PER, BLOCK)
        prob_grad = jnp.einsum('qhd,pkhd->hqpk', grad_blocks[index].astype(jnp.float32), value_block.astype(jnp.float32))
        prob_grad = prob_grad.reshape(HEADS, BLOCK, PER * BLOCK)
        score_grad = attention * (prob_grad - jnp.transpose(row_dots[index])[:, :, None]) * score_scale
        score_grad = score_grad.astype(jnp.bfloat16).reshape(HEADS, BLOCK, PER, BLOCK).astype(jnp.float32)
        query_grad = jnp.einsum('hqpk,pkhd->qhd', score_grad, key_block.astype(jnp.float32))
        key_grad = jnp.einsum('hqpk,qhd->pkhd', score_grad, queries[index].astype(jnp.float32))
        value_grad = jnp.einsum('hqpk,qhd->pkhd', attention_low.astype(jnp.float32), grad_blocks[index].astype(jnp.float32))
        return ((key_table.at[slots].add(key_grad), value_table.at[slots].add(value_grad)), query_grad.astype(jnp.bfloat16))

    def partition_backward(carry, rank):
        key_sums, value_sums = carry
        blank_table = jnp.zeros((table_size, BLOCK, HEADS, HD), jnp.float32)
        indices = rank * BLK + jnp.arange(BLK, dtype=jnp.int32)
        (key_table, value_table), query_grads = lax.scan(block_backward, (blank_table, blank_table), indices)
        remote_keys = lax.optimization_barrier(key_table[BLK:].astype(jnp.bfloat16)).astype(jnp.float32)
        remote_values = lax.optimization_barrier(value_table[BLK:].astype(jnp.bfloat16)).astype(jnp.float32)
        targets = (jnp.arange(N_NODE, dtype=jnp.int32)[:, None] * BLK + wanted[rank]).reshape(-1).astype(jnp.int32)
        key_sums = key_sums.at[indices].add(key_table[:BLK]).at[targets].add(remote_keys)
        value_sums = value_sums.at[indices].add(value_table[:BLK]).at[targets].add(remote_values)
        return ((key_sums, value_sums), query_grads)
    blank = jnp.zeros((block_total, BLOCK, HEADS, HD), jnp.float32)
    (key_sums, value_sums), query_grads = lax.scan(partition_backward, (blank, blank), jnp.arange(N_NODE, dtype=jnp.int32))
    query_grads = query_grads.reshape(block_total, BLOCK, HEADS, HD)
    projected_grad = jnp.stack([query_grads, key_sums.astype(jnp.bfloat16), value_sums.astype(jnp.bfloat16)], axis=3)
    projected_grad = projected_grad.reshape(NODES, 3 * D)
    feature_grad = (norm_grad + jnp.dot(projected_grad, in_weight.T, preferred_element_type=jnp.float32)).astype(jnp.bfloat16)
    in_weight_grad = jnp.dot(features.T, projected_grad, preferred_element_type=jnp.float32) * NODES ** (-0.5)
    return (output, feature_grad, in_weight_grad, out_weight_grad)
```

```python
import functools
import math

import jax
import jax.numpy as jnp
from jax import lax
from jax.experimental import pallas as pl
from jax.experimental.pallas import tpu as pltpu
from jax.sharding import PartitionSpec as P

HEADS = 4
HD = 64
BLOCK = 128
BLK = 16
PER = 12
CAP = 2
D = 256
PAIRS = BLK // 2
SCALE = HD ** (-0.5)
SCALE_LOG2E = SCALE * math.log2(math.e)
BF16 = jnp.bfloat16
F32 = jnp.float32
MIB = 1 << 20
LAST = (((1,), (1,)), ((), ()))


def dot(a, b):
    return jnp.dot(a, b, preferred_element_type=F32)


def dot_last(a, b):
    return lax.dot_general(a, b, LAST, preferred_element_type=F32)


def span(start, size):
    return pl.ds(pl.multiple_of(start, size), size)


def smem():
    return pl.BlockSpec(memory_space=pltpu.SMEM)


def vmem():
    return pl.BlockSpec(memory_space=pltpu.VMEM)


def call(kernel, name, outs, in_specs, limit, flops=0, scratch=()):
    return pl.pallas_call(
        kernel,
        name=name,
        out_shape=tuple(jax.ShapeDtypeStruct(shape, kind) for shape, kind in outs),
        in_specs=in_specs,
        out_specs=tuple(vmem() for _ in outs),
        scratch_shapes=scratch,
        compiler_params=pltpu.CompilerParams(vmem_limit_bytes=limit),
        cost_estimate=pl.CostEstimate(flops=flops, bytes_accessed=4 * MIB, transcendentals=0),
    )


def project_kernel(head_ref, req_ref, x0, x1, x2, x3, w_ref, qz_ref, kv_ref, out_ref):
    head = head_ref[0]
    rows = x0.shape[0]
    for part, x_ref in enumerate((x0, x1, x2, x3)):
        at = span((head ^ part) * rows, rows)
        y = dot(x_ref[...], w_ref[...]).astype(BF16)
        qz_ref[at, :] = y[:, :BLOCK]
        kv_ref[at, :] = y[:, BLOCK:]

    @pl.loop(0, out_ref.shape[0])
    def _(i):
        out_ref[i] = kv_ref[span(req_ref[i] * BLOCK, BLOCK), :]


def transpose_kernel(head_ref, x0, x1, x2, x3, kv_ref, xt_ref, kvt_ref):
    head = head_ref[0]
    rows = x0.shape[0]
    for part, x_ref in enumerate((x0, x1, x2, x3)):
        at = span((head ^ part) * rows, rows)
        xt_ref[:, at] = x_ref[...].T
    for i in range(BLK):
        kvt_ref[i] = kv_ref[i * BLOCK : (i + 1) * BLOCK, :].T


def forward_kernel(
    slot_ref, count_ref, qz_ref, kv_ref, kvt_ref, inc_ref,
    att_ref, attt_ref, table_ref, tablet_ref, top_ref, inv_ref,
):
    for i in range(BLK):
        table_ref[i] = kv_ref[i * BLOCK : (i + 1) * BLOCK, :]
        tablet_ref[i] = kvt_ref[i]

    @pl.loop(0, inc_ref.shape[0])
    def _(i):
        block = inc_ref[i]
        table_ref[BLK + i] = block
        tablet_ref[BLK + i] = block.T

    def one(i):
        slots = [slot_ref[i * PER + j] for j in range(PER)]
        count = count_ref[i]
        keys = jnp.concatenate([table_ref[s] for s in slots], axis=0)
        raw = dot_last(keys, qz_ref[span(i * BLOCK, BLOCK), :])
        raw = jnp.concatenate(
            [
                jnp.where(j < count, raw[j * BLOCK : (j + 1) * BLOCK], -1e30)
                for j in range(PER)
            ],
            axis=0,
        )
        top = jnp.max(raw, axis=0, keepdims=True)
        raised = jnp.exp2((raw - top) * SCALE_LOG2E)
        inverse = 1.0 / jnp.sum(raised, axis=0, keepdims=True)
        low = (raised * inverse).astype(BF16)
        values = jnp.concatenate([tablet_ref[s, HD:, :] for s in slots], axis=1)
        result = dot(values, low)
        attt_ref[:, span(i * BLOCK, BLOCK)] = result.astype(BF16)
        top_ref[i] = jnp.broadcast_to(top, (8, BLOCK))
        inv_ref[i] = jnp.broadcast_to(inverse, (8, BLOCK))
        return result

    @pl.loop(0, PAIRS)
    def _(t):
        first = one(2 * t)
        second = one(2 * t + 1)
        both = jnp.concatenate([first, second], axis=0)
        att_ref[span(t * BLOCK, BLOCK), :] = both.T.astype(BF16)


def middle_kernel(
    head_ref, x0, x1, x2, x3, c0, c1, c2, c3, a0, a1, a2, a3, attt_ref, w_ref,
    out_ref, grad_ref, gz_ref, dots_ref, owg_ref, wide_ref, pad_ref,
):
    head = head_ref[0]
    rows = x0.shape[0]
    own_w = w_ref[span(head * HD, HD), :]
    wide_ref[...] = jnp.zeros_like(wide_ref)
    for part in range(4):
        piece = w_ref[span((head ^ part) * HD, HD), :]
        at = (2 * part) * HD
        wide_ref[at : at + HD, :D] = piece
        wide_ref[at + HD : at + 2 * HD, D:] = piece
    pad_ref[:HD, :] = jnp.zeros((HD, D), BF16)
    pad_ref[HD:, :] = own_w
    a_refs = (a0, a1, a2, a3)
    owg = jnp.zeros((HD, D), F32)
    for part, (x_ref, c_ref) in enumerate(zip((x0, x1, x2, x3), (c0, c1, c2, c3))):
        group = head ^ part
        for pair in range(rows // (2 * BLOCK)):
            t = group * (rows // (2 * BLOCK)) + pair
            lhs = jnp.concatenate([a[span(t * BLOCK, BLOCK), :] for a in a_refs], axis=1)
            product = dot(lhs, wide_ref[...])
            for half in range(2):
                local = (2 * pair + half) * BLOCK
                block = 2 * t + half
                at = span(block * BLOCK, BLOCK)
                summed = x_ref[local : local + BLOCK, :].astype(F32) + product[:, half * D : (half + 1) * D]
                inverse = lax.rsqrt(jnp.mean(summed * summed, axis=-1, keepdims=True) + 1e-06)
                normed = summed * inverse
                upstream = c_ref[local : local + BLOCK, :].astype(F32)
                grad = (upstream - normed * jnp.mean(upstream * normed, axis=-1, keepdims=True)) * inverse
                low = grad.astype(BF16)
                if part == 0:
                    out_ref[local : local + BLOCK, :] = normed.astype(BF16)
                    grad_ref[local : local + BLOCK, :] = grad
                gz_ref[at, :] = dot_last(low, pad_ref[...]).astype(BF16)
                turned = dot_last(own_w, low).astype(BF16).astype(F32)
                attended = attt_ref[:, at]
                sums = jnp.sum(turned * attended.astype(F32), axis=0, keepdims=True)
                dots_ref[block] = jnp.broadcast_to(sums, (8, BLOCK))
                owg += dot(attended, low)
    owg_ref[...] = owg


def backward_kernel(
    slot_ref, count_ref, qz_ref, gz_ref, table_ref, tablet_ref, top_ref, inv_ref, dots_ref,
    own_ref, leave_ref, dq_ref, dqt_ref, acc_ref,
):
    acc_ref[...] = jnp.zeros_like(acc_ref)

    def one(i):
        slots = [slot_ref[i * PER + j] for j in range(PER)]
        count = count_ref[i]
        at = span(i * BLOCK, BLOCK)
        keys = jnp.concatenate([table_ref[s] for s in slots], axis=0)
        rows = jnp.concatenate([qz_ref[at, :], gz_ref[at, :]], axis=0)
        both = dot_last(keys, rows)
        top = top_ref[i, :1, :]
        inverse = inv_ref[i, :1, :]
        dots = dots_ref[i, :1, :]
        weights, grads = [], []
        for j in range(PER):
            here = both[j * BLOCK : (j + 1) * BLOCK]
            weight = jnp.exp2((here[:, :BLOCK] - top) * SCALE_LOG2E) * inverse
            weight = jnp.where(j < count, weight, 0.0)
            weights.append(weight.astype(BF16))
            grads.append((weight * (here[:, BLOCK:] - dots) * SCALE).astype(BF16))
        score_grad = jnp.concatenate(grads, axis=0)
        low = jnp.concatenate(weights, axis=0)
        pair_grads = dot(jnp.concatenate([score_grad, low], axis=1), rows)
        for j in range(PER):
            acc_ref[slots[j]] += pair_grads[j * BLOCK : (j + 1) * BLOCK]
        turned = jnp.concatenate([tablet_ref[s, :HD, :] for s in slots], axis=1)
        result = dot(turned, score_grad)
        dqt_ref[:, at] = result.astype(BF16)
        return result

    @pl.loop(0, PAIRS)
    def _(t):
        first = one(2 * t)
        second = one(2 * t + 1)
        both = jnp.concatenate([first, second], axis=0)
        dq_ref[span(t * BLOCK, BLOCK), :] = both.T.astype(BF16)

    own_ref[...] = acc_ref[:BLK]

    @pl.loop(0, leave_ref.shape[0])
    def _(i):
        leave_ref[i] = acc_ref[BLK + i].astype(BF16)


def query_weight_kernel(head_ref, dqt_ref, x0, x1, x2, x3, out_ref):
    head = head_ref[0]
    rows = x0.shape[0]
    total = jnp.zeros((HD, D), F32)
    for part, x_ref in enumerate((x0, x1, x2, x3)):
        total += dot(dqt_ref[:, span((head ^ part) * rows, rows)], x_ref[...])
    out_ref[...] = total


def collect_kernel(req_ref, own_ref, back_ref, xt_ref, kvg_ref, wg_ref, sum_ref):
    sum_ref[...] = own_ref[...]

    @pl.loop(0, back_ref.shape[0])
    def _(i):
        sum_ref[req_ref[i]] += back_ref[i].astype(F32)

    for i in range(BLK):
        kvg_ref[i * BLOCK : (i + 1) * BLOCK, :] = sum_ref[i].astype(BF16)
    wg_ref[...] = dot(xt_ref[...], kvg_ref[...])


def finish_kernel(grad_ref, dq_ref, kv_ref, wq_ref, wkv_ref, out_ref):
    rows = out_ref.shape[0]
    kv = jnp.concatenate([kv_ref[g] for g in range(4)], axis=1)
    base = grad_ref[...] + dot(kv, wkv_ref[...])
    for pair in range(rows // (2 * BLOCK)):
        lhs = jnp.concatenate(
            [dq_ref[g, pair * BLOCK : (pair + 1) * BLOCK, :] for g in range(4)], axis=1
        )
        product = dot(lhs, wq_ref[...])
        for half in range(2):
            at = (2 * pair + half) * BLOCK
            out_ref[at : at + BLOCK, :] = (
                base[at : at + BLOCK] + product[:, half * D : (half + 1) * D]
            ).astype(BF16)


def on_device(features, in_weight, out_weight, cotangent, key_slots, block_count, wanted):
    head_count = lax.axis_size("head")
    node_count = lax.axis_size("node")
    rows = features.shape[0]
    node_rows = rows * head_count
    total_nodes = node_rows * node_count
    remote = node_count * CAP
    table_size = BLK + remote
    limit = (14 + table_size // 4) * MIB
    head = lax.axis_index("head")
    head_word = head.astype(jnp.int32).reshape(1)

    def swap(value, axis, mask):
        size = lax.axis_size(axis)
        return lax.ppermute(value, axis, [(i, i ^ mask) for i in range(size)])

    def gather_heads(value):
        across = swap(value, "head", 2)
        beside = swap(value, "head", 1)
        return (value, beside, across, swap(across, "head", 1))

    def add_nodes(value):
        mask = 1
        while mask < node_count:
            value = value + swap(value, "node", mask)
            mask *= 2
        return value

    xs = gather_heads(features)
    requests = lax.all_to_all(
        wanted.reshape(node_count, CAP), "node", split_axis=0, concat_axis=0, tiled=True
    ).reshape(-1)
    own_in = lax.dynamic_slice(in_weight, (0, head * (3 * HD)), (D, 3 * HD))
    wide_in = jnp.concatenate([own_in[:, :HD], jnp.zeros((D, HD), BF16), own_in[:, HD:]], axis=1)
    in_turned = in_weight.T.reshape(HEADS, 3 * HD, D)
    wkv = in_turned[:, HD:].reshape(HEADS * 2 * HD, D)
    wq = in_turned[:, :HD]
    blank = jnp.zeros_like(wq)
    wq = jnp.stack(
        [jnp.concatenate([wq, blank], axis=2), jnp.concatenate([blank, wq], axis=2)], axis=1
    ).reshape(HEADS * 2 * HD, 2 * D)
    slots = key_slots.reshape(-1)

    qz, kv, outgoing = call(
        project_kernel,
        "project",
        [
            ((node_rows, BLOCK), BF16),
            ((node_rows, BLOCK), BF16),
            ((remote, BLOCK, BLOCK), BF16),
        ],
        [smem(), smem()] + [vmem()] * 5,
        limit,
        flops=2 * node_rows * D * D,
    )(head_word, requests, *xs, wide_in)
    incoming = lax.all_to_all(outgoing, "node", split_axis=0, concat_axis=0, tiled=True)
    cs = gather_heads(cotangent)
    xt, kvt = call(
        transpose_kernel,
        "transpose",
        [((D, node_rows), BF16), ((BLK, BLOCK, BLOCK), BF16)],
        [smem()] + [vmem()] * 5,
        limit,
        flops=2 * node_rows * D * D,
    )(head_word, *xs, kv)
    att, attt, table, tablet, top, inv = call(
        forward_kernel,
        "forward",
        [
            ((PAIRS * BLOCK, BLOCK), BF16),
            ((HD, node_rows), BF16),
            ((table_size, BLOCK, BLOCK), BF16),
            ((table_size, BLOCK, BLOCK), BF16),
            ((BLK, 8, BLOCK), F32),
            ((BLK, 8, BLOCK), F32),
        ],
        [smem(), smem()] + [vmem()] * 4,
        limit,
        flops=4 * node_rows * PER * BLOCK * BLOCK,
    )(slots, block_count, qz, kv, kvt, incoming)
    parts = gather_heads(att)
    output, norm_grad, gz, dots, owg = call(
        middle_kernel,
        "middle",
        [
            ((rows, D), BF16),
            ((rows, D), F32),
            ((node_rows, BLOCK), BF16),
            ((BLK, 8, BLOCK), F32),
            ((HD, D), F32),
        ],
        [smem()] + [vmem()] * 14,
        limit,
        flops=8 * node_rows * D * D,
        scratch=[pltpu.VMEM((2 * D, 2 * D), BF16), pltpu.VMEM((BLOCK, D), BF16)],
    )(head_word, *xs, *cs, *parts, attt, out_weight)
    own, leaving, dq, dqt = call(
        backward_kernel,
        "backward",
        [
            ((BLK, BLOCK, BLOCK), F32),
            ((remote, BLOCK, BLOCK), BF16),
            ((PAIRS * BLOCK, BLOCK), BF16),
            ((HD, node_rows), BF16),
        ],
        [smem(), smem()] + [vmem()] * 7,
        limit,
        flops=10 * node_rows * PER * BLOCK * BLOCK,
        scratch=[pltpu.VMEM((table_size, BLOCK, BLOCK), F32)],
    )(slots, block_count, qz, gz, table, tablet, top, inv, dots)
    returned = lax.all_to_all(leaving, "node", split_axis=0, concat_axis=0, tiled=True)
    dq_rows = lax.all_to_all(
        dq.reshape(head_count, rows // 2, BLOCK), "head", split_axis=0, concat_axis=0, tiled=True
    )
    (query_wg,) = call(
        query_weight_kernel,
        "query_weight",
        [((HD, D), F32)],
        [smem()] + [vmem()] * 5,
        limit,
        flops=2 * node_rows * D * HD,
    )(head_word, dqt, *xs)
    kvg, pair_wg = call(
        collect_kernel,
        "collect",
        [((node_rows, BLOCK), BF16), ((D, BLOCK), F32)],
        [smem()] + [vmem()] * 3,
        limit,
        flops=2 * node_rows * D * BLOCK,
        scratch=[pltpu.VMEM((BLK, BLOCK, BLOCK), F32)],
    )(requests, own, returned, xt)
    kv_rows = lax.all_to_all(
        kvg.reshape(head_count, rows, BLOCK), "head", split_axis=0, concat_axis=0, tiled=True
    )
    (feature_grad,) = call(
        finish_kernel,
        "finish",
        [((rows, D), BF16)],
        [vmem()] * 5,
        limit,
        flops=4 * rows * 3 * D * D,
    )(norm_grad, dq_rows, kv_rows, wq, wkv)
    owg = add_nodes(owg)
    query_wg = add_nodes(query_wg)
    pair_wg = add_nodes(pair_wg)
    grad_factor = total_nodes ** (-0.5)
    return (
        output,
        feature_grad,
        jnp.concatenate([query_wg.T, pair_wg], axis=1) * grad_factor,
        owg * grad_factor,
    )


def solution(mesh):
    placed = (
        P(("node", "head"), None),
        P(),
        P(),
        P(("node", "head"), None),
        P("node", None),
        P("node"),
        P("node", None, None),
    )
    return jax.shard_map(
        on_device,
        mesh=mesh,
        in_specs=placed,
        out_specs=(
            P(("node", "head"), None),
            P(("node", "head"), None),
            P(None, "head"),
            P("head", None),
        ),
        check_vma=False,
    )
```

```python
import functools
import math

import jax
import jax.numpy as jnp
from jax import lax
from jax.experimental import pallas as pl
from jax.experimental.pallas import tpu as pltpu
from jax.sharding import PartitionSpec as P

HEADS = 4
HD = 64
BLOCK = 128
BLK = 16
PER = 12
CAP = 2
D = 256
PAIRS = BLK // 2
SCALE = HD ** (-0.5)
SCALE_LOG2E = SCALE * math.log2(math.e)
BF16 = jnp.bfloat16
F32 = jnp.float32
MIB = 1 << 20
LAST = (((1,), (1,)), ((), ()))


def dot(a, b):
    return jnp.dot(a, b, preferred_element_type=F32)


def dot_last(a, b):
    return lax.dot_general(a, b, LAST, preferred_element_type=F32)


def span(start, size):
    return pl.ds(pl.multiple_of(start, size), size)


def smem():
    return pl.BlockSpec(memory_space=pltpu.SMEM)


def vmem():
    return pl.BlockSpec(memory_space=pltpu.VMEM)


def call(kernel, name, outs, in_specs, limit, flops=0, scratch=()):
    return pl.pallas_call(
        kernel,
        name=name,
        out_shape=tuple(jax.ShapeDtypeStruct(shape, kind) for shape, kind in outs),
        in_specs=in_specs,
        out_specs=tuple(vmem() for _ in outs),
        scratch_shapes=scratch,
        compiler_params=pltpu.CompilerParams(vmem_limit_bytes=limit),
        cost_estimate=pl.CostEstimate(flops=flops, bytes_accessed=4 * MIB, transcendentals=0),
    )


def project_kernel(count, place_ref, *refs):
    wanted_refs, refs = refs[:count], refs[count:]
    x_refs, in_ref, refs = refs[:4], refs[4], refs[5:]
    qz_ref, kv_ref, refs = refs[0], refs[1], refs[2:]
    out_refs, wide_ref = refs[:count], refs[count]
    head, node = place_ref[0], place_ref[1]
    rows = x_refs[0].shape[0]
    wide_ref[:, HD:BLOCK] = jnp.zeros((D, HD), BF16)
    for g in range(HEADS):

        @pl.when(head == g)
        def _():
            at = g * 3 * HD
            wide_ref[:, :HD] = in_ref[:, at : at + HD]
            wide_ref[:, BLOCK:] = in_ref[:, at + HD : at + 3 * HD]

    for part in range(4):
        at = span((head ^ part) * rows, rows)
        y = dot(x_refs[part][...], wide_ref[...]).astype(BF16)
        qz_ref[at, :] = y[:, :BLOCK]
        kv_ref[at, :] = y[:, BLOCK:]
    for m in range(count):
        for c in range(CAP):
            block = wanted_refs[m][node * CAP + c]
            out_refs[m][c] = kv_ref[span(block * BLOCK, BLOCK), :]


def prepare_kernel(place_ref, x0, x1, x2, x3, kv_ref, in_ref, xt_ref, kvt_ref, wkv_ref, wq_ref, k_ref, q_ref):
    head = place_ref[0]
    rows = x0.shape[0]
    for part, x_ref in enumerate((x0, x1, x2, x3)):
        xt_ref[:, span((head ^ part) * rows, rows)] = x_ref[...].T
    for i in range(BLK):
        kvt_ref[i] = kv_ref[i * BLOCK : (i + 1) * BLOCK, :].T
    blank = jnp.zeros((D, HD), BF16)
    for g in range(HEADS):
        at = g * 3 * HD
        query = in_ref[:, at : at + HD]
        k_ref[g] = in_ref[:, at + HD : at + 3 * HD]
        q_ref[g, :D] = jnp.concatenate([query, blank], axis=1)
        q_ref[g, D:] = jnp.concatenate([blank, query], axis=1)
    for part in range(4):
        lanes = slice(part * BLOCK, (part + 1) * BLOCK)
        wkv_ref[:, lanes] = k_ref[head ^ part]
        wq_ref[:, lanes] = q_ref[head ^ part]


def forward_kernel(count, place_ref, slot_ref, count_ref, qz_ref, kv_ref, kvt_ref, *refs):
    in_refs, refs = refs[:count], refs[count:]
    att_ref, attt_ref, table_ref, tablet_ref, top_ref, inv_ref, even_ref, odd_ref = refs
    node = place_ref[1]
    for i in range(BLK):
        table_ref[i] = kv_ref[i * BLOCK : (i + 1) * BLOCK, :]
        tablet_ref[i] = kvt_ref[i]
    for m in range(count):
        for c in range(CAP):
            block = in_refs[m][c]
            at = BLK + (node ^ m) * CAP + c
            table_ref[at] = block
            tablet_ref[at] = block.T

    def slots_of(i):
        return [slot_ref[i, j] for j in range(PER)]

    def score(i, raw_ref):
        live = count_ref[i]
        keys = jnp.concatenate([table_ref[s] for s in slots_of(i)], axis=0)
        raw = dot_last(keys, qz_ref[span(i * BLOCK, BLOCK), :])
        top = None
        for j in range(PER):
            here = jnp.where(j < live, raw[j * BLOCK : (j + 1) * BLOCK], -1e30)
            raw_ref[j * BLOCK : (j + 1) * BLOCK, :] = here
            here = here.reshape(BLOCK // 8, 8, BLOCK)
            highest = jnp.max(here, axis=0)
            top = highest if top is None else jnp.maximum(top, highest)
        return jnp.max(top, axis=0, keepdims=True)

    def attend(i, raw_ref, top):
        total = None
        lows = []
        for j in range(PER):
            raised = jnp.exp2((raw_ref[j * BLOCK : (j + 1) * BLOCK, :] - top) * SCALE_LOG2E)
            lows.append(raised.astype(BF16))
            part = jnp.sum(raised.reshape(BLOCK // 8, 8, BLOCK), axis=0)
            total = part if total is None else total + part
        inverse = 1.0 / jnp.sum(total, axis=0, keepdims=True)
        values = jnp.concatenate([tablet_ref[s, HD:, :] for s in slots_of(i)], axis=1)
        result = dot(values, jnp.concatenate(lows, axis=0)) * inverse
        attt_ref[:, span(i * BLOCK, BLOCK)] = result.astype(BF16)
        top_ref[i] = jnp.broadcast_to(top, (8, BLOCK))
        inv_ref[i] = jnp.broadcast_to(inverse, (8, BLOCK))
        return result

    def pair(t, even_top):
        odd_top = score(2 * t + 1, odd_ref)
        first = attend(2 * t, even_ref, even_top)
        even_top = score(jnp.minimum(2 * t + 2, BLK - 1), even_ref)
        second = attend(2 * t + 1, odd_ref, odd_top)
        both = jnp.concatenate([first, second], axis=0)
        att_ref[span(t * BLOCK, BLOCK), :] = both.T.astype(BF16)
        return even_top

    lax.fori_loop(0, PAIRS, pair, score(0, even_ref))


def middle_kernel(
    place_ref, x0, x1, x2, x3, c0, c1, c2, c3, a0, a1, a2, a3, attt_ref, w_ref,
    out_ref, grad_ref, gz_ref, dots_ref, owg_ref, wide_ref, pad_ref,
):
    head = place_ref[0]
    rows = x0.shape[0]
    own_w = w_ref[span(head * HD, HD), :]
    wide_ref[...] = jnp.zeros_like(wide_ref)
    for part in range(4):
        piece = w_ref[span((head ^ part) * HD, HD), :]
        at = (2 * part) * HD
        wide_ref[at : at + HD, :D] = piece
        wide_ref[at + HD : at + 2 * HD, D:] = piece
    pad_ref[:HD, :] = jnp.zeros((HD, D), BF16)
    pad_ref[HD:, :] = own_w
    a_refs = (a0, a1, a2, a3)
    owg = jnp.zeros((HD, D), F32)
    for part, (x_ref, c_ref) in enumerate(zip((x0, x1, x2, x3), (c0, c1, c2, c3))):
        group = head ^ part
        for pair in range(rows // (2 * BLOCK)):
            t = group * (rows // (2 * BLOCK)) + pair
            lhs = jnp.concatenate([a[span(t * BLOCK, BLOCK), :] for a in a_refs], axis=1)
            product = dot(lhs, wide_ref[...])
            for half in range(2):
                local = (2 * pair + half) * BLOCK
                block = 2 * t + half
                at = span(block * BLOCK, BLOCK)
                summed = x_ref[local : local + BLOCK, :].astype(F32) + product[:, half * D : (half + 1) * D]
                inverse = lax.rsqrt(jnp.mean(summed * summed, axis=-1, keepdims=True) + 1e-06)
                normed = summed * inverse
                upstream = c_ref[local : local + BLOCK, :].astype(F32)
                grad = (upstream - normed * jnp.mean(upstream * normed, axis=-1, keepdims=True)) * inverse
                low = grad.astype(BF16)
                if part == 0:
                    out_ref[local : local + BLOCK, :] = normed.astype(BF16)
                    grad_ref[local : local + BLOCK, :] = grad
                gz_ref[at, :] = dot_last(low, pad_ref[...]).astype(BF16)
                turned = dot_last(own_w, low).astype(BF16).astype(F32)
                attended = attt_ref[:, at]
                sums = jnp.sum(turned * attended.astype(F32), axis=0, keepdims=True)
                dots_ref[block] = jnp.broadcast_to(sums, (8, BLOCK))
                owg += dot(attended, low)
    owg_ref[...] = owg


def backward_kernel(
    count, place_ref, slot_ref, count_ref, qz_ref, gz_ref, table_ref, tablet_ref, top_ref, inv_ref, dots_ref, *refs
):
    own_ref, dqt_ref, refs = refs[0], refs[1], refs[2:]
    dq_refs, leave_refs = refs[:4], refs[4 : 4 + count]
    acc_ref, dq_ref = refs[4 + count :]
    head, node = place_ref[0], place_ref[1]
    acc_ref[...] = jnp.zeros_like(acc_ref)

    def one(i):
        slots = [slot_ref[i, j] for j in range(PER)]
        live = count_ref[i]
        at = span(i * BLOCK, BLOCK)
        keys = jnp.concatenate([table_ref[s] for s in slots], axis=0)
        rows = jnp.concatenate([qz_ref[at, :], gz_ref[at, :]], axis=0)
        both = dot_last(keys, rows)
        top = top_ref[i, :1, :]
        inverse = inv_ref[i, :1, :]
        dots = dots_ref[i, :1, :]
        weights, grads = [], []
        for j in range(PER):
            here = both[j * BLOCK : (j + 1) * BLOCK]
            weight = jnp.exp2((here[:, :BLOCK] - top) * SCALE_LOG2E) * inverse
            weight = jnp.where(j < live, weight, 0.0)
            weights.append(weight.astype(BF16))
            grads.append((weight * (here[:, BLOCK:] - dots) * SCALE).astype(BF16))
        score_grad = jnp.concatenate(grads, axis=0)
        low = jnp.concatenate(weights, axis=0)
        pair_grads = dot(jnp.concatenate([score_grad, low], axis=1), rows)
        for j in range(PER):
            acc_ref[slots[j]] += pair_grads[j * BLOCK : (j + 1) * BLOCK]
        turned = jnp.concatenate([tablet_ref[s, :HD, :] for s in slots], axis=1)
        result = dot(turned, score_grad)
        dqt_ref[:, at] = result.astype(BF16)
        return result

    @pl.loop(0, PAIRS)
    def _(t):
        first = one(2 * t)
        second = one(2 * t + 1)
        both = jnp.concatenate([first, second], axis=0)
        dq_ref[span(t * BLOCK, BLOCK), :] = both.T.astype(BF16)

    own_ref[...] = acc_ref[:BLK]
    for m in range(count):
        for c in range(CAP):
            leave_refs[m][c] = acc_ref[BLK + (node ^ m) * CAP + c].astype(BF16)
    for part in range(4):
        size = dq_refs[part].shape[0]
        dq_refs[part][...] = dq_ref[span((head ^ part) * size, size), :]


def early_weight_kernel(place_ref, dqt_ref, x0, x1, x2, x3, owg_ref, out_ref):
    head = place_ref[0]
    rows = x0.shape[0]
    total = jnp.zeros((HD, D), F32)
    for part, x_ref in enumerate((x0, x1, x2, x3)):
        total += dot(dqt_ref[:, span((head ^ part) * rows, rows)], x_ref[...])
    out_ref[:HD, :] = owg_ref[...]
    out_ref[HD:, :] = total


def collect_kernel(count, place_ref, *refs):
    wanted_refs, refs = refs[:count], refs[count:]
    own_ref, xt_ref, refs = refs[0], refs[1], refs[2:]
    back_refs, refs = refs[:count], refs[count:]
    kvg_refs, wg_ref, sum_ref = refs[:4], refs[4], refs[5]
    head, node = place_ref[0], place_ref[1]
    sum_ref[...] = own_ref[...]
    for m in range(count):
        for c in range(CAP):
            sum_ref[wanted_refs[m][node * CAP + c]] += back_refs[m][c].astype(F32)
    total = jnp.zeros((D, BLOCK), F32)
    for part in range(4):
        rows = kvg_refs[part].shape[0]
        first = (head ^ part) * (rows // BLOCK)
        for i in range(rows // BLOCK):
            kvg_refs[part][i * BLOCK : (i + 1) * BLOCK, :] = sum_ref[first + i].astype(BF16)
        total += dot(xt_ref[:, span((head ^ part) * rows, rows)], kvg_refs[part][...])
    wg_ref[...] = total.T


def finish_kernel(grad_ref, d0, d1, d2, d3, k0, k1, k2, k3, wq_ref, wkv_ref, out_ref):
    rows = out_ref.shape[0]
    kv = jnp.concatenate([k[...] for k in (k0, k1, k2, k3)], axis=1)
    base = grad_ref[...] + dot_last(kv, wkv_ref[...])
    for pair in range(rows // (2 * BLOCK)):
        lhs = jnp.concatenate(
            [d[pair * BLOCK : (pair + 1) * BLOCK, :] for d in (d0, d1, d2, d3)], axis=1
        )
        product = dot_last(lhs, wq_ref[...])
        for half in range(2):
            at = (2 * pair + half) * BLOCK
            out_ref[at : at + BLOCK, :] = (
                base[at : at + BLOCK] + product[:, half * D : (half + 1) * D]
            ).astype(BF16)


def on_device(features, in_weight, out_weight, cotangent, key_slots, block_count, wanted):
    head_count = lax.axis_size("head")
    node_count = lax.axis_size("node")
    rows = features.shape[0]
    node_rows = rows * head_count
    total_nodes = node_rows * node_count
    table_size = BLK + node_count * CAP
    limit = (14 + table_size // 4) * MIB
    place = jnp.stack([lax.axis_index("head"), lax.axis_index("node")]).astype(jnp.int32)
    block_set = (CAP, BLOCK, BLOCK)

    def swap(value, axis, mask):
        size = lax.axis_size(axis)
        return lax.ppermute(value, axis, [(i, i ^ mask) for i in range(size)])

    def gather_heads(value):
        across = swap(value, "head", 2)
        beside = swap(value, "head", 1)
        return (value, beside, across, swap(across, "head", 1))

    def exchange(pieces, axis):
        moved = list(pieces)
        for mask in reversed(range(1, len(pieces))):
            moved[mask] = swap(pieces[mask], axis, mask)
        return moved

    def add_nodes(value):
        mask = 1
        while mask < node_count:
            value = value + swap(value, "node", mask)
            mask *= 2
        return value

    xs = gather_heads(features)
    wants = exchange([wanted.reshape(-1)] * node_count, "node")
    qz, kv, *outgoing = call(
        functools.partial(project_kernel, node_count),
        "project",
        [((node_rows, BLOCK), BF16)] * 2 + [(block_set, BF16)] * node_count,
        [smem()] * (1 + node_count) + [vmem()] * 5,
        limit,
        flops=2 * node_rows * D * D,
        scratch=[pltpu.VMEM((D, D), BF16)],
    )(place, *wants, *xs, in_weight)
    incoming = exchange(outgoing, "node")
    cs = gather_heads(cotangent)
    xt, kvt, wkv, wq = call(
        prepare_kernel,
        "prepare",
        [
            ((D, node_rows), BF16),
            ((BLK, BLOCK, BLOCK), BF16),
            ((D, 2 * D), BF16),
            ((2 * D, 2 * D), BF16),
        ],
        [smem()] + [vmem()] * 6,
        limit,
        flops=2 * node_rows * D * D,
        scratch=[pltpu.VMEM((HEADS, D, BLOCK), BF16), pltpu.VMEM((HEADS, 2 * D, BLOCK), BF16)],
    )(place, *xs, kv, in_weight)
    att, attt, table, tablet, top, inv = call(
        functools.partial(forward_kernel, node_count),
        "forward",
        [
            ((PAIRS * BLOCK, BLOCK), BF16),
            ((HD, node_rows), BF16),
            ((table_size, BLOCK, BLOCK), BF16),
            ((table_size, BLOCK, BLOCK), BF16),
            ((BLK, 8, BLOCK), F32),
            ((BLK, 8, BLOCK), F32),
        ],
        [smem()] * 3 + [vmem()] * (3 + node_count),
        limit,
        flops=4 * node_rows * PER * BLOCK * BLOCK,
        scratch=[pltpu.VMEM((PER * BLOCK, BLOCK), F32)] * 2,
    )(place, key_slots, block_count, qz, kv, kvt, *incoming)
    parts = gather_heads(att)
    output, norm_grad, gz, dots, owg = call(
        middle_kernel,
        "middle",
        [
            ((rows, D), BF16),
            ((rows, D), F32),
            ((node_rows, BLOCK), BF16),
            ((BLK, 8, BLOCK), F32),
            ((HD, D), F32),
        ],
        [smem()] + [vmem()] * 14,
        limit,
        flops=8 * node_rows * D * D,
        scratch=[pltpu.VMEM((2 * D, 2 * D), BF16), pltpu.VMEM((BLOCK, D), BF16)],
    )(place, *xs, *cs, *parts, attt, out_weight)
    own, dqt, *rest = call(
        functools.partial(backward_kernel, node_count),
        "backward",
        [((BLK, BLOCK, BLOCK), F32), ((HD, node_rows), BF16)]
        + [((rows // 2, BLOCK), BF16)] * 4
        + [(block_set, BF16)] * node_count,
        [smem()] * 3 + [vmem()] * 7,
        limit,
        flops=10 * node_rows * PER * BLOCK * BLOCK,
        scratch=[
            pltpu.VMEM((table_size, BLOCK, BLOCK), F32),
            pltpu.VMEM((PAIRS * BLOCK, BLOCK), BF16),
        ],
    )(place, key_slots, block_count, qz, gz, table, tablet, top, inv, dots)
    returned = exchange(rest[4:], "node")
    dq_rows = exchange(rest[:4], "head")
    (early,) = call(
        early_weight_kernel,
        "early_weight",
        [((2 * HD, D), F32)],
        [smem()] + [vmem()] * 6,
        limit,
        flops=2 * node_rows * D * HD,
    )(place, dqt, *xs, owg)
    early = add_nodes(early)
    *kvg, late = call(
        functools.partial(collect_kernel, node_count),
        "collect",
        [((rows, BLOCK), BF16)] * 4 + [((BLOCK, D), F32)],
        [smem()] * (1 + node_count) + [vmem()] * (2 + node_count),
        limit,
        flops=2 * node_rows * D * BLOCK,
        scratch=[pltpu.VMEM((BLK, BLOCK, BLOCK), F32)],
    )(place, *wants, own, xt, *returned)
    kv_rows = exchange(kvg, "head")
    (feature_grad,) = call(
        finish_kernel,
        "finish",
        [((rows, D), BF16)],
        [vmem()] * 11,
        limit,
        flops=4 * rows * 3 * D * D,
    )(norm_grad, *dq_rows, *kv_rows, wq, wkv)
    late = add_nodes(late)
    grad_factor = total_nodes ** (-0.5)
    in_grad = jnp.concatenate([early[HD:], late], axis=0) * grad_factor
    return (output, feature_grad, in_grad.T, early[:HD] * grad_factor)


def solution(mesh):
    placed = (
        P(("node", "head"), None),
        P(),
        P(),
        P(("node", "head"), None),
        P("node", None),
        P("node"),
        P("node", None, None),
    )
    return jax.shard_map(
        on_device,
        mesh=mesh,
        in_specs=placed,
        out_specs=(
            P(("node", "head"), None),
            P(("node", "head"), None),
            P(None, "head"),
            P("head", None),
        ),
        check_vma=False,
    )
```

```python
import functools
import math

import jax
import jax.numpy as jnp
from jax import lax
from jax.experimental import pallas as pl
from jax.experimental.pallas import tpu as pltpu
from jax.sharding import PartitionSpec as P

HEADS = 4
HD = 64
BLOCK = 128
BLK = 16
PER = 12
CAP = 2
D = 256
PAIRS = BLK // 2
SCALE = HD ** (-0.5)
SCALE_LOG2E = SCALE * math.log2(math.e)
BF16 = jnp.bfloat16
F32 = jnp.float32
MIB = 1 << 20
LAST = (((1,), (1,)), ((), ()))


def dot(a, b):
    return jnp.dot(a, b, preferred_element_type=F32)


def dot_last(a, b):
    return lax.dot_general(a, b, LAST, preferred_element_type=F32)


def span(start, size):
    return pl.ds(pl.multiple_of(start, size), size)


def smem():
    return pl.BlockSpec(memory_space=pltpu.SMEM)


def vmem():
    return pl.BlockSpec(memory_space=pltpu.VMEM)


def later():
    return pl.BlockSpec(memory_space=pl.ANY)


def call(kernel, name, outs, in_specs, limit, flops=0, scratch=()):
    return pl.pallas_call(
        kernel,
        name=name,
        out_shape=tuple(jax.ShapeDtypeStruct(shape, kind) for shape, kind in outs),
        in_specs=in_specs,
        out_specs=tuple(vmem() for _ in outs),
        scratch_shapes=scratch,
        compiler_params=pltpu.CompilerParams(vmem_limit_bytes=limit),
        cost_estimate=pl.CostEstimate(flops=flops, bytes_accessed=4 * MIB, transcendentals=0),
    )


def top_shift(count):
    return count.bit_length() - 3


def group_of(node, shift):
    return (node >> shift) & 3


def split(value, group, piece_refs):
    size = value.shape[0] // 4
    for g in range(4):
        for m in range(4):

            @pl.when((group ^ m) == g)
            def _():
                piece_refs[m][...] = value[g * size : (g + 1) * size, :]


def split_kernel(shift, place_ref, value_ref, *piece_refs):
    split(value_ref[...], group_of(place_ref[1], shift), piece_refs)


def join(piece_refs, group, g):
    value = piece_refs[0][...]
    for m in range(1, 4):
        value = jnp.where((group ^ m) == g, piece_refs[m][...], value)
    return value


def join_kernel(shift, place_ref, p0, p1, p2, p3, out_ref):
    group = group_of(place_ref[1], shift)
    out_ref[...] = jnp.concatenate([join((p0, p1, p2, p3), group, g) for g in range(4)], axis=0)


def result_kernel(shift, factor, place_ref, e0, e1, e2, e3, l0, l1, l2, l3, in_ref, out_ref):
    group = group_of(place_ref[1], shift)
    early = [join((e0, e1, e2, e3), group, g) * factor for g in range(4)]
    late = [join((l0, l1, l2, l3), group, g) * factor for g in range(4)]
    out_ref[...] = jnp.concatenate(early[:2], axis=0)
    in_ref[...] = jnp.concatenate(early[2:] + late, axis=0)


def project_kernel(count, place_ref, *refs):
    wanted_ref, x_refs, in_ref, refs = refs[0], refs[1:5], refs[5], refs[6:]
    qz_ref, kv_ref, refs = refs[0], refs[1], refs[2:]
    out_refs, wide_ref = refs[:count], refs[count]
    head, node = place_ref[0], place_ref[1]
    rows = x_refs[0].shape[0]
    wide_ref[:, HD:BLOCK] = jnp.zeros((D, HD), BF16)
    for g in range(HEADS):

        @pl.when(head == g)
        def _():
            at = g * 3 * HD
            wide_ref[:, :HD] = in_ref[:, at : at + HD]
            wide_ref[:, BLOCK:] = in_ref[:, at + HD : at + 3 * HD]

    for part in range(4):
        at = span((head ^ part) * rows, rows)
        y = dot(x_refs[part][...], wide_ref[...]).astype(BF16)
        qz_ref[at, :] = y[:, :BLOCK]
        kv_ref[at, :] = y[:, BLOCK:]
    for m in range(count):
        for c in range(CAP):
            block = wanted_ref[node ^ m, 0, c]
            out_refs[m][c] = kv_ref[span(block * BLOCK, BLOCK), :]


def prepare_kernel(place_ref, x0, x1, x2, x3, kv_ref, in_ref, xt_ref, kvt_ref, wkv_ref, wq_ref, k_ref, q_ref):
    head = place_ref[0]
    rows = x0.shape[0]
    for part, x_ref in enumerate((x0, x1, x2, x3)):
        xt_ref[:, span((head ^ part) * rows, rows)] = x_ref[...].T
    for i in range(BLK):
        kvt_ref[i] = kv_ref[i * BLOCK : (i + 1) * BLOCK, :].T
    blank = jnp.zeros((D, HD), BF16)
    for g in range(HEADS):
        at = g * 3 * HD
        query = in_ref[:, at : at + HD]
        k_ref[g] = in_ref[:, at + HD : at + 3 * HD]
        q_ref[g, :D] = jnp.concatenate([query, blank], axis=1)
        q_ref[g, D:] = jnp.concatenate([blank, query], axis=1)
    for part in range(4):
        lanes = slice(part * BLOCK, (part + 1) * BLOCK)
        wkv_ref[:, lanes] = k_ref[head ^ part]
        wq_ref[:, lanes] = q_ref[head ^ part]


def forward_kernel(count, place_ref, slot_ref, count_ref, qz_ref, kv_ref, kvt_ref, *refs):
    in_refs, refs = refs[:count], refs[-8:]
    att_ref, attt_ref, table_ref, tablet_ref, top_ref, inv_ref, even_ref, odd_ref = refs
    node = place_ref[1]
    for i in range(BLK):
        table_ref[i] = kv_ref[i * BLOCK : (i + 1) * BLOCK, :]
        tablet_ref[i] = kvt_ref[i]
    for m in range(count):
        for c in range(CAP):
            block = in_refs[m][c]
            at = BLK + (node ^ m) * CAP + c
            table_ref[at] = block
            tablet_ref[at] = block.T

    def slots_of(i):
        return [slot_ref[i, j] for j in range(PER)]

    def score(i, raw_ref):
        live = count_ref[i]
        keys = jnp.concatenate([table_ref[s] for s in slots_of(i)], axis=0)
        raw = dot_last(keys, qz_ref[span(i * BLOCK, BLOCK), :])
        top = None
        for j in range(PER):
            here = jnp.where(j < live, raw[j * BLOCK : (j + 1) * BLOCK], -1e30)
            raw_ref[j * BLOCK : (j + 1) * BLOCK, :] = here
            here = here.reshape(BLOCK // 8, 8, BLOCK)
            highest = jnp.max(here, axis=0)
            top = highest if top is None else jnp.maximum(top, highest)
        return jnp.max(top, axis=0, keepdims=True)

    def attend(i, raw_ref, top):
        total = None
        lows = []
        for j in range(PER):
            raised = jnp.exp2((raw_ref[j * BLOCK : (j + 1) * BLOCK, :] - top) * SCALE_LOG2E)
            lows.append(raised.astype(BF16))
            part = jnp.sum(raised.reshape(BLOCK // 8, 8, BLOCK), axis=0)
            total = part if total is None else total + part
        inverse = 1.0 / jnp.sum(total, axis=0, keepdims=True)
        values = jnp.concatenate([tablet_ref[s, HD:, :] for s in slots_of(i)], axis=1)
        result = dot(values, jnp.concatenate(lows, axis=0)) * inverse
        attt_ref[:, span(i * BLOCK, BLOCK)] = result.astype(BF16)
        top_ref[i] = jnp.broadcast_to(top, (8, BLOCK))
        inv_ref[i] = jnp.broadcast_to(inverse, (8, BLOCK))
        return result

    def pair(t, even_top):
        odd_top = score(2 * t + 1, odd_ref)
        first = attend(2 * t, even_ref, even_top)
        even_top = score(jnp.minimum(2 * t + 2, BLK - 1), even_ref)
        second = attend(2 * t + 1, odd_ref, odd_top)
        both = jnp.concatenate([first, second], axis=0)
        att_ref[span(t * BLOCK, BLOCK), :] = both.T.astype(BF16)
        return even_top

    lax.fori_loop(0, PAIRS, pair, score(0, even_ref))


def middle_kernel(
    place_ref, x0, x1, x2, x3, c0, c1, c2, c3, a0, a1, a2, a3, attt_ref, w_ref,
    out_ref, grad_ref, gz_ref, dots_ref, owg_ref, wide_ref, pad_ref,
):
    head = place_ref[0]
    rows = x0.shape[0]
    own_w = w_ref[span(head * HD, HD), :]
    wide_ref[...] = jnp.zeros_like(wide_ref)
    for part in range(4):
        piece = w_ref[span((head ^ part) * HD, HD), :]
        at = (2 * part) * HD
        wide_ref[at : at + HD, :D] = piece
        wide_ref[at + HD : at + 2 * HD, D:] = piece
    pad_ref[:HD, :] = jnp.zeros((HD, D), BF16)
    pad_ref[HD:, :] = own_w
    a_refs = (a0, a1, a2, a3)
    owg = jnp.zeros((HD, D), F32)
    for part, (x_ref, c_ref) in enumerate(zip((x0, x1, x2, x3), (c0, c1, c2, c3))):
        group = head ^ part
        for pair in range(rows // (2 * BLOCK)):
            t = group * (rows // (2 * BLOCK)) + pair
            lhs = jnp.concatenate([a[span(t * BLOCK, BLOCK), :] for a in a_refs], axis=1)
            product = dot(lhs, wide_ref[...])
            for half in range(2):
                local = (2 * pair + half) * BLOCK
                block = 2 * t + half
                at = span(block * BLOCK, BLOCK)
                summed = x_ref[local : local + BLOCK, :].astype(F32) + product[:, half * D : (half + 1) * D]
                inverse = lax.rsqrt(jnp.mean(summed * summed, axis=-1, keepdims=True) + 1e-06)
                normed = summed * inverse
                upstream = c_ref[local : local + BLOCK, :].astype(F32)
                grad = (upstream - normed * jnp.mean(upstream * normed, axis=-1, keepdims=True)) * inverse
                low = grad.astype(BF16)
                if part == 0:
                    out_ref[local : local + BLOCK, :] = normed.astype(BF16)
                    grad_ref[local : local + BLOCK, :] = grad
                gz_ref[at, :] = dot_last(low, pad_ref[...]).astype(BF16)
                turned = dot_last(own_w, low).astype(BF16).astype(F32)
                attended = attt_ref[:, at]
                sums = jnp.sum(turned * attended.astype(F32), axis=0, keepdims=True)
                dots_ref[block] = jnp.broadcast_to(sums, (8, BLOCK))
                owg += dot(attended, low)
    owg_ref[...] = owg


def backward_kernel(
    count, place_ref, slot_ref, count_ref, qz_ref, gz_ref, table_ref, tablet_ref, top_ref, inv_ref, dots_ref, *refs
):
    own_ref, dqt_ref, refs = refs[0], refs[1], refs[2:]
    dq_refs, leave_refs = refs[:4], refs[4 : 4 + count]
    acc_ref, dq_ref = refs[4 + count :]
    head, node = place_ref[0], place_ref[1]
    acc_ref[...] = jnp.zeros_like(acc_ref)

    def one(i):
        slots = [slot_ref[i, j] for j in range(PER)]
        live = count_ref[i]
        at = span(i * BLOCK, BLOCK)
        keys = jnp.concatenate([table_ref[s] for s in slots], axis=0)
        rows = jnp.concatenate([qz_ref[at, :], gz_ref[at, :]], axis=0)
        both = dot_last(keys, rows)
        top = top_ref[i, :1, :]
        inverse = inv_ref[i, :1, :]
        dots = dots_ref[i, :1, :]
        weights, grads = [], []
        for j in range(PER):
            here = both[j * BLOCK : (j + 1) * BLOCK]
            weight = jnp.exp2((here[:, :BLOCK] - top) * SCALE_LOG2E) * inverse
            weight = jnp.where(j < live, weight, 0.0)
            weights.append(weight.astype(BF16))
            grads.append((weight * (here[:, BLOCK:] - dots) * SCALE).astype(BF16))
        score_grad = jnp.concatenate(grads, axis=0)
        low = jnp.concatenate(weights, axis=0)
        pair_grads = dot(jnp.concatenate([score_grad, low], axis=1), rows)
        for j in range(PER):
            acc_ref[slots[j]] += pair_grads[j * BLOCK : (j + 1) * BLOCK]
        turned = jnp.concatenate([tablet_ref[s, :HD, :] for s in slots], axis=1)
        result = dot(turned, score_grad)
        dqt_ref[:, at] = result.astype(BF16)
        return result

    @pl.loop(0, PAIRS)
    def _(t):
        first = one(2 * t)
        second = one(2 * t + 1)
        both = jnp.concatenate([first, second], axis=0)
        dq_ref[span(t * BLOCK, BLOCK), :] = both.T.astype(BF16)

    own_ref[...] = acc_ref[:BLK]
    for m in range(count):
        for c in range(CAP):
            leave_refs[m][c] = acc_ref[BLK + (node ^ m) * CAP + c].astype(BF16)
    for part in range(4):
        size = dq_refs[part].shape[0]
        dq_refs[part][...] = dq_ref[span((head ^ part) * size, size), :]


def early_weight_kernel(count, place_ref, dqt_ref, x0, x1, x2, x3, owg_ref, *piece_refs):
    head, node = place_ref[0], place_ref[1]
    rows = x0.shape[0]
    total = jnp.zeros((HD, D), F32)
    for part, x_ref in enumerate((x0, x1, x2, x3)):
        total += dot(dqt_ref[:, span((head ^ part) * rows, rows)], x_ref[...])
    both = jnp.concatenate([owg_ref[...], total], axis=0)
    split(both, group_of(node, top_shift(count)), piece_refs)


def collect_kernel(count, place_ref, *refs):
    wanted_ref, own_ref, xt_ref, refs = refs[0], refs[1], refs[2], refs[3:]
    back_refs, refs = refs[:count], refs[-9:]
    kvg_refs, piece_refs, sum_ref = refs[:4], refs[4:8], refs[8]
    head, node = place_ref[0], place_ref[1]
    sum_ref[...] = own_ref[...]
    for m in range(count):
        for c in range(CAP):
            sum_ref[wanted_ref[node ^ m, 0, c]] += back_refs[m][c].astype(F32)
    total = jnp.zeros((D, BLOCK), F32)
    for part in range(4):
        rows = kvg_refs[part].shape[0]
        first = (head ^ part) * (rows // BLOCK)
        for i in range(rows // BLOCK):
            kvg_refs[part][i * BLOCK : (i + 1) * BLOCK, :] = sum_ref[first + i].astype(BF16)
        total += dot(xt_ref[:, span((head ^ part) * rows, rows)], kvg_refs[part][...])
    split(total.T, group_of(node, top_shift(count)), piece_refs)


def finish_kernel(grad_ref, d0, d1, d2, d3, k0, k1, k2, k3, wq_ref, wkv_ref, out_ref):
    rows = out_ref.shape[0]
    kv = jnp.concatenate([k[...] for k in (k0, k1, k2, k3)], axis=1)
    base = grad_ref[...] + dot_last(kv, wkv_ref[...])
    for pair in range(rows // (2 * BLOCK)):
        lhs = jnp.concatenate(
            [d[pair * BLOCK : (pair + 1) * BLOCK, :] for d in (d0, d1, d2, d3)], axis=1
        )
        product = dot_last(lhs, wq_ref[...])
        for half in range(2):
            at = (2 * pair + half) * BLOCK
            out_ref[at : at + BLOCK, :] = (
                base[at : at + BLOCK] + product[:, half * D : (half + 1) * D]
            ).astype(BF16)


def on_device(features, in_weight, out_weight, cotangent, key_slots, block_count, wanted):
    head_count = lax.axis_size("head")
    node_count = lax.axis_size("node")
    rows = features.shape[0]
    node_rows = rows * head_count
    total_nodes = node_rows * node_count
    table_size = BLK + node_count * CAP
    limit = (14 + table_size // 4) * MIB
    place = jnp.stack([lax.axis_index("head"), lax.axis_index("node")]).astype(jnp.int32)
    block_set = (CAP, BLOCK, BLOCK)

    def swap(value, axis, mask):
        size = lax.axis_size(axis)
        return lax.ppermute(value, axis, [(i, i ^ mask) for i in range(size)])

    def gather_heads(value):
        across = swap(value, "head", 2)
        beside = swap(value, "head", 1)
        return (value, beside, across, swap(across, "head", 1))

    def exchange(pieces, axis, unit=1):
        moved = list(pieces)
        for mask in reversed(range(1, len(pieces))):
            moved[mask] = swap(pieces[mask], axis, mask * unit)
        return moved

    def add_nodes(pieces, shift):
        moved = exchange(pieces, "node", 1 << shift)
        total = (moved[0] + moved[1]) + (moved[2] + moved[3])
        piece_rows = total.shape[0]
        if shift == 1:
            total = total + swap(total, "node", 1)
        elif shift > 1:
            lower = call(
                functools.partial(split_kernel, shift - 2),
                "split",
                [((piece_rows // 4, D), F32)] * 4,
                [smem(), vmem()],
                limit,
            )(place, total)
            (total,) = call(
                functools.partial(join_kernel, shift - 2),
                "join",
                [((piece_rows, D), F32)],
                [smem()] + [vmem()] * 4,
                limit,
            )(place, *add_nodes(lower, shift - 2))
        return exchange([total] * 4, "node", 1 << shift)

    xs = gather_heads(features)
    wants = lax.all_to_all(
        wanted.reshape(node_count, 1, CAP), "node", split_axis=0, concat_axis=0, tiled=True
    )
    qz, kv, *outgoing = call(
        functools.partial(project_kernel, node_count),
        "project",
        [((node_rows, BLOCK), BF16)] * 2 + [(block_set, BF16)] * node_count,
        [smem()] * 2 + [vmem()] * 5,
        limit,
        flops=2 * node_rows * D * D,
        scratch=[pltpu.VMEM((D, D), BF16)],
    )(place, wants, *xs, in_weight)
    incoming = exchange(outgoing, "node")
    cs = gather_heads(cotangent)
    xt, kvt, wkv, wq = call(
        prepare_kernel,
        "prepare",
        [
            ((D, node_rows), BF16),
            ((BLK, BLOCK, BLOCK), BF16),
            ((D, 2 * D), BF16),
            ((2 * D, 2 * D), BF16),
        ],
        [smem()] + [vmem()] * 6,
        limit,
        flops=2 * node_rows * D * D,
        scratch=[pltpu.VMEM((HEADS, D, BLOCK), BF16), pltpu.VMEM((HEADS, 2 * D, BLOCK), BF16)],
    )(place, *xs, kv, in_weight)
    att, attt, table, tablet, top, inv = call(
        functools.partial(forward_kernel, node_count),
        "forward",
        [
            ((PAIRS * BLOCK, BLOCK), BF16),
            ((HD, node_rows), BF16),
            ((table_size, BLOCK, BLOCK), BF16),
            ((table_size, BLOCK, BLOCK), BF16),
            ((BLK, 8, BLOCK), F32),
            ((BLK, 8, BLOCK), F32),
        ],
        [smem()] * 3 + [vmem()] * (3 + node_count) + [later()] * 3,
        limit,
        flops=4 * node_rows * PER * BLOCK * BLOCK,
        scratch=[pltpu.VMEM((PER * BLOCK, BLOCK), F32)] * 2,
    )(place, key_slots, block_count, qz, kv, kvt, *incoming, *cs[1:])
    parts = gather_heads(att)
    output, norm_grad, gz, dots, owg = call(
        middle_kernel,
        "middle",
        [
            ((rows, D), BF16),
            ((rows, D), F32),
            ((node_rows, BLOCK), BF16),
            ((BLK, 8, BLOCK), F32),
            ((HD, D), F32),
        ],
        [smem()] + [vmem()] * 14,
        limit,
        flops=8 * node_rows * D * D,
        scratch=[pltpu.VMEM((2 * D, 2 * D), BF16), pltpu.VMEM((BLOCK, D), BF16)],
    )(place, *xs, *cs, *parts, attt, out_weight)
    own, dqt, *rest = call(
        functools.partial(backward_kernel, node_count),
        "backward",
        [((BLK, BLOCK, BLOCK), F32), ((HD, node_rows), BF16)]
        + [((rows // 2, BLOCK), BF16)] * 4
        + [(block_set, BF16)] * node_count,
        [smem()] * 3 + [vmem()] * 7,
        limit,
        flops=10 * node_rows * PER * BLOCK * BLOCK,
        scratch=[
            pltpu.VMEM((table_size, BLOCK, BLOCK), F32),
            pltpu.VMEM((PAIRS * BLOCK, BLOCK), BF16),
        ],
    )(place, key_slots, block_count, qz, gz, table, tablet, top, inv, dots)
    returned = exchange(rest[4:], "node")
    dq_rows = exchange(rest[:4], "head")
    shift = top_shift(node_count)
    piece = ((HD // 2, D), F32)
    early = call(
        functools.partial(early_weight_kernel, node_count),
        "early_weight",
        [piece] * 4,
        [smem()] + [vmem()] * 6,
        limit,
        flops=2 * node_rows * D * HD,
    )(place, dqt, *xs, owg)
    early = add_nodes(early, shift)
    collected = call(
        functools.partial(collect_kernel, node_count),
        "collect",
        [((rows, BLOCK), BF16)] * 4 + [piece] * 4,
        [smem()] * 2 + [vmem()] * (2 + node_count) + [later()] * 7,
        limit,
        flops=2 * node_rows * D * BLOCK,
        scratch=[pltpu.VMEM((BLK, BLOCK, BLOCK), F32)],
    )(place, wants, own, xt, *returned, *dq_rows[1:], *early)
    kvg, late = collected[:4], collected[4:]
    kv_rows = exchange(kvg, "head")
    (feature_grad,) = call(
        finish_kernel,
        "finish",
        [((rows, D), BF16)],
        [vmem()] * 11,
        limit,
        flops=4 * rows * 3 * D * D,
    )(norm_grad, *dq_rows, *kv_rows, wq, wkv)
    late = add_nodes(late, shift)
    in_grad, out_grad = call(
        functools.partial(result_kernel, shift, total_nodes ** (-0.5)),
        "result",
        [((3 * HD, D), F32), ((HD, D), F32)],
        [smem()] + [vmem()] * 8,
        limit,
    )(place, *early, *late)
    return (output, feature_grad, in_grad.T, out_grad)


def solution(mesh):
    placed = (
        P(("node", "head"), None),
        P(),
        P(),
        P(("node", "head"), None),
        P("node", None),
        P("node"),
        P("node", None, None),
    )
    return jax.shard_map(
        on_device,
        mesh=mesh,
        in_specs=placed,
        out_specs=(
            P(("node", "head"), None),
            P(("node", "head"), None),
            P(None, "head"),
            P("head", None),
        ),
        check_vma=False,
    )
```

```python
import functools
import math

import jax
import jax.numpy as jnp
from jax import lax
from jax.experimental import pallas as pl
from jax.experimental.pallas import tpu as pltpu
from jax.sharding import PartitionSpec as P

HEADS = 4
HD = 64
BLOCK = 128
BLK = 16
PER = 12
CAP = 2
D = 256
PAIRS = BLK // 2
SCALE = HD ** (-0.5)
SCALE_LOG2E = SCALE * math.log2(math.e)
BF16 = jnp.bfloat16
F32 = jnp.float32
MIB = 1 << 20
LAST = (((1,), (1,)), ((), ()))


def dot(a, b):
    return jnp.dot(a, b, preferred_element_type=F32)


def dot_last(a, b):
    return lax.dot_general(a, b, LAST, preferred_element_type=F32)


def span(start, size):
    return pl.ds(pl.multiple_of(start, size), size)


def smem():
    return pl.BlockSpec(memory_space=pltpu.SMEM)


def vmem():
    return pl.BlockSpec(memory_space=pltpu.VMEM)


def later():
    return pl.BlockSpec(memory_space=pl.ANY)


def call(kernel, name, outs, in_specs, limit, flops=0, scratch=()):
    return pl.pallas_call(
        kernel,
        name=name,
        out_shape=tuple(jax.ShapeDtypeStruct(shape, kind) for shape, kind in outs),
        in_specs=in_specs,
        out_specs=tuple(vmem() for _ in outs),
        scratch_shapes=scratch,
        compiler_params=pltpu.CompilerParams(vmem_limit_bytes=limit),
        cost_estimate=pl.CostEstimate(flops=flops, bytes_accessed=4 * MIB, transcendentals=0),
    )


def top_shift(count):
    return count.bit_length() - 3


def group_of(node, shift):
    return (node >> shift) & 3


def split(value, group, piece_refs):
    size = value.shape[0] // 4
    for g in range(4):
        for m in range(4):

            @pl.when((group ^ m) == g)
            def _():
                piece_refs[m][...] = value[g * size : (g + 1) * size, :]


def split_kernel(shift, place_ref, value_ref, *piece_refs):
    split(value_ref[...], group_of(place_ref[1], shift), piece_refs)


def join(piece_refs, group, g):
    value = piece_refs[0][...]
    for m in range(1, 4):
        value = jnp.where((group ^ m) == g, piece_refs[m][...], value)
    return value


def join_kernel(shift, place_ref, p0, p1, p2, p3, out_ref):
    group = group_of(place_ref[1], shift)
    out_ref[...] = jnp.concatenate([join((p0, p1, p2, p3), group, g) for g in range(4)], axis=0)


def result_kernel(shift, factor, place_ref, owg_ref, l0, l1, l2, l3, in_ref, out_ref):
    group = group_of(place_ref[1], shift)
    out_ref[...] = owg_ref[...] * factor
    in_ref[...] = jnp.concatenate([join((l0, l1, l2, l3), group, g) for g in range(4)], axis=0) * factor


def project_kernel(place_ref, x_ref, in_ref, *refs):
    q_refs, kv_refs = refs[:4], refs[4:8]
    wq_ref, wkv_ref, q_ref, k_ref = refs[8:]
    head = place_ref[0]
    blank = jnp.zeros((D, HD), BF16)
    for g in range(HEADS):
        at = g * 3 * HD
        query = in_ref[:, at : at + HD]
        k_ref[g] = in_ref[:, at + HD : at + 3 * HD]
        q_ref[g, :D] = jnp.concatenate([query, blank], axis=1)
        q_ref[g, D:] = jnp.concatenate([blank, query], axis=1)
    for part in range(4):
        lanes = slice(part * BLOCK, (part + 1) * BLOCK)
        wkv_ref[:, lanes] = k_ref[head ^ part]
        wq_ref[:, lanes] = q_ref[head ^ part]
    kv = dot(x_ref[...], wkv_ref[...]).astype(BF16)
    for part in range(4):
        kv_refs[part][...] = kv[:, part * BLOCK : (part + 1) * BLOCK]
    for pair in range(x_ref.shape[0] // (2 * BLOCK)):
        at = 2 * pair * BLOCK
        lhs = jnp.concatenate(
            [x_ref[at : at + BLOCK, :], x_ref[at + BLOCK : at + 2 * BLOCK, :]], axis=1
        )
        q = dot(lhs, wq_ref[...]).astype(BF16)
        for part in range(4):
            q_refs[part][pair * BLOCK : (pair + 1) * BLOCK, :] = q[:, part * BLOCK : (part + 1) * BLOCK]


def select_kernel(count, place_ref, wanted_ref, k0, k1, k2, k3, x_ref, *refs):
    kv_ref, x_out_ref = refs[0], refs[1]
    out_refs = refs[2:]
    head, node = place_ref[0], place_ref[1]
    rows = k0.shape[0]
    for part, k_ref in enumerate((k0, k1, k2, k3)):
        kv_ref[span((head ^ part) * rows, rows), :] = k_ref[...]
    for m in range(count):
        for c in range(CAP):
            block = wanted_ref[node ^ m, node * CAP + c]
            out_refs[m][c] = kv_ref[span(block * BLOCK, BLOCK), :]
    x_out_ref[...] = x_ref[...]


def turn_kernel(kv_ref, kvt_ref):
    for i in range(BLK):
        kvt_ref[i] = kv_ref[i * BLOCK : (i + 1) * BLOCK, :].T


def turn_rows_kernel(place_ref, x0, x1, x2, x3, xt_ref):
    head = place_ref[0]
    rows = x0.shape[0]
    for part, x_ref in enumerate((x0, x1, x2, x3)):
        xt_ref[:, span((head ^ part) * rows, rows)] = x_ref[...].T


def forward_kernel(count, place_ref, slot_ref, count_ref, q0, q1, q2, q3, kv_ref, kvt_ref, *refs):
    in_refs, refs = refs[:count], refs[-12:]
    att_refs, refs = refs[:4], refs[4:]
    att_ref, qz_ref, table_ref, tablet_ref, top_ref, inv_ref, even_ref, odd_ref = refs
    head, node = place_ref[0], place_ref[1]
    blank = jnp.zeros((BLOCK, HD), BF16)
    for part, q_ref in enumerate((q0, q1, q2, q3)):
        pairs = q_ref.shape[0] // BLOCK
        for pair in range(pairs):
            pack = q_ref[pair * BLOCK : (pair + 1) * BLOCK, :]
            at = ((head ^ part) * pairs + pair) * 2
            qz_ref[span(at * BLOCK, BLOCK), :] = jnp.concatenate([pack[:, :HD], blank], axis=1)
            qz_ref[span((at + 1) * BLOCK, BLOCK), :] = jnp.concatenate([pack[:, HD:], blank], axis=1)
    for i in range(BLK):
        table_ref[i] = kv_ref[i * BLOCK : (i + 1) * BLOCK, :]
        tablet_ref[i] = kvt_ref[i]
    for m in range(count):
        for c in range(CAP):
            block = in_refs[m][c]
            at = BLK + (node ^ m) * CAP + c
            table_ref[at] = block
            tablet_ref[at] = block.T

    def slots_of(i):
        return [slot_ref[i, j] for j in range(PER)]

    def score(i, raw_ref):
        live = count_ref[i]
        keys = jnp.concatenate([table_ref[s] for s in slots_of(i)], axis=0)
        raw = dot_last(keys, qz_ref[span(i * BLOCK, BLOCK), :])
        top = None
        for j in range(PER):
            here = jnp.where(j < live, raw[j * BLOCK : (j + 1) * BLOCK], -1e30)
            raw_ref[j * BLOCK : (j + 1) * BLOCK, :] = here
            here = here.reshape(BLOCK // 8, 8, BLOCK)
            highest = jnp.max(here, axis=0)
            top = highest if top is None else jnp.maximum(top, highest)
        return jnp.max(top, axis=0, keepdims=True)

    def attend(i, raw_ref, top):
        total = None
        lows = []
        for j in range(PER):
            raised = jnp.exp2((raw_ref[j * BLOCK : (j + 1) * BLOCK, :] - top) * SCALE_LOG2E)
            lows.append(raised.astype(BF16))
            part = jnp.sum(raised.reshape(BLOCK // 8, 8, BLOCK), axis=0)
            total = part if total is None else total + part
        inverse = 1.0 / jnp.sum(total, axis=0, keepdims=True)
        values = jnp.concatenate([tablet_ref[s, HD:, :] for s in slots_of(i)], axis=1)
        result = dot(values, jnp.concatenate(lows, axis=0)) * inverse
        top_ref[i] = jnp.broadcast_to(top, (8, BLOCK))
        inv_ref[i] = jnp.broadcast_to(inverse, (8, BLOCK))
        return result

    def pair(t, even_top):
        odd_top = score(2 * t + 1, odd_ref)
        first = attend(2 * t, even_ref, even_top)
        even_top = score(jnp.minimum(2 * t + 2, BLK - 1), even_ref)
        second = attend(2 * t + 1, odd_ref, odd_top)
        both = jnp.concatenate([first, second], axis=0)
        att_ref[span(t * BLOCK, BLOCK), :] = both.T.astype(BF16)
        return even_top

    lax.fori_loop(0, PAIRS, pair, score(0, even_ref))
    for part in range(4):
        size = att_refs[part].shape[0]
        att_refs[part][...] = att_ref[span((head ^ part) * size, size), :]


def middle_kernel(
    place_ref, x_ref, c_ref, a0, a1, a2, a3, w_ref,
    out_ref, grad_ref, low_ref, g0, g1, g2, g3, wide_ref,
):
    head = place_ref[0]
    wide_ref[...] = jnp.zeros_like(wide_ref)
    for part in range(4):
        piece = w_ref[span((head ^ part) * HD, HD), :]
        at = (2 * part) * HD
        wide_ref[at : at + HD, :D] = piece
        wide_ref[at + HD : at + 2 * HD, D:] = piece
    for pair in range(x_ref.shape[0] // (2 * BLOCK)):
        pack = slice(pair * BLOCK, (pair + 1) * BLOCK)
        lhs = jnp.concatenate([a[pack, :] for a in (a0, a1, a2, a3)], axis=1)
        product = dot(lhs, wide_ref[...])
        lows = []
        for half in range(2):
            at = slice((2 * pair + half) * BLOCK, (2 * pair + half + 1) * BLOCK)
            summed = x_ref[at, :].astype(F32) + product[:, half * D : (half + 1) * D]
            inverse = lax.rsqrt(jnp.mean(summed * summed, axis=-1, keepdims=True) + 1e-06)
            normed = summed * inverse
            upstream = c_ref[at, :].astype(F32)
            grad = (upstream - normed * jnp.mean(upstream * normed, axis=-1, keepdims=True)) * inverse
            low = grad.astype(BF16)
            out_ref[at, :] = normed.astype(BF16)
            grad_ref[at, :] = grad
            low_ref[at, :] = low
            lows.append(low)
        gate = dot_last(jnp.concatenate(lows, axis=1), wide_ref[...]).astype(BF16)
        for part, g_ref in enumerate((g0, g1, g2, g3)):
            g_ref[pack, :] = gate[:, part * BLOCK : (part + 1) * BLOCK]


def out_weight_kernel(place_ref, low_ref, a0, a1, a2, a3, out_ref):
    head = place_ref[0]
    total = jnp.zeros((2 * D, 2 * D), F32)
    for pair in range(low_ref.shape[0] // (2 * BLOCK)):
        pack = slice(pair * BLOCK, (pair + 1) * BLOCK)
        at = 2 * pair * BLOCK
        lhs = jnp.concatenate([a[pack, :].T for a in (a0, a1, a2, a3)], axis=0)
        rhs = jnp.concatenate(
            [low_ref[at : at + BLOCK, :], low_ref[at + BLOCK : at + 2 * BLOCK, :]], axis=1
        )
        total += dot(lhs, rhs)
    for part in range(4):
        at = 2 * part * HD
        out_ref[span((head ^ part) * HD, HD), :] = total[at : at + HD, :D] + total[at + HD : at + 2 * HD, D:]


def backward_kernel(
    count, place_ref, slot_ref, count_ref, qz_ref, g0, g1, g2, g3, att_ref, table_ref, tablet_ref, top_ref, inv_ref, *refs
):
    own_ref, dqt_ref, refs = refs[0], refs[1], refs[2:]
    dq_refs, leave_refs = refs[:4], refs[4 : 4 + count]
    acc_ref, dq_ref, gz_ref, dots_ref = refs[4 + count :]
    head, node = place_ref[0], place_ref[1]
    acc_ref[...] = jnp.zeros_like(acc_ref)
    blank = jnp.zeros((BLOCK, HD), BF16)
    for part, g_ref in enumerate((g0, g1, g2, g3)):
        pairs = g_ref.shape[0] // BLOCK
        for pair in range(pairs):
            pack = g_ref[pair * BLOCK : (pair + 1) * BLOCK, :]
            t = (head ^ part) * pairs + pair
            gz_ref[span(2 * t * BLOCK, BLOCK), :] = jnp.concatenate([blank, pack[:, :HD]], axis=1)
            gz_ref[span((2 * t + 1) * BLOCK, BLOCK), :] = jnp.concatenate([blank, pack[:, HD:]], axis=1)
            products = (pack.astype(F32) * att_ref[span(t * BLOCK, BLOCK), :].astype(F32)).T
            for half in range(2):
                sums = jnp.sum(products[half * HD : (half + 1) * HD], axis=0, keepdims=True)
                dots_ref[2 * t + half] = jnp.broadcast_to(sums, (8, BLOCK))

    def one(i):
        slots = [slot_ref[i, j] for j in range(PER)]
        live = count_ref[i]
        at = span(i * BLOCK, BLOCK)
        keys = jnp.concatenate([table_ref[s] for s in slots], axis=0)
        rows = jnp.concatenate([qz_ref[at, :], gz_ref[at, :]], axis=0)
        both = dot_last(keys, rows)
        top = top_ref[i, :1, :]
        inverse = inv_ref[i, :1, :]
        dots = dots_ref[i, :1, :]
        weights, grads = [], []
        for j in range(PER):
            here = both[j * BLOCK : (j + 1) * BLOCK]
            weight = jnp.exp2((here[:, :BLOCK] - top) * SCALE_LOG2E) * inverse
            weight = jnp.where(j < live, weight, 0.0)
            weights.append(weight.astype(BF16))
            grads.append((weight * (here[:, BLOCK:] - dots) * SCALE).astype(BF16))
        score_grad = jnp.concatenate(grads, axis=0)
        low = jnp.concatenate(weights, axis=0)
        pair_grads = dot(jnp.concatenate([score_grad, low], axis=1), rows)
        for j in range(PER):
            acc_ref[slots[j]] += pair_grads[j * BLOCK : (j + 1) * BLOCK]
        turned = jnp.concatenate([tablet_ref[s, :HD, :] for s in slots], axis=1)
        result = dot(turned, score_grad)
        dqt_ref[:, at] = result.astype(BF16)
        return result

    @pl.loop(0, PAIRS)
    def _(t):
        first = one(2 * t)
        second = one(2 * t + 1)
        both = jnp.concatenate([first, second], axis=0)
        dq_ref[span(t * BLOCK, BLOCK), :] = both.T.astype(BF16)

    own_ref[...] = acc_ref[:BLK]
    for m in range(count):
        for c in range(CAP):
            leave_refs[m][c] = acc_ref[BLK + (node ^ m) * CAP + c].astype(BF16)
    for part in range(4):
        size = dq_refs[part].shape[0]
        dq_refs[part][...] = dq_ref[span((head ^ part) * size, size), :]


def query_weight_kernel(place_ref, dqt_ref, x0, x1, x2, x3, after_ref, out_ref):
    head = place_ref[0]
    rows = x0.shape[0]
    total = jnp.zeros((HD, D), F32)
    for part, x_ref in enumerate((x0, x1, x2, x3)):
        total += dot(dqt_ref[:, span((head ^ part) * rows, rows)], x_ref[...])
    out_ref[...] = total


def collect_kernel(count, place_ref, wanted_ref, own_ref, xt_ref, qwg_ref, *refs):
    back_refs, refs = refs[:count], refs[-9:]
    kvg_refs, piece_refs, sum_ref = refs[:4], refs[4:8], refs[8]
    head, node = place_ref[0], place_ref[1]
    sum_ref[...] = own_ref[...]
    for m in range(count):
        for c in range(CAP):
            sum_ref[wanted_ref[node ^ m, node * CAP + c]] += back_refs[m][c].astype(F32)
    total = jnp.zeros((D, BLOCK), F32)
    for part in range(4):
        rows = kvg_refs[part].shape[0]
        first = (head ^ part) * (rows // BLOCK)
        for i in range(rows // BLOCK):
            kvg_refs[part][i * BLOCK : (i + 1) * BLOCK, :] = sum_ref[first + i].astype(BF16)
        total += dot(xt_ref[:, span((head ^ part) * rows, rows)], kvg_refs[part][...])
    both = jnp.concatenate([qwg_ref[...], total.T], axis=0)
    split(both, group_of(node, top_shift(count)), piece_refs)


def finish_kernel(grad_ref, d0, d1, d2, d3, k0, k1, k2, k3, wq_ref, wkv_ref, out_ref):
    rows = out_ref.shape[0]
    kv = jnp.concatenate([k[...] for k in (k0, k1, k2, k3)], axis=1)
    base = grad_ref[...] + dot_last(kv, wkv_ref[...])
    for pair in range(rows // (2 * BLOCK)):
        lhs = jnp.concatenate(
            [d[pair * BLOCK : (pair + 1) * BLOCK, :] for d in (d0, d1, d2, d3)], axis=1
        )
        product = dot_last(lhs, wq_ref[...])
        for half in range(2):
            at = (2 * pair + half) * BLOCK
            out_ref[at : at + BLOCK, :] = (
                base[at : at + BLOCK] + product[:, half * D : (half + 1) * D]
            ).astype(BF16)


def on_device(features, in_weight, out_weight, cotangent, key_slots, block_count, wanted):
    head_count = lax.axis_size("head")
    node_count = lax.axis_size("node")
    rows = features.shape[0]
    node_rows = rows * head_count
    total_nodes = node_rows * node_count
    table_size = BLK + node_count * CAP
    limit = (14 + table_size // 4) * MIB
    place = jnp.stack([lax.axis_index("head"), lax.axis_index("node")]).astype(jnp.int32)
    block_set = ((CAP, BLOCK, BLOCK), BF16)
    pack = ((rows // 2, BLOCK), BF16)
    full = ((rows, BLOCK), BF16)

    def swap(value, axis, mask):
        size = lax.axis_size(axis)
        return lax.ppermute(value, axis, [(i, i ^ mask) for i in range(size)])

    def gather_heads(value):
        across = swap(value, "head", 2)
        beside = swap(value, "head", 1)
        return (value, beside, across, swap(across, "head", 1))

    def exchange(pieces, axis, unit=1):
        moved = list(pieces)
        for mask in reversed(range(1, len(pieces))):
            moved[mask] = swap(pieces[mask], axis, mask * unit)
        return moved

    def add_nodes(pieces, shift):
        moved = exchange(pieces, "node", 1 << shift)
        total = (moved[0] + moved[1]) + (moved[2] + moved[3])
        piece_rows = total.shape[0]
        if shift == 1:
            total = total + swap(total, "node", 1)
        elif shift > 1:
            lower = call(
                functools.partial(split_kernel, shift - 2),
                "split",
                [((piece_rows // 4, D), F32)] * 4,
                [smem(), vmem()],
                limit,
            )(place, total)
            (total,) = call(
                functools.partial(join_kernel, shift - 2),
                "join",
                [((piece_rows, D), F32)],
                [smem()] + [vmem()] * 4,
                limit,
            )(place, *add_nodes(lower, shift - 2))
        return exchange([total] * 4, "node", 1 << shift)

    wants = lax.all_gather(wanted.reshape(1, node_count * CAP), "node", axis=0, tiled=True)
    projected = call(
        project_kernel,
        "project",
        [pack] * 4 + [full] * 4 + [((2 * D, 2 * D), BF16), ((D, 2 * D), BF16)],
        [smem()] + [vmem()] * 2,
        limit,
        flops=2 * rows * 3 * D * D,
        scratch=[pltpu.VMEM((HEADS, 2 * D, BLOCK), BF16), pltpu.VMEM((HEADS, D, BLOCK), BF16)],
    )(place, features, in_weight)
    wq, wkv = projected[8:]
    kv_parts = exchange(projected[4:8], "head")
    kv, features_late, *outgoing = call(
        functools.partial(select_kernel, node_count),
        "select",
        [((node_rows, BLOCK), BF16), ((rows, D), BF16)] + [block_set] * node_count,
        [smem()] * 2 + [vmem()] * 5,
        limit,
    )(place, wants, *kv_parts, features)
    incoming = exchange(outgoing, "node")
    q_parts = exchange(projected[:4], "head")
    xs = gather_heads(features_late)
    (kvt,) = call(
        turn_kernel, "turn", [((BLK, BLOCK, BLOCK), BF16)], [vmem()], limit, flops=node_rows * D * D
    )(kv)
    forward = call(
        functools.partial(forward_kernel, node_count),
        "forward",
        [pack] * 4
        + [
            ((PAIRS * BLOCK, BLOCK), BF16),
            ((node_rows, BLOCK), BF16),
            ((table_size, BLOCK, BLOCK), BF16),
            ((table_size, BLOCK, BLOCK), BF16),
            ((BLK, 8, BLOCK), F32),
            ((BLK, 8, BLOCK), F32),
        ],
        [smem()] * 3 + [vmem()] * (6 + node_count) + [later()] * 3,
        limit,
        flops=4 * node_rows * PER * BLOCK * BLOCK,
        scratch=[pltpu.VMEM((PER * BLOCK, BLOCK), F32)] * 2,
    )(place, key_slots, block_count, *q_parts, kv, kvt, *incoming, *xs[1:])
    att, qz, table, tablet, top, inv = forward[4:]
    att_parts = exchange(forward[:4], "head")
    output, norm_grad, low, *gates = call(
        middle_kernel,
        "middle",
        [((rows, D), BF16), ((rows, D), F32), ((rows, D), BF16)] + [pack] * 4,
        [smem()] + [vmem()] * 7,
        limit,
        flops=8 * rows * D * D,
        scratch=[pltpu.VMEM((2 * D, 2 * D), BF16)],
    )(place, features, cotangent, *att_parts, out_weight)
    gates = exchange(gates, "head")
    (owg,) = call(
        out_weight_kernel,
        "out_weight",
        [((D, D), F32)],
        [smem()] + [vmem()] * 5,
        limit,
        flops=8 * rows * D * D,
    )(place, low, *att_parts)
    owg = lax.psum(lax.psum_scatter(owg, "head", scatter_dimension=0, tiled=True), "node")
    (xt,) = call(
        turn_rows_kernel,
        "turn_rows",
        [((D, node_rows), BF16)],
        [smem()] + [vmem()] * 4,
        limit,
        flops=node_rows * D * D,
    )(place, *xs)
    own, dqt, *rest = call(
        functools.partial(backward_kernel, node_count),
        "backward",
        [((BLK, BLOCK, BLOCK), F32), ((HD, node_rows), BF16)] + [pack] * 4 + [block_set] * node_count,
        [smem()] * 3 + [vmem()] * 10,
        limit,
        flops=10 * node_rows * PER * BLOCK * BLOCK,
        scratch=[
            pltpu.VMEM((table_size, BLOCK, BLOCK), F32),
            pltpu.VMEM((PAIRS * BLOCK, BLOCK), BF16),
            pltpu.VMEM((node_rows, BLOCK), BF16),
            pltpu.VMEM((BLK, 8, BLOCK), F32),
        ],
    )(place, key_slots, block_count, qz, *gates, att, table, tablet, top, inv)
    returned = exchange(rest[4:], "node")
    dq_rows = exchange(rest[:4], "head")
    (query_wg,) = call(
        query_weight_kernel,
        "query_weight",
        [((HD, D), F32)],
        [smem()] + [vmem()] * 5 + [later()],
        limit,
        flops=2 * node_rows * D * HD,
    )(place, dqt, *xs, returned[-1])
    shift = top_shift(node_count)
    collected = call(
        functools.partial(collect_kernel, node_count),
        "collect",
        [full] * 4 + [((3 * HD // 4, D), F32)] * 4,
        [smem()] * 2 + [vmem()] * (3 + node_count) + [later()] * 3,
        limit,
        flops=2 * node_rows * D * BLOCK,
        scratch=[pltpu.VMEM((BLK, BLOCK, BLOCK), F32)],
    )(place, wants, own, xt, query_wg, *returned, *dq_rows[1:])
    kvg, late = collected[:4], collected[4:]
    kv_rows = exchange(kvg, "head")
    (feature_grad,) = call(
        finish_kernel,
        "finish",
        [((rows, D), BF16)],
        [vmem()] * 11,
        limit,
        flops=4 * rows * 3 * D * D,
    )(norm_grad, *dq_rows, *kv_rows, wq, wkv)
    late = add_nodes(late, shift)
    in_grad, out_grad = call(
        functools.partial(result_kernel, shift, total_nodes ** (-0.5)),
        "result",
        [((3 * HD, D), F32), ((HD, D), F32)],
        [smem()] + [vmem()] * 5,
        limit,
    )(place, owg, *late)
    return (output, feature_grad, in_grad.T, out_grad)


def solution(mesh):
    placed = (
        P(("node", "head"), None),
        P(),
        P(),
        P(("node", "head"), None),
        P("node", None),
        P("node"),
        P("node", None, None),
    )
    return jax.shard_map(
        on_device,
        mesh=mesh,
        in_specs=placed,
        out_specs=(
            P(("node", "head"), None),
            P(("node", "head"), None),
            P(None, "head"),
            P("head", None),
        ),
        check_vma=False,
    )
```

```python
import functools
import math

import jax
import jax.numpy as jnp
from jax import lax
from jax.experimental import pallas as pl
from jax.experimental.pallas import tpu as pltpu
from jax.sharding import PartitionSpec as P

HEADS = 4
HD = 64
BLOCK = 128
BLK = 16
PER = 12
CAP = 2
D = 256
PAIRS = BLK // 2
SCALE = HD ** (-0.5)
SCALE_LOG2E = SCALE * math.log2(math.e)
BF16 = jnp.bfloat16
F32 = jnp.float32
MIB = 1 << 20
LAST = (((1,), (1,)), ((), ()))


def dot(a, b):
    return jnp.dot(a, b, preferred_element_type=F32)


def dot_last(a, b):
    return lax.dot_general(a, b, LAST, preferred_element_type=F32)


def span(start, size):
    return pl.ds(pl.multiple_of(start, size), size)


def smem():
    return pl.BlockSpec(memory_space=pltpu.SMEM)


def vmem():
    return pl.BlockSpec(memory_space=pltpu.VMEM)


def later():
    return pl.BlockSpec(memory_space=pl.ANY)


def call(kernel, name, outs, in_specs, limit, flops=0, scratch=()):
    return pl.pallas_call(
        kernel,
        name=name,
        out_shape=tuple(jax.ShapeDtypeStruct(shape, kind) for shape, kind in outs),
        in_specs=in_specs,
        out_specs=tuple(vmem() for _ in outs),
        scratch_shapes=scratch,
        compiler_params=pltpu.CompilerParams(vmem_limit_bytes=limit),
        cost_estimate=pl.CostEstimate(flops=flops, bytes_accessed=4 * MIB, transcendentals=0),
    )


def top_shift(count):
    return count.bit_length() - 3


def group_of(node, shift):
    return (node >> shift) & 3


def split(value, group, piece_refs):
    size = value.shape[0] // 4
    for g in range(4):
        for m in range(4):

            @pl.when((group ^ m) == g)
            def _():
                piece_refs[m][...] = value[g * size : (g + 1) * size, :]


def split_kernel(shift, place_ref, value_ref, *piece_refs):
    split(value_ref[...], group_of(place_ref[1], shift), piece_refs)


def join(piece_refs, group, g):
    value = piece_refs[0][...]
    for m in range(1, 4):
        value = jnp.where((group ^ m) == g, piece_refs[m][...], value)
    return value


def join_kernel(shift, place_ref, p0, p1, p2, p3, out_ref):
    group = group_of(place_ref[1], shift)
    out_ref[...] = jnp.concatenate([join((p0, p1, p2, p3), group, g) for g in range(4)], axis=0)


def result_kernel(shift, factor, place_ref, l0, l1, l2, l3, in_ref, out_ref):
    group = group_of(place_ref[1], shift)
    pieces = [join((l0, l1, l2, l3), group, g) * factor for g in range(4)]
    out_ref[...] = pieces[0]
    in_ref[...] = jnp.concatenate(pieces[1:], axis=0)


def fence_kernel(*refs):
    pass


def fence(values, after):
    count = len(values)
    return pl.pallas_call(
        fence_kernel,
        name="fence",
        out_shape=tuple(jax.ShapeDtypeStruct(v.shape, v.dtype) for v in values),
        in_specs=[later()] * (count + len(after)),
        out_specs=(later(),) * count,
        input_output_aliases={i: i for i in range(count)},
    )(*values, *after)


def project_kernel(count, place_ref, *refs):
    wanted_refs, refs = refs[:count], refs[count:]
    x_refs, in_ref, refs = refs[:4], refs[4], refs[5:]
    qz_ref, kv_ref, refs = refs[0], refs[1], refs[2:]
    out_refs, wide_ref = refs[:count], refs[count]
    head, node = place_ref[0], place_ref[1]
    rows = x_refs[0].shape[0]
    wide_ref[:, HD:BLOCK] = jnp.zeros((D, HD), BF16)
    for g in range(HEADS):

        @pl.when(head == g)
        def _():
            at = g * 3 * HD
            wide_ref[:, :HD] = in_ref[:, at : at + HD]
            wide_ref[:, BLOCK:] = in_ref[:, at + HD : at + 3 * HD]

    for part in range(4):
        at = span((head ^ part) * rows, rows)
        y = dot(x_refs[part][...], wide_ref[...]).astype(BF16)
        qz_ref[at, :] = y[:, :BLOCK]
        kv_ref[at, :] = y[:, BLOCK:]
    for m in range(count):
        for c in range(CAP):
            block = wanted_refs[m][node * CAP + c]
            out_refs[m][c] = kv_ref[span(block * BLOCK, BLOCK), :]


def prepare_kernel(place_ref, x0, x1, x2, x3, kv_ref, in_ref, c_ref, xt_ref, kvt_ref, wkv_ref, wq_ref, c_out_ref, k_ref, q_ref):
    c_out_ref[...] = c_ref[...]
    head = place_ref[0]
    rows = x0.shape[0]
    for part, x_ref in enumerate((x0, x1, x2, x3)):
        xt_ref[:, span((head ^ part) * rows, rows)] = x_ref[...].T
    for i in range(BLK):
        kvt_ref[i] = kv_ref[i * BLOCK : (i + 1) * BLOCK, :].T
    blank = jnp.zeros((D, HD), BF16)
    for g in range(HEADS):
        at = g * 3 * HD
        query = in_ref[:, at : at + HD]
        k_ref[g] = in_ref[:, at + HD : at + 3 * HD]
        q_ref[g, :D] = jnp.concatenate([query, blank], axis=1)
        q_ref[g, D:] = jnp.concatenate([blank, query], axis=1)
    for part in range(4):
        lanes = slice(part * BLOCK, (part + 1) * BLOCK)
        wkv_ref[:, lanes] = k_ref[head ^ part]
        wq_ref[:, lanes] = q_ref[head ^ part]


def forward_kernel(count, place_ref, slot_ref, count_ref, qz_ref, kv_ref, kvt_ref, *refs):
    in_refs, refs = refs[:count], refs[-8:]
    att_ref, attt_ref, table_ref, tablet_ref, top_ref, inv_ref, even_ref, odd_ref = refs
    node = place_ref[1]
    for i in range(BLK):
        table_ref[i] = kv_ref[i * BLOCK : (i + 1) * BLOCK, :]
        tablet_ref[i] = kvt_ref[i]
    for m in range(count):
        for c in range(CAP):
            block = in_refs[m][c]
            at = BLK + (node ^ m) * CAP + c
            table_ref[at] = block
            tablet_ref[at] = block.T

    def slots_of(i):
        return [slot_ref[i, j] for j in range(PER)]

    def score(i, raw_ref):
        live = count_ref[i]
        keys = jnp.concatenate([table_ref[s] for s in slots_of(i)], axis=0)
        raw = dot_last(keys, qz_ref[span(i * BLOCK, BLOCK), :])
        top = None
        for j in range(PER):
            here = jnp.where(j < live, raw[j * BLOCK : (j + 1) * BLOCK], -1e30)
            raw_ref[j * BLOCK : (j + 1) * BLOCK, :] = here
            here = here.reshape(BLOCK // 8, 8, BLOCK)
            highest = jnp.max(here, axis=0)
            top = highest if top is None else jnp.maximum(top, highest)
        return jnp.max(top, axis=0, keepdims=True)

    def attend(i, raw_ref, top):
        total = None
        lows = []
        for j in range(PER):
            raised = jnp.exp2((raw_ref[j * BLOCK : (j + 1) * BLOCK, :] - top) * SCALE_LOG2E)
            lows.append(raised.astype(BF16))
            part = jnp.sum(raised.reshape(BLOCK // 8, 8, BLOCK), axis=0)
            total = part if total is None else total + part
        inverse = 1.0 / jnp.sum(total, axis=0, keepdims=True)
        values = jnp.concatenate([tablet_ref[s, HD:, :] for s in slots_of(i)], axis=1)
        result = dot(values, jnp.concatenate(lows, axis=0)) * inverse
        attt_ref[:, span(i * BLOCK, BLOCK)] = result.astype(BF16)
        top_ref[i] = jnp.broadcast_to(top, (8, BLOCK))
        inv_ref[i] = jnp.broadcast_to(inverse, (8, BLOCK))
        return result

    def pair(t, even_top):
        odd_top = score(2 * t + 1, odd_ref)
        first = attend(2 * t, even_ref, even_top)
        even_top = score(jnp.minimum(2 * t + 2, BLK - 1), even_ref)
        second = attend(2 * t + 1, odd_ref, odd_top)
        both = jnp.concatenate([first, second], axis=0)
        att_ref[span(t * BLOCK, BLOCK), :] = both.T.astype(BF16)
        return even_top

    lax.fori_loop(0, PAIRS, pair, score(0, even_ref))


def middle_kernel(
    place_ref, x0, x1, x2, x3, c0, c1, c2, c3, a0, a1, a2, a3, attt_ref, w_ref,
    out_ref, grad_ref, gz_ref, dots_ref, owg_ref, wide_ref, pad_ref,
):
    head = place_ref[0]
    rows = x0.shape[0]
    own_w = w_ref[span(head * HD, HD), :]
    wide_ref[...] = jnp.zeros_like(wide_ref)
    for part in range(4):
        piece = w_ref[span((head ^ part) * HD, HD), :]
        at = (2 * part) * HD
        wide_ref[at : at + HD, :D] = piece
        wide_ref[at + HD : at + 2 * HD, D:] = piece
    pad_ref[:HD, :] = jnp.zeros((HD, D), BF16)
    pad_ref[HD:, :] = own_w
    a_refs = (a0, a1, a2, a3)
    owg = jnp.zeros((HD, D), F32)
    for part, (x_ref, c_ref) in enumerate(zip((x0, x1, x2, x3), (c0, c1, c2, c3))):
        group = head ^ part
        for pair in range(rows // (2 * BLOCK)):
            t = group * (rows // (2 * BLOCK)) + pair
            lhs = jnp.concatenate([a[span(t * BLOCK, BLOCK), :] for a in a_refs], axis=1)
            product = dot(lhs, wide_ref[...])
            for half in range(2):
                local = (2 * pair + half) * BLOCK
                block = 2 * t + half
                at = span(block * BLOCK, BLOCK)
                summed = x_ref[local : local + BLOCK, :].astype(F32) + product[:, half * D : (half + 1) * D]
                inverse = lax.rsqrt(jnp.mean(summed * summed, axis=-1, keepdims=True) + 1e-06)
                normed = summed * inverse
                upstream = c_ref[local : local + BLOCK, :].astype(F32)
                grad = (upstream - normed * jnp.mean(upstream * normed, axis=-1, keepdims=True)) * inverse
                low = grad.astype(BF16)
                if part == 0:
                    out_ref[local : local + BLOCK, :] = normed.astype(BF16)
                    grad_ref[local : local + BLOCK, :] = grad
                gz_ref[at, :] = dot_last(low, pad_ref[...]).astype(BF16)
                turned = dot_last(own_w, low).astype(BF16).astype(F32)
                attended = attt_ref[:, at]
                sums = jnp.sum(turned * attended.astype(F32), axis=0, keepdims=True)
                dots_ref[block] = jnp.broadcast_to(sums, (8, BLOCK))
                owg += dot(attended, low)
    owg_ref[...] = owg


def backward_kernel(
    count, place_ref, slot_ref, count_ref, qz_ref, gz_ref, table_ref, tablet_ref, top_ref, inv_ref, dots_ref, *refs
):
    own_ref, dqt_ref, refs = refs[0], refs[1], refs[2:]
    dq_refs, leave_refs = refs[:4], refs[4 : 4 + count]
    acc_ref, dq_ref = refs[4 + count :]
    head, node = place_ref[0], place_ref[1]
    acc_ref[...] = jnp.zeros_like(acc_ref)

    def one(i):
        slots = [slot_ref[i, j] for j in range(PER)]
        live = count_ref[i]
        at = span(i * BLOCK, BLOCK)
        keys = jnp.concatenate([table_ref[s] for s in slots], axis=0)
        rows = jnp.concatenate([qz_ref[at, :], gz_ref[at, :]], axis=0)
        both = dot_last(keys, rows)
        top = top_ref[i, :1, :]
        inverse = inv_ref[i, :1, :]
        dots = dots_ref[i, :1, :]
        weights, grads = [], []
        for j in range(PER):
            here = both[j * BLOCK : (j + 1) * BLOCK]
            weight = jnp.exp2((here[:, :BLOCK] - top) * SCALE_LOG2E) * inverse
            weight = jnp.where(j < live, weight, 0.0)
            weights.append(weight.astype(BF16))
            grads.append((weight * (here[:, BLOCK:] - dots) * SCALE).astype(BF16))
        score_grad = jnp.concatenate(grads, axis=0)
        low = jnp.concatenate(weights, axis=0)
        pair_grads = dot(jnp.concatenate([score_grad, low], axis=1), rows)
        for j in range(PER):
            acc_ref[slots[j]] += pair_grads[j * BLOCK : (j + 1) * BLOCK]
        turned = jnp.concatenate([tablet_ref[s, :HD, :] for s in slots], axis=1)
        result = dot(turned, score_grad)
        dqt_ref[:, at] = result.astype(BF16)
        return result

    @pl.loop(0, PAIRS)
    def _(t):
        first = one(2 * t)
        second = one(2 * t + 1)
        both = jnp.concatenate([first, second], axis=0)
        dq_ref[span(t * BLOCK, BLOCK), :] = both.T.astype(BF16)

    own_ref[...] = acc_ref[:BLK]
    for m in range(count):
        for c in range(CAP):
            leave_refs[m][c] = acc_ref[BLK + (node ^ m) * CAP + c].astype(BF16)
    for part in range(4):
        size = dq_refs[part].shape[0]
        dq_refs[part][...] = dq_ref[span((head ^ part) * size, size), :]


def query_weight_kernel(place_ref, dqt_ref, x0, x1, x2, x3, out_ref):
    head = place_ref[0]
    rows = x0.shape[0]
    total = jnp.zeros((HD, D), F32)
    for part, x_ref in enumerate((x0, x1, x2, x3)):
        total += dot(dqt_ref[:, span((head ^ part) * rows, rows)], x_ref[...])
    out_ref[...] = total


def collect_kernel(count, place_ref, *refs):
    wanted_refs, refs = refs[:count], refs[count:]
    own_ref, back_refs, refs = refs[0], refs[1 : 1 + count], refs[-5:]
    kvg_refs, sum_ref = refs[:4], refs[4]
    head, node = place_ref[0], place_ref[1]
    sum_ref[...] = own_ref[...]
    for m in range(count):
        for c in range(CAP):
            sum_ref[wanted_refs[m][node * CAP + c]] += back_refs[m][c].astype(F32)
    for part in range(4):
        size = kvg_refs[part].shape[0] // BLOCK
        first = (head ^ part) * size
        for i in range(size):
            kvg_refs[part][i * BLOCK : (i + 1) * BLOCK, :] = sum_ref[first + i].astype(BF16)


def late_weight_kernel(count, place_ref, k0, k1, k2, k3, xt_ref, owg_ref, qwg_ref, *piece_refs):
    head, node = place_ref[0], place_ref[1]
    total = jnp.zeros((D, BLOCK), F32)
    for part, k_ref in enumerate((k0, k1, k2, k3)):
        rows = k_ref.shape[0]
        total += dot(xt_ref[:, span((head ^ part) * rows, rows)], k_ref[...])
    every = jnp.concatenate([owg_ref[...], qwg_ref[...], total.T], axis=0)
    split(every, group_of(node, top_shift(count)), piece_refs)


def finish_kernel(grad_ref, d0, d1, d2, d3, k0, k1, k2, k3, wq_ref, wkv_ref, out_ref):
    rows = out_ref.shape[0]
    kv = jnp.concatenate([k[...] for k in (k0, k1, k2, k3)], axis=1)
    base = grad_ref[...] + dot_last(kv, wkv_ref[...])
    for pair in range(rows // (2 * BLOCK)):
        lhs = jnp.concatenate(
            [d[pair * BLOCK : (pair + 1) * BLOCK, :] for d in (d0, d1, d2, d3)], axis=1
        )
        product = dot_last(lhs, wq_ref[...])
        for half in range(2):
            at = (2 * pair + half) * BLOCK
            out_ref[at : at + BLOCK, :] = (
                base[at : at + BLOCK] + product[:, half * D : (half + 1) * D]
            ).astype(BF16)


def on_device(features, in_weight, out_weight, cotangent, key_slots, block_count, wanted):
    head_count = lax.axis_size("head")
    node_count = lax.axis_size("node")
    rows = features.shape[0]
    node_rows = rows * head_count
    total_nodes = node_rows * node_count
    table_size = BLK + node_count * CAP
    limit = (14 + table_size // 4) * MIB
    place = jnp.stack([lax.axis_index("head"), lax.axis_index("node")]).astype(jnp.int32)
    block_set = (CAP, BLOCK, BLOCK)

    def swap(value, axis, mask):
        size = lax.axis_size(axis)
        return lax.ppermute(value, axis, [(i, i ^ mask) for i in range(size)])

    def gather_heads(value):
        across = swap(value, "head", 2)
        beside = swap(value, "head", 1)
        return (value, beside, across, swap(across, "head", 1))

    def exchange(pieces, axis, unit=1):
        moved = list(pieces)
        for mask in reversed(range(1, len(pieces))):
            moved[mask] = swap(pieces[mask], axis, mask * unit)
        return moved

    def add_nodes(pieces, shift):
        moved = exchange(pieces, "node", 1 << shift)
        total = (moved[0] + moved[1]) + (moved[2] + moved[3])
        piece_rows = total.shape[0]
        if shift == 1:
            total = total + swap(total, "node", 1)
        elif shift > 1:
            lower = call(
                functools.partial(split_kernel, shift - 2),
                "split",
                [((piece_rows // 4, D), F32)] * 4,
                [smem(), vmem()],
                limit,
            )(place, total)
            (total,) = call(
                functools.partial(join_kernel, shift - 2),
                "join",
                [((piece_rows, D), F32)],
                [smem()] + [vmem()] * 4,
                limit,
            )(place, *add_nodes(lower, shift - 2))
        return exchange([total] * 4, "node", 1 << shift)

    across = swap(features, "head", 2)
    beside = swap(features, "head", 1)
    wants = exchange([wanted.reshape(-1)] * node_count, "node")
    (across,) = fence([across], wants[1:])
    xs = (features, beside, across, swap(across, "head", 1))
    qz, kv, *outgoing = call(
        functools.partial(project_kernel, node_count),
        "project",
        [((node_rows, BLOCK), BF16)] * 2 + [(block_set, BF16)] * node_count,
        [smem()] * (1 + node_count) + [vmem()] * 5,
        limit,
        flops=2 * node_rows * D * D,
        scratch=[pltpu.VMEM((D, D), BF16)],
    )(place, *wants, *xs, in_weight)
    incoming = exchange(outgoing, "node")
    xt, kvt, wkv, wq, upstream = call(
        prepare_kernel,
        "prepare",
        [
            ((D, node_rows), BF16),
            ((BLK, BLOCK, BLOCK), BF16),
            ((D, 2 * D), BF16),
            ((2 * D, 2 * D), BF16),
            ((rows, D), BF16),
        ],
        [smem()] + [vmem()] * 7,
        limit,
        flops=2 * node_rows * D * D,
        scratch=[pltpu.VMEM((HEADS, D, BLOCK), BF16), pltpu.VMEM((HEADS, 2 * D, BLOCK), BF16)],
    )(place, *xs, kv, in_weight, cotangent)
    cs = gather_heads(upstream)
    att, attt, table, tablet, top, inv = call(
        functools.partial(forward_kernel, node_count),
        "forward",
        [
            ((PAIRS * BLOCK, BLOCK), BF16),
            ((HD, node_rows), BF16),
            ((table_size, BLOCK, BLOCK), BF16),
            ((table_size, BLOCK, BLOCK), BF16),
            ((BLK, 8, BLOCK), F32),
            ((BLK, 8, BLOCK), F32),
        ],
        [smem()] * 3 + [vmem()] * (3 + node_count) + [later()] * 3,
        limit,
        flops=4 * node_rows * PER * BLOCK * BLOCK,
        scratch=[pltpu.VMEM((PER * BLOCK, BLOCK), F32)] * 2,
    )(place, key_slots, block_count, qz, kv, kvt, *incoming, *cs[1:])
    parts = gather_heads(att)
    output, norm_grad, gz, dots, owg = call(
        middle_kernel,
        "middle",
        [
            ((rows, D), BF16),
            ((rows, D), F32),
            ((node_rows, BLOCK), BF16),
            ((BLK, 8, BLOCK), F32),
            ((HD, D), F32),
        ],
        [smem()] + [vmem()] * 14,
        limit,
        flops=8 * node_rows * D * D,
        scratch=[pltpu.VMEM((2 * D, 2 * D), BF16), pltpu.VMEM((BLOCK, D), BF16)],
    )(place, *xs, *cs, *parts, attt, out_weight)
    own, dqt, *rest = call(
        functools.partial(backward_kernel, node_count),
        "backward",
        [((BLK, BLOCK, BLOCK), F32), ((HD, node_rows), BF16)]
        + [((rows // 2, BLOCK), BF16)] * 4
        + [(block_set, BF16)] * node_count,
        [smem()] * 3 + [vmem()] * 7,
        limit,
        flops=10 * node_rows * PER * BLOCK * BLOCK,
        scratch=[
            pltpu.VMEM((table_size, BLOCK, BLOCK), F32),
            pltpu.VMEM((PAIRS * BLOCK, BLOCK), BF16),
        ],
    )(place, key_slots, block_count, qz, gz, table, tablet, top, inv, dots)
    returned = exchange(rest[4:], "node")
    (query_wg,) = call(
        query_weight_kernel,
        "query_weight",
        [((HD, D), F32)],
        [smem()] + [vmem()] * 5,
        limit,
        flops=2 * node_rows * D * HD,
    )(place, dqt, *xs)
    dq_rows = exchange(fence(rest[:4], [query_wg]), "head")
    kvg = call(
        functools.partial(collect_kernel, node_count),
        "collect",
        [((rows, BLOCK), BF16)] * 4,
        [smem()] * (1 + node_count) + [vmem()] * (1 + node_count) + [later()] * 3,
        limit,
        scratch=[pltpu.VMEM((BLK, BLOCK, BLOCK), F32)],
    )(place, *wants, own, *returned, *dq_rows[1:])
    kv_rows = exchange(kvg, "head")
    (feature_grad,) = call(
        finish_kernel,
        "finish",
        [((rows, D), BF16)],
        [vmem()] * 11,
        limit,
        flops=4 * rows * 3 * D * D,
    )(norm_grad, *dq_rows, *kv_rows, wq, wkv)
    shift = top_shift(node_count)
    late = call(
        functools.partial(late_weight_kernel, node_count),
        "late_weight",
        [((HD, D), F32)] * 4,
        [smem()] + [vmem()] * 7,
        limit,
        flops=2 * node_rows * D * BLOCK,
    )(place, *kvg, xt, owg, query_wg)
    late = add_nodes(late, shift)
    in_grad, out_grad = call(
        functools.partial(result_kernel, shift, total_nodes ** (-0.5)),
        "result",
        [((3 * HD, D), F32), ((HD, D), F32)],
        [smem()] + [vmem()] * 4,
        limit,
    )(place, *late)
    return (output, feature_grad, in_grad.T, out_grad)


def solution(mesh):
    placed = (
        P(("node", "head"), None),
        P(),
        P(),
        P(("node", "head"), None),
        P("node", None),
        P("node"),
        P("node", None, None),
    )
    return jax.shard_map(
        on_device,
        mesh=mesh,
        in_specs=placed,
        out_specs=(
            P(("node", "head"), None),
            P(("node", "head"), None),
            P(None, "head"),
            P("head", None),
        ),
        check_vma=False,
    )
```

```python
import functools
import math

import jax
import jax.numpy as jnp
from jax import lax
from jax.experimental import pallas as pl
from jax.experimental.pallas import tpu as pltpu
from jax.sharding import PartitionSpec as P

HEADS = 4
HD = 64
BLOCK = 128
BLK = 16
PER = 12
CAP = 2
D = 256
PAIRS = BLK // 2
SCALE = HD ** (-0.5)
SCALE_LOG2E = SCALE * math.log2(math.e)
BF16 = jnp.bfloat16
F32 = jnp.float32
MIB = 1 << 20
LAST = (((1,), (1,)), ((), ()))


def dot(a, b):
    return jnp.dot(a, b, preferred_element_type=F32)


def dot_last(a, b):
    return lax.dot_general(a, b, LAST, preferred_element_type=F32)


def span(start, size):
    return pl.ds(pl.multiple_of(start, size), size)


def smem():
    return pl.BlockSpec(memory_space=pltpu.SMEM)


def vmem():
    return pl.BlockSpec(memory_space=pltpu.VMEM)


def later():
    return pl.BlockSpec(memory_space=pl.ANY)


def hbm():
    return pl.BlockSpec(memory_space=pltpu.HBM)


def call(kernel, name, outs, in_specs, limit, flops=0, scratch=()):
    return pl.pallas_call(
        kernel,
        name=name,
        out_shape=tuple(jax.ShapeDtypeStruct(shape, kind) for shape, kind in outs),
        in_specs=in_specs,
        out_specs=tuple(vmem() for _ in outs),
        scratch_shapes=scratch,
        compiler_params=pltpu.CompilerParams(vmem_limit_bytes=limit),
        cost_estimate=pl.CostEstimate(flops=flops, bytes_accessed=4 * MIB, transcendentals=0),
    )


def top_shift(count):
    return count.bit_length() - 3


def group_of(node, shift):
    return (node >> shift) & 3


def split(value, group, piece_refs):
    size = value.shape[0] // 4
    for g in range(4):
        for m in range(4):

            @pl.when((group ^ m) == g)
            def _():
                piece_refs[m][...] = value[g * size : (g + 1) * size, :]


def split_kernel(shift, place_ref, value_ref, *piece_refs):
    split(value_ref[...], group_of(place_ref[1], shift), piece_refs)


def join(piece_refs, group, g):
    value = piece_refs[0][...]
    for m in range(1, 4):
        value = jnp.where((group ^ m) == g, piece_refs[m][...], value)
    return value


def join_kernel(shift, place_ref, p0, p1, p2, p3, out_ref):
    group = group_of(place_ref[1], shift)
    out_ref[...] = jnp.concatenate([join((p0, p1, p2, p3), group, g) for g in range(4)], axis=0)


def result_kernel(shift, factor, place_ref, l0, l1, l2, l3, in_ref, out_ref):
    group = group_of(place_ref[1], shift)
    pieces = [join((l0, l1, l2, l3), group, g) * factor for g in range(4)]
    out_ref[...] = pieces[0]
    in_ref[...] = jnp.concatenate(pieces[1:], axis=0)


def carry_kernel(value_ref, after_ref, out_ref):
    out_ref[...] = value_ref[...]


def fence_kernel(*refs):
    pass


def fence(values, after):
    count = len(values)
    return pl.pallas_call(
        fence_kernel,
        name="fence",
        out_shape=tuple(jax.ShapeDtypeStruct(v.shape, v.dtype) for v in values),
        in_specs=[later()] * (count + len(after)),
        out_specs=(later(),) * count,
        input_output_aliases={i: i for i in range(count)},
    )(*values, *after)


def project_kernel(count, place_ref, wanted_ref, x_from, x1, x2, x3, in_from, *refs):
    qz_ref, kv_ref, refs = refs[0], refs[1], refs[2:]
    out_refs, (wide_ref, x_ref, in_ref, sems) = refs[:count], refs[count:]
    x_copy = pltpu.make_async_copy(x_from, x_ref, sems.at[0])
    in_copy = pltpu.make_async_copy(in_from, in_ref, sems.at[1])
    in_copy.start()
    x_copy.start()
    x_refs = (x_ref, x1, x2, x3)
    head, node = place_ref[0], place_ref[1]
    rows = x_ref.shape[0]
    in_copy.wait()
    wide_ref[:, HD:BLOCK] = jnp.zeros((D, HD), BF16)
    for g in range(HEADS):

        @pl.when(head == g)
        def _():
            at = g * 3 * HD
            wide_ref[:, :HD] = in_ref[:, at : at + HD]
            wide_ref[:, BLOCK:] = in_ref[:, at + HD : at + 3 * HD]

    for part in (1, 2, 3, 0):
        if part == 0:
            x_copy.wait()
        at = span((head ^ part) * rows, rows)
        y = dot(x_refs[part][...], wide_ref[...]).astype(BF16)
        qz_ref[at, :] = y[:, :BLOCK]
        kv_ref[at, :] = y[:, BLOCK:]
    for m in range(count):
        for c in range(CAP):
            block = wanted_ref[node ^ m, 0, c]
            out_refs[m][c] = kv_ref[span(block * BLOCK, BLOCK), :]


def prepare_kernel(place_ref, x0, x1, x2, x3, kv_ref, in_ref, xt_ref, kvt_ref, wkv_ref, wq_ref, k_ref, q_ref):
    head = place_ref[0]
    rows = x0.shape[0]
    for part, x_ref in enumerate((x0, x1, x2, x3)):
        xt_ref[:, span((head ^ part) * rows, rows)] = x_ref[...].T
    for i in range(BLK):
        kvt_ref[i] = kv_ref[i * BLOCK : (i + 1) * BLOCK, :].T
    blank = jnp.zeros((D, HD), BF16)
    for g in range(HEADS):
        at = g * 3 * HD
        query = in_ref[:, at : at + HD]
        k_ref[g] = in_ref[:, at + HD : at + 3 * HD]
        q_ref[g, :D] = jnp.concatenate([query, blank], axis=1)
        q_ref[g, D:] = jnp.concatenate([blank, query], axis=1)
    for part in range(4):
        lanes = slice(part * BLOCK, (part + 1) * BLOCK)
        wkv_ref[:, lanes] = k_ref[head ^ part]
        wq_ref[:, lanes] = q_ref[head ^ part]


def forward_kernel(count, place_ref, slot_ref, count_ref, qz_ref, kv_ref, kvt_ref, *refs):
    in_refs, refs = refs[:count][::-1], refs[-8:]
    att_ref, attt_ref, table_ref, tablet_ref, top_ref, inv_ref, even_ref, odd_ref = refs
    node = place_ref[1]
    for i in range(BLK):
        table_ref[i] = kv_ref[i * BLOCK : (i + 1) * BLOCK, :]
        tablet_ref[i] = kvt_ref[i]
    for m in range(count):
        for c in range(CAP):
            block = in_refs[m][c]
            at = BLK + (node ^ m) * CAP + c
            table_ref[at] = block
            tablet_ref[at] = block.T

    def slots_of(i):
        return [slot_ref[i, j] for j in range(PER)]

    def score(i, raw_ref):
        live = count_ref[i]
        keys = jnp.concatenate([table_ref[s] for s in slots_of(i)], axis=0)
        raw = dot_last(keys, qz_ref[span(i * BLOCK, BLOCK), :])
        top = None
        for j in range(PER):
            here = jnp.where(j < live, raw[j * BLOCK : (j + 1) * BLOCK], -1e30)
            raw_ref[j * BLOCK : (j + 1) * BLOCK, :] = here
            here = here.reshape(BLOCK // 8, 8, BLOCK)
            highest = jnp.max(here, axis=0)
            top = highest if top is None else jnp.maximum(top, highest)
        return jnp.max(top, axis=0, keepdims=True)

    def attend(i, raw_ref, top):
        total = None
        lows = []
        for j in range(PER):
            raised = jnp.exp2((raw_ref[j * BLOCK : (j + 1) * BLOCK, :] - top) * SCALE_LOG2E)
            lows.append(raised.astype(BF16))
            part = jnp.sum(raised.reshape(BLOCK // 8, 8, BLOCK), axis=0)
            total = part if total is None else total + part
        inverse = 1.0 / jnp.sum(total, axis=0, keepdims=True)
        values = jnp.concatenate([tablet_ref[s, HD:, :] for s in slots_of(i)], axis=1)
        result = dot(values, jnp.concatenate(lows, axis=0)) * inverse
        attt_ref[:, span(i * BLOCK, BLOCK)] = result.astype(BF16)
        top_ref[i] = jnp.broadcast_to(top, (8, BLOCK))
        inv_ref[i] = jnp.broadcast_to(inverse, (8, BLOCK))
        return result

    def pair(t, even_top):
        odd_top = score(2 * t + 1, odd_ref)
        first = attend(2 * t, even_ref, even_top)
        even_top = score(jnp.minimum(2 * t + 2, BLK - 1), even_ref)
        second = attend(2 * t + 1, odd_ref, odd_top)
        both = jnp.concatenate([first, second], axis=0)
        att_ref[span(t * BLOCK, BLOCK), :] = both.T.astype(BF16)
        return even_top

    lax.fori_loop(0, PAIRS, pair, score(0, even_ref))


def middle_kernel(
    place_ref, x0, x1, x2, x3, c0, c1, c2, c3, a0, a1, a2, a3, attt_ref, w_ref,
    out_ref, grad_ref, gz_ref, dots_ref, owg_ref, wide_ref, pad_ref,
):
    head = place_ref[0]
    rows = x0.shape[0]
    own_w = w_ref[span(head * HD, HD), :]
    wide_ref[...] = jnp.zeros_like(wide_ref)
    for part in range(4):
        piece = w_ref[span((head ^ part) * HD, HD), :]
        at = (2 * part) * HD
        wide_ref[at : at + HD, :D] = piece
        wide_ref[at + HD : at + 2 * HD, D:] = piece
    pad_ref[:HD, :] = jnp.zeros((HD, D), BF16)
    pad_ref[HD:, :] = own_w
    a_refs = (a0, a1, a2, a3)
    owg = jnp.zeros((HD, D), F32)
    pairs = rows // (2 * BLOCK)
    for part, (x_ref, c_ref) in enumerate(zip((x0, x1, x2, x3), (c0, c1, c2, c3))):
        group = head ^ part
        at = span(group * (rows // 2), rows // 2)
        lhs = jnp.concatenate([a[at, :] for a in a_refs], axis=1)
        product = dot(lhs, wide_ref[...])
        lows = []
        for i in range(2 * pairs):
            local = slice(i * BLOCK, (i + 1) * BLOCK)
            pair, half = i // 2, i % 2
            summed = x_ref[local, :].astype(F32) + product[
                pair * BLOCK : (pair + 1) * BLOCK, half * D : (half + 1) * D
            ]
            inverse = lax.rsqrt(jnp.mean(summed * summed, axis=-1, keepdims=True) + 1e-06)
            normed = summed * inverse
            upstream = c_ref[local, :].astype(F32)
            grad = (upstream - normed * jnp.mean(upstream * normed, axis=-1, keepdims=True)) * inverse
            lows.append(grad.astype(BF16))
            if part == 0:
                out_ref[local, :] = normed.astype(BF16)
                grad_ref[local, :] = grad
        low = jnp.concatenate(lows, axis=0)
        at = span(group * rows, rows)
        gz_ref[at, :] = dot_last(low, pad_ref[...]).astype(BF16)
        turned = dot_last(own_w, low).astype(BF16).astype(F32)
        attended = attt_ref[:, at]
        sums = jnp.sum(turned * attended.astype(F32), axis=0, keepdims=True)
        for i in range(2 * pairs):
            dots_ref[group * (2 * pairs) + i] = jnp.broadcast_to(
                sums[:, i * BLOCK : (i + 1) * BLOCK], (8, BLOCK)
            )
        owg += dot(attended, low)
    owg_ref[...] = owg


def backward_kernel(
    count, place_ref, slot_ref, count_ref, qz_ref, gz_ref, table_ref, tablet_ref, top_ref, inv_ref, dots_ref, *refs
):
    own_ref, dqt_ref, refs = refs[0], refs[1], refs[2:]
    dq_refs, leave_refs = refs[:4], refs[4 : 4 + count]
    acc_ref, dq_ref, even_ref, odd_ref = refs[4 + count :]
    head, node = place_ref[0], place_ref[1]
    acc_ref[...] = jnp.zeros_like(acc_ref)

    def slots_of(i):
        return [slot_ref[i, j] for j in range(PER)]

    def rows_of(i):
        at = span(i * BLOCK, BLOCK)
        return jnp.concatenate([qz_ref[at, :], gz_ref[at, :]], axis=0)

    def score(i, both_ref):
        keys = jnp.concatenate([table_ref[s] for s in slots_of(i)], axis=0)
        both_ref[...] = dot_last(keys, rows_of(i))

    def spread(i, both_ref):
        slots = slots_of(i)
        live = count_ref[i]
        top = top_ref[i, :1, :]
        inverse = inv_ref[i, :1, :]
        dots = dots_ref[i, :1, :]
        weights, grads = [], []
        for j in range(PER):
            here = slice(j * BLOCK, (j + 1) * BLOCK)
            weight = jnp.exp2((both_ref[here, :BLOCK] - top) * SCALE_LOG2E) * inverse
            weight = jnp.where(j < live, weight, 0.0)
            weights.append(weight.astype(BF16))
            grads.append((weight * (both_ref[here, BLOCK:] - dots) * SCALE).astype(BF16))
        score_grad = jnp.concatenate(grads, axis=0)
        low = jnp.concatenate(weights, axis=0)
        pair_grads = dot(jnp.concatenate([score_grad, low], axis=1), rows_of(i))
        for j in range(PER):
            acc_ref[slots[j]] += pair_grads[j * BLOCK : (j + 1) * BLOCK]
        turned = jnp.concatenate([tablet_ref[s, :HD, :] for s in slots], axis=1)
        result = dot(turned, score_grad)
        dqt_ref[:, span(i * BLOCK, BLOCK)] = result.astype(BF16)
        return result

    score(0, even_ref)

    @pl.loop(0, PAIRS)
    def _(t):
        score(2 * t + 1, odd_ref)
        first = spread(2 * t, even_ref)
        score(jnp.minimum(2 * t + 2, BLK - 1), even_ref)
        second = spread(2 * t + 1, odd_ref)
        both = jnp.concatenate([first, second], axis=0)
        dq_ref[span(t * BLOCK, BLOCK), :] = both.T.astype(BF16)

    own_ref[...] = acc_ref[:BLK]
    for m in range(count):
        for c in range(CAP):
            leave_refs[m][c] = acc_ref[BLK + (node ^ m) * CAP + c].astype(BF16)
    for part in range(4):
        size = dq_refs[part].shape[0]
        dq_refs[part][...] = dq_ref[span((head ^ part) * size, size), :]


def query_weight_kernel(place_ref, dqt_ref, x0, x1, x2, x3, out_ref):
    head = place_ref[0]
    rows = x0.shape[0]
    total = jnp.zeros((HD, D), F32)
    for part, x_ref in enumerate((x0, x1, x2, x3)):
        total += dot(dqt_ref[:, span((head ^ part) * rows, rows)], x_ref[...])
    out_ref[...] = total


def collect_kernel(count, place_ref, *refs):
    wanted_ref, own_ref, back_refs, refs = refs[0], refs[1], refs[2 : 2 + count][::-1], refs[-5:]
    kvg_refs, sum_ref = refs[:4], refs[4]
    head, node = place_ref[0], place_ref[1]
    sum_ref[...] = own_ref[...]
    for m in range(count):
        for c in range(CAP):
            sum_ref[wanted_ref[node ^ m, 0, c]] += back_refs[m][c].astype(F32)
    for part in range(4):
        size = kvg_refs[part].shape[0] // BLOCK
        first = (head ^ part) * size
        for i in range(size):
            kvg_refs[part][i * BLOCK : (i + 1) * BLOCK, :] = sum_ref[first + i].astype(BF16)


def late_weight_kernel(count, place_ref, k0, k1, k2, k3, xt_ref, owg_ref, qwg_ref, *piece_refs):
    head, node = place_ref[0], place_ref[1]
    total = jnp.zeros((D, BLOCK), F32)
    for part, k_ref in enumerate((k0, k1, k2, k3)):
        rows = k_ref.shape[0]
        total += dot(xt_ref[:, span((head ^ part) * rows, rows)], k_ref[...])
    every = jnp.concatenate([owg_ref[...], qwg_ref[...], total.T], axis=0)
    split(every, group_of(node, top_shift(count)), piece_refs)


def finish_kernel(grad_ref, d0, d1, d2, d3, k0, k1, k2, k3, wq_ref, wkv_ref, out_ref):
    rows = out_ref.shape[0]
    kv = jnp.concatenate([k[...] for k in (k0, k1, k2, k3)], axis=1)
    base = grad_ref[...] + dot_last(kv, wkv_ref[...])
    for pair in range(rows // (2 * BLOCK)):
        lhs = jnp.concatenate(
            [d[pair * BLOCK : (pair + 1) * BLOCK, :] for d in (d0, d1, d2, d3)], axis=1
        )
        product = dot_last(lhs, wq_ref[...])
        for half in range(2):
            at = (2 * pair + half) * BLOCK
            out_ref[at : at + BLOCK, :] = (
                base[at : at + BLOCK] + product[:, half * D : (half + 1) * D]
            ).astype(BF16)


def on_device(features, in_weight, out_weight, cotangent, key_slots, block_count, wanted):
    head_count = lax.axis_size("head")
    node_count = lax.axis_size("node")
    rows = features.shape[0]
    node_rows = rows * head_count
    total_nodes = node_rows * node_count
    table_size = BLK + node_count * CAP
    limit = (14 + table_size // 4) * MIB
    place = jnp.stack([lax.axis_index("head"), lax.axis_index("node")]).astype(jnp.int32)
    block_set = (CAP, BLOCK, BLOCK)

    def swap(value, axis, mask):
        size = lax.axis_size(axis)
        return lax.ppermute(value, axis, [(i, i ^ mask) for i in range(size)])

    def gather_heads(value):
        across = swap(value, "head", 2)
        beside = swap(value, "head", 1)
        return (value, beside, across, swap(across, "head", 1))

    def exchange(pieces, axis, unit=1):
        moved = list(pieces)
        for mask in reversed(range(1, len(pieces))):
            moved[mask] = swap(pieces[mask], axis, mask * unit)
        return moved

    def add_nodes(pieces, shift):
        moved = exchange(pieces, "node", 1 << shift)
        total = (moved[0] + moved[1]) + (moved[2] + moved[3])
        piece_rows = total.shape[0]
        if shift == 1:
            total = total + swap(total, "node", 1)
        elif shift > 1:
            lower = call(
                functools.partial(split_kernel, shift - 2),
                "split",
                [((piece_rows // 4, D), F32)] * 4,
                [smem(), vmem()],
                limit,
            )(place, total)
            (total,) = call(
                functools.partial(join_kernel, shift - 2),
                "join",
                [((piece_rows, D), F32)],
                [smem()] + [vmem()] * 4,
                limit,
            )(place, *add_nodes(lower, shift - 2))
        return exchange([total] * 4, "node", 1 << shift)

    across = swap(features, "head", 2)
    beside = swap(features, "head", 1)
    wants = lax.all_to_all(
        wanted.reshape(node_count, 1, CAP), "node", split_axis=0, concat_axis=0, tiled=True
    )
    (upstream,) = call(carry_kernel, "carry", [((rows, D), BF16)], [vmem(), later()], limit)(
        cotangent, across
    )
    (across,) = fence([across], [wants])
    xs = (features, beside, across, swap(across, "head", 1))
    c_across = swap(upstream, "head", 2)
    qz, kv, *outgoing = call(
        functools.partial(project_kernel, node_count),
        "project",
        [((node_rows, BLOCK), BF16)] * 2 + [(block_set, BF16)] * node_count,
        [smem()] * 2 + [hbm()] + [vmem()] * 3 + [hbm()],
        limit,
        flops=2 * node_rows * D * D,
        scratch=[
            pltpu.VMEM((D, D), BF16),
            pltpu.VMEM((rows, D), BF16),
            pltpu.VMEM((D, 3 * D), BF16),
            pltpu.SemaphoreType.DMA((2,)),
        ],
    )(place, wants, *xs, in_weight)
    incoming = exchange(outgoing, "node")
    xt, kvt, wkv, wq = call(
        prepare_kernel,
        "prepare",
        [
            ((D, node_rows), BF16),
            ((BLK, BLOCK, BLOCK), BF16),
            ((D, 2 * D), BF16),
            ((2 * D, 2 * D), BF16),
        ],
        [smem()] + [vmem()] * 6,
        limit,
        flops=2 * node_rows * D * D,
        scratch=[pltpu.VMEM((HEADS, D, BLOCK), BF16), pltpu.VMEM((HEADS, 2 * D, BLOCK), BF16)],
    )(place, *xs, kv, in_weight)
    late_own, late_across = fence([upstream, c_across], [incoming[1]])
    cs = (upstream, swap(late_own, "head", 1), c_across, swap(late_across, "head", 1))
    att, attt, table, tablet, top, inv = call(
        functools.partial(forward_kernel, node_count),
        "forward",
        [
            ((PAIRS * BLOCK, BLOCK), BF16),
            ((HD, node_rows), BF16),
            ((table_size, BLOCK, BLOCK), BF16),
            ((table_size, BLOCK, BLOCK), BF16),
            ((BLK, 8, BLOCK), F32),
            ((BLK, 8, BLOCK), F32),
        ],
        [smem()] * 3 + [vmem()] * (3 + node_count) + [later()] * 3,
        limit,
        flops=4 * node_rows * PER * BLOCK * BLOCK,
        scratch=[pltpu.VMEM((PER * BLOCK, BLOCK), F32)] * 2,
    )(place, key_slots, block_count, qz, kv, kvt, *incoming[::-1], *cs[1:])
    parts = gather_heads(att)
    output, norm_grad, gz, dots, owg = call(
        middle_kernel,
        "middle",
        [
            ((rows, D), BF16),
            ((rows, D), F32),
            ((node_rows, BLOCK), BF16),
            ((BLK, 8, BLOCK), F32),
            ((HD, D), F32),
        ],
        [smem()] + [vmem()] * 14,
        limit,
        flops=8 * node_rows * D * D,
        scratch=[pltpu.VMEM((2 * D, 2 * D), BF16), pltpu.VMEM((BLOCK, D), BF16)],
    )(place, *xs, *cs, *parts, attt, out_weight)
    own, dqt, *rest = call(
        functools.partial(backward_kernel, node_count),
        "backward",
        [((BLK, BLOCK, BLOCK), F32), ((HD, node_rows), BF16)]
        + [((rows // 2, BLOCK), BF16)] * 4
        + [(block_set, BF16)] * node_count,
        [smem()] * 3 + [vmem()] * 7,
        limit,
        flops=10 * node_rows * PER * BLOCK * BLOCK,
        scratch=[
            pltpu.VMEM((table_size, BLOCK, BLOCK), F32),
            pltpu.VMEM((PAIRS * BLOCK, BLOCK), BF16),
            pltpu.VMEM((PER * BLOCK, 2 * BLOCK), F32),
            pltpu.VMEM((PER * BLOCK, 2 * BLOCK), F32),
        ],
    )(place, key_slots, block_count, qz, gz, table, tablet, top, inv, dots)
    returned = exchange(rest[4:], "node")
    (query_wg,) = call(
        query_weight_kernel,
        "query_weight",
        [((HD, D), F32)],
        [smem()] + [vmem()] * 5,
        limit,
        flops=2 * node_rows * D * HD,
    )(place, dqt, *xs)
    dq_rows = exchange(fence(rest[:4], [query_wg, returned[-1]]), "head")
    kvg = call(
        functools.partial(collect_kernel, node_count),
        "collect",
        [((rows, BLOCK), BF16)] * 4,
        [smem()] * 2 + [vmem()] * (1 + node_count) + [later()] * 3,
        limit,
        scratch=[pltpu.VMEM((BLK, BLOCK, BLOCK), F32)],
    )(place, wants, own, *returned[::-1], *dq_rows[1:])
    kv_rows = exchange(kvg, "head")
    (feature_grad,) = call(
        finish_kernel,
        "finish",
        [((rows, D), BF16)],
        [vmem()] * 11,
        limit,
        flops=4 * rows * 3 * D * D,
    )(norm_grad, *dq_rows, *kv_rows, wq, wkv)
    shift = top_shift(node_count)
    late = call(
        functools.partial(late_weight_kernel, node_count),
        "late_weight",
        [((HD, D), F32)] * 4,
        [smem()] + [vmem()] * 7,
        limit,
        flops=2 * node_rows * D * BLOCK,
    )(place, *kvg, xt, owg, query_wg)
    late = add_nodes(late, shift)
    in_grad, out_grad = call(
        functools.partial(result_kernel, shift, total_nodes ** (-0.5)),
        "result",
        [((3 * HD, D), F32), ((HD, D), F32)],
        [smem()] + [vmem()] * 4,
        limit,
    )(place, *late)
    return (output, feature_grad, in_grad.T, out_grad)


def solution(mesh):
    placed = (
        P(("node", "head"), None),
        P(),
        P(),
        P(("node", "head"), None),
        P("node", None),
        P("node"),
        P("node", None, None),
    )
    return jax.shard_map(
        on_device,
        mesh=mesh,
        in_specs=placed,
        out_specs=(
            P(("node", "head"), None),
            P(("node", "head"), None),
            P(None, "head"),
            P("head", None),
        ),
        check_vma=False,
    )
```

```python
import functools
import math

import jax
import jax.numpy as jnp
from jax import lax
from jax.experimental import pallas as pl
from jax.experimental.pallas import tpu as pltpu
from jax.sharding import PartitionSpec as P

HEADS = 4
HD = 64
BLOCK = 128
BLK = 16
PER = 12
CAP = 2
D = 256
PAIRS = BLK // 2
SCALE = HD ** (-0.5)
SCALE_LOG2E = SCALE * math.log2(math.e)
BF16 = jnp.bfloat16
F32 = jnp.float32
MIB = 1 << 20
LAST = (((1,), (1,)), ((), ()))


def dot(a, b):
    return jnp.dot(a, b, preferred_element_type=F32)


def dot_last(a, b):
    return lax.dot_general(a, b, LAST, preferred_element_type=F32)


def span(start, size):
    return pl.ds(pl.multiple_of(start, size), size)


def smem():
    return pl.BlockSpec(memory_space=pltpu.SMEM)


def vmem():
    return pl.BlockSpec(memory_space=pltpu.VMEM)


def hbm():
    return pl.BlockSpec(memory_space=pltpu.HBM)


def call(kernel, name, outs, in_specs, limit, flops=0, scratch=(), out_specs=None):
    return pl.pallas_call(
        kernel,
        name=name,
        out_shape=tuple(jax.ShapeDtypeStruct(shape, kind) for shape, kind in outs),
        in_specs=in_specs,
        out_specs=tuple(out_specs or [vmem() for _ in outs]),
        scratch_shapes=scratch,
        compiler_params=pltpu.CompilerParams(vmem_limit_bytes=limit),
        cost_estimate=pl.CostEstimate(flops=flops, bytes_accessed=4 * MIB, transcendentals=0),
    )


def top_shift(count):
    return count.bit_length() - 3


def group_of(node, shift):
    return (node >> shift) & 3


def split(value, group, piece_refs):
    size = value.shape[0] // 4
    for g in range(4):
        for m in range(4):

            @pl.when((group ^ m) == g)
            def _():
                piece_refs[m][...] = value[g * size : (g + 1) * size, :]


def split_kernel(shift, place_ref, value_ref, *piece_refs):
    split(value_ref[...], group_of(place_ref[1], shift), piece_refs)


def join(piece_refs, group, g):
    value = piece_refs[0][...]
    for m in range(1, 4):
        value = jnp.where((group ^ m) == g, piece_refs[m][...], value)
    return value


def join_kernel(shift, place_ref, p0, p1, p2, p3, out_ref):
    group = group_of(place_ref[1], shift)
    out_ref[...] = jnp.concatenate([join((p0, p1, p2, p3), group, g) for g in range(4)], axis=0)


def result_kernel(shift, factor, place_ref, l0, l1, l2, l3, in_ref, out_ref):
    group = group_of(place_ref[1], shift)
    pieces = [join((l0, l1, l2, l3), group, g) * factor for g in range(4)]
    out_ref[...] = pieces[0]
    in_ref[...] = jnp.concatenate(pieces[1:], axis=0)


def pair_kernel(own_ref, across_ref, *refs):
    out_ref = refs[-1]
    rows = own_ref.shape[0]
    out_ref[:rows, :] = own_ref[...]
    out_ref[rows:, :] = across_ref[...]


def parts_of(pair_ref, other_ref):
    rows = pair_ref.shape[0] // 2
    return (pair_ref.at[:rows], other_ref.at[:rows], pair_ref.at[rows:], other_ref.at[rows:])


def project_kernel(count, place_ref, wanted_ref, pair_ref, other_ref, in_from, c_from, *refs):
    qz_ref, kv_ref, c_ref, refs = refs[0], refs[1], refs[2], refs[3:]
    out_refs, (wide_ref, in_ref, sems) = refs[:count], refs[count:]
    c_copy = pltpu.make_async_copy(c_from, c_ref, sems.at[0])
    in_copy = pltpu.make_async_copy(in_from, in_ref, sems.at[1])
    in_copy.start()
    c_copy.start()
    x_refs = parts_of(pair_ref, other_ref)
    head, node = place_ref[0], place_ref[1]
    rows = x_refs[0].shape[0]
    in_copy.wait()
    wide_ref[:, HD:BLOCK] = jnp.zeros((D, HD), BF16)
    for g in range(HEADS):

        @pl.when(head == g)
        def _():
            at = g * 3 * HD
            wide_ref[:, :HD] = in_ref[:, at : at + HD]
            wide_ref[:, BLOCK:] = in_ref[:, at + HD : at + 3 * HD]

    for part in range(4):
        at = span((head ^ part) * rows, rows)
        y = dot(x_refs[part][...], wide_ref[...]).astype(BF16)
        qz_ref[at, :] = y[:, :BLOCK]
        kv_ref[at, :] = y[:, BLOCK:]
    for m in range(count):
        for c in range(CAP):
            block = wanted_ref[node ^ m, 0, c]
            out_refs[m][c] = kv_ref[span(block * BLOCK, BLOCK), :]
    c_copy.wait()


def prepare_kernel(place_ref, pair_ref, other_ref, kv_ref, xt_ref, kvt_ref):
    head = place_ref[0]
    rows = pair_ref.shape[0] // 2
    for part, x_ref in enumerate(parts_of(pair_ref, other_ref)):
        xt_ref[:, span((head ^ part) * rows, rows)] = x_ref[...].T
    for i in range(BLK):
        kvt_ref[i] = kv_ref[i * BLOCK : (i + 1) * BLOCK, :].T


def forward_kernel(count, place_ref, slot_ref, count_ref, qz_ref, kv_ref, kvt_ref, *refs):
    in_refs, refs = refs[:count][::-1], refs[-8:]
    att_ref, attt_ref, table_ref, tablet_ref, top_ref, inv_ref, even_ref, odd_ref = refs
    node = place_ref[1]
    for i in range(BLK):
        table_ref[i] = kv_ref[i * BLOCK : (i + 1) * BLOCK, :]
        tablet_ref[i] = kvt_ref[i]
    for m in range(count):
        for c in range(CAP):
            block = in_refs[m][c]
            at = BLK + (node ^ m) * CAP + c
            table_ref[at] = block
            tablet_ref[at] = block.T

    def slots_of(i):
        return [slot_ref[i, j] for j in range(PER)]

    def score(i, raw_ref):
        live = count_ref[i]
        keys = jnp.concatenate([table_ref[s] for s in slots_of(i)], axis=0)
        raw = dot_last(keys, qz_ref[span(i * BLOCK, BLOCK), :])
        top = None
        for j in range(PER):
            here = jnp.where(j < live, raw[j * BLOCK : (j + 1) * BLOCK], -1e30)
            raw_ref[j * BLOCK : (j + 1) * BLOCK, :] = here
            here = here.reshape(BLOCK // 8, 8, BLOCK)
            highest = jnp.max(here, axis=0)
            top = highest if top is None else jnp.maximum(top, highest)
        return jnp.max(top, axis=0, keepdims=True)

    def attend(i, raw_ref, top):
        total = None
        lows = []
        for j in range(PER):
            raised = jnp.exp2((raw_ref[j * BLOCK : (j + 1) * BLOCK, :] - top) * SCALE_LOG2E)
            lows.append(raised.astype(BF16))
            part = jnp.sum(raised.reshape(BLOCK // 8, 8, BLOCK), axis=0)
            total = part if total is None else total + part
        inverse = 1.0 / jnp.sum(total, axis=0, keepdims=True)
        values = jnp.concatenate([tablet_ref[s, HD:, :] for s in slots_of(i)], axis=1)
        result = dot(values, jnp.concatenate(lows, axis=0)) * inverse
        attt_ref[:, span(i * BLOCK, BLOCK)] = result.astype(BF16)
        top_ref[i] = jnp.broadcast_to(top, (8, BLOCK))
        inv_ref[i] = jnp.broadcast_to(inverse, (8, BLOCK))
        return result

    def pair(t, even_top):
        odd_top = score(2 * t + 1, odd_ref)
        first = attend(2 * t, even_ref, even_top)
        even_top = score(jnp.minimum(2 * t + 2, BLK - 1), even_ref)
        second = attend(2 * t + 1, odd_ref, odd_top)
        both = jnp.concatenate([first, second], axis=0)
        att_ref[span(t * BLOCK, BLOCK), :] = both.T.astype(BF16)
        return even_top

    lax.fori_loop(0, PAIRS, pair, score(0, even_ref))


def middle_kernel(
    place_ref, x_pair, x_other, c_pair, c_other, a_pair, a_other, attt_ref, w_ref,
    out_ref, grad_out, gz_ref, dots_ref, owg_ref, wide_ref, pad_ref, grad_ref, sem,
):
    head = place_ref[0]
    rows = grad_ref.shape[0]
    grad_copy = pltpu.make_async_copy(grad_ref, grad_out, sem)
    own_w = w_ref[span(head * HD, HD), :]
    wide_ref[...] = jnp.zeros_like(wide_ref)
    for part in range(4):
        piece = w_ref[span((head ^ part) * HD, HD), :]
        at = (2 * part) * HD
        wide_ref[at : at + HD, :D] = piece
        wide_ref[at + HD : at + 2 * HD, D:] = piece
    pad_ref[:HD, :] = jnp.zeros((HD, D), BF16)
    pad_ref[HD:, :] = own_w
    a_refs = parts_of(a_pair, a_other)
    owg = jnp.zeros((HD, D), F32)
    pairs = rows // (2 * BLOCK)
    for part, (x_ref, c_ref) in enumerate(zip(parts_of(x_pair, x_other), parts_of(c_pair, c_other))):
        group = head ^ part
        at = span(group * (rows // 2), rows // 2)
        lhs = jnp.concatenate([a[at, :] for a in a_refs], axis=1)
        product = dot(lhs, wide_ref[...])
        lows = []
        for i in range(2 * pairs):
            local = slice(i * BLOCK, (i + 1) * BLOCK)
            pair, half = i // 2, i % 2
            summed = x_ref[local, :].astype(F32) + product[
                pair * BLOCK : (pair + 1) * BLOCK, half * D : (half + 1) * D
            ]
            inverse = lax.rsqrt(jnp.mean(summed * summed, axis=-1, keepdims=True) + 1e-06)
            normed = summed * inverse
            upstream = c_ref[local, :].astype(F32)
            grad = (upstream - normed * jnp.mean(upstream * normed, axis=-1, keepdims=True)) * inverse
            lows.append(grad.astype(BF16))
            if part == 0:
                out_ref[local, :] = normed.astype(BF16)
                grad_ref[local, :] = grad
        if part == 0:
            grad_copy.start()
        low = jnp.concatenate(lows, axis=0)
        at = span(group * rows, rows)
        gz_ref[at, :] = dot_last(low, pad_ref[...]).astype(BF16)
        turned = dot_last(own_w, low).astype(BF16).astype(F32)
        attended = attt_ref[:, at]
        sums = jnp.sum(turned * attended.astype(F32), axis=0, keepdims=True)
        for i in range(2 * pairs):
            dots_ref[group * (2 * pairs) + i] = jnp.broadcast_to(
                sums[:, i * BLOCK : (i + 1) * BLOCK], (8, BLOCK)
            )
        owg += dot(attended, low)
    owg_ref[...] = owg
    grad_copy.wait()


def backward_kernel(
    count, place_ref, slot_ref, count_ref, qz_ref, gz_ref, table_ref, tablet_ref, top_ref, inv_ref, dots_ref, *refs
):
    own_ref, dqt_ref, refs = refs[0], refs[1], refs[2:]
    dq_refs, leave_refs = refs[:4], refs[4 : 4 + count]
    acc_ref, dq_ref, even_ref, odd_ref = refs[4 + count :]
    head, node = place_ref[0], place_ref[1]
    acc_ref[...] = jnp.zeros_like(acc_ref)

    def slots_of(i):
        return [slot_ref[i, j] for j in range(PER)]

    def rows_of(i):
        at = span(i * BLOCK, BLOCK)
        return jnp.concatenate([qz_ref[at, :], gz_ref[at, :]], axis=0)

    def score(i, both_ref):
        keys = jnp.concatenate([table_ref[s] for s in slots_of(i)], axis=0)
        both_ref[...] = dot_last(keys, rows_of(i))

    def spread(i, both_ref):
        slots = slots_of(i)
        live = count_ref[i]
        top = top_ref[i, :1, :]
        inverse = inv_ref[i, :1, :]
        dots = dots_ref[i, :1, :]
        weights, grads = [], []
        for j in range(PER):
            here = slice(j * BLOCK, (j + 1) * BLOCK)
            weight = jnp.exp2((both_ref[here, :BLOCK] - top) * SCALE_LOG2E) * inverse
            weight = jnp.where(j < live, weight, 0.0)
            weights.append(weight.astype(BF16))
            grads.append((weight * (both_ref[here, BLOCK:] - dots) * SCALE).astype(BF16))
        score_grad = jnp.concatenate(grads, axis=0)
        low = jnp.concatenate(weights, axis=0)
        pair_grads = dot(jnp.concatenate([score_grad, low], axis=1), rows_of(i))
        for j in range(PER):
            acc_ref[slots[j]] += pair_grads[j * BLOCK : (j + 1) * BLOCK]
        turned = jnp.concatenate([tablet_ref[s, :HD, :] for s in slots], axis=1)
        result = dot(turned, score_grad)
        dqt_ref[:, span(i * BLOCK, BLOCK)] = result.astype(BF16)
        return result

    score(0, even_ref)

    @pl.loop(0, PAIRS)
    def _(t):
        score(2 * t + 1, odd_ref)
        first = spread(2 * t, even_ref)
        score(jnp.minimum(2 * t + 2, BLK - 1), even_ref)
        second = spread(2 * t + 1, odd_ref)
        both = jnp.concatenate([first, second], axis=0)
        dq_ref[span(t * BLOCK, BLOCK), :] = both.T.astype(BF16)

    own_ref[...] = acc_ref[:BLK]
    for m in range(count):
        for c in range(CAP):
            leave_refs[m][c] = acc_ref[BLK + (node ^ m) * CAP + c].astype(BF16)
    for part in range(4):
        size = dq_refs[part].shape[0]
        dq_refs[part][...] = dq_ref[span((head ^ part) * size, size), :]


def query_weight_kernel(place_ref, dqt_ref, pair_ref, other_ref, in_ref, out_ref, wkv_ref, wq_ref, k_ref, q_ref):
    head = place_ref[0]
    rows = pair_ref.shape[0] // 2
    total = jnp.zeros((HD, D), F32)
    for part, x_ref in enumerate(parts_of(pair_ref, other_ref)):
        total += dot(dqt_ref[:, span((head ^ part) * rows, rows)], x_ref[...])
    out_ref[...] = total
    blank = jnp.zeros((D, HD), BF16)
    for g in range(HEADS):
        at = g * 3 * HD
        query = in_ref[:, at : at + HD]
        k_ref[g] = in_ref[:, at + HD : at + 3 * HD]
        q_ref[g, :D] = jnp.concatenate([query, blank], axis=1)
        q_ref[g, D:] = jnp.concatenate([blank, query], axis=1)
    for part in range(4):
        lanes = slice(part * BLOCK, (part + 1) * BLOCK)
        wkv_ref[:, lanes] = k_ref[head ^ part]
        wq_ref[:, lanes] = q_ref[head ^ part]


def collect_kernel(count, place_ref, wanted_ref, own_ref, *refs):
    back_refs, dq_refs, refs = refs[:count][::-1], refs[count : count + 4], refs[count + 4 :]
    send_refs, sum_ref = refs[:4], refs[4]
    head, node = place_ref[0], place_ref[1]
    sum_ref[...] = own_ref[...]
    for m in range(count):
        for c in range(CAP):
            sum_ref[wanted_ref[node ^ m, 0, c]] += back_refs[m][c].astype(F32)
    for part in range(4):
        rows = 2 * dq_refs[part].shape[0]
        first = (head ^ part) * (rows // BLOCK)
        for i in range(rows // BLOCK):
            send_refs[part][i * BLOCK : (i + 1) * BLOCK, :] = sum_ref[first + i].astype(BF16)
        send_refs[part][rows:, :] = dq_refs[part][...]


def late_weight_kernel(count, place_ref, s0, s1, s2, s3, xt_ref, owg_ref, qwg_ref, *piece_refs):
    head, node = place_ref[0], place_ref[1]
    total = jnp.zeros((D, BLOCK), F32)
    for part, s_ref in enumerate((s0, s1, s2, s3)):
        rows = xt_ref.shape[1] // 4
        total += dot(xt_ref[:, span((head ^ part) * rows, rows)], s_ref[:rows, :])
    every = jnp.concatenate([owg_ref[...], qwg_ref[...], total.T], axis=0)
    split(every, group_of(node, top_shift(count)), piece_refs)


def finish_kernel(grad_from, s0, s1, s2, s3, wq_ref, wkv_ref, out_ref, grad_ref, sem):
    grad_copy = pltpu.make_async_copy(grad_from, grad_ref, sem)
    grad_copy.start()
    rows = out_ref.shape[0]
    s_refs = (s0, s1, s2, s3)
    kv = jnp.concatenate([s[:rows, :] for s in s_refs], axis=1)
    base = dot_last(kv, wkv_ref[...])
    lhs = jnp.concatenate([s[rows:, :] for s in s_refs], axis=1)
    product = dot_last(lhs, wq_ref[...])
    grad_copy.wait()
    for i in range(rows // BLOCK):
        at = slice(i * BLOCK, (i + 1) * BLOCK)
        pack = slice(i // 2 * BLOCK, (i // 2 + 1) * BLOCK)
        half = i % 2
        out_ref[at, :] = (
            grad_ref[at, :] + base[at] + product[pack, half * D : (half + 1) * D]
        ).astype(BF16)


def on_device(features, in_weight, out_weight, cotangent, key_slots, block_count, wanted):
    head_count = lax.axis_size("head")
    node_count = lax.axis_size("node")
    rows = features.shape[0]
    node_rows = rows * head_count
    total_nodes = node_rows * node_count
    table_size = BLK + node_count * CAP
    limit = (14 + table_size // 4) * MIB
    place = jnp.stack([lax.axis_index("head"), lax.axis_index("node")]).astype(jnp.int32)
    block_set = (CAP, BLOCK, BLOCK)

    def swap(value, axis, mask):
        size = lax.axis_size(axis)
        return lax.ppermute(value, axis, [(i, i ^ mask) for i in range(size)])

    def pair_up(value, across, after=()):
        (pair,) = call(
            pair_kernel,
            "pair",
            [((2 * value.shape[0], value.shape[1]), value.dtype)],
            [vmem()] * (2 + len(after)),
            4 * MIB,
        )(value, across, *after)
        return pair, swap(pair, "head", 1)

    def exchange(pieces, axis, unit=1):
        moved = list(pieces)
        for mask in reversed(range(1, len(pieces))):
            moved[mask] = swap(pieces[mask], axis, mask * unit)
        return moved

    def add_nodes(pieces, shift):
        moved = exchange(pieces, "node", 1 << shift)
        total = (moved[0] + moved[1]) + (moved[2] + moved[3])
        piece_rows = total.shape[0]
        if shift == 1:
            total = total + swap(total, "node", 1)
        elif shift > 1:
            lower = call(
                functools.partial(split_kernel, shift - 2),
                "split",
                [((piece_rows // 4, D), F32)] * 4,
                [smem(), vmem()],
                limit,
            )(place, total)
            (total,) = call(
                functools.partial(join_kernel, shift - 2),
                "join",
                [((piece_rows, D), F32)],
                [smem()] + [vmem()] * 4,
                limit,
            )(place, *add_nodes(lower, shift - 2))
        return exchange([total] * 4, "node", 1 << shift)

    across = swap(features, "head", 2)
    wants = lax.all_to_all(
        wanted.reshape(node_count, 1, CAP), "node", split_axis=0, concat_axis=0, tiled=True
    )
    xs = pair_up(features, across, [wants])
    qz, kv, upstream, *outgoing = call(
        functools.partial(project_kernel, node_count),
        "project",
        [((node_rows, BLOCK), BF16)] * 2 + [((rows, D), BF16)] + [(block_set, BF16)] * node_count,
        [smem()] * 2 + [vmem()] * 2 + [hbm()] * 2,
        limit,
        flops=2 * node_rows * D * D,
        scratch=[
            pltpu.VMEM((D, D), BF16),
            pltpu.VMEM((D, 3 * D), BF16),
            pltpu.SemaphoreType.DMA((2,)),
        ],
    )(place, wants, *xs, in_weight, cotangent)
    incoming = exchange(outgoing, "node")
    c_across = swap(upstream, "head", 2)
    xt, kvt = call(
        prepare_kernel,
        "prepare",
        [((D, node_rows), BF16), ((BLK, BLOCK, BLOCK), BF16)],
        [smem()] + [vmem()] * 3,
        limit,
        flops=2 * node_rows * D * D,
    )(place, *xs, kv)
    att, attt, table, tablet, top, inv = call(
        functools.partial(forward_kernel, node_count),
        "forward",
        [
            ((PAIRS * BLOCK, BLOCK), BF16),
            ((HD, node_rows), BF16),
            ((table_size, BLOCK, BLOCK), BF16),
            ((table_size, BLOCK, BLOCK), BF16),
            ((BLK, 8, BLOCK), F32),
            ((BLK, 8, BLOCK), F32),
        ],
        [smem()] * 3 + [vmem()] * (4 + node_count),
        limit,
        flops=4 * node_rows * PER * BLOCK * BLOCK,
        scratch=[pltpu.VMEM((PER * BLOCK, BLOCK), F32)] * 2,
    )(place, key_slots, block_count, qz, kv, kvt, *incoming[::-1], c_across)
    parts = pair_up(att, swap(att, "head", 2))
    cs = pair_up(upstream, c_across, [top])
    output, norm_grad, gz, dots, owg = call(
        middle_kernel,
        "middle",
        [
            ((rows, D), BF16),
            ((rows, D), F32),
            ((node_rows, BLOCK), BF16),
            ((BLK, 8, BLOCK), F32),
            ((HD, D), F32),
        ],
        [smem()] + [vmem()] * 8,
        limit,
        flops=8 * node_rows * D * D,
        scratch=[
            pltpu.VMEM((2 * D, 2 * D), BF16),
            pltpu.VMEM((BLOCK, D), BF16),
            pltpu.VMEM((rows, D), F32),
            pltpu.SemaphoreType.DMA,
        ],
        out_specs=[vmem(), hbm()] + [vmem()] * 3,
    )(place, *xs, *cs, *parts, attt, out_weight)
    own, dqt, *rest = call(
        functools.partial(backward_kernel, node_count),
        "backward",
        [((BLK, BLOCK, BLOCK), F32), ((HD, node_rows), BF16)]
        + [((rows // 2, BLOCK), BF16)] * 4
        + [(block_set, BF16)] * node_count,
        [smem()] * 3 + [vmem()] * 7,
        limit,
        flops=10 * node_rows * PER * BLOCK * BLOCK,
        scratch=[
            pltpu.VMEM((table_size, BLOCK, BLOCK), F32),
            pltpu.VMEM((PAIRS * BLOCK, BLOCK), BF16),
            pltpu.VMEM((PER * BLOCK, 2 * BLOCK), F32),
            pltpu.VMEM((PER * BLOCK, 2 * BLOCK), F32),
        ],
    )(place, key_slots, block_count, qz, gz, table, tablet, top, inv, dots)
    returned = exchange(rest[4:], "node")
    query_wg, wkv, wq = call(
        query_weight_kernel,
        "query_weight",
        [((HD, D), F32), ((D, 2 * D), BF16), ((2 * D, 2 * D), BF16)],
        [smem()] + [vmem()] * 4,
        limit,
        flops=2 * node_rows * D * HD,
        scratch=[pltpu.VMEM((HEADS, D, BLOCK), BF16), pltpu.VMEM((HEADS, 2 * D, BLOCK), BF16)],
    )(place, dqt, *xs, in_weight)
    sends = call(
        functools.partial(collect_kernel, node_count),
        "collect",
        [((rows * 3 // 2, BLOCK), BF16)] * 4,
        [smem()] * 2 + [vmem()] * (5 + node_count),
        limit,
        scratch=[pltpu.VMEM((BLK, BLOCK, BLOCK), F32)],
    )(place, wants, own, *returned[::-1], *rest[:4])
    arrived = exchange(sends, "head")
    (feature_grad,) = call(
        finish_kernel,
        "finish",
        [((rows, D), BF16)],
        [hbm()] + [vmem()] * 6,
        limit,
        flops=4 * rows * 3 * D * D,
        scratch=[pltpu.VMEM((rows, D), F32), pltpu.SemaphoreType.DMA],
    )(norm_grad, *arrived, wq, wkv)
    shift = top_shift(node_count)
    late = call(
        functools.partial(late_weight_kernel, node_count),
        "late_weight",
        [((HD, D), F32)] * 4,
        [smem()] + [vmem()] * 7,
        limit,
        flops=2 * node_rows * D * BLOCK,
    )(place, *sends, xt, owg, query_wg)
    late = add_nodes(late, shift)
    in_grad, out_grad = call(
        functools.partial(result_kernel, shift, total_nodes ** (-0.5)),
        "result",
        [((3 * HD, D), F32), ((HD, D), F32)],
        [smem()] + [vmem()] * 4,
        limit,
    )(place, *late)
    return (output, feature_grad, in_grad.T, out_grad)


def solution(mesh):
    placed = (
        P(("node", "head"), None),
        P(),
        P(),
        P(("node", "head"), None),
        P("node", None),
        P("node"),
        P("node", None, None),
    )
    return jax.shard_map(
        on_device,
        mesh=mesh,
        in_specs=placed,
        out_specs=(
            P(("node", "head"), None),
            P(("node", "head"), None),
            P(None, "head"),
            P("head", None),
        ),
        check_vma=False,
    )
```

```python
import functools
import math

import jax
import jax.numpy as jnp
from jax import lax
from jax.experimental import pallas as pl
from jax.experimental.pallas import tpu as pltpu
from jax.sharding import PartitionSpec as P

HEADS = 4
HD = 64
BLOCK = 128
BLK = 16
PER = 12
CAP = 2
D = 256
PAIRS = BLK // 2
SCALE = HD ** (-0.5)
SCALE_LOG2E = SCALE * math.log2(math.e)
BF16 = jnp.bfloat16
F32 = jnp.float32
MIB = 1 << 20
LAST = (((1,), (1,)), ((), ()))


def dot(a, b):
    return jnp.dot(a, b, preferred_element_type=F32)


def dot_last(a, b):
    return lax.dot_general(a, b, LAST, preferred_element_type=F32)


def span(start, size):
    return pl.ds(pl.multiple_of(start, size), size)


def smem():
    return pl.BlockSpec(memory_space=pltpu.SMEM)


def vmem():
    return pl.BlockSpec(memory_space=pltpu.VMEM)


def hbm():
    return pl.BlockSpec(memory_space=pltpu.HBM)


def call(kernel, name, outs, in_specs, limit, flops=0, scratch=(), out_specs=None):
    return pl.pallas_call(
        kernel,
        name=name,
        out_shape=tuple(jax.ShapeDtypeStruct(shape, kind) for shape, kind in outs),
        in_specs=in_specs,
        out_specs=tuple(out_specs or [vmem() for _ in outs]),
        scratch_shapes=scratch,
        compiler_params=pltpu.CompilerParams(vmem_limit_bytes=limit),
        cost_estimate=pl.CostEstimate(flops=flops, bytes_accessed=4 * MIB, transcendentals=0),
    )


def top_shift(count):
    return count.bit_length() - 3


def group_of(node, shift):
    return (node >> shift) & 3


def split(value, group, piece_refs):
    size = value.shape[0] // 4
    for g in range(4):
        for m in range(4):

            @pl.when((group ^ m) == g)
            def _():
                piece_refs[m][...] = value[g * size : (g + 1) * size, :]


def split_kernel(shift, place_ref, value_ref, *piece_refs):
    split(value_ref[...], group_of(place_ref[1], shift), piece_refs)


def join(piece_refs, group, g):
    value = piece_refs[0][...]
    for m in range(1, 4):
        value = jnp.where((group ^ m) == g, piece_refs[m][...], value)
    return value


def join_kernel(shift, place_ref, p0, p1, p2, p3, out_ref):
    group = group_of(place_ref[1], shift)
    out_ref[...] = jnp.concatenate([join((p0, p1, p2, p3), group, g) for g in range(4)], axis=0)


def sum_kernel(factor, *refs):
    refs, out_ref = refs[:4], refs[-1]
    out_ref[...] = ((refs[0][...] + refs[1][...]) + (refs[2][...] + refs[3][...])) * factor


def result_kernel(shift, place_ref, l0, l1, l2, l3, after_ref, in_ref, out_ref, sems):
    group = group_of(place_ref[1], shift)
    copies = []
    for m, piece_ref in enumerate((l0, l1, l2, l3)):
        at = group ^ m
        first = pltpu.make_async_copy(piece_ref, out_ref, sems.at[m])

        @pl.when(at == 0)
        def _():
            first.start()

        @pl.when(at > 0)
        def _():
            rows = in_ref.at[span((at - 1) * HD, HD), :]
            pltpu.make_async_copy(piece_ref, rows, sems.at[m]).start()

        copies.append(first)
    for copy in copies:
        copy.wait()


def pair_kernel(own_ref, across_ref, *refs):
    out_ref = refs[-1]
    rows = own_ref.shape[0]
    out_ref[:rows, :] = own_ref[...]
    out_ref[rows:, :] = across_ref[...]


def parts_of(pair_ref, other_ref):
    rows = pair_ref.shape[0] // 2
    return (pair_ref.at[:rows], other_ref.at[:rows], pair_ref.at[rows:], other_ref.at[rows:])


def issue_order(count):
    near, far = list(range(1, count // 2)), list(range(count // 2, count))
    return [0] + far[:2] + near + far[2:]


def by_mask(refs):
    order = issue_order(len(refs))
    return [refs[order.index(m)] for m in range(len(refs))]


def project_kernel(count, place_ref, wanted_ref, pair_ref, other_ref, in_from, *refs):
    qz_ref, kv_ref, refs = refs[0], refs[1], refs[2:]
    out_refs, (wide_ref, in_ref, sem) = refs[:count], refs[count:]
    in_copy = pltpu.make_async_copy(in_from, in_ref, sem)
    in_copy.start()
    x_refs = parts_of(pair_ref, other_ref)
    head, node = place_ref[0], place_ref[1]
    rows = x_refs[0].shape[0]
    in_copy.wait()
    wide_ref[:, HD:BLOCK] = jnp.zeros((D, HD), BF16)
    for g in range(HEADS):

        @pl.when(head == g)
        def _():
            at = g * 3 * HD
            wide_ref[:, :HD] = in_ref[:, at : at + HD]
            wide_ref[:, BLOCK:] = in_ref[:, at + HD : at + 3 * HD]

    for part in range(4):
        at = span((head ^ part) * rows, rows)
        y = dot(x_refs[part][...], wide_ref[...]).astype(BF16)
        qz_ref[at, :] = y[:, :BLOCK]
        kv_ref[at, :] = y[:, BLOCK:]
    for m in range(count):
        for c in range(CAP):
            block = wanted_ref[node ^ m, 0, c]
            out_refs[m][c] = kv_ref[span(block * BLOCK, BLOCK), :]


def prepare_kernel(place_ref, pair_ref, other_ref, kv_ref, after_ref, xt_ref, kvt_ref):
    head = place_ref[0]
    rows = pair_ref.shape[0] // 2
    for part, x_ref in enumerate(parts_of(pair_ref, other_ref)):
        xt_ref[:, span((head ^ part) * rows, rows)] = x_ref[...].T
    for i in range(BLK):
        kvt_ref[i] = kv_ref[i * BLOCK : (i + 1) * BLOCK, :].T


def forward_kernel(count, place_ref, slot_from, count_from, qz_ref, kv_ref, kvt_ref, *refs):
    in_refs, refs = by_mask(refs[:count]), refs[count:]
    att_ref, attt_ref, table_ref, tablet_ref, top_ref, inv_ref, refs = *refs[:6], refs[6:]
    even_ref, odd_ref, slot_ref, count_ref, sems = refs
    slot_copy = pltpu.make_async_copy(slot_from, slot_ref, sems.at[0])
    count_copy = pltpu.make_async_copy(count_from, count_ref, sems.at[1])
    slot_copy.start()
    count_copy.start()
    node = place_ref[1]
    for i in range(BLK):
        table_ref[i] = kv_ref[i * BLOCK : (i + 1) * BLOCK, :]
        tablet_ref[i] = kvt_ref[i]
    for m in range(count):
        for c in range(CAP):
            block = in_refs[m][c]
            at = BLK + (node ^ m) * CAP + c
            table_ref[at] = block
            tablet_ref[at] = block.T
    slot_copy.wait()
    count_copy.wait()

    def slots_of(i):
        return [slot_ref[i, j] for j in range(PER)]

    def score(i, raw_ref):
        live = count_ref[i]
        keys = jnp.concatenate([table_ref[s] for s in slots_of(i)], axis=0)
        raw = dot_last(keys, qz_ref[span(i * BLOCK, BLOCK), :])
        top = None
        for j in range(PER):
            here = jnp.where(j < live, raw[j * BLOCK : (j + 1) * BLOCK], -1e30)
            raw_ref[j * BLOCK : (j + 1) * BLOCK, :] = here
            here = here.reshape(BLOCK // 8, 8, BLOCK)
            highest = jnp.max(here, axis=0)
            top = highest if top is None else jnp.maximum(top, highest)
        return jnp.max(top, axis=0, keepdims=True)

    def attend(i, raw_ref, top):
        total = None
        lows = []
        for j in range(PER):
            raised = jnp.exp2((raw_ref[j * BLOCK : (j + 1) * BLOCK, :] - top) * SCALE_LOG2E)
            lows.append(raised.astype(BF16))
            part = jnp.sum(raised.reshape(BLOCK // 8, 8, BLOCK), axis=0)
            total = part if total is None else total + part
        inverse = 1.0 / jnp.sum(total, axis=0, keepdims=True)
        values = jnp.concatenate([tablet_ref[s, HD:, :] for s in slots_of(i)], axis=1)
        result = dot(values, jnp.concatenate(lows, axis=0)) * inverse
        attt_ref[:, span(i * BLOCK, BLOCK)] = result.astype(BF16)
        top_ref[i] = jnp.broadcast_to(top, (8, BLOCK))
        inv_ref[i] = jnp.broadcast_to(inverse, (8, BLOCK))
        return result

    def pair(t, even_top):
        odd_top = score(2 * t + 1, odd_ref)
        first = attend(2 * t, even_ref, even_top)
        even_top = score(jnp.minimum(2 * t + 2, BLK - 1), even_ref)
        second = attend(2 * t + 1, odd_ref, odd_top)
        both = jnp.concatenate([first, second], axis=0)
        att_ref[span(t * BLOCK, BLOCK), :] = both.T.astype(BF16)
        return even_top

    lax.fori_loop(0, PAIRS, pair, score(0, even_ref))


def middle_kernel(
    place_ref, x_pair, x_other, c_pair, c_other, a_pair, a_other, attt_ref, w_ref,
    out_ref, grad_out, gz_ref, dots_ref, owg_ref, wide_ref, pad_ref, grad_ref, sem,
):
    head = place_ref[0]
    rows = grad_ref.shape[0]
    grad_copy = pltpu.make_async_copy(grad_ref, grad_out, sem)
    own_w = w_ref[span(head * HD, HD), :]
    wide_ref[...] = jnp.zeros_like(wide_ref)
    for part in range(4):
        piece = w_ref[span((head ^ part) * HD, HD), :]
        at = (2 * part) * HD
        wide_ref[at : at + HD, :D] = piece
        wide_ref[at + HD : at + 2 * HD, D:] = piece
    pad_ref[:HD, :] = jnp.zeros((HD, D), BF16)
    pad_ref[HD:, :] = own_w
    a_refs = parts_of(a_pair, a_other)
    owg = jnp.zeros((HD, D), F32)
    pairs = rows // (2 * BLOCK)
    for part, (x_ref, c_ref) in enumerate(zip(parts_of(x_pair, x_other), parts_of(c_pair, c_other))):
        group = head ^ part
        at = span(group * (rows // 2), rows // 2)
        lhs = jnp.concatenate([a[at, :] for a in a_refs], axis=1)
        product = dot(lhs, wide_ref[...])
        lows = []
        for i in range(2 * pairs):
            local = slice(i * BLOCK, (i + 1) * BLOCK)
            pair, half = i // 2, i % 2
            summed = x_ref[local, :].astype(F32) + product[
                pair * BLOCK : (pair + 1) * BLOCK, half * D : (half + 1) * D
            ]
            inverse = lax.rsqrt(jnp.mean(summed * summed, axis=-1, keepdims=True) + 1e-06)
            normed = summed * inverse
            upstream = c_ref[local, :].astype(F32)
            grad = (upstream - normed * jnp.mean(upstream * normed, axis=-1, keepdims=True)) * inverse
            lows.append(grad.astype(BF16))
            if part == 0:
                out_ref[local, :] = normed.astype(BF16)
                grad_ref[local, :] = grad
        if part == 0:
            grad_copy.start()
        low = jnp.concatenate(lows, axis=0)
        at = span(group * rows, rows)
        gz_ref[at, :] = dot_last(low, pad_ref[...]).astype(BF16)
        turned = dot_last(own_w, low).astype(BF16).astype(F32)
        attended = attt_ref[:, at]
        sums = jnp.sum(turned * attended.astype(F32), axis=0, keepdims=True)
        for i in range(2 * pairs):
            dots_ref[group * (2 * pairs) + i] = jnp.broadcast_to(
                sums[:, i * BLOCK : (i + 1) * BLOCK], (8, BLOCK)
            )
        owg += dot(attended, low)
    owg_ref[...] = owg
    grad_copy.wait()


def backward_kernel(
    count, place_ref, slot_ref, count_ref, qz_ref, gz_ref, table_ref, tablet_ref, top_ref, inv_ref, dots_ref, *refs
):
    own_ref, dqt_ref, refs = refs[0], refs[1], refs[2:]
    dq_refs, leave_refs = refs[:4], refs[4 : 4 + count]
    acc_ref, dq_ref, even_ref, odd_ref = refs[4 + count :]
    head, node = place_ref[0], place_ref[1]
    acc_ref[...] = jnp.zeros_like(acc_ref)

    def slots_of(i):
        return [slot_ref[i, j] for j in range(PER)]

    def rows_of(i):
        at = span(i * BLOCK, BLOCK)
        return jnp.concatenate([qz_ref[at, :], gz_ref[at, :]], axis=0)

    def score(i, both_ref):
        keys = jnp.concatenate([table_ref[s] for s in slots_of(i)], axis=0)
        both_ref[...] = dot_last(keys, rows_of(i))

    def spread(i, both_ref):
        slots = slots_of(i)
        live = count_ref[i]
        top = top_ref[i, :1, :]
        inverse = inv_ref[i, :1, :]
        dots = dots_ref[i, :1, :]
        weights, grads = [], []
        for j in range(PER):
            here = slice(j * BLOCK, (j + 1) * BLOCK)
            weight = jnp.exp2((both_ref[here, :BLOCK] - top) * SCALE_LOG2E) * inverse
            weight = jnp.where(j < live, weight, 0.0)
            weights.append(weight.astype(BF16))
            grads.append((weight * (both_ref[here, BLOCK:] - dots) * SCALE).astype(BF16))
        score_grad = jnp.concatenate(grads, axis=0)
        low = jnp.concatenate(weights, axis=0)
        pair_grads = dot(jnp.concatenate([score_grad, low], axis=1), rows_of(i))
        for j in range(PER):
            acc_ref[slots[j]] += pair_grads[j * BLOCK : (j + 1) * BLOCK]
        turned = jnp.concatenate([tablet_ref[s, :HD, :] for s in slots], axis=1)
        result = dot(turned, score_grad)
        dqt_ref[:, span(i * BLOCK, BLOCK)] = result.astype(BF16)
        return result

    score(0, even_ref)

    @pl.loop(0, PAIRS)
    def _(t):
        score(2 * t + 1, odd_ref)
        first = spread(2 * t, even_ref)
        score(jnp.minimum(2 * t + 2, BLK - 1), even_ref)
        second = spread(2 * t + 1, odd_ref)
        both = jnp.concatenate([first, second], axis=0)
        dq_ref[span(t * BLOCK, BLOCK), :] = both.T.astype(BF16)

    own_ref[...] = acc_ref[:BLK]
    for m in range(count):
        for c in range(CAP):
            leave_refs[m][c] = acc_ref[BLK + (node ^ m) * CAP + c].astype(BF16)
    for part in range(4):
        size = dq_refs[part].shape[0]
        dq_refs[part][...] = dq_ref[span((head ^ part) * size, size), :]


def query_weight_kernel(place_ref, dqt_ref, pair_ref, other_ref, in_ref, out_ref, wkv_ref, wq_ref, k_ref, q_ref):
    head = place_ref[0]
    rows = pair_ref.shape[0] // 2
    total = jnp.zeros((HD, D), F32)
    for part, x_ref in enumerate(parts_of(pair_ref, other_ref)):
        total += dot(dqt_ref[:, span((head ^ part) * rows, rows)], x_ref[...])
    out_ref[...] = total
    blank = jnp.zeros((D, HD), BF16)
    for g in range(HEADS):
        at = g * 3 * HD
        query = in_ref[:, at : at + HD]
        k_ref[g] = in_ref[:, at + HD : at + 3 * HD]
        q_ref[g, :D] = jnp.concatenate([query, blank], axis=1)
        q_ref[g, D:] = jnp.concatenate([blank, query], axis=1)
    for part in range(4):
        lanes = slice(part * BLOCK, (part + 1) * BLOCK)
        wkv_ref[:, lanes] = k_ref[head ^ part]
        wq_ref[:, lanes] = q_ref[head ^ part]


def collect_kernel(count, place_ref, wanted_ref, own_ref, *refs):
    back_refs, dq_refs, refs = by_mask(refs[:count]), refs[count : count + 4], refs[count + 4 :]
    xt_ref, owg_ref, qwg_ref, refs = *refs[:3], refs[3:]
    send_refs, piece_refs, sum_ref = refs[:4], refs[4:8], refs[8]
    head, node = place_ref[0], place_ref[1]
    sum_ref[...] = own_ref[...]
    for m in range(count):
        for c in range(CAP):
            sum_ref[wanted_ref[node ^ m, 0, c]] += back_refs[m][c].astype(F32)
    for part in range(4):
        rows = 2 * dq_refs[part].shape[0]
        first = (head ^ part) * (rows // BLOCK)
        for i in range(rows // BLOCK):
            send_refs[part][i * BLOCK : (i + 1) * BLOCK, :] = sum_ref[first + i].astype(BF16)
        send_refs[part][rows:, :] = dq_refs[part][...]
    total = jnp.zeros((D, BLOCK), F32)
    for part in range(4):
        rows = 2 * dq_refs[part].shape[0]
        total += dot(xt_ref[:, span((head ^ part) * rows, rows)], send_refs[part][:rows, :])
    every = jnp.concatenate([owg_ref[...], qwg_ref[...], total.T], axis=0)
    split(every, group_of(node, top_shift(count)), piece_refs)


def finish_kernel(grad_from, s0, s3, s2, s1, wq_ref, wkv_ref, out_ref, grad_ref, sem):
    grad_copy = pltpu.make_async_copy(grad_from, grad_ref, sem)
    grad_copy.start()
    rows = out_ref.shape[0]
    s_refs = (s0, s1, s2, s3)
    kv = jnp.concatenate([s[:rows, :] for s in s_refs], axis=1)
    base = dot_last(kv, wkv_ref[...])
    lhs = jnp.concatenate([s[rows:, :] for s in s_refs], axis=1)
    product = dot_last(lhs, wq_ref[...])
    grad_copy.wait()
    for i in range(rows // BLOCK):
        at = slice(i * BLOCK, (i + 1) * BLOCK)
        pack = slice(i // 2 * BLOCK, (i // 2 + 1) * BLOCK)
        half = i % 2
        out_ref[at, :] = (
            grad_ref[at, :] + base[at] + product[pack, half * D : (half + 1) * D]
        ).astype(BF16)


def on_device(features, in_weight, out_weight, cotangent, key_slots, block_count, wanted):
    head_count = lax.axis_size("head")
    node_count = lax.axis_size("node")
    rows = features.shape[0]
    node_rows = rows * head_count
    total_nodes = node_rows * node_count
    table_size = BLK + node_count * CAP
    limit = (14 + table_size // 4) * MIB
    place = jnp.stack([lax.axis_index("head"), lax.axis_index("node")]).astype(jnp.int32)
    block_set = (CAP, BLOCK, BLOCK)

    def swap(value, axis, mask):
        size = lax.axis_size(axis)
        return lax.ppermute(value, axis, [(i, i ^ mask) for i in range(size)])

    def pair_up(value, across, after=()):
        (pair,) = call(
            pair_kernel,
            "pair",
            [((2 * value.shape[0], value.shape[1]), value.dtype)],
            [vmem()] * (2 + len(after)),
            4 * MIB,
        )(value, across, *after)
        return pair, swap(pair, "head", 1)

    def exchange(pieces, axis, unit=1):
        moved = list(pieces)
        for mask in reversed(range(1, len(pieces))):
            moved[mask] = swap(pieces[mask], axis, mask * unit)
        return moved

    def add_nodes(pieces, shift, factor, after=()):
        moved = exchange(pieces, "node", 1 << shift)
        piece = (pieces[0].shape, F32)
        (total,) = call(
            functools.partial(sum_kernel, factor),
            "sum",
            [piece],
            [vmem()] * (4 + len(after)),
            4 * MIB,
        )(moved[0], *moved[:0:-1], *after)
        if shift == 1:
            total = total + swap(total, "node", 1)
        elif shift > 1:
            lower = call(
                functools.partial(split_kernel, shift - 2),
                "split",
                [((piece[0][0] // 4, D), F32)] * 4,
                [smem(), vmem()],
                limit,
            )(place, total)
            (total,) = call(
                functools.partial(join_kernel, shift - 2),
                "join",
                [piece],
                [smem()] + [vmem()] * 4,
                limit,
            )(place, *add_nodes(lower, shift - 2, 1.0))
        return exchange([total] * 4, "node", 1 << shift)

    order = issue_order(node_count)
    across = swap(features, "head", 2)
    c_across = swap(cotangent, "head", 2)
    wants = lax.all_to_all(
        wanted.reshape(node_count, 1, CAP), "node", split_axis=0, concat_axis=0, tiled=True
    )
    xs = pair_up(features, across, [wants])
    qz, kv, *outgoing = call(
        functools.partial(project_kernel, node_count),
        "project",
        [((node_rows, BLOCK), BF16)] * 2 + [(block_set, BF16)] * node_count,
        [smem()] * 2 + [vmem()] * 2 + [hbm()],
        limit,
        flops=2 * node_rows * D * D,
        scratch=[
            pltpu.VMEM((D, D), BF16),
            pltpu.VMEM((D, 3 * D), BF16),
            pltpu.SemaphoreType.DMA,
        ],
    )(place, wants, *xs, in_weight)
    incoming = exchange(outgoing, "node")
    xt, kvt = call(
        prepare_kernel,
        "prepare",
        [((D, node_rows), BF16), ((BLK, BLOCK, BLOCK), BF16)],
        [smem()] + [vmem()] * 4,
        limit,
        flops=2 * node_rows * D * D,
    )(place, *xs, kv, c_across)
    att, attt, table, tablet, top, inv = call(
        functools.partial(forward_kernel, node_count),
        "forward",
        [
            ((PAIRS * BLOCK, BLOCK), BF16),
            ((HD, node_rows), BF16),
            ((table_size, BLOCK, BLOCK), BF16),
            ((table_size, BLOCK, BLOCK), BF16),
            ((BLK, 8, BLOCK), F32),
            ((BLK, 8, BLOCK), F32),
        ],
        [smem(), hbm(), hbm()] + [vmem()] * (3 + node_count),
        limit,
        flops=4 * node_rows * PER * BLOCK * BLOCK,
        scratch=[pltpu.VMEM((PER * BLOCK, BLOCK), F32)] * 2
        + [
            pltpu.SMEM((BLK, PER), jnp.int32),
            pltpu.SMEM((BLK,), jnp.int32),
            pltpu.SemaphoreType.DMA((2,)),
        ],
    )(place, key_slots, block_count, qz, kv, kvt, *[incoming[m] for m in order])
    parts = pair_up(att, swap(att, "head", 2))
    cs = pair_up(cotangent, c_across, [top])
    output, norm_grad, gz, dots, owg = call(
        middle_kernel,
        "middle",
        [
            ((rows, D), BF16),
            ((rows, D), F32),
            ((node_rows, BLOCK), BF16),
            ((BLK, 8, BLOCK), F32),
            ((HD, D), F32),
        ],
        [smem()] + [vmem()] * 8,
        limit,
        flops=8 * node_rows * D * D,
        scratch=[
            pltpu.VMEM((2 * D, 2 * D), BF16),
            pltpu.VMEM((BLOCK, D), BF16),
            pltpu.VMEM((rows, D), F32),
            pltpu.SemaphoreType.DMA,
        ],
        out_specs=[vmem(), hbm()] + [vmem()] * 3,
    )(place, *xs, *cs, *parts, attt, out_weight)
    own, dqt, *rest = call(
        functools.partial(backward_kernel, node_count),
        "backward",
        [((BLK, BLOCK, BLOCK), F32), ((HD, node_rows), BF16)]
        + [((rows // 2, BLOCK), BF16)] * 4
        + [(block_set, BF16)] * node_count,
        [smem()] * 3 + [vmem()] * 7,
        limit,
        flops=10 * node_rows * PER * BLOCK * BLOCK,
        scratch=[
            pltpu.VMEM((table_size, BLOCK, BLOCK), F32),
            pltpu.VMEM((PAIRS * BLOCK, BLOCK), BF16),
            pltpu.VMEM((PER * BLOCK, 2 * BLOCK), F32),
            pltpu.VMEM((PER * BLOCK, 2 * BLOCK), F32),
        ],
    )(place, key_slots, block_count, qz, gz, table, tablet, top, inv, dots)
    returned = exchange(rest[4:], "node")
    query_wg, wkv, wq = call(
        query_weight_kernel,
        "query_weight",
        [((HD, D), F32), ((D, 2 * D), BF16), ((2 * D, 2 * D), BF16)],
        [smem()] + [vmem()] * 4,
        limit,
        flops=2 * node_rows * D * HD,
        scratch=[pltpu.VMEM((HEADS, D, BLOCK), BF16), pltpu.VMEM((HEADS, 2 * D, BLOCK), BF16)],
    )(place, dqt, *xs, in_weight)
    collected = call(
        functools.partial(collect_kernel, node_count),
        "collect",
        [((rows * 3 // 2, BLOCK), BF16)] * 4 + [((HD, D), F32)] * 4,
        [smem()] * 2 + [vmem()] * (8 + node_count),
        limit,
        flops=2 * node_rows * D * BLOCK,
        scratch=[pltpu.VMEM((BLK, BLOCK, BLOCK), F32)],
    )(place, wants, own, *[returned[m] for m in order], *rest[:4], xt, owg, query_wg)
    arrived = exchange(collected[:4], "head")
    (feature_grad,) = call(
        finish_kernel,
        "finish",
        [((rows, D), BF16)],
        [hbm()] + [vmem()] * 6,
        limit,
        flops=4 * rows * 3 * D * D,
        scratch=[pltpu.VMEM((rows, D), F32), pltpu.SemaphoreType.DMA],
    )(norm_grad, arrived[0], *arrived[:0:-1], wq, wkv)
    shift = top_shift(node_count)
    factor = total_nodes ** (-0.5)
    late = add_nodes(collected[4:], shift, factor)
    in_grad, out_grad = call(
        functools.partial(result_kernel, shift),
        "result",
        [((3 * HD, D), F32), ((HD, D), F32)],
        [smem()] + [vmem()] * 4 + [hbm()],
        limit,
        scratch=[pltpu.SemaphoreType.DMA((4,))],
        out_specs=[hbm(), hbm()],
    )(place, *late, feature_grad)
    return (output, feature_grad, in_grad.T, out_grad)


def solution(mesh):
    placed = (
        P(("node", "head"), None),
        P(),
        P(),
        P(("node", "head"), None),
        P("node", None),
        P("node"),
        P("node", None, None),
    )
    return jax.shard_map(
        on_device,
        mesh=mesh,
        in_specs=placed,
        out_specs=(
            P(("node", "head"), None),
            P(("node", "head"), None),
            P(None, "head"),
            P("head", None),
        ),
        check_vma=False,
    )
```

```python
import functools
import math

import jax
import jax.numpy as jnp
from jax import lax
from jax.experimental import pallas as pl
from jax.experimental.pallas import tpu as pltpu
from jax.sharding import PartitionSpec as P

HEADS = 4
HD = 64
BLOCK = 128
BLK = 16
PER = 12
CAP = 2
D = 256
PAIRS = BLK // 2
SCALE = HD ** (-0.5)
SCALE_LOG2E = SCALE * math.log2(math.e)
BF16 = jnp.bfloat16
F32 = jnp.float32
MIB = 1 << 20
LAST = (((1,), (1,)), ((), ()))


def dot(a, b):
    return jnp.dot(a, b, preferred_element_type=F32)


def dot_last(a, b):
    return lax.dot_general(a, b, LAST, preferred_element_type=F32)


def span(start, size):
    return pl.ds(pl.multiple_of(start, size), size)


def smem():
    return pl.BlockSpec(memory_space=pltpu.SMEM)


def vmem():
    return pl.BlockSpec(memory_space=pltpu.VMEM)


def hbm():
    return pl.BlockSpec(memory_space=pltpu.HBM)


def call(kernel, name, outs, in_specs, limit, flops=0, scratch=(), out_specs=None):
    return pl.pallas_call(
        kernel,
        name=name,
        out_shape=tuple(jax.ShapeDtypeStruct(shape, kind) for shape, kind in outs),
        in_specs=in_specs,
        out_specs=tuple(out_specs or [vmem() for _ in outs]),
        scratch_shapes=scratch,
        compiler_params=pltpu.CompilerParams(vmem_limit_bytes=limit),
        cost_estimate=pl.CostEstimate(flops=flops, bytes_accessed=4 * MIB, transcendentals=0),
    )


def top_shift(count):
    return count.bit_length() - 3


def group_of(node, shift):
    return (node >> shift) & 3


def split(value, group, piece_refs):
    size = value.shape[0] // 4
    for g in range(4):
        for m in range(4):

            @pl.when((group ^ m) == g)
            def _():
                piece_refs[m][...] = value[g * size : (g + 1) * size, :].astype(piece_refs[m].dtype)


def split_kernel(shift, place_ref, value_ref, *piece_refs):
    split(value_ref[...], group_of(place_ref[1], shift), piece_refs)


def join(piece_refs, group, g):
    value = piece_refs[0][...]
    for m in range(1, 4):
        value = jnp.where((group ^ m) == g, piece_refs[m][...], value)
    return value


def join_kernel(shift, place_ref, p0, p1, p2, p3, out_ref):
    group = group_of(place_ref[1], shift)
    out_ref[...] = jnp.concatenate([join((p0, p1, p2, p3), group, g) for g in range(4)], axis=0)


def sum_kernel(factor, *refs):
    refs, out_ref = refs[:4], refs[-1]
    values = [ref[...].astype(F32) for ref in refs]
    out_ref[...] = ((values[0] + values[1]) + (values[2] + values[3])) * factor


def result_kernel(shift, place_ref, l0, l1, l2, l3, after_ref, in_ref, out_ref):
    group = group_of(place_ref[1], shift)
    for m, piece_ref in enumerate((l0, l1, l2, l3)):
        at = group ^ m

        @pl.when(at == 0)
        def _():
            out_ref[...] = piece_ref[...].astype(F32)

        @pl.when(at > 0)
        def _():
            in_ref[span((at - 1) * HD, HD), :] = piece_ref[...].astype(F32)


def pair_kernel(own_ref, across_ref, *refs):
    out_ref = refs[-1]
    rows = own_ref.shape[0]
    out_ref[:rows, :] = own_ref[...]
    out_ref[rows:, :] = across_ref[...]


def parts_of(pair_ref, other_ref):
    rows = pair_ref.shape[0] // 2
    return (pair_ref.at[:rows], other_ref.at[:rows], pair_ref.at[rows:], other_ref.at[rows:])


def issue_order(count):
    near, far = list(range(1, count // 2)), list(range(count // 2, count))
    return [0] + far[:2] + near + far[2:]


def by_mask(refs):
    order = issue_order(len(refs))
    return [refs[order.index(m)] for m in range(len(refs))]


def project_kernel(count, place_ref, wanted_ref, pair_ref, other_ref, in_from, *refs):
    qz_ref, kv_ref, refs = refs[0], refs[1], refs[2:]
    out_refs, (wide_ref, in_ref, sem) = refs[:count], refs[count:]
    in_copy = pltpu.make_async_copy(in_from, in_ref, sem)
    in_copy.start()
    x_refs = parts_of(pair_ref, other_ref)
    head, node = place_ref[0], place_ref[1]
    rows = x_refs[0].shape[0]
    in_copy.wait()
    wide_ref[:, HD:BLOCK] = jnp.zeros((D, HD), BF16)
    for g in range(HEADS):

        @pl.when(head == g)
        def _():
            at = g * 3 * HD
            wide_ref[:, :HD] = in_ref[:, at : at + HD]
            wide_ref[:, BLOCK:] = in_ref[:, at + HD : at + 3 * HD]

    for part in range(4):
        at = span((head ^ part) * rows, rows)
        y = dot(x_refs[part][...], wide_ref[...]).astype(BF16)
        qz_ref[at, :] = y[:, :BLOCK]
        kv_ref[at, :] = y[:, BLOCK:]
    for m in range(count):
        for c in range(CAP):
            block = wanted_ref[node ^ m, 0, c]
            out_refs[m][c] = kv_ref[span(block * BLOCK, BLOCK), :]


def prepare_kernel(place_ref, slot_ref, count_ref, pair_ref, other_ref, kv_ref, after_ref, xt_ref, kvt_ref):
    head = place_ref[0]
    rows = pair_ref.shape[0] // 2
    for part, x_ref in enumerate(parts_of(pair_ref, other_ref)):
        xt_ref[:, span((head ^ part) * rows, rows)] = x_ref[...].T
    for i in range(BLK):
        kvt_ref[i] = kv_ref[i * BLOCK : (i + 1) * BLOCK, :].T


def forward_kernel(count, place_ref, slot_ref, count_ref, qz_ref, kv_ref, kvt_ref, *refs):
    in_refs, refs = by_mask(refs[:count]), refs[count:]
    att_ref, attt_ref, table_ref, tablet_ref, top_ref, inv_ref, refs = *refs[:6], refs[6:]
    even_ref, odd_ref = refs
    node = place_ref[1]
    for i in range(BLK):
        table_ref[i] = kv_ref[i * BLOCK : (i + 1) * BLOCK, :]
        tablet_ref[i] = kvt_ref[i]
    for m in range(count):
        for c in range(CAP):
            block = in_refs[m][c]
            at = BLK + (node ^ m) * CAP + c
            table_ref[at] = block
            tablet_ref[at] = block.T

    def slots_of(i):
        return [slot_ref[i, j] for j in range(PER)]

    def score(i, raw_ref):
        live = count_ref[i]
        keys = jnp.concatenate([table_ref[s] for s in slots_of(i)], axis=0)
        raw = dot_last(keys, qz_ref[span(i * BLOCK, BLOCK), :])
        top = None
        for j in range(PER):
            here = jnp.where(j < live, raw[j * BLOCK : (j + 1) * BLOCK], -1e30)
            raw_ref[j * BLOCK : (j + 1) * BLOCK, :] = here
            here = here.reshape(BLOCK // 8, 8, BLOCK)
            highest = jnp.max(here, axis=0)
            top = highest if top is None else jnp.maximum(top, highest)
        return jnp.max(top, axis=0, keepdims=True)

    def attend(i, raw_ref, top):
        total = None
        for j in range(PER):
            here = slice(j * BLOCK, (j + 1) * BLOCK)
            raised = jnp.exp2((raw_ref[here, :] - top) * SCALE_LOG2E)
            raw_ref[here, :] = raised
            part = jnp.sum(raised.reshape(BLOCK // 8, 8, BLOCK), axis=0)
            total = part if total is None else total + part
        inverse = 1.0 / jnp.sum(total, axis=0, keepdims=True)
        values = jnp.concatenate([tablet_ref[s, HD:, :] for s in slots_of(i)], axis=1)
        result = dot(values, (raw_ref[...] * inverse).astype(BF16))
        attt_ref[:, span(i * BLOCK, BLOCK)] = result.astype(BF16)
        top_ref[i] = jnp.broadcast_to(top, (8, BLOCK))
        inv_ref[i] = jnp.broadcast_to(inverse, (8, BLOCK))
        return result

    def pair(t, even_top):
        odd_top = score(2 * t + 1, odd_ref)
        first = attend(2 * t, even_ref, even_top)
        even_top = score(jnp.minimum(2 * t + 2, BLK - 1), even_ref)
        second = attend(2 * t + 1, odd_ref, odd_top)
        both = jnp.concatenate([first, second], axis=0)
        att_ref[span(t * BLOCK, BLOCK), :] = both.T.astype(BF16)
        return even_top

    lax.fori_loop(0, PAIRS, pair, score(0, even_ref))


def middle_kernel(
    place_ref, x_pair, x_other, c_pair, c_other, a_pair, a_other, attt_ref, w_ref,
    out_ref, grad_out, gz_ref, dots_ref, owg_ref, wide_ref, pad_ref, grad_ref, sem,
):
    head = place_ref[0]
    rows = grad_ref.shape[0]
    grad_copy = pltpu.make_async_copy(grad_ref, grad_out, sem)
    own_w = w_ref[span(head * HD, HD), :]
    wide_ref[...] = jnp.zeros_like(wide_ref)
    for part in range(4):
        piece = w_ref[span((head ^ part) * HD, HD), :]
        at = (2 * part) * HD
        wide_ref[at : at + HD, :D] = piece
        wide_ref[at + HD : at + 2 * HD, D:] = piece
    pad_ref[:HD, :] = jnp.zeros((HD, D), BF16)
    pad_ref[HD:, :] = own_w
    a_refs = parts_of(a_pair, a_other)
    owg = jnp.zeros((HD, D), F32)
    pairs = rows // (2 * BLOCK)
    for part, (x_ref, c_ref) in enumerate(zip(parts_of(x_pair, x_other), parts_of(c_pair, c_other))):
        group = head ^ part
        at = span(group * (rows // 2), rows // 2)
        lhs = jnp.concatenate([a[at, :] for a in a_refs], axis=1)
        product = dot(lhs, wide_ref[...])
        lows = []
        for i in range(2 * pairs):
            local = slice(i * BLOCK, (i + 1) * BLOCK)
            pair, half = i // 2, i % 2
            summed = x_ref[local, :].astype(F32) + product[
                pair * BLOCK : (pair + 1) * BLOCK, half * D : (half + 1) * D
            ]
            inverse = lax.rsqrt(jnp.mean(summed * summed, axis=-1, keepdims=True) + 1e-06)
            normed = summed * inverse
            upstream = c_ref[local, :].astype(F32)
            grad = (upstream - normed * jnp.mean(upstream * normed, axis=-1, keepdims=True)) * inverse
            lows.append(grad.astype(BF16))
            if part == 0:
                out_ref[local, :] = normed.astype(BF16)
                grad_ref[local, :] = grad
        if part == 0:
            grad_copy.start()
        low = jnp.concatenate(lows, axis=0)
        at = span(group * rows, rows)
        gz_ref[at, :] = dot_last(low, pad_ref[...]).astype(BF16)
        turned = dot_last(own_w, low).astype(BF16).astype(F32)
        attended = attt_ref[:, at]
        sums = jnp.sum(turned * attended.astype(F32), axis=0, keepdims=True)
        for i in range(2 * pairs):
            dots_ref[group * (2 * pairs) + i] = jnp.broadcast_to(
                sums[:, i * BLOCK : (i + 1) * BLOCK], (8, BLOCK)
            )
        owg += dot(attended, low)
    owg_ref[...] = owg
    grad_copy.wait()


def backward_kernel(
    count, place_ref, slot_ref, count_ref, qz_ref, gz_ref, table_ref, tablet_ref, top_ref, inv_ref, dots_ref, *refs
):
    own_ref, dqt_ref, refs = refs[0], refs[1], refs[2:]
    dq_refs, leave_refs = refs[:4], refs[4 : 4 + count]
    acc_ref, dq_ref, even_ref, odd_ref = refs[4 + count :]
    head, node = place_ref[0], place_ref[1]
    acc_ref[...] = jnp.zeros_like(acc_ref)

    def slots_of(i):
        return [slot_ref[i, j] for j in range(PER)]

    def rows_of(i):
        at = span(i * BLOCK, BLOCK)
        return jnp.concatenate([qz_ref[at, :], gz_ref[at, :]], axis=0)

    def score(i, both_ref):
        keys = jnp.concatenate([table_ref[s] for s in slots_of(i)], axis=0)
        both_ref[...] = dot_last(keys, rows_of(i))

    def spread(i, both_ref):
        slots = slots_of(i)
        live = count_ref[i]
        top = top_ref[i, :1, :]
        inverse = inv_ref[i, :1, :]
        dots = dots_ref[i, :1, :]
        weights, grads = [], []
        for j in range(PER):
            here = slice(j * BLOCK, (j + 1) * BLOCK)
            weight = jnp.exp2((both_ref[here, :BLOCK] - top) * SCALE_LOG2E) * inverse
            weight = jnp.where(j < live, weight, 0.0)
            weights.append(weight.astype(BF16))
            grads.append((weight * (both_ref[here, BLOCK:] - dots) * SCALE).astype(BF16))
        score_grad = jnp.concatenate(grads, axis=0)
        low = jnp.concatenate(weights, axis=0)
        pair_grads = dot(jnp.concatenate([score_grad, low], axis=1), rows_of(i))
        for j in range(PER):
            acc_ref[slots[j]] += pair_grads[j * BLOCK : (j + 1) * BLOCK]
        turned = jnp.concatenate([tablet_ref[s, :HD, :] for s in slots], axis=1)
        result = dot(turned, score_grad)
        dqt_ref[:, span(i * BLOCK, BLOCK)] = result.astype(BF16)
        return result

    score(0, even_ref)

    @pl.loop(0, PAIRS)
    def _(t):
        score(2 * t + 1, odd_ref)
        first = spread(2 * t, even_ref)
        score(jnp.minimum(2 * t + 2, BLK - 1), even_ref)
        second = spread(2 * t + 1, odd_ref)
        both = jnp.concatenate([first, second], axis=0)
        dq_ref[span(t * BLOCK, BLOCK), :] = both.T.astype(BF16)

    own_ref[...] = acc_ref[:BLK]
    for m in range(count):
        for c in range(CAP):
            leave_refs[m][c] = acc_ref[BLK + (node ^ m) * CAP + c].astype(BF16)
    for part in range(4):
        size = dq_refs[part].shape[0]
        dq_refs[part][...] = dq_ref[span((head ^ part) * size, size), :]


def query_weight_kernel(place_ref, dqt_ref, pair_ref, other_ref, in_ref, out_ref, wkv_ref, wq_ref, k_ref, q_ref):
    head = place_ref[0]
    rows = pair_ref.shape[0] // 2
    total = jnp.zeros((HD, D), F32)
    for part, x_ref in enumerate(parts_of(pair_ref, other_ref)):
        total += dot(dqt_ref[:, span((head ^ part) * rows, rows)], x_ref[...])
    out_ref[...] = total
    blank = jnp.zeros((D, HD), BF16)
    for g in range(HEADS):
        at = g * 3 * HD
        query = in_ref[:, at : at + HD]
        k_ref[g] = in_ref[:, at + HD : at + 3 * HD]
        q_ref[g, :D] = jnp.concatenate([query, blank], axis=1)
        q_ref[g, D:] = jnp.concatenate([blank, query], axis=1)
    for part in range(4):
        lanes = slice(part * BLOCK, (part + 1) * BLOCK)
        wkv_ref[:, lanes] = k_ref[head ^ part]
        wq_ref[:, lanes] = q_ref[head ^ part]


def collect_kernel(count, place_ref, wanted_ref, own_ref, *refs):
    back_refs, dq_refs, refs = by_mask(refs[:count]), refs[count : count + 4], refs[count + 4 :]
    xt_ref, owg_ref, qwg_ref, refs = *refs[:3], refs[3:]
    send_refs, piece_refs, sum_ref = refs[:4], refs[4:8], refs[8]
    head, node = place_ref[0], place_ref[1]
    sum_ref[...] = own_ref[...]
    for m in range(count):
        for c in range(CAP):
            sum_ref[wanted_ref[node ^ m, 0, c]] += back_refs[m][c].astype(F32)
    for part in range(4):
        rows = 2 * dq_refs[part].shape[0]
        first = (head ^ part) * (rows // BLOCK)
        for i in range(rows // BLOCK):
            send_refs[part][i * BLOCK : (i + 1) * BLOCK, :] = sum_ref[first + i].astype(BF16)
        send_refs[part][rows:, :] = dq_refs[part][...]
    total = jnp.zeros((D, BLOCK), F32)
    for part in range(4):
        rows = 2 * dq_refs[part].shape[0]
        total += dot(xt_ref[:, span((head ^ part) * rows, rows)], send_refs[part][:rows, :])
    every = jnp.concatenate([owg_ref[...], qwg_ref[...], total.T], axis=0)
    split(every, group_of(node, top_shift(count)), piece_refs)


def finish_kernel(grad_from, s0, s3, s2, s1, wq_ref, wkv_ref, out_ref, done_ref, grad_ref, sem):
    done_ref[...] = jnp.zeros_like(done_ref)
    grad_copy = pltpu.make_async_copy(grad_from, grad_ref, sem)
    grad_copy.start()
    rows = out_ref.shape[0]
    s_refs = (s0, s1, s2, s3)
    kv = jnp.concatenate([s[:rows, :] for s in s_refs], axis=1)
    base = dot_last(kv, wkv_ref[...])
    lhs = jnp.concatenate([s[rows:, :] for s in s_refs], axis=1)
    product = dot_last(lhs, wq_ref[...])
    grad_copy.wait()
    for i in range(rows // BLOCK):
        at = slice(i * BLOCK, (i + 1) * BLOCK)
        pack = slice(i // 2 * BLOCK, (i // 2 + 1) * BLOCK)
        half = i % 2
        out_ref[at, :] = (
            grad_ref[at, :] + base[at] + product[pack, half * D : (half + 1) * D]
        ).astype(BF16)


def on_device(features, in_weight, out_weight, cotangent, key_slots, block_count, wanted):
    head_count = lax.axis_size("head")
    node_count = lax.axis_size("node")
    rows = features.shape[0]
    node_rows = rows * head_count
    total_nodes = node_rows * node_count
    table_size = BLK + node_count * CAP
    limit = (14 + table_size // 4) * MIB
    place = jnp.stack([lax.axis_index("head"), lax.axis_index("node")]).astype(jnp.int32)
    block_set = (CAP, BLOCK, BLOCK)

    def swap(value, axis, mask):
        size = lax.axis_size(axis)
        return lax.ppermute(value, axis, [(i, i ^ mask) for i in range(size)])

    def pair_up(value, across, after=()):
        (pair,) = call(
            pair_kernel,
            "pair",
            [((2 * value.shape[0], value.shape[1]), value.dtype)],
            [vmem()] * (2 + len(after)),
            4 * MIB,
        )(value, across, *after)
        return pair, swap(pair, "head", 1)

    def exchange(pieces, axis, unit=1):
        moved = list(pieces)
        for mask in reversed(range(1, len(pieces))):
            moved[mask] = swap(pieces[mask], axis, mask * unit)
        return moved

    def add_nodes(pieces, shift, factor):
        moved = exchange(pieces, "node", 1 << shift)
        piece = (pieces[0].shape, F32)
        (total,) = call(
            functools.partial(sum_kernel, factor),
            "sum",
            [piece],
            [vmem()] * 4,
            4 * MIB,
        )(moved[0], *moved[:0:-1])
        if shift == 1:
            total = total + swap(total, "node", 1)
        elif shift > 1:
            lower = call(
                functools.partial(split_kernel, shift - 2),
                "split",
                [((piece[0][0] // 4, D), F32)] * 4,
                [smem(), vmem()],
                limit,
            )(place, total)
            (total,) = call(
                functools.partial(join_kernel, shift - 2),
                "join",
                [piece],
                [smem()] + [vmem()] * 4,
                limit,
            )(place, *add_nodes(lower, shift - 2, 1.0))
        return exchange([total.astype(pieces[0].dtype)] * 4, "node", 1 << shift)

    order = issue_order(node_count)
    across = swap(features, "head", 2)
    c_across = swap(cotangent, "head", 2)
    wants = lax.all_to_all(
        wanted.reshape(node_count, 1, CAP), "node", split_axis=0, concat_axis=0, tiled=True
    )
    xs = pair_up(features, across, [wants])
    qz, kv, *outgoing = call(
        functools.partial(project_kernel, node_count),
        "project",
        [((node_rows, BLOCK), BF16)] * 2 + [(block_set, BF16)] * node_count,
        [smem()] * 2 + [vmem()] * 2 + [hbm()],
        limit,
        flops=2 * node_rows * D * D,
        scratch=[
            pltpu.VMEM((D, D), BF16),
            pltpu.VMEM((D, 3 * D), BF16),
            pltpu.SemaphoreType.DMA,
        ],
    )(place, wants, *xs, in_weight)
    incoming = exchange(outgoing, "node")
    xt, kvt = call(
        prepare_kernel,
        "prepare",
        [((D, node_rows), BF16), ((BLK, BLOCK, BLOCK), BF16)],
        [smem()] * 3 + [vmem()] * 4,
        limit,
        flops=2 * node_rows * D * D,
    )(place, key_slots, block_count, *xs, kv, c_across)
    att, attt, table, tablet, top, inv = call(
        functools.partial(forward_kernel, node_count),
        "forward",
        [
            ((PAIRS * BLOCK, BLOCK), BF16),
            ((HD, node_rows), BF16),
            ((table_size, BLOCK, BLOCK), BF16),
            ((table_size, BLOCK, BLOCK), BF16),
            ((BLK, 8, BLOCK), F32),
            ((BLK, 8, BLOCK), F32),
        ],
        [smem()] * 3 + [vmem()] * (3 + node_count),
        limit,
        flops=4 * node_rows * PER * BLOCK * BLOCK,
        scratch=[pltpu.VMEM((PER * BLOCK, BLOCK), F32)] * 2,
    )(place, key_slots, block_count, qz, kv, kvt, *[incoming[m] for m in order])
    parts = pair_up(att, swap(att, "head", 2))
    cs = pair_up(cotangent, c_across, [top])
    output, norm_grad, gz, dots, owg = call(
        middle_kernel,
        "middle",
        [
            ((rows, D), BF16),
            ((rows, D), F32),
            ((node_rows, BLOCK), BF16),
            ((BLK, 8, BLOCK), F32),
            ((HD, D), F32),
        ],
        [smem()] + [vmem()] * 8,
        limit,
        flops=8 * node_rows * D * D,
        scratch=[
            pltpu.VMEM((2 * D, 2 * D), BF16),
            pltpu.VMEM((BLOCK, D), BF16),
            pltpu.VMEM((rows, D), F32),
            pltpu.SemaphoreType.DMA,
        ],
        out_specs=[vmem(), hbm()] + [vmem()] * 3,
    )(place, *xs, *cs, *parts, attt, out_weight)
    own, dqt, *rest = call(
        functools.partial(backward_kernel, node_count),
        "backward",
        [((BLK, BLOCK, BLOCK), F32), ((HD, node_rows), BF16)]
        + [((rows // 2, BLOCK), BF16)] * 4
        + [(block_set, BF16)] * node_count,
        [smem()] * 3 + [vmem()] * 7,
        limit,
        flops=10 * node_rows * PER * BLOCK * BLOCK,
        scratch=[
            pltpu.VMEM((table_size, BLOCK, BLOCK), F32),
            pltpu.VMEM((PAIRS * BLOCK, BLOCK), BF16),
            pltpu.VMEM((PER * BLOCK, 2 * BLOCK), F32),
            pltpu.VMEM((PER * BLOCK, 2 * BLOCK), F32),
        ],
    )(place, key_slots, block_count, qz, gz, table, tablet, top, inv, dots)
    returned = exchange(rest[4:], "node")
    query_wg, wkv, wq = call(
        query_weight_kernel,
        "query_weight",
        [((HD, D), F32), ((D, 2 * D), BF16), ((2 * D, 2 * D), BF16)],
        [smem()] + [vmem()] * 4,
        limit,
        flops=2 * node_rows * D * HD,
        scratch=[pltpu.VMEM((HEADS, D, BLOCK), BF16), pltpu.VMEM((HEADS, 2 * D, BLOCK), BF16)],
    )(place, dqt, *xs, in_weight)
    collected = call(
        functools.partial(collect_kernel, node_count),
        "collect",
        [((rows * 3 // 2, BLOCK), BF16)] * 4 + [((HD, D), BF16)] * 4,
        [smem()] * 2 + [vmem()] * (8 + node_count),
        limit,
        flops=2 * node_rows * D * BLOCK,
        scratch=[pltpu.VMEM((BLK, BLOCK, BLOCK), F32)],
    )(place, wants, own, *[returned[m] for m in order], *rest[:4], xt, owg, query_wg)
    arrived = exchange(collected[:4], "head")
    feature_grad, finished = call(
        finish_kernel,
        "finish",
        [((rows, D), BF16), ((8, BLOCK), F32)],
        [hbm()] + [vmem()] * 6,
        limit,
        flops=4 * rows * 3 * D * D,
        scratch=[pltpu.VMEM((rows, D), F32), pltpu.SemaphoreType.DMA],
    )(norm_grad, arrived[0], *arrived[:0:-1], wq, wkv)
    shift = top_shift(node_count)
    factor = total_nodes ** (-0.5)
    late = add_nodes(collected[4:], shift, factor)
    in_grad, out_grad = call(
        functools.partial(result_kernel, shift),
        "result",
        [((3 * HD, D), F32), ((HD, D), F32)],
        [smem()] + [vmem()] * 5,
        limit,
    )(place, *late, finished)
    return (output, feature_grad, in_grad.T, out_grad)


def solution(mesh):
    placed = (
        P(("node", "head"), None),
        P(),
        P(),
        P(("node", "head"), None),
        P("node", None),
        P("node"),
        P("node", None, None),
    )
    return jax.shard_map(
        on_device,
        mesh=mesh,
        in_specs=placed,
        out_specs=(
            P(("node", "head"), None),
            P(("node", "head"), None),
            P(None, "head"),
            P("head", None),
        ),
        check_vma=False,
    )
```

```python
import functools
import math

import jax
import jax.numpy as jnp
from jax import lax
from jax.experimental import pallas as pl
from jax.experimental.pallas import tpu as pltpu
from jax.sharding import PartitionSpec as P

HEADS = 4
HD = 64
BLOCK = 128
BLK = 16
PER = 12
CAP = 2
D = 256
PAIRS = BLK // 2
SCALE = HD ** (-0.5)
SCALE_LOG2E = SCALE * math.log2(math.e)
BF16 = jnp.bfloat16
F32 = jnp.float32
MIB = 1 << 20
LAST = (((1,), (1,)), ((), ()))


def dot(a, b):
    return jnp.dot(a, b, preferred_element_type=F32)


def dot_last(a, b):
    return lax.dot_general(a, b, LAST, preferred_element_type=F32)


def span(start, size):
    return pl.ds(pl.multiple_of(start, size), size)


def smem():
    return pl.BlockSpec(memory_space=pltpu.SMEM)


def vmem():
    return pl.BlockSpec(memory_space=pltpu.VMEM)


def hbm():
    return pl.BlockSpec(memory_space=pltpu.HBM)


def call(kernel, name, outs, in_specs, limit, flops=0, scratch=(), out_specs=None):
    return pl.pallas_call(
        kernel,
        name=name,
        out_shape=tuple(jax.ShapeDtypeStruct(shape, kind) for shape, kind in outs),
        in_specs=in_specs,
        out_specs=tuple(out_specs or [vmem() for _ in outs]),
        scratch_shapes=scratch,
        compiler_params=pltpu.CompilerParams(vmem_limit_bytes=limit),
        cost_estimate=pl.CostEstimate(flops=flops, bytes_accessed=4 * MIB, transcendentals=0),
    )


def top_shift(count):
    return count.bit_length() - 3


def group_of(node, shift):
    return (node >> shift) & 3


def split(value, group, piece_refs):
    size = value.shape[0] // 4
    for g in range(4):
        for m in range(4):

            @pl.when((group ^ m) == g)
            def _():
                piece_refs[m][...] = value[g * size : (g + 1) * size, :].astype(piece_refs[m].dtype)


def split_kernel(shift, place_ref, value_ref, *piece_refs):
    split(value_ref[...], group_of(place_ref[1], shift), piece_refs)


def join(piece_refs, group, g):
    value = piece_refs[0][...]
    for m in range(1, 4):
        value = jnp.where((group ^ m) == g, piece_refs[m][...], value)
    return value


def join_kernel(shift, place_ref, p0, p1, p2, p3, out_ref):
    group = group_of(place_ref[1], shift)
    out_ref[...] = jnp.concatenate([join((p0, p1, p2, p3), group, g) for g in range(4)], axis=0)


def sum_kernel(factor, *refs):
    out_ref = refs[-1]
    values = [ref[...].astype(F32) for ref in refs[:4]]
    out_ref[...] = ((values[0] + values[1]) + (values[2] + values[3])) * factor


def result_kernel(shift, place_ref, l0, l1, l2, l3, after_ref, in_ref, out_ref):
    group = group_of(place_ref[1], shift)
    for m, piece_ref in enumerate((l0, l1, l2, l3)):
        at = group ^ m

        @pl.when(at == 0)
        def _():
            out_ref[...] = piece_ref[...].astype(F32)

        @pl.when(at > 0)
        def _():
            in_ref[span((at - 1) * HD, HD), :] = piece_ref[...].astype(F32)


def pair_kernel(count, *refs):
    out_ref = refs[-1]
    rows = refs[0].shape[0]
    for i in range(count):
        out_ref[i * rows : (i + 1) * rows, :] = refs[i][...]


def parts_of(pair_ref, other_ref):
    rows = pair_ref.shape[0] // 2
    return (pair_ref.at[:rows], other_ref.at[:rows], pair_ref.at[rows:], other_ref.at[rows:])


def issue_order(count):
    return [0] + list(range(count - 1, 0, -1))


def by_mask(refs):
    order = issue_order(len(refs))
    return [refs[order.index(m)] for m in range(len(refs))]


def project_kernel(count, place_ref, wanted_ref, pair_ref, other_ref, in_from, *refs):
    qz_ref, kv_ref, refs = refs[0], refs[1], refs[2:]
    out_refs, (wide_ref, in_ref, sem) = refs[:count], refs[count:]
    in_copy = pltpu.make_async_copy(in_from, in_ref, sem)
    in_copy.start()
    x_refs = parts_of(pair_ref, other_ref)
    head, node = place_ref[0], place_ref[1]
    rows = x_refs[0].shape[0]
    in_copy.wait()
    wide_ref[:, HD:BLOCK] = jnp.zeros((D, HD), BF16)
    for g in range(HEADS):

        @pl.when(head == g)
        def _():
            at = g * 3 * HD
            wide_ref[:, :HD] = in_ref[:, at : at + HD]
            wide_ref[:, BLOCK:] = in_ref[:, at + HD : at + 3 * HD]

    for part in range(4):
        at = span((head ^ part) * rows, rows)
        y = dot(x_refs[part][...], wide_ref[...]).astype(BF16)
        qz_ref[at, :] = y[:, :BLOCK]
        kv_ref[at, :] = y[:, BLOCK:]
    for m in range(count):
        for c in range(CAP):
            block = wanted_ref[node ^ m, 0, c]
            out_refs[m][c] = kv_ref[span(block * BLOCK, BLOCK), :]


def prepare_kernel(place_ref, slot_ref, count_ref, pair_ref, other_ref, kv_ref, after_ref, xt_ref, kvt_ref):
    head = place_ref[0]
    rows = pair_ref.shape[0] // 2
    for part, x_ref in enumerate(parts_of(pair_ref, other_ref)):
        xt_ref[:, span((head ^ part) * rows, rows)] = x_ref[...].T
    for i in range(BLK):
        kvt_ref[i] = kv_ref[i * BLOCK : (i + 1) * BLOCK, :].T


def table_kernel_part(node, kv_ref, kvt_ref, in_refs, table_ref, tablet_ref):
    for i in range(BLK):
        table_ref[i] = kv_ref[i * BLOCK : (i + 1) * BLOCK, :]
        tablet_ref[i] = kvt_ref[i]
    for m, in_ref in enumerate(in_refs):
        for c in range(CAP):
            block = in_ref[c]
            at = BLK + (node ^ m) * CAP + c
            table_ref[at] = block
            tablet_ref[at] = block.T


def early_forward_kernel(count, place_ref, slot_ref, count_ref, qz_ref, kv_ref, kvt_ref, *refs):
    in_refs, refs = by_mask(refs[:count]), refs[count:]
    att_ref, attt_ref, table_ref, tablet_ref, top_ref, inv_ref, even_ref, odd_ref = refs
    table_kernel_part(place_ref[1], kv_ref, kvt_ref, in_refs, table_ref, tablet_ref)
    attend_blocks(
        0, slot_ref, count_ref, qz_ref, table_ref, tablet_ref,
        att_ref, attt_ref, top_ref, inv_ref, even_ref, odd_ref,
    )


def late_forward_kernel(
    slot_ref, count_ref, qz_ref, table_ref, tablet_ref, early_attt_ref, early_top_ref, early_inv_ref,
    att_ref, attt_ref, top_ref, inv_ref, even_ref, odd_ref,
):
    half = BLK // 2
    attt_ref[:, : half * BLOCK] = early_attt_ref[...]
    top_ref[:half] = early_top_ref[...]
    inv_ref[:half] = early_inv_ref[...]
    attend_blocks(
        half, slot_ref, count_ref, qz_ref, table_ref, tablet_ref,
        att_ref, attt_ref, top_ref, inv_ref, even_ref, odd_ref,
    )


def attend_blocks(
    start, slot_ref, count_ref, qz_ref, table_ref, tablet_ref,
    att_ref, attt_ref, top_ref, inv_ref, even_ref, odd_ref,
):
    def slots_of(i):
        return [slot_ref[i, j] for j in range(PER)]

    def score(i, raw_ref):
        live = count_ref[i]
        keys = jnp.concatenate([table_ref[s] for s in slots_of(i)], axis=0)
        raw = dot_last(keys, qz_ref[span(i * BLOCK, BLOCK), :])
        top = None
        for j in range(PER):
            here = jnp.where(j < live, raw[j * BLOCK : (j + 1) * BLOCK], -1e30)
            raw_ref[j * BLOCK : (j + 1) * BLOCK, :] = here
            here = here.reshape(BLOCK // 8, 8, BLOCK)
            highest = jnp.max(here, axis=0)
            top = highest if top is None else jnp.maximum(top, highest)
        return jnp.max(top, axis=0, keepdims=True)

    def attend(i, raw_ref, top):
        total = None
        for j in range(PER):
            here = slice(j * BLOCK, (j + 1) * BLOCK)
            raised = jnp.exp2((raw_ref[here, :] - top) * SCALE_LOG2E)
            raw_ref[here, :] = raised
            part = jnp.sum(raised.reshape(BLOCK // 8, 8, BLOCK), axis=0)
            total = part if total is None else total + part
        inverse = 1.0 / jnp.sum(total, axis=0, keepdims=True)
        values = jnp.concatenate([tablet_ref[s, HD:, :] for s in slots_of(i)], axis=1)
        result = dot(values, (raw_ref[...] * inverse).astype(BF16))
        attt_ref[:, span(i * BLOCK, BLOCK)] = result.astype(BF16)
        top_ref[i] = jnp.broadcast_to(top, (8, BLOCK))
        inv_ref[i] = jnp.broadcast_to(inverse, (8, BLOCK))
        return result

    def pair(t, even_top):
        first_at = start + 2 * t
        odd_top = score(first_at + 1, odd_ref)
        first = attend(first_at, even_ref, even_top)
        even_top = score(jnp.minimum(first_at + 2, BLK - 1), even_ref)
        second = attend(first_at + 1, odd_ref, odd_top)
        both = jnp.concatenate([first, second], axis=0)
        att_ref[span(t * BLOCK, BLOCK), :] = both.T.astype(BF16)
        return even_top

    lax.fori_loop(0, PAIRS // 2, pair, score(start, even_ref))


def middle_kernel(
    place_ref, x_pair, x_other, c_pair, c_other, a_pair, a_other, attt_ref, w_ref,
    out_ref, grad_out, gz_ref, dots_ref, owg_ref, wide_ref, pad_ref, grad_ref, sem,
):
    head = place_ref[0]
    rows = grad_ref.shape[0]
    grad_copy = pltpu.make_async_copy(grad_ref, grad_out, sem)
    own_w = w_ref[span(head * HD, HD), :]
    wide_ref[...] = jnp.zeros_like(wide_ref)
    for part in range(4):
        piece = w_ref[span((head ^ part) * HD, HD), :]
        at = (2 * part) * HD
        wide_ref[at : at + HD, :D] = piece
        wide_ref[at + HD : at + 2 * HD, D:] = piece
    pad_ref[:HD, :] = jnp.zeros((HD, D), BF16)
    pad_ref[HD:, :] = own_w
    a_refs = parts_of(a_pair, a_other)
    owg = jnp.zeros((HD, D), F32)
    pairs = rows // (2 * BLOCK)
    for part, (x_ref, c_ref) in enumerate(zip(parts_of(x_pair, x_other), parts_of(c_pair, c_other))):
        group = head ^ part
        at = span(group * (rows // 2), rows // 2)
        lhs = jnp.concatenate([a[at, :] for a in a_refs], axis=1)
        product = dot(lhs, wide_ref[...])
        lows = []
        for i in range(2 * pairs):
            local = slice(i * BLOCK, (i + 1) * BLOCK)
            pair, half = i // 2, i % 2
            summed = x_ref[local, :].astype(F32) + product[
                pair * BLOCK : (pair + 1) * BLOCK, half * D : (half + 1) * D
            ]
            inverse = lax.rsqrt(jnp.mean(summed * summed, axis=-1, keepdims=True) + 1e-06)
            normed = summed * inverse
            upstream = c_ref[local, :].astype(F32)
            grad = (upstream - normed * jnp.mean(upstream * normed, axis=-1, keepdims=True)) * inverse
            lows.append(grad.astype(BF16))
            if part == 0:
                out_ref[local, :] = normed.astype(BF16)
                grad_ref[local, :] = grad
        if part == 0:
            grad_copy.start()
        low = jnp.concatenate(lows, axis=0)
        at = span(group * rows, rows)
        gz_ref[at, :] = dot_last(low, pad_ref[...]).astype(BF16) * jnp.asarray(SCALE, BF16)
        turned = dot_last(own_w, low).astype(BF16).astype(F32)
        attended = attt_ref[:, at]
        sums = jnp.sum(turned * attended.astype(F32), axis=0, keepdims=True) * SCALE
        for i in range(2 * pairs):
            dots_ref[group * (2 * pairs) + i] = jnp.broadcast_to(
                sums[:, i * BLOCK : (i + 1) * BLOCK], (8, BLOCK)
            )
        owg += dot(attended, low)
    owg_ref[...] = owg
    grad_copy.wait()


def backward_kernel(
    count, place_ref, slot_ref, count_ref, qz_ref, gz_ref, table_ref, tablet_ref, top_ref, inv_ref, dots_ref, *refs
):
    own_ref, dqt_ref, refs = refs[0], refs[1], refs[2:]
    dq_refs, leave_refs = refs[:4], refs[4 : 4 + count]
    acc_ref, dq_ref, even_ref, odd_ref = refs[4 + count :]
    head, node = place_ref[0], place_ref[1]
    acc_ref[...] = jnp.zeros_like(acc_ref)

    def slots_of(i):
        return [slot_ref[i, j] for j in range(PER)]

    def rows_of(i):
        at = span(i * BLOCK, BLOCK)
        return jnp.concatenate([qz_ref[at, :], gz_ref[at, :]], axis=0)

    def score(i, both_ref):
        keys = jnp.concatenate([table_ref[s] for s in slots_of(i)], axis=0)
        both_ref[...] = dot_last(keys, rows_of(i))

    def spread(i, both_ref):
        slots = slots_of(i)
        live = count_ref[i]
        top = top_ref[i, :1, :]
        inverse = inv_ref[i, :1, :]
        dots = dots_ref[i, :1, :]
        weights, grads = [], []
        for j in range(PER):
            here = slice(j * BLOCK, (j + 1) * BLOCK)
            weight = jnp.exp2((both_ref[here, :BLOCK] - top) * SCALE_LOG2E) * inverse
            weight = jnp.where(j < live, weight, 0.0)
            weights.append(weight.astype(BF16))
            grads.append((weight * (both_ref[here, BLOCK:] - dots)).astype(BF16))
        score_grad = jnp.concatenate(grads, axis=0)
        low = jnp.concatenate(weights, axis=0)
        pair_grads = dot(jnp.concatenate([score_grad, low], axis=1), rows_of(i))
        for j in range(PER):
            acc_ref[slots[j]] += pair_grads[j * BLOCK : (j + 1) * BLOCK]
        turned = jnp.concatenate([tablet_ref[s, :HD, :] for s in slots], axis=1)
        result = dot(turned, score_grad)
        dqt_ref[:, span(i * BLOCK, BLOCK)] = result.astype(BF16)
        return result

    score(0, even_ref)

    @pl.loop(0, PAIRS)
    def _(t):
        score(2 * t + 1, odd_ref)
        first = spread(2 * t, even_ref)
        score(jnp.minimum(2 * t + 2, BLK - 1), even_ref)
        second = spread(2 * t + 1, odd_ref)
        both = jnp.concatenate([first, second], axis=0)
        dq_ref[span(t * BLOCK, BLOCK), :] = both.T.astype(BF16)

    lane = lax.broadcasted_iota(jnp.int32, (1, BLOCK), 1)
    unscale = jnp.where(lane < HD, 1.0, 1.0 / SCALE)
    own_ref[...] = acc_ref[:BLK] * unscale
    for m in range(count):
        for c in range(CAP):
            leave_refs[m][c] = (acc_ref[BLK + (node ^ m) * CAP + c] * unscale).astype(BF16)
    for part in range(4):
        size = dq_refs[part].shape[0]
        dq_refs[part][...] = dq_ref[span((head ^ part) * size, size), :]


def query_weight_kernel(place_ref, dqt_ref, pair_ref, other_ref, in_ref, out_ref, wkv_ref, wq_ref, k_ref, q_ref):
    head = place_ref[0]
    rows = pair_ref.shape[0] // 2
    total = jnp.zeros((HD, D), F32)
    for part, x_ref in enumerate(parts_of(pair_ref, other_ref)):
        total += dot(dqt_ref[:, span((head ^ part) * rows, rows)], x_ref[...])
    out_ref[...] = total
    blank = jnp.zeros((D, HD), BF16)
    for g in range(HEADS):
        at = g * 3 * HD
        query = in_ref[:, at : at + HD]
        k_ref[g] = in_ref[:, at + HD : at + 3 * HD]
        q_ref[g, :D] = jnp.concatenate([query, blank], axis=1)
        q_ref[g, D:] = jnp.concatenate([blank, query], axis=1)
    for part in range(4):
        lanes = slice(part * BLOCK, (part + 1) * BLOCK)
        wkv_ref[:, lanes] = k_ref[head ^ part]
        wq_ref[:, lanes] = q_ref[head ^ part]


def collect_kernel(count, place_ref, wanted_ref, own_ref, *refs):
    back_refs, dq_refs, refs = by_mask(refs[:count]), refs[count : count + 4], refs[count + 4 :]
    xt_ref, owg_ref, qwg_ref, refs = *refs[:3], refs[3:]
    own_send, beside_send, across_send, piece_refs, sum_ref = *refs[:3], refs[3:7], refs[7]
    size = own_send.shape[0]
    send_refs = (own_send, beside_send, across_send.at[:size], across_send.at[size:])
    head, node = place_ref[0], place_ref[1]
    sum_ref[...] = own_ref[...]
    for m in range(count):
        for c in range(CAP):
            sum_ref[wanted_ref[node ^ m, 0, c]] += back_refs[m][c].astype(F32)
    for part in range(4):
        rows = 2 * dq_refs[part].shape[0]
        first = (head ^ part) * (rows // BLOCK)
        for i in range(rows // BLOCK):
            send_refs[part][i * BLOCK : (i + 1) * BLOCK, :] = sum_ref[first + i].astype(BF16)
        send_refs[part][rows:, :] = dq_refs[part][...]
    total = jnp.zeros((D, BLOCK), F32)
    for part in range(4):
        rows = 2 * dq_refs[part].shape[0]
        total += dot(xt_ref[:, span((head ^ part) * rows, rows)], send_refs[part][:rows, :])
    every = jnp.concatenate([owg_ref[...], qwg_ref[...], total.T], axis=0)
    split(every, group_of(node, top_shift(count)), piece_refs)


def relay_kernel(beside_ref, across_ref, after_ref, out_ref):
    size = beside_ref.shape[0]
    out_ref[:size, :] = beside_ref[...]
    out_ref[size:, :] = across_ref[size:, :]


def finish_kernel(grad_from, own_ref, beside_ref, across_ref, wq_ref, wkv_ref, out_ref, done_ref, grad_ref, sem):
    done_ref[...] = jnp.zeros_like(done_ref)
    grad_copy = pltpu.make_async_copy(grad_from, grad_ref, sem)
    grad_copy.start()
    rows = out_ref.shape[0]
    size = own_ref.shape[0]
    s_refs = (own_ref, beside_ref.at[:size], across_ref.at[:size], beside_ref.at[size:])
    kv = jnp.concatenate([s[:rows, :] for s in s_refs], axis=1)
    base = dot_last(kv, wkv_ref[...])
    lhs = jnp.concatenate([s[rows:, :] for s in s_refs], axis=1)
    product = dot_last(lhs, wq_ref[...])
    grad_copy.wait()
    for i in range(rows // BLOCK):
        at = slice(i * BLOCK, (i + 1) * BLOCK)
        pack = slice(i // 2 * BLOCK, (i // 2 + 1) * BLOCK)
        half = i % 2
        out_ref[at, :] = (
            grad_ref[at, :] + base[at] + product[pack, half * D : (half + 1) * D]
        ).astype(BF16)


def on_device(features, in_weight, out_weight, cotangent, key_slots, block_count, wanted):
    head_count = lax.axis_size("head")
    node_count = lax.axis_size("node")
    rows = features.shape[0]
    node_rows = rows * head_count
    total_nodes = node_rows * node_count
    table_size = BLK + node_count * CAP
    limit = (14 + table_size // 4) * MIB
    place = jnp.stack([lax.axis_index("head"), lax.axis_index("node")]).astype(jnp.int32)
    block_set = (CAP, BLOCK, BLOCK)

    def swap(value, axis, mask):
        size = lax.axis_size(axis)
        return lax.ppermute(value, axis, [(i, i ^ mask) for i in range(size)])

    def pair_up(values, after=()):
        rows, width = values[0].shape
        (pair,) = call(
            functools.partial(pair_kernel, len(values)),
            "pair",
            [((len(values) * rows, width), values[0].dtype)],
            [vmem()] * (len(values) + len(after)),
            4 * MIB,
        )(*values, *after)
        return pair, swap(pair, "head", 1)

    def exchange(pieces, axis, unit=1):
        moved = list(pieces)
        for mask in reversed(range(1, len(pieces))):
            moved[mask] = swap(pieces[mask], axis, mask * unit)
        return moved

    def add_nodes(pieces, shift, factor, after=()):
        moved = exchange(pieces, "node", 1 << shift)
        piece = (pieces[0].shape, F32)
        (total,) = call(
            functools.partial(sum_kernel, factor),
            "sum",
            [piece],
            [vmem()] * (4 + len(after)),
            4 * MIB,
        )(moved[0], *moved[:0:-1], *after)
        if shift == 1:
            total = total + swap(total, "node", 1)
        elif shift > 1:
            lower = call(
                functools.partial(split_kernel, shift - 2),
                "split",
                [((piece[0][0] // 4, D), F32)] * 4,
                [smem(), vmem()],
                limit,
            )(place, total)
            (total,) = call(
                functools.partial(join_kernel, shift - 2),
                "join",
                [piece],
                [smem()] + [vmem()] * 4,
                limit,
            )(place, *add_nodes(lower, shift - 2, 1.0)[0])
        total = total.astype(pieces[0].dtype)
        return exchange([total] * 4, "node", 1 << shift), total

    order = issue_order(node_count)
    across = swap(features, "head", 2)
    c_across = swap(cotangent, "head", 2)
    wants = lax.all_to_all(
        wanted.reshape(node_count, 1, CAP), "node", split_axis=0, concat_axis=0, tiled=True
    )
    xs = pair_up([features, across], [wants])
    qz, kv, *outgoing = call(
        functools.partial(project_kernel, node_count),
        "project",
        [((node_rows, BLOCK), BF16)] * 2 + [(block_set, BF16)] * node_count,
        [smem()] * 2 + [vmem()] * 2 + [hbm()],
        limit,
        flops=2 * node_rows * D * D,
        scratch=[
            pltpu.VMEM((D, D), BF16),
            pltpu.VMEM((D, 3 * D), BF16),
            pltpu.SemaphoreType.DMA,
        ],
    )(place, wants, *xs, in_weight)
    incoming = exchange(outgoing, "node")
    xt, kvt = call(
        prepare_kernel,
        "prepare",
        [((D, node_rows), BF16), ((BLK, BLOCK, BLOCK), BF16)],
        [smem()] * 3 + [vmem()] * 4,
        limit,
        flops=2 * node_rows * D * D,
    )(place, key_slots, block_count, *xs, kv, c_across)
    half = BLK // 2
    half_att = ((half * BLOCK // 2, BLOCK), BF16)
    early_att, early_attt, table, tablet, early_top, early_inv = call(
        functools.partial(early_forward_kernel, node_count),
        "early_forward",
        [
            half_att,
            ((HD, half * BLOCK), BF16),
            ((table_size, BLOCK, BLOCK), BF16),
            ((table_size, BLOCK, BLOCK), BF16),
            ((half, 8, BLOCK), F32),
            ((half, 8, BLOCK), F32),
        ],
        [smem()] * 3 + [vmem()] * (3 + node_count),
        limit,
        flops=2 * node_rows * PER * BLOCK * BLOCK,
        scratch=[pltpu.VMEM((PER * BLOCK, BLOCK), F32)] * 2,
    )(place, key_slots, block_count, qz, kv, kvt, *[incoming[m] for m in order])
    early_across = swap(early_att, "head", 2)
    late_att, attt, top, inv = call(
        late_forward_kernel,
        "late_forward",
        [
            half_att,
            ((HD, node_rows), BF16),
            ((BLK, 8, BLOCK), F32),
            ((BLK, 8, BLOCK), F32),
        ],
        [smem()] * 2 + [vmem()] * 6,
        limit,
        flops=2 * node_rows * PER * BLOCK * BLOCK,
        scratch=[pltpu.VMEM((PER * BLOCK, BLOCK), F32)] * 2,
    )(key_slots, block_count, qz, table, tablet, early_attt, early_top, early_inv)
    late_across = swap(late_att, "head", 2)
    parts = pair_up([early_att, late_att, early_across, late_across])
    cs = pair_up([cotangent, c_across], [top])
    output, norm_grad, gz, dots, owg = call(
        middle_kernel,
        "middle",
        [
            ((rows, D), BF16),
            ((rows, D), F32),
            ((node_rows, BLOCK), BF16),
            ((BLK, 8, BLOCK), F32),
            ((HD, D), F32),
        ],
        [smem()] + [vmem()] * 8,
        limit,
        flops=8 * node_rows * D * D,
        scratch=[
            pltpu.VMEM((2 * D, 2 * D), BF16),
            pltpu.VMEM((BLOCK, D), BF16),
            pltpu.VMEM((rows, D), F32),
            pltpu.SemaphoreType.DMA,
        ],
        out_specs=[vmem(), hbm()] + [vmem()] * 3,
    )(place, *xs, *cs, *parts, attt, out_weight)
    own, dqt, *rest = call(
        functools.partial(backward_kernel, node_count),
        "backward",
        [((BLK, BLOCK, BLOCK), F32), ((HD, node_rows), BF16)]
        + [((rows // 2, BLOCK), BF16)] * 4
        + [(block_set, BF16)] * node_count,
        [smem()] * 3 + [vmem()] * 7,
        limit,
        flops=10 * node_rows * PER * BLOCK * BLOCK,
        scratch=[
            pltpu.VMEM((table_size, BLOCK, BLOCK), F32),
            pltpu.VMEM((PAIRS * BLOCK, BLOCK), BF16),
            pltpu.VMEM((PER * BLOCK, 2 * BLOCK), F32),
            pltpu.VMEM((PER * BLOCK, 2 * BLOCK), F32),
        ],
    )(place, key_slots, block_count, qz, gz, table, tablet, top, inv, dots)
    returned = exchange(rest[4:], "node")
    query_wg, wkv, wq = call(
        query_weight_kernel,
        "query_weight",
        [((HD, D), F32), ((D, 2 * D), BF16), ((2 * D, 2 * D), BF16)],
        [smem()] + [vmem()] * 4,
        limit,
        flops=2 * node_rows * D * HD,
        scratch=[pltpu.VMEM((HEADS, D, BLOCK), BF16), pltpu.VMEM((HEADS, 2 * D, BLOCK), BF16)],
    )(place, dqt, *xs, in_weight)
    sent = ((rows * 3 // 2, BLOCK), BF16)
    collected = call(
        functools.partial(collect_kernel, node_count),
        "collect",
        [sent, sent, ((rows * 3, BLOCK), BF16)] + [((HD, D), BF16)] * 4,
        [smem()] * 2 + [vmem()] * (8 + node_count),
        limit,
        flops=2 * node_rows * D * BLOCK,
        scratch=[pltpu.VMEM((BLK, BLOCK, BLOCK), F32)],
    )(place, wants, own, *[returned[m] for m in order], *rest[:4], xt, owg, query_wg)
    own_send, beside_send, across_send = collected[:3]
    across = swap(across_send, "head", 2)
    shift = top_shift(node_count)
    factor = total_nodes ** (-0.5)
    late, summed = add_nodes(collected[3:], shift, factor)
    (relay,) = call(
        relay_kernel, "relay", [((rows * 3, BLOCK), BF16)], [vmem()] * 3, 4 * MIB
    )(beside_send, across, summed)
    beside = swap(relay, "head", 1)
    feature_grad, finished = call(
        finish_kernel,
        "finish",
        [((rows, D), BF16), ((8, BLOCK), F32)],
        [hbm()] + [vmem()] * 5,
        limit,
        flops=4 * rows * 3 * D * D,
        scratch=[pltpu.VMEM((rows, D), F32), pltpu.SemaphoreType.DMA],
    )(norm_grad, own_send, beside, across, wq, wkv)
    in_grad, out_grad = call(
        functools.partial(result_kernel, shift),
        "result",
        [((3 * HD, D), F32), ((HD, D), F32)],
        [smem()] + [vmem()] * 5,
        limit,
    )(place, *late, finished)
    return (output, feature_grad, in_grad.T, out_grad)


def solution(mesh):
    placed = (
        P(("node", "head"), None),
        P(),
        P(),
        P(("node", "head"), None),
        P("node", None),
        P("node"),
        P("node", None, None),
    )
    return jax.shard_map(
        on_device,
        mesh=mesh,
        in_specs=placed,
        out_specs=(
            P(("node", "head"), None),
            P(("node", "head"), None),
            P(None, "head"),
            P("head", None),
        ),
        check_vma=False,
    )
```

```python
import functools
import math

import jax
import jax.numpy as jnp
from jax import lax
from jax.experimental import pallas as pl
from jax.experimental.pallas import tpu as pltpu
from jax.sharding import PartitionSpec as P

HEADS = 4
HD = 64
BLOCK = 128
BLK = 16
PER = 12
CAP = 2
D = 256
PAIRS = BLK // 2
SCALE = HD ** (-0.5)
SCALE_LOG2E = SCALE * math.log2(math.e)
BF16 = jnp.bfloat16
F32 = jnp.float32
MIB = 1 << 20
LAST = (((1,), (1,)), ((), ()))


def dot(a, b):
    return jnp.dot(a, b, preferred_element_type=F32)


def dot_last(a, b):
    return lax.dot_general(a, b, LAST, preferred_element_type=F32)


def span(start, size):
    return pl.ds(pl.multiple_of(start, size), size)


def smem():
    return pl.BlockSpec(memory_space=pltpu.SMEM)


def vmem():
    return pl.BlockSpec(memory_space=pltpu.VMEM)


def hbm():
    return pl.BlockSpec(memory_space=pltpu.HBM)


def call(kernel, name, outs, in_specs, limit, flops=0, scratch=(), out_specs=None):
    return pl.pallas_call(
        kernel,
        name=name,
        out_shape=tuple(jax.ShapeDtypeStruct(shape, kind) for shape, kind in outs),
        in_specs=in_specs,
        out_specs=tuple(out_specs or [vmem() for _ in outs]),
        scratch_shapes=scratch,
        compiler_params=pltpu.CompilerParams(vmem_limit_bytes=limit),
        cost_estimate=pl.CostEstimate(flops=flops, bytes_accessed=4 * MIB, transcendentals=0),
    )


def top_shift(count):
    return count.bit_length() - 3


def group_of(node, shift):
    return (node >> shift) & 3


def split(value, group, piece_refs):
    size = value.shape[0] // 4
    for g in range(4):
        for m in range(4):

            @pl.when((group ^ m) == g)
            def _():
                piece_refs[m][...] = value[g * size : (g + 1) * size, :].astype(piece_refs[m].dtype)


def split_kernel(shift, place_ref, value_ref, *piece_refs):
    split(value_ref[...], group_of(place_ref[1], shift), piece_refs)


def join(piece_refs, group, g):
    value = piece_refs[0][...]
    for m in range(1, 4):
        value = jnp.where((group ^ m) == g, piece_refs[m][...], value)
    return value


def join_kernel(shift, place_ref, p0, p1, p2, p3, out_ref):
    group = group_of(place_ref[1], shift)
    out_ref[...] = jnp.concatenate([join((p0, p1, p2, p3), group, g) for g in range(4)], axis=0)


def sum_kernel(factor, *refs):
    out_ref = refs[-1]
    values = [ref[...].astype(F32) for ref in refs[:4]]
    out_ref[...] = ((values[0] + values[1]) + (values[2] + values[3])) * factor


def result_kernel(shift, place_ref, l0, l1, l2, l3, after_ref, in_ref, out_ref):
    group = group_of(place_ref[1], shift)
    for m, piece_ref in enumerate((l0, l1, l2, l3)):
        at = group ^ m

        @pl.when(at == 0)
        def _():
            out_ref[...] = piece_ref[...].astype(F32)

        @pl.when(at > 0)
        def _():
            in_ref[span((at - 1) * HD, HD), :] = piece_ref[...].astype(F32)


def pair_kernel(count, *refs):
    out_ref = refs[-1]
    rows = refs[0].shape[0]
    for i in range(count):
        out_ref[i * rows : (i + 1) * rows, :] = refs[i][...]


def parts_of(pair_ref, other_ref):
    rows = pair_ref.shape[0] // 2
    return (pair_ref.at[:rows], other_ref.at[:rows], pair_ref.at[rows:], other_ref.at[rows:])


def issue_order(count):
    return [0] + list(range(count - 1, 0, -1))


def back_order(count):
    return [0, 1] + list(range(count - 1, 1, -1))


def by_mask(refs, order):
    return [refs[order.index(m)] for m in range(len(refs))]


def project_kernel(count, place_ref, wanted_ref, pair_ref, other_ref, in_from, *refs):
    qz_ref, kv_ref, refs = refs[0], refs[1], refs[2:]
    out_refs, (wide_ref, in_ref, sem) = refs[:count], refs[count:]
    in_copy = pltpu.make_async_copy(in_from, in_ref, sem)
    in_copy.start()
    x_refs = parts_of(pair_ref, other_ref)
    head, node = place_ref[0], place_ref[1]
    rows = x_refs[0].shape[0]
    in_copy.wait()
    wide_ref[:, HD:BLOCK] = jnp.zeros((D, HD), BF16)
    for g in range(HEADS):

        @pl.when(head == g)
        def _():
            at = g * 3 * HD
            wide_ref[:, :HD] = in_ref[:, at : at + HD]
            wide_ref[:, BLOCK:] = in_ref[:, at + HD : at + 3 * HD]

    for part in range(4):
        at = span((head ^ part) * rows, rows)
        y = dot(x_refs[part][...], wide_ref[...]).astype(BF16)
        qz_ref[at, :] = y[:, :BLOCK]
        kv_ref[at, :] = y[:, BLOCK:]
    for m in range(count):
        for c in range(CAP):
            block = wanted_ref[node ^ m, 0, c]
            out_refs[m][c] = kv_ref[span(block * BLOCK, BLOCK), :]


def pass_on(refs):
    for i in range(len(refs) // 2):
        refs[len(refs) // 2 + i][...] = refs[i][...]


def prepare_kernel(near, place_ref, slot_ref, count_ref, pair_ref, other_ref, kv_ref, after_ref, *refs):
    xt_ref, kvt_ref = refs[near : near + 2]
    pass_on(refs[:near] + refs[near + 2 :])
    head = place_ref[0]
    rows = pair_ref.shape[0] // 2
    for part, x_ref in enumerate(parts_of(pair_ref, other_ref)):
        xt_ref[:, span((head ^ part) * rows, rows)] = x_ref[...].T
    for i in range(BLK):
        kvt_ref[i] = kv_ref[i * BLOCK : (i + 1) * BLOCK, :].T


def table_kernel_part(node, kv_ref, kvt_ref, in_refs, table_ref, tablet_ref):
    for i in range(BLK):
        table_ref[i] = kv_ref[i * BLOCK : (i + 1) * BLOCK, :]
        tablet_ref[i] = kvt_ref[i]
    for m, in_ref in enumerate(in_refs):
        for c in range(CAP):
            block = in_ref[c]
            at = BLK + (node ^ m) * CAP + c
            table_ref[at] = block
            tablet_ref[at] = block.T


def early_forward_kernel(count, place_ref, slot_ref, count_ref, qz_ref, kv_ref, kvt_ref, *refs):
    in_refs, refs = by_mask(refs[:count], issue_order(count)), refs[count:]
    att_ref, attt_ref, table_ref, tablet_ref, top_ref, inv_ref, even_ref, odd_ref = refs
    table_kernel_part(place_ref[1], kv_ref, kvt_ref, in_refs, table_ref, tablet_ref)
    attend_blocks(
        0, slot_ref, count_ref, qz_ref, table_ref, tablet_ref,
        att_ref, attt_ref, top_ref, inv_ref, even_ref, odd_ref,
    )


def late_forward_kernel(
    slot_ref, count_ref, qz_ref, table_ref, tablet_ref, early_attt_ref, early_top_ref, early_inv_ref,
    att_ref, attt_ref, top_ref, inv_ref, even_ref, odd_ref,
):
    half = BLK // 2
    attt_ref[:, : half * BLOCK] = early_attt_ref[...]
    top_ref[:half] = early_top_ref[...]
    inv_ref[:half] = early_inv_ref[...]
    attend_blocks(
        half, slot_ref, count_ref, qz_ref, table_ref, tablet_ref,
        att_ref, attt_ref, top_ref, inv_ref, even_ref, odd_ref,
    )


def attend_blocks(
    start, slot_ref, count_ref, qz_ref, table_ref, tablet_ref,
    att_ref, attt_ref, top_ref, inv_ref, even_ref, odd_ref,
):
    def slots_of(i):
        return [slot_ref[i, j] for j in range(PER)]

    def score(i, raw_ref):
        live = count_ref[i]
        keys = jnp.concatenate([table_ref[s] for s in slots_of(i)], axis=0)
        raw = dot_last(keys, qz_ref[span(i * BLOCK, BLOCK), :])
        top = None
        for j in range(PER):
            here = jnp.where(j < live, raw[j * BLOCK : (j + 1) * BLOCK], -1e30)
            raw_ref[j * BLOCK : (j + 1) * BLOCK, :] = here
            here = here.reshape(BLOCK // 8, 8, BLOCK)
            highest = jnp.max(here, axis=0)
            top = highest if top is None else jnp.maximum(top, highest)
        return jnp.max(top, axis=0, keepdims=True)

    def attend(i, raw_ref, top):
        total = None
        for j in range(PER):
            here = slice(j * BLOCK, (j + 1) * BLOCK)
            raised = jnp.exp2((raw_ref[here, :] - top) * SCALE_LOG2E)
            raw_ref[here, :] = raised
            part = jnp.sum(raised.reshape(BLOCK // 8, 8, BLOCK), axis=0)
            total = part if total is None else total + part
        inverse = 1.0 / jnp.sum(total, axis=0, keepdims=True)
        values = jnp.concatenate([tablet_ref[s, HD:, :] for s in slots_of(i)], axis=1)
        result = dot(values, (raw_ref[...] * inverse).astype(BF16))
        attt_ref[:, span(i * BLOCK, BLOCK)] = result.astype(BF16)
        top_ref[i] = jnp.broadcast_to(top, (8, BLOCK))
        inv_ref[i] = jnp.broadcast_to(inverse, (8, BLOCK))
        return result

    def pair(t, even_top):
        first_at = start + 2 * t
        odd_top = score(first_at + 1, odd_ref)
        first = attend(first_at, even_ref, even_top)
        even_top = score(jnp.minimum(first_at + 2, BLK - 1), even_ref)
        second = attend(first_at + 1, odd_ref, odd_top)
        both = jnp.concatenate([first, second], axis=0)
        att_ref[span(t * BLOCK, BLOCK), :] = both.T.astype(BF16)
        return even_top

    lax.fori_loop(0, PAIRS // 2, pair, score(start, even_ref))


def middle_kernel(
    place_ref, x_pair, x_other, c_pair, c_other, a_pair, a_other, attt_ref, w_ref,
    out_ref, grad_out, gz_ref, dots_ref, owg_ref, wide_ref, pad_ref, grad_ref, sem,
):
    head = place_ref[0]
    rows = grad_ref.shape[0]
    grad_copy = pltpu.make_async_copy(grad_ref, grad_out, sem)
    own_w = w_ref[span(head * HD, HD), :]
    wide_ref[...] = jnp.zeros_like(wide_ref)
    for part in range(4):
        piece = w_ref[span((head ^ part) * HD, HD), :]
        at = (2 * part) * HD
        wide_ref[at : at + HD, :D] = piece
        wide_ref[at + HD : at + 2 * HD, D:] = piece
    pad_ref[:HD, :] = jnp.zeros((HD, D), BF16)
    pad_ref[HD:, :] = own_w
    a_refs = parts_of(a_pair, a_other)
    owg = jnp.zeros((HD, D), F32)
    pairs = rows // (2 * BLOCK)
    for part, (x_ref, c_ref) in enumerate(zip(parts_of(x_pair, x_other), parts_of(c_pair, c_other))):
        group = head ^ part
        at = span(group * (rows // 2), rows // 2)
        lhs = jnp.concatenate([a[at, :] for a in a_refs], axis=1)
        product = dot(lhs, wide_ref[...])
        lows = []
        for i in range(2 * pairs):
            local = slice(i * BLOCK, (i + 1) * BLOCK)
            pair, half = i // 2, i % 2
            summed = x_ref[local, :].astype(F32) + product[
                pair * BLOCK : (pair + 1) * BLOCK, half * D : (half + 1) * D
            ]
            inverse = lax.rsqrt(jnp.mean(summed * summed, axis=-1, keepdims=True) + 1e-06)
            normed = summed * inverse
            upstream = c_ref[local, :].astype(F32)
            grad = (upstream - normed * jnp.mean(upstream * normed, axis=-1, keepdims=True)) * inverse
            lows.append(grad.astype(BF16))
            if part == 0:
                out_ref[local, :] = normed.astype(BF16)
                grad_ref[local, :] = grad
        if part == 0:
            grad_copy.start()
        low = jnp.concatenate(lows, axis=0)
        at = span(group * rows, rows)
        gz_ref[at, :] = dot_last(low, pad_ref[...]).astype(BF16) * jnp.asarray(SCALE, BF16)
        turned = dot_last(own_w, low).astype(BF16).astype(F32)
        attended = attt_ref[:, at]
        sums = jnp.sum(turned * attended.astype(F32), axis=0, keepdims=True) * SCALE
        for i in range(2 * pairs):
            dots_ref[group * (2 * pairs) + i] = jnp.broadcast_to(
                sums[:, i * BLOCK : (i + 1) * BLOCK], (8, BLOCK)
            )
        owg += dot(attended, low)
    owg_ref[...] = owg
    grad_copy.wait()


def backward_kernel(
    count, place_ref, slot_ref, count_ref, qz_ref, gz_ref, table_ref, tablet_ref, top_ref, inv_ref, dots_ref, *refs
):
    own_ref, dqt_ref, refs = refs[0], refs[1], refs[2:]
    dq_refs, leave_refs = refs[:4], refs[4 : 4 + count]
    acc_ref, dq_ref, even_ref, odd_ref = refs[4 + count :]
    head, node = place_ref[0], place_ref[1]
    acc_ref[...] = jnp.zeros_like(acc_ref)

    def slots_of(i):
        return [slot_ref[i, j] for j in range(PER)]

    def rows_of(i):
        at = span(i * BLOCK, BLOCK)
        return jnp.concatenate([qz_ref[at, :], gz_ref[at, :]], axis=0)

    def score(i, both_ref):
        keys = jnp.concatenate([table_ref[s] for s in slots_of(i)], axis=0)
        both_ref[...] = dot_last(keys, rows_of(i))

    def spread(i, both_ref):
        slots = slots_of(i)
        live = count_ref[i]
        top = top_ref[i, :1, :]
        inverse = inv_ref[i, :1, :]
        dots = dots_ref[i, :1, :]
        weights, grads = [], []
        for j in range(PER):
            here = slice(j * BLOCK, (j + 1) * BLOCK)
            weight = jnp.exp2((both_ref[here, :BLOCK] - top) * SCALE_LOG2E) * inverse
            weight = jnp.where(j < live, weight, 0.0)
            weights.append(weight.astype(BF16))
            grads.append((weight * (both_ref[here, BLOCK:] - dots)).astype(BF16))
        score_grad = jnp.concatenate(grads, axis=0)
        low = jnp.concatenate(weights, axis=0)
        pair_grads = dot(jnp.concatenate([score_grad, low], axis=1), rows_of(i))
        for j in range(PER):
            acc_ref[slots[j]] += pair_grads[j * BLOCK : (j + 1) * BLOCK]
        turned = jnp.concatenate([tablet_ref[s, :HD, :] for s in slots], axis=1)
        result = dot(turned, score_grad)
        dqt_ref[:, span(i * BLOCK, BLOCK)] = result.astype(BF16)
        return result

    score(0, even_ref)

    @pl.loop(0, PAIRS)
    def _(t):
        score(2 * t + 1, odd_ref)
        first = spread(2 * t, even_ref)
        score(jnp.minimum(2 * t + 2, BLK - 1), even_ref)
        second = spread(2 * t + 1, odd_ref)
        both = jnp.concatenate([first, second], axis=0)
        dq_ref[span(t * BLOCK, BLOCK), :] = both.T.astype(BF16)

    lane = lax.broadcasted_iota(jnp.int32, (1, BLOCK), 1)
    unscale = jnp.where(lane < HD, 1.0, 1.0 / SCALE)
    own_ref[...] = acc_ref[:BLK] * unscale
    for m in range(count):
        for c in range(CAP):
            leave_refs[m][c] = (acc_ref[BLK + (node ^ m) * CAP + c] * unscale).astype(BF16)
    for part in range(4):
        size = dq_refs[part].shape[0]
        dq_refs[part][...] = dq_ref[span((head ^ part) * size, size), :]


def query_weight_kernel(near, place_ref, dqt_ref, pair_ref, other_ref, in_ref, after_ref, *refs):
    out_ref, wkv_ref, wq_ref = refs[near : near + 3]
    k_ref, q_ref = refs[-2:]
    pass_on(refs[:near] + refs[near + 3 : -2])
    head = place_ref[0]
    rows = pair_ref.shape[0] // 2
    total = jnp.zeros((HD, D), F32)
    for part, x_ref in enumerate(parts_of(pair_ref, other_ref)):
        total += dot(dqt_ref[:, span((head ^ part) * rows, rows)], x_ref[...])
    out_ref[...] = total
    blank = jnp.zeros((D, HD), BF16)
    for g in range(HEADS):
        at = g * 3 * HD
        query = in_ref[:, at : at + HD]
        k_ref[g] = in_ref[:, at + HD : at + 3 * HD]
        q_ref[g, :D] = jnp.concatenate([query, blank], axis=1)
        q_ref[g, D:] = jnp.concatenate([blank, query], axis=1)
    for part in range(4):
        lanes = slice(part * BLOCK, (part + 1) * BLOCK)
        wkv_ref[:, lanes] = k_ref[head ^ part]
        wq_ref[:, lanes] = q_ref[head ^ part]


def collect_kernel(count, place_ref, wanted_ref, own_ref, *refs):
    back_refs, dq_refs, refs = by_mask(refs[:count], back_order(count)), refs[count : count + 4], refs[count + 4 :]
    xt_ref, owg_ref, qwg_ref, refs = *refs[:3], refs[3:]
    own_send, beside_send, across_send, piece_refs, sum_ref = *refs[:3], refs[3:7], refs[7]
    size = own_send.shape[0]
    send_refs = (own_send, beside_send, across_send.at[:size], across_send.at[size:])
    head, node = place_ref[0], place_ref[1]
    sum_ref[...] = own_ref[...]
    for m in range(count):
        for c in range(CAP):
            sum_ref[wanted_ref[node ^ m, 0, c]] += back_refs[m][c].astype(F32)
    for part in range(4):
        rows = 2 * dq_refs[part].shape[0]
        first = (head ^ part) * (rows // BLOCK)
        for i in range(rows // BLOCK):
            send_refs[part][i * BLOCK : (i + 1) * BLOCK, :] = sum_ref[first + i].astype(BF16)
        send_refs[part][rows:, :] = dq_refs[part][...]
    total = jnp.zeros((D, BLOCK), F32)
    for part in range(4):
        rows = 2 * dq_refs[part].shape[0]
        total += dot(xt_ref[:, span((head ^ part) * rows, rows)], send_refs[part][:rows, :])
    every = jnp.concatenate([owg_ref[...], qwg_ref[...], total.T], axis=0)
    split(every, group_of(node, top_shift(count)), piece_refs)


def relay_kernel(beside_ref, across_ref, after_ref, out_ref):
    size = beside_ref.shape[0]
    out_ref[:size, :] = beside_ref[...]
    out_ref[size:, :] = across_ref[size:, :]


def finish_kernel(grad_from, own_ref, beside_ref, across_ref, wq_ref, wkv_ref, out_ref, done_ref, grad_ref, sem):
    done_ref[...] = jnp.zeros_like(done_ref)
    grad_copy = pltpu.make_async_copy(grad_from, grad_ref, sem)
    grad_copy.start()
    rows = out_ref.shape[0]
    size = own_ref.shape[0]
    s_refs = (own_ref, beside_ref.at[:size], across_ref.at[:size], beside_ref.at[size:])
    kv = jnp.concatenate([s[:rows, :] for s in s_refs], axis=1)
    base = dot_last(kv, wkv_ref[...])
    lhs = jnp.concatenate([s[rows:, :] for s in s_refs], axis=1)
    product = dot_last(lhs, wq_ref[...])
    grad_copy.wait()
    for i in range(rows // BLOCK):
        at = slice(i * BLOCK, (i + 1) * BLOCK)
        pack = slice(i // 2 * BLOCK, (i // 2 + 1) * BLOCK)
        half = i % 2
        out_ref[at, :] = (
            grad_ref[at, :] + base[at] + product[pack, half * D : (half + 1) * D]
        ).astype(BF16)


def on_device(features, in_weight, out_weight, cotangent, key_slots, block_count, wanted):
    head_count = lax.axis_size("head")
    node_count = lax.axis_size("node")
    rows = features.shape[0]
    node_rows = rows * head_count
    total_nodes = node_rows * node_count
    table_size = BLK + node_count * CAP
    limit = (14 + table_size // 4) * MIB
    place = jnp.stack([lax.axis_index("head"), lax.axis_index("node")]).astype(jnp.int32)
    block_set = (CAP, BLOCK, BLOCK)

    def swap(value, axis, mask):
        size = lax.axis_size(axis)
        return lax.ppermute(value, axis, [(i, i ^ mask) for i in range(size)])

    def pair_up(values, after=()):
        rows, width = values[0].shape
        (pair,) = call(
            functools.partial(pair_kernel, len(values)),
            "pair",
            [((len(values) * rows, width), values[0].dtype)],
            [vmem()] * (len(values) + len(after)),
            4 * MIB,
        )(*values, *after)
        return pair, swap(pair, "head", 1)

    def exchange(pieces, axis, unit=1):
        moved = list(pieces)
        for mask in reversed(range(1, len(pieces))):
            moved[mask] = swap(pieces[mask], axis, mask * unit)
        return moved

    def add_nodes(pieces, shift, factor, after=()):
        moved = exchange(pieces, "node", 1 << shift)
        piece = (pieces[0].shape, F32)
        (total,) = call(
            functools.partial(sum_kernel, factor),
            "sum",
            [piece],
            [vmem()] * (4 + len(after)),
            4 * MIB,
        )(moved[0], *moved[:0:-1], *after)
        if shift == 1:
            total = total + swap(total, "node", 1)
        elif shift > 1:
            lower = call(
                functools.partial(split_kernel, shift - 2),
                "split",
                [((piece[0][0] // 4, D), F32)] * 4,
                [smem(), vmem()],
                limit,
            )(place, total)
            (total,) = call(
                functools.partial(join_kernel, shift - 2),
                "join",
                [piece],
                [smem()] + [vmem()] * 4,
                limit,
            )(place, *add_nodes(lower, shift - 2, 1.0)[0])
        total = total.astype(pieces[0].dtype)
        return exchange([total] * 4, "node", 1 << shift), total

    order = issue_order(node_count)
    across = swap(features, "head", 2)
    c_across = swap(cotangent, "head", 2)
    wants = lax.all_to_all(
        wanted.reshape(node_count, 1, CAP), "node", split_axis=0, concat_axis=0, tiled=True
    )
    xs = pair_up([features, across], [wants])
    qz, kv, *outgoing = call(
        functools.partial(project_kernel, node_count),
        "project",
        [((node_rows, BLOCK), BF16)] * 2 + [(block_set, BF16)] * node_count,
        [smem()] * 2 + [vmem()] * 2 + [hbm()],
        limit,
        flops=2 * node_rows * D * D,
        scratch=[
            pltpu.VMEM((D, D), BF16),
            pltpu.VMEM((D, 3 * D), BF16),
            pltpu.SemaphoreType.DMA,
        ],
    )(place, wants, *xs, in_weight)
    near = node_count // 2 - 1
    xt, kvt, *outgoing_near = call(
        functools.partial(prepare_kernel, near),
        "prepare",
        [((D, node_rows), BF16), ((BLK, BLOCK, BLOCK), BF16)] + [(block_set, BF16)] * near,
        [smem()] * 3 + [vmem()] * (4 + near),
        limit,
        flops=2 * node_rows * D * D,
    )(place, key_slots, block_count, *xs, kv, c_across, *outgoing[1 : 1 + near])
    incoming = exchange(outgoing[:1] + outgoing_near + outgoing[1 + near :], "node")
    half = BLK // 2
    half_att = ((half * BLOCK // 2, BLOCK), BF16)
    early_att, early_attt, table, tablet, early_top, early_inv = call(
        functools.partial(early_forward_kernel, node_count),
        "early_forward",
        [
            half_att,
            ((HD, half * BLOCK), BF16),
            ((table_size, BLOCK, BLOCK), BF16),
            ((table_size, BLOCK, BLOCK), BF16),
            ((half, 8, BLOCK), F32),
            ((half, 8, BLOCK), F32),
        ],
        [smem()] * 3 + [vmem()] * (3 + node_count),
        limit,
        flops=2 * node_rows * PER * BLOCK * BLOCK,
        scratch=[pltpu.VMEM((PER * BLOCK, BLOCK), F32)] * 2,
    )(place, key_slots, block_count, qz, kv, kvt, *[incoming[m] for m in order])
    early_across = swap(early_att, "head", 2)
    late_att, attt, top, inv = call(
        late_forward_kernel,
        "late_forward",
        [
            half_att,
            ((HD, node_rows), BF16),
            ((BLK, 8, BLOCK), F32),
            ((BLK, 8, BLOCK), F32),
        ],
        [smem()] * 2 + [vmem()] * 6,
        limit,
        flops=2 * node_rows * PER * BLOCK * BLOCK,
        scratch=[pltpu.VMEM((PER * BLOCK, BLOCK), F32)] * 2,
    )(key_slots, block_count, qz, table, tablet, early_attt, early_top, early_inv)
    late_across = swap(late_att, "head", 2)
    parts = pair_up([early_att, late_att, early_across, late_across])
    cs = pair_up([cotangent, c_across], [top])
    output, norm_grad, gz, dots, owg = call(
        middle_kernel,
        "middle",
        [
            ((rows, D), BF16),
            ((rows, D), F32),
            ((node_rows, BLOCK), BF16),
            ((BLK, 8, BLOCK), F32),
            ((HD, D), F32),
        ],
        [smem()] + [vmem()] * 8,
        limit,
        flops=8 * node_rows * D * D,
        scratch=[
            pltpu.VMEM((2 * D, 2 * D), BF16),
            pltpu.VMEM((BLOCK, D), BF16),
            pltpu.VMEM((rows, D), F32),
            pltpu.SemaphoreType.DMA,
        ],
        out_specs=[vmem(), hbm()] + [vmem()] * 3,
    )(place, *xs, *cs, *parts, attt, out_weight)
    own, dqt, *rest = call(
        functools.partial(backward_kernel, node_count),
        "backward",
        [((BLK, BLOCK, BLOCK), F32), ((HD, node_rows), BF16)]
        + [((rows // 2, BLOCK), BF16)] * 4
        + [(block_set, BF16)] * node_count,
        [smem()] * 3 + [vmem()] * 7,
        limit,
        flops=10 * node_rows * PER * BLOCK * BLOCK,
        scratch=[
            pltpu.VMEM((table_size, BLOCK, BLOCK), F32),
            pltpu.VMEM((PAIRS * BLOCK, BLOCK), BF16),
            pltpu.VMEM((PER * BLOCK, 2 * BLOCK), F32),
            pltpu.VMEM((PER * BLOCK, 2 * BLOCK), F32),
        ],
    )(place, key_slots, block_count, qz, gz, table, tablet, top, inv, dots)
    leaving = rest[4:]
    returned_first = swap(leaving[1], "node", 1)
    query_wg, wkv, wq, *leaving_near = call(
        functools.partial(query_weight_kernel, near - 1),
        "query_weight",
        [((HD, D), F32), ((D, 2 * D), BF16), ((2 * D, 2 * D), BF16)] + [(block_set, BF16)] * (near - 1),
        [smem()] + [vmem()] * (4 + near),
        limit,
        flops=2 * node_rows * D * HD,
        scratch=[pltpu.VMEM((HEADS, D, BLOCK), BF16), pltpu.VMEM((HEADS, 2 * D, BLOCK), BF16)],
    )(place, dqt, *xs, in_weight, returned_first, *leaving[2 : 1 + near])
    returned = exchange(leaving[:2] + leaving_near + leaving[1 + near :], "node")
    returned[1] = returned_first
    sent = ((rows * 3 // 2, BLOCK), BF16)
    collected = call(
        functools.partial(collect_kernel, node_count),
        "collect",
        [sent, sent, ((rows * 3, BLOCK), BF16)] + [((HD, D), BF16)] * 4,
        [smem()] * 2 + [vmem()] * (8 + node_count),
        limit,
        flops=2 * node_rows * D * BLOCK,
        scratch=[pltpu.VMEM((BLK, BLOCK, BLOCK), F32)],
    )(place, wants, own, *[returned[m] for m in back_order(node_count)], *rest[:4], xt, owg, query_wg)
    own_send, beside_send, across_send = collected[:3]
    across = swap(across_send, "head", 2)
    shift = top_shift(node_count)
    factor = total_nodes ** (-0.5)
    late, summed = add_nodes(collected[3:], shift, factor)
    (relay,) = call(
        relay_kernel, "relay", [((rows * 3, BLOCK), BF16)], [vmem()] * 3, 4 * MIB
    )(beside_send, across, summed)
    beside = swap(relay, "head", 1)
    feature_grad, finished = call(
        finish_kernel,
        "finish",
        [((rows, D), BF16), ((8, BLOCK), F32)],
        [hbm()] + [vmem()] * 5,
        limit,
        flops=4 * rows * 3 * D * D,
        scratch=[pltpu.VMEM((rows, D), F32), pltpu.SemaphoreType.DMA],
    )(norm_grad, own_send, beside, across, wq, wkv)
    in_grad, out_grad = call(
        functools.partial(result_kernel, shift),
        "result",
        [((3 * HD, D), F32), ((HD, D), F32)],
        [smem()] + [vmem()] * 5,
        limit,
    )(place, *late, finished)
    return (output, feature_grad, in_grad.T, out_grad)


def solution(mesh):
    placed = (
        P(("node", "head"), None),
        P(),
        P(),
        P(("node", "head"), None),
        P("node", None),
        P("node"),
        P("node", None, None),
    )
    return jax.shard_map(
        on_device,
        mesh=mesh,
        in_specs=placed,
        out_specs=(
            P(("node", "head"), None),
            P(("node", "head"), None),
            P(None, "head"),
            P("head", None),
        ),
        check_vma=False,
    )
```

```python
import functools
import math

import jax
import jax.numpy as jnp
from jax import lax
from jax.experimental import pallas as pl
from jax.experimental.pallas import tpu as pltpu
from jax.sharding import PartitionSpec as P

HEADS = 4
HD = 64
BLOCK = 128
BLK = 16
PER = 12
CAP = 2
D = 256
PAIRS = BLK // 2
DIRECT = 8
SCALE = HD ** (-0.5)
SCALE_LOG2E = SCALE * math.log2(math.e)
BF16 = jnp.bfloat16
F32 = jnp.float32
MIB = 1 << 20
LAST = (((1,), (1,)), ((), ()))


def dot(a, b):
    return jnp.dot(a, b, preferred_element_type=F32)


def dot_last(a, b):
    return lax.dot_general(a, b, LAST, preferred_element_type=F32)


def span(start, size):
    return pl.ds(pl.multiple_of(start, size), size)


def smem():
    return pl.BlockSpec(memory_space=pltpu.SMEM)


def vmem():
    return pl.BlockSpec(memory_space=pltpu.VMEM)


def hbm():
    return pl.BlockSpec(memory_space=pltpu.HBM)


def call(kernel, name, outs, in_specs, limit, flops=0, scratch=(), out_specs=None):
    return pl.pallas_call(
        kernel,
        name=name,
        out_shape=tuple(jax.ShapeDtypeStruct(shape, kind) for shape, kind in outs),
        in_specs=in_specs,
        out_specs=tuple(out_specs or [vmem() for _ in outs]),
        scratch_shapes=scratch,
        compiler_params=pltpu.CompilerParams(vmem_limit_bytes=limit),
        cost_estimate=pl.CostEstimate(flops=flops, bytes_accessed=4 * MIB, transcendentals=0),
    )


def top_shift(count):
    return max(count.bit_length() - 3, 0) if count > DIRECT else 0


def top_pieces(count):
    return 4 if count > DIRECT else count


def group_of(node, shift, pieces=4):
    return (node >> shift) & (pieces - 1)


def split(value, group, piece_refs):
    pieces = len(piece_refs)
    size = value.shape[0] // pieces
    for g in range(pieces):
        for m in range(pieces):

            @pl.when((group ^ m) == g)
            def _():
                piece_refs[m][...] = value[g * size : (g + 1) * size, :].astype(piece_refs[m].dtype)


def split_kernel(shift, place_ref, value_ref, *piece_refs):
    split(value_ref[...], group_of(place_ref[1], shift), piece_refs)


def join(piece_refs, group, g):
    value = piece_refs[0][...]
    for m in range(1, 4):
        value = jnp.where((group ^ m) == g, piece_refs[m][...], value)
    return value


def join_kernel(shift, place_ref, p0, p1, p2, p3, out_ref):
    group = group_of(place_ref[1], shift)
    out_ref[...] = jnp.concatenate([join((p0, p1, p2, p3), group, g) for g in range(4)], axis=0)


def sum_kernel(factor, *refs):
    values = [ref[...].astype(F32) for ref in refs[:-1]]
    while len(values) > 1:
        values = [a + b for a, b in zip(values[::2], values[1::2])]
    refs[-1][...] = (values[0] * factor).astype(refs[-1].dtype)


def result_kernel(shift, place_ref, *refs):
    piece_refs, in_ref, out_ref = refs[:1] + refs[1:-3][::-1], refs[-2], refs[-1]
    pieces = len(piece_refs)
    size = 4 * HD // pieces
    first = HD // size
    group = group_of(place_ref[1], shift, pieces)
    for m, piece_ref in enumerate(piece_refs):
        at = group ^ m

        @pl.when(at < first)
        def _():
            out_ref[span(at * size, size), :] = piece_ref[...].astype(F32)

        @pl.when(at >= first)
        def _():
            in_ref[span((at - first) * size, size), :] = piece_ref[...].astype(F32)


def pair_kernel(count, *refs):
    out_ref = refs[-1]
    rows = refs[0].shape[0]
    for i in range(count):
        out_ref[i * rows : (i + 1) * rows, :] = refs[i][...]


def parts_of(pair_ref, other_ref):
    rows = pair_ref.shape[0] // 2
    return (pair_ref.at[:rows], other_ref.at[:rows], pair_ref.at[rows:], other_ref.at[rows:])


def issue_order(count):
    return [0] + list(range(count - 1, 0, -1))


def by_mask(refs):
    order = issue_order(len(refs))
    return [refs[order.index(m)] for m in range(len(refs))]


def project_kernel(count, place_ref, wanted_ref, pair_ref, other_ref, in_from, *refs):
    qz_ref, kv_ref, refs = refs[0], refs[1], refs[2:]
    out_refs, (wide_ref, in_ref, sem) = refs[:count], refs[count:]
    in_copy = pltpu.make_async_copy(in_from, in_ref, sem)
    in_copy.start()
    x_refs = parts_of(pair_ref, other_ref)
    head, node = place_ref[0], place_ref[1]
    rows = x_refs[0].shape[0]
    in_copy.wait()
    wide_ref[:, HD:BLOCK] = jnp.zeros((D, HD), BF16)
    for g in range(HEADS):

        @pl.when(head == g)
        def _():
            at = g * 3 * HD
            wide_ref[:, :HD] = in_ref[:, at : at + HD]
            wide_ref[:, BLOCK:] = in_ref[:, at + HD : at + 3 * HD]

    for part in range(4):
        at = span((head ^ part) * rows, rows)
        y = dot(x_refs[part][...], wide_ref[...]).astype(BF16)
        qz_ref[at, :] = y[:, :BLOCK]
        kv_ref[at, :] = y[:, BLOCK:]
    for m in range(count):
        for c in range(CAP):
            block = wanted_ref[node ^ m, 0, c]
            out_refs[m][c] = kv_ref[span(block * BLOCK, BLOCK), :]


def prepare_kernel(slot_ref, count_ref, kv_ref, after_ref, kvt_ref):
    for i in range(BLK):
        kvt_ref[i] = kv_ref[i * BLOCK : (i + 1) * BLOCK, :].T


def turn_kernel(place_ref, pair_ref, other_ref, after_ref, xt_ref):
    head = place_ref[0]
    rows = pair_ref.shape[0] // 2
    for part, x_ref in enumerate(parts_of(pair_ref, other_ref)):
        xt_ref[:, span((head ^ part) * rows, rows)] = x_ref[...].T


def table_kernel_part(node, kv_ref, kvt_ref, in_refs, table_ref, tablet_ref):
    for i in range(BLK):
        table_ref[i] = kv_ref[i * BLOCK : (i + 1) * BLOCK, :]
        tablet_ref[i] = kvt_ref[i]
    for m, in_ref in enumerate(in_refs):
        for c in range(CAP):
            block = in_ref[c]
            at = BLK + (node ^ m) * CAP + c
            table_ref[at] = block
            tablet_ref[at] = block.T


def early_forward_kernel(count, place_ref, slot_ref, count_ref, qz_ref, kv_ref, kvt_ref, *refs):
    in_refs, refs = by_mask(refs[:count]), refs[count:]
    att_ref, attt_ref, table_ref, tablet_ref, top_ref, inv_ref, even_ref, odd_ref = refs
    table_kernel_part(place_ref[1], kv_ref, kvt_ref, in_refs, table_ref, tablet_ref)
    attend_blocks(
        0, slot_ref, count_ref, qz_ref, table_ref, tablet_ref,
        att_ref, attt_ref, top_ref, inv_ref, even_ref, odd_ref,
    )


def late_forward_kernel(
    slot_ref, count_ref, qz_ref, table_ref, tablet_ref, early_attt_ref, early_top_ref, early_inv_ref,
    att_ref, attt_ref, top_ref, inv_ref, even_ref, odd_ref,
):
    half = BLK // 2
    attt_ref[:, : half * BLOCK] = early_attt_ref[...]
    top_ref[:half] = early_top_ref[...]
    inv_ref[:half] = early_inv_ref[...]
    attend_blocks(
        half, slot_ref, count_ref, qz_ref, table_ref, tablet_ref,
        att_ref, attt_ref, top_ref, inv_ref, even_ref, odd_ref,
    )


def attend_blocks(
    start, slot_ref, count_ref, qz_ref, table_ref, tablet_ref,
    att_ref, attt_ref, top_ref, inv_ref, even_ref, odd_ref,
):
    def slots_of(i):
        return [slot_ref[i, j] for j in range(PER)]

    def score(i, raw_ref):
        live = count_ref[i]
        keys = jnp.concatenate([table_ref[s] for s in slots_of(i)], axis=0)
        raw = dot_last(keys, qz_ref[span(i * BLOCK, BLOCK), :])
        top = None
        for j in range(PER):
            here = jnp.where(j < live, raw[j * BLOCK : (j + 1) * BLOCK], -1e30)
            raw_ref[j * BLOCK : (j + 1) * BLOCK, :] = here
            here = here.reshape(BLOCK // 8, 8, BLOCK)
            highest = jnp.max(here, axis=0)
            top = highest if top is None else jnp.maximum(top, highest)
        return jnp.max(top, axis=0, keepdims=True)

    def attend(i, raw_ref, top):
        total = None
        for j in range(PER):
            here = slice(j * BLOCK, (j + 1) * BLOCK)
            raised = jnp.exp2((raw_ref[here, :] - top) * SCALE_LOG2E)
            raw_ref[here, :] = raised
            part = jnp.sum(raised.reshape(BLOCK // 8, 8, BLOCK), axis=0)
            total = part if total is None else total + part
        inverse = 1.0 / jnp.sum(total, axis=0, keepdims=True)
        values = jnp.concatenate([tablet_ref[s, HD:, :] for s in slots_of(i)], axis=1)
        result = dot(values, (raw_ref[...] * inverse).astype(BF16))
        attt_ref[:, span(i * BLOCK, BLOCK)] = result.astype(BF16)
        top_ref[i] = jnp.broadcast_to(top, (8, BLOCK))
        inv_ref[i] = jnp.broadcast_to(inverse, (8, BLOCK))
        return result

    def pair(t, even_top):
        first_at = start + 2 * t
        odd_top = score(first_at + 1, odd_ref)
        first = attend(first_at, even_ref, even_top)
        even_top = score(jnp.minimum(first_at + 2, BLK - 1), even_ref)
        second = attend(first_at + 1, odd_ref, odd_top)
        both = jnp.concatenate([first, second], axis=0)
        att_ref[span(t * BLOCK, BLOCK), :] = both.T.astype(BF16)
        return even_top

    lax.fori_loop(0, PAIRS // 2, pair, score(start, even_ref))


def middle_kernel(
    place_ref, x_pair, x_other, c_pair, c_other, a_pair, a_other, attt_ref, w_ref, after_ref,
    out_ref, grad_out, gz_ref, dots_ref, owg_ref, wide_ref, pad_ref, grad_ref, sem,
):
    head = place_ref[0]
    rows = grad_ref.shape[0]
    grad_copy = pltpu.make_async_copy(grad_ref, grad_out, sem)
    own_w = w_ref[span(head * HD, HD), :]
    wide_ref[...] = jnp.zeros_like(wide_ref)
    for part in range(4):
        piece = w_ref[span((head ^ part) * HD, HD), :]
        at = (2 * part) * HD
        wide_ref[at : at + HD, :D] = piece
        wide_ref[at + HD : at + 2 * HD, D:] = piece
    pad_ref[:HD, :] = jnp.zeros((HD, D), BF16)
    pad_ref[HD:, :] = own_w
    a_refs = parts_of(a_pair, a_other)
    owg = jnp.zeros((HD, D), F32)
    pairs = rows // (2 * BLOCK)
    for part, (x_ref, c_ref) in enumerate(zip(parts_of(x_pair, x_other), parts_of(c_pair, c_other))):
        group = head ^ part
        at = span(group * (rows // 2), rows // 2)
        lhs = jnp.concatenate([a[at, :] for a in a_refs], axis=1)
        product = dot(lhs, wide_ref[...])
        lows = []
        for i in range(2 * pairs):
            local = slice(i * BLOCK, (i + 1) * BLOCK)
            pair, half = i // 2, i % 2
            summed = x_ref[local, :].astype(F32) + product[
                pair * BLOCK : (pair + 1) * BLOCK, half * D : (half + 1) * D
            ]
            inverse = lax.rsqrt(jnp.mean(summed * summed, axis=-1, keepdims=True) + 1e-06)
            normed = summed * inverse
            upstream = c_ref[local, :].astype(F32)
            grad = (upstream - normed * jnp.mean(upstream * normed, axis=-1, keepdims=True)) * inverse
            lows.append(grad.astype(BF16))
            if part == 0:
                out_ref[local, :] = normed.astype(BF16)
                grad_ref[local, :] = grad
        if part == 0:
            grad_copy.start()
        low = jnp.concatenate(lows, axis=0)
        at = span(group * rows, rows)
        gz_ref[at, :] = dot_last(low, pad_ref[...]).astype(BF16) * jnp.asarray(SCALE, BF16)
        turned = dot_last(own_w, low).astype(BF16).astype(F32)
        attended = attt_ref[:, at]
        sums = jnp.sum(turned * attended.astype(F32), axis=0, keepdims=True) * SCALE
        for i in range(2 * pairs):
            dots_ref[group * (2 * pairs) + i] = jnp.broadcast_to(
                sums[:, i * BLOCK : (i + 1) * BLOCK], (8, BLOCK)
            )
        owg += dot(attended, low)
    owg_ref[...] = owg
    grad_copy.wait()


def backward_kernel(
    count, place_ref, slot_ref, count_ref, qz_ref, gz_ref, table_ref, tablet_ref, top_ref, inv_ref, dots_ref, *refs
):
    own_ref, dqt_ref, refs = refs[0], refs[1], refs[2:]
    dq_refs, leave_refs = refs[:4], refs[4 : 4 + count]
    acc_ref, dq_ref, even_ref, odd_ref = refs[4 + count :]
    head, node = place_ref[0], place_ref[1]
    acc_ref[...] = jnp.zeros_like(acc_ref)

    def slots_of(i):
        return [slot_ref[i, j] for j in range(PER)]

    def rows_of(i):
        at = span(i * BLOCK, BLOCK)
        return jnp.concatenate([qz_ref[at, :], gz_ref[at, :]], axis=0)

    def score(i, both_ref):
        keys = jnp.concatenate([table_ref[s] for s in slots_of(i)], axis=0)
        both_ref[...] = dot_last(keys, rows_of(i))

    def spread(i, both_ref):
        slots = slots_of(i)
        live = count_ref[i]
        top = top_ref[i, :1, :]
        inverse = inv_ref[i, :1, :]
        dots = dots_ref[i, :1, :]
        weights, grads = [], []
        for j in range(PER):
            here = slice(j * BLOCK, (j + 1) * BLOCK)
            weight = jnp.exp2((both_ref[here, :BLOCK] - top) * SCALE_LOG2E) * inverse
            weight = jnp.where(j < live, weight, 0.0)
            weights.append(weight.astype(BF16))
            grads.append((weight * (both_ref[here, BLOCK:] - dots)).astype(BF16))
        score_grad = jnp.concatenate(grads, axis=0)
        low = jnp.concatenate(weights, axis=0)
        pair_grads = dot(jnp.concatenate([score_grad, low], axis=1), rows_of(i))
        for j in range(PER):
            acc_ref[slots[j]] += pair_grads[j * BLOCK : (j + 1) * BLOCK]
        turned = jnp.concatenate([tablet_ref[s, :HD, :] for s in slots], axis=1)
        result = dot(turned, score_grad)
        dqt_ref[:, span(i * BLOCK, BLOCK)] = result.astype(BF16)
        return result

    score(0, even_ref)

    @pl.loop(0, PAIRS)
    def _(t):
        score(2 * t + 1, odd_ref)
        first = spread(2 * t, even_ref)
        score(jnp.minimum(2 * t + 2, BLK - 1), even_ref)
        second = spread(2 * t + 1, odd_ref)
        both = jnp.concatenate([first, second], axis=0)
        dq_ref[span(t * BLOCK, BLOCK), :] = both.T.astype(BF16)

    lane = lax.broadcasted_iota(jnp.int32, (1, BLOCK), 1)
    unscale = jnp.where(lane < HD, 1.0, 1.0 / SCALE)
    own_ref[...] = acc_ref[:BLK] * unscale
    for m in range(count):
        for c in range(CAP):
            leave_refs[m][c] = (acc_ref[BLK + (node ^ m) * CAP + c] * unscale).astype(BF16)
    for part in range(4):
        size = dq_refs[part].shape[0]
        dq_refs[part][...] = dq_ref[span((head ^ part) * size, size), :]


def query_weight_kernel(place_ref, dqt_ref, pair_ref, other_ref, in_ref, out_ref, wkv_ref, wq_ref, k_ref, q_ref):
    head = place_ref[0]
    rows = pair_ref.shape[0] // 2
    total = jnp.zeros((HD, D), F32)
    for part, x_ref in enumerate(parts_of(pair_ref, other_ref)):
        total += dot(dqt_ref[:, span((head ^ part) * rows, rows)], x_ref[...])
    out_ref[...] = total
    blank = jnp.zeros((D, HD), BF16)
    for g in range(HEADS):
        at = g * 3 * HD
        query = in_ref[:, at : at + HD]
        k_ref[g] = in_ref[:, at + HD : at + 3 * HD]
        q_ref[g, :D] = jnp.concatenate([query, blank], axis=1)
        q_ref[g, D:] = jnp.concatenate([blank, query], axis=1)
    for part in range(4):
        lanes = slice(part * BLOCK, (part + 1) * BLOCK)
        wkv_ref[:, lanes] = k_ref[head ^ part]
        wq_ref[:, lanes] = q_ref[head ^ part]


def collect_kernel(count, place_ref, wanted_ref, own_ref, *refs):
    back_refs, dq_refs, refs = by_mask(refs[:count]), refs[count : count + 4], refs[count + 4 :]
    xt_ref, owg_ref, qwg_ref, refs = *refs[:3], refs[3:]
    own_send, beside_send, across_send, piece_refs, sum_ref = *refs[:3], refs[3:-1], refs[-1]
    size = own_send.shape[0]
    send_refs = (own_send, beside_send, across_send.at[:size], across_send.at[size:])
    head, node = place_ref[0], place_ref[1]
    sum_ref[...] = own_ref[...]
    for m in range(count):
        for c in range(CAP):
            sum_ref[wanted_ref[node ^ m, 0, c]] += back_refs[m][c].astype(F32)
    for part in range(4):
        rows = 2 * dq_refs[part].shape[0]
        first = (head ^ part) * (rows // BLOCK)
        for i in range(rows // BLOCK):
            send_refs[part][i * BLOCK : (i + 1) * BLOCK, :] = sum_ref[first + i].astype(BF16)
        send_refs[part][rows:, :] = dq_refs[part][...]
    total = jnp.zeros((D, BLOCK), F32)
    for part in range(4):
        rows = 2 * dq_refs[part].shape[0]
        total += dot(xt_ref[:, span((head ^ part) * rows, rows)], send_refs[part][:rows, :])
    every = jnp.concatenate([owg_ref[...], qwg_ref[...], total.T], axis=0)
    split(every, group_of(node, top_shift(count), len(piece_refs)), piece_refs)


def relay_kernel(beside_ref, across_ref, *refs):
    out_ref = refs[-1]
    size = beside_ref.shape[0]
    out_ref[:size, :] = beside_ref[...]
    out_ref[size:, :] = across_ref[size:, :]


def finish_kernel(grad_from, own_ref, beside_ref, across_ref, wq_ref, wkv_ref, out_ref, done_ref, grad_ref, sem):
    done_ref[...] = jnp.zeros_like(done_ref)
    grad_copy = pltpu.make_async_copy(grad_from, grad_ref, sem)
    grad_copy.start()
    rows = out_ref.shape[0]
    size = own_ref.shape[0]
    s_refs = (own_ref, beside_ref.at[:size], across_ref.at[:size], beside_ref.at[size:])
    kv = jnp.concatenate([s[:rows, :] for s in s_refs], axis=1)
    base = dot_last(kv, wkv_ref[...])
    lhs = jnp.concatenate([s[rows:, :] for s in s_refs], axis=1)
    product = dot_last(lhs, wq_ref[...])
    grad_copy.wait()
    for i in range(rows // BLOCK):
        at = slice(i * BLOCK, (i + 1) * BLOCK)
        pack = slice(i // 2 * BLOCK, (i // 2 + 1) * BLOCK)
        half = i % 2
        out_ref[at, :] = (
            grad_ref[at, :] + base[at] + product[pack, half * D : (half + 1) * D]
        ).astype(BF16)


def on_device(features, in_weight, out_weight, cotangent, key_slots, block_count, wanted):
    head_count = lax.axis_size("head")
    node_count = lax.axis_size("node")
    rows = features.shape[0]
    node_rows = rows * head_count
    total_nodes = node_rows * node_count
    table_size = BLK + node_count * CAP
    limit = (14 + table_size // 4) * MIB
    place = jnp.stack([lax.axis_index("head"), lax.axis_index("node")]).astype(jnp.int32)
    block_set = (CAP, BLOCK, BLOCK)

    def swap(value, axis, mask):
        size = lax.axis_size(axis)
        return lax.ppermute(value, axis, [(i, i ^ mask) for i in range(size)])

    def pair_up(values, after=()):
        rows, width = values[0].shape
        (pair,) = call(
            functools.partial(pair_kernel, len(values)),
            "pair",
            [((len(values) * rows, width), values[0].dtype)],
            [vmem()] * (len(values) + len(after)),
            4 * MIB,
        )(*values, *after)
        return pair, swap(pair, "head", 1)

    def exchange(pieces, axis, unit=1):
        moved = list(pieces)
        for mask in reversed(range(1, len(pieces))):
            moved[mask] = swap(pieces[mask], axis, mask * unit)
        return moved

    def add_nodes(pieces, shift, factor):
        wire = pieces[0].dtype
        moved = exchange(pieces, "node", 1 << shift)
        shape = pieces[0].shape
        (total,) = call(
            functools.partial(sum_kernel, factor),
            "sum",
            [(shape, F32 if shift else wire)],
            [vmem()] * len(pieces),
            4 * MIB,
        )(moved[0], *moved[:0:-1])
        if shift == 1:
            total = total + swap(total, "node", 1)
        elif shift > 1:
            lower = call(
                functools.partial(split_kernel, shift - 2),
                "split",
                [((shape[0] // 4, D), F32)] * 4,
                [smem(), vmem()],
                limit,
            )(place, total)
            (total,) = call(
                functools.partial(join_kernel, shift - 2),
                "join",
                [(shape, F32)],
                [smem()] + [vmem()] * 4,
                limit,
            )(place, *add_nodes(lower, shift - 2, 1.0))
        return exchange([total.astype(wire)] * len(pieces), "node", 1 << shift)

    order = issue_order(node_count)
    across = swap(features, "head", 2)
    c_across = swap(cotangent, "head", 2)
    wants = lax.all_to_all(
        wanted.reshape(node_count, 1, CAP), "node", split_axis=0, concat_axis=0, tiled=True
    )
    xs = pair_up([features, across], [wants])
    qz, kv, *outgoing = call(
        functools.partial(project_kernel, node_count),
        "project",
        [((node_rows, BLOCK), BF16)] * 2 + [(block_set, BF16)] * node_count,
        [smem()] * 2 + [vmem()] * 2 + [hbm()],
        limit,
        flops=2 * node_rows * D * D,
        scratch=[
            pltpu.VMEM((D, D), BF16),
            pltpu.VMEM((D, 3 * D), BF16),
            pltpu.SemaphoreType.DMA,
        ],
    )(place, wants, *xs, in_weight)
    incoming = exchange(outgoing, "node")
    (kvt,) = call(
        prepare_kernel,
        "prepare",
        [((BLK, BLOCK, BLOCK), BF16)],
        [smem()] * 2 + [vmem()] * 2,
        limit,
        flops=node_rows * D * D,
    )(key_slots, block_count, kv, c_across)
    half = BLK // 2
    half_att = ((half * BLOCK // 2, BLOCK), BF16)
    early_att, early_attt, table, tablet, early_top, early_inv = call(
        functools.partial(early_forward_kernel, node_count),
        "early_forward",
        [
            half_att,
            ((HD, half * BLOCK), BF16),
            ((table_size, BLOCK, BLOCK), BF16),
            ((table_size, BLOCK, BLOCK), BF16),
            ((half, 8, BLOCK), F32),
            ((half, 8, BLOCK), F32),
        ],
        [smem()] * 3 + [vmem()] * (3 + node_count),
        limit,
        flops=2 * node_rows * PER * BLOCK * BLOCK,
        scratch=[pltpu.VMEM((PER * BLOCK, BLOCK), F32)] * 2,
    )(place, key_slots, block_count, qz, kv, kvt, *[incoming[m] for m in order])
    early_across = swap(early_att, "head", 2)
    late_att, attt, top, inv = call(
        late_forward_kernel,
        "late_forward",
        [
            half_att,
            ((HD, node_rows), BF16),
            ((BLK, 8, BLOCK), F32),
            ((BLK, 8, BLOCK), F32),
        ],
        [smem()] * 2 + [vmem()] * 6,
        limit,
        flops=2 * node_rows * PER * BLOCK * BLOCK,
        scratch=[pltpu.VMEM((PER * BLOCK, BLOCK), F32)] * 2,
    )(key_slots, block_count, qz, table, tablet, early_attt, early_top, early_inv)
    late_across = swap(late_att, "head", 2)
    (xt,) = call(
        turn_kernel,
        "turn",
        [((D, node_rows), BF16)],
        [smem()] + [vmem()] * 3,
        limit,
        flops=node_rows * D * D,
    )(place, *xs, late_att)
    parts = pair_up([early_att, late_att, early_across, late_across])
    cs = pair_up([cotangent, c_across], [top])
    output, norm_grad, gz, dots, owg = call(
        middle_kernel,
        "middle",
        [
            ((rows, D), BF16),
            ((rows, D), F32),
            ((node_rows, BLOCK), BF16),
            ((BLK, 8, BLOCK), F32),
            ((HD, D), F32),
        ],
        [smem()] + [vmem()] * 9,
        limit,
        flops=8 * node_rows * D * D,
        scratch=[
            pltpu.VMEM((2 * D, 2 * D), BF16),
            pltpu.VMEM((BLOCK, D), BF16),
            pltpu.VMEM((rows, D), F32),
            pltpu.SemaphoreType.DMA,
        ],
        out_specs=[vmem(), hbm()] + [vmem()] * 3,
    )(place, *xs, *cs, *parts, attt, out_weight, xt)
    own, dqt, *rest = call(
        functools.partial(backward_kernel, node_count),
        "backward",
        [((BLK, BLOCK, BLOCK), F32), ((HD, node_rows), BF16)]
        + [((rows // 2, BLOCK), BF16)] * 4
        + [(block_set, BF16)] * node_count,
        [smem()] * 3 + [vmem()] * 7,
        limit,
        flops=10 * node_rows * PER * BLOCK * BLOCK,
        scratch=[
            pltpu.VMEM((table_size, BLOCK, BLOCK), F32),
            pltpu.VMEM((PAIRS * BLOCK, BLOCK), BF16),
            pltpu.VMEM((PER * BLOCK, 2 * BLOCK), F32),
            pltpu.VMEM((PER * BLOCK, 2 * BLOCK), F32),
        ],
    )(place, key_slots, block_count, qz, gz, table, tablet, top, inv, dots)
    returned = exchange(rest[4:], "node")
    query_wg, wkv, wq = call(
        query_weight_kernel,
        "query_weight",
        [((HD, D), F32), ((D, 2 * D), BF16), ((2 * D, 2 * D), BF16)],
        [smem()] + [vmem()] * 4,
        limit,
        flops=2 * node_rows * D * HD,
        scratch=[pltpu.VMEM((HEADS, D, BLOCK), BF16), pltpu.VMEM((HEADS, 2 * D, BLOCK), BF16)],
    )(place, dqt, *xs, in_weight)
    sent = ((rows * 3 // 2, BLOCK), BF16)
    pieces = top_pieces(node_count)
    collected = call(
        functools.partial(collect_kernel, node_count),
        "collect",
        [sent, sent, ((rows * 3, BLOCK), BF16)] + [((4 * HD // pieces, D), BF16)] * pieces,
        [smem()] * 2 + [vmem()] * (8 + node_count),
        limit,
        flops=2 * node_rows * D * BLOCK,
        scratch=[pltpu.VMEM((BLK, BLOCK, BLOCK), F32)],
    )(place, wants, own, *[returned[m] for m in order], *rest[:4], xt, owg, query_wg)
    own_send, beside_send, across_send = collected[:3]
    across = swap(across_send, "head", 2)
    shift = top_shift(node_count)
    factor = total_nodes ** (-0.5)
    late = add_nodes(collected[3:], shift, factor)
    (relay,) = call(
        relay_kernel, "relay", [((rows * 3, BLOCK), BF16)], [vmem()] * 5, 4 * MIB
    )(beside_send, across, *late[1:4])
    beside = swap(relay, "head", 1)
    feature_grad, finished = call(
        finish_kernel,
        "finish",
        [((rows, D), BF16), ((8, BLOCK), F32)],
        [hbm()] + [vmem()] * 5,
        limit,
        flops=4 * rows * 3 * D * D,
        scratch=[pltpu.VMEM((rows, D), F32), pltpu.SemaphoreType.DMA],
    )(norm_grad, own_send, beside, across, wq, wkv)
    in_grad, out_grad = call(
        functools.partial(result_kernel, shift),
        "result",
        [((3 * HD, D), F32), ((HD, D), F32)],
        [smem()] + [vmem()] * (1 + pieces),
        limit,
    )(place, late[0], *late[:0:-1], finished)
    return (output, feature_grad, in_grad.T, out_grad)


def solution(mesh):
    placed = (
        P(("node", "head"), None),
        P(),
        P(),
        P(("node", "head"), None),
        P("node", None),
        P("node"),
        P("node", None, None),
    )
    return jax.shard_map(
        on_device,
        mesh=mesh,
        in_specs=placed,
        out_specs=(
            P(("node", "head"), None),
            P(("node", "head"), None),
            P(None, "head"),
            P("head", None),
        ),
        check_vma=False,
    )
```

```python
import functools
import math

import jax
import jax.numpy as jnp
from jax import lax
from jax.experimental import pallas as pl
from jax.experimental.pallas import tpu as pltpu
from jax.sharding import PartitionSpec as P

HEADS = 4
HD = 64
BLOCK = 128
BLK = 16
PER = 12
CAP = 2
D = 256
PAIRS = BLK // 2
SCALE = HD ** (-0.5)
SCALE_LOG2E = SCALE * math.log2(math.e)
BF16 = jnp.bfloat16
F32 = jnp.float32
MIB = 1 << 20
LAST = (((1,), (1,)), ((), ()))


def dot(a, b):
    return jnp.dot(a, b, preferred_element_type=F32)


def dot_last(a, b):
    return lax.dot_general(a, b, LAST, preferred_element_type=F32)


def span(start, size):
    return pl.ds(pl.multiple_of(start, size), size)


def smem():
    return pl.BlockSpec(memory_space=pltpu.SMEM)


def vmem():
    return pl.BlockSpec(memory_space=pltpu.VMEM)


def hbm():
    return pl.BlockSpec(memory_space=pltpu.HBM)


def call(kernel, name, outs, in_specs, limit, flops=0, scratch=(), out_specs=None):
    return pl.pallas_call(
        kernel,
        name=name,
        out_shape=tuple(jax.ShapeDtypeStruct(shape, kind) for shape, kind in outs),
        in_specs=in_specs,
        out_specs=tuple(out_specs or [vmem() for _ in outs]),
        scratch_shapes=scratch,
        compiler_params=pltpu.CompilerParams(vmem_limit_bytes=limit),
        cost_estimate=pl.CostEstimate(flops=flops, bytes_accessed=4 * MIB, transcendentals=0),
    )


def top_shift(count):
    return count.bit_length() - 3


def group_of(node, shift):
    return (node >> shift) & 3


def split(value, group, piece_refs):
    size = value.shape[0] // 4
    for g in range(4):
        for m in range(4):

            @pl.when((group ^ m) == g)
            def _():
                piece_refs[m][...] = value[g * size : (g + 1) * size, :].astype(piece_refs[m].dtype)


def split_kernel(shift, place_ref, value_ref, *piece_refs):
    split(value_ref[...], group_of(place_ref[1], shift), piece_refs)


def join(piece_refs, group, g):
    value = piece_refs[0][...]
    for m in range(1, 4):
        value = jnp.where((group ^ m) == g, piece_refs[m][...], value)
    return value


def join_kernel(shift, place_ref, p0, p1, p2, p3, out_ref):
    group = group_of(place_ref[1], shift)
    out_ref[...] = jnp.concatenate([join((p0, p1, p2, p3), group, g) for g in range(4)], axis=0)


def sum_kernel(factor, *refs):
    out_ref = refs[-1]
    values = [ref[...].astype(F32) for ref in refs[:4]]
    out_ref[...] = ((values[0] + values[1]) + (values[2] + values[3])) * factor


def result_kernel(shift, place_ref, l0, l1, l2, l3, after_ref, in_ref, out_ref):
    group = group_of(place_ref[1], shift)
    for m, piece_ref in enumerate((l0, l1, l2, l3)):
        at = group ^ m

        @pl.when(at == 0)
        def _():
            out_ref[...] = piece_ref[...].astype(F32)

        @pl.when(at > 0)
        def _():
            in_ref[span((at - 1) * HD, HD), :] = piece_ref[...].astype(F32)


def pair_kernel(count, *refs):
    out_ref = refs[-1]
    rows = refs[0].shape[0]
    for i in range(count):
        out_ref[i * rows : (i + 1) * rows, :] = refs[i][...]


def parts_of(pair_ref, other_ref):
    rows = pair_ref.shape[0] // 2
    return (pair_ref.at[:rows], other_ref.at[:rows], pair_ref.at[rows:], other_ref.at[rows:])


def issue_order(count):
    return [0] + list(range(count - 1, 0, -1))


def back_order(count):
    near, far = list(range(1, count // 2)), list(range(count // 2, count))
    return [0] + far[:2] + near + far[2:]


def by_mask(refs, order):
    return [refs[order.index(m)] for m in range(len(refs))]


def project_kernel(count, place_ref, wanted_ref, pair_ref, other_ref, in_from, *refs):
    qz_ref, kv_ref, refs = refs[0], refs[1], refs[2:]
    out_refs, (wide_ref, in_ref, sem) = refs[:count], refs[count:]
    in_copy = pltpu.make_async_copy(in_from, in_ref, sem)
    in_copy.start()
    x_refs = parts_of(pair_ref, other_ref)
    head, node = place_ref[0], place_ref[1]
    rows = x_refs[0].shape[0]
    in_copy.wait()
    wide_ref[:, HD:BLOCK] = jnp.zeros((D, HD), BF16)
    for g in range(HEADS):

        @pl.when(head == g)
        def _():
            at = g * 3 * HD
            wide_ref[:, :HD] = in_ref[:, at : at + HD]
            wide_ref[:, BLOCK:] = in_ref[:, at + HD : at + 3 * HD]

    for part in range(4):
        at = span((head ^ part) * rows, rows)
        y = dot(x_refs[part][...], wide_ref[...]).astype(BF16)
        qz_ref[at, :] = y[:, :BLOCK]
        kv_ref[at, :] = y[:, BLOCK:]
    for m in range(count):
        for c in range(CAP):
            block = wanted_ref[node ^ m, 0, c]
            out_refs[m][c] = kv_ref[span(block * BLOCK, BLOCK), :]


def prepare_kernel(place_ref, slot_ref, count_ref, pair_ref, other_ref, kv_ref, after_ref, xt_ref, kvt_ref):
    head = place_ref[0]
    rows = pair_ref.shape[0] // 2
    for part, x_ref in enumerate(parts_of(pair_ref, other_ref)):
        xt_ref[:, span((head ^ part) * rows, rows)] = x_ref[...].T
    for i in range(BLK):
        kvt_ref[i] = kv_ref[i * BLOCK : (i + 1) * BLOCK, :].T


def table_kernel_part(node, kv_ref, kvt_ref, in_refs, table_ref, tablet_ref):
    for i in range(BLK):
        table_ref[i] = kv_ref[i * BLOCK : (i + 1) * BLOCK, :]
        tablet_ref[i] = kvt_ref[i]
    for m, in_ref in enumerate(in_refs):
        for c in range(CAP):
            block = in_ref[c]
            at = BLK + (node ^ m) * CAP + c
            table_ref[at] = block
            tablet_ref[at] = block.T


def early_forward_kernel(count, place_ref, slot_ref, count_ref, qz_ref, kv_ref, kvt_ref, *refs):
    in_refs, refs = by_mask(refs[:count], issue_order(count)), refs[count:]
    att_ref, attt_ref, table_ref, tablet_ref, top_ref, inv_ref, even_ref, odd_ref = refs
    table_kernel_part(place_ref[1], kv_ref, kvt_ref, in_refs, table_ref, tablet_ref)
    attend_blocks(
        0, slot_ref, count_ref, qz_ref, table_ref, tablet_ref,
        att_ref, attt_ref, top_ref, inv_ref, even_ref, odd_ref,
    )


def late_forward_kernel(
    slot_ref, count_ref, qz_ref, table_ref, tablet_ref, early_attt_ref, early_top_ref, early_inv_ref,
    att_ref, attt_ref, top_ref, inv_ref, even_ref, odd_ref,
):
    half = BLK // 2
    attt_ref[:, : half * BLOCK] = early_attt_ref[...]
    top_ref[:half] = early_top_ref[...]
    inv_ref[:half] = early_inv_ref[...]
    attend_blocks(
        half, slot_ref, count_ref, qz_ref, table_ref, tablet_ref,
        att_ref, attt_ref, top_ref, inv_ref, even_ref, odd_ref,
    )


def attend_blocks(
    start, slot_ref, count_ref, qz_ref, table_ref, tablet_ref,
    att_ref, attt_ref, top_ref, inv_ref, even_ref, odd_ref,
):
    def slots_of(i):
        return [slot_ref[i, j] for j in range(PER)]

    def score(i, raw_ref):
        live = count_ref[i]
        keys = jnp.concatenate([table_ref[s] for s in slots_of(i)], axis=0)
        raw = dot_last(keys, qz_ref[span(i * BLOCK, BLOCK), :])
        top = None
        for j in range(PER):
            here = jnp.where(j < live, raw[j * BLOCK : (j + 1) * BLOCK], -1e30)
            raw_ref[j * BLOCK : (j + 1) * BLOCK, :] = here
            here = here.reshape(BLOCK // 8, 8, BLOCK)
            highest = jnp.max(here, axis=0)
            top = highest if top is None else jnp.maximum(top, highest)
        return jnp.max(top, axis=0, keepdims=True)

    def attend(i, raw_ref, top):
        total = None
        for j in range(PER):
            here = slice(j * BLOCK, (j + 1) * BLOCK)
            raised = jnp.exp2((raw_ref[here, :] - top) * SCALE_LOG2E)
            raw_ref[here, :] = raised
            part = jnp.sum(raised.reshape(BLOCK // 8, 8, BLOCK), axis=0)
            total = part if total is None else total + part
        inverse = 1.0 / jnp.sum(total, axis=0, keepdims=True)
        values = jnp.concatenate([tablet_ref[s, HD:, :] for s in slots_of(i)], axis=1)
        result = dot(values, (raw_ref[...] * inverse).astype(BF16))
        attt_ref[:, span(i * BLOCK, BLOCK)] = result.astype(BF16)
        top_ref[i] = jnp.broadcast_to(top, (8, BLOCK))
        inv_ref[i] = jnp.broadcast_to(inverse, (8, BLOCK))
        return result

    def pair(t, even_top):
        first_at = start + 2 * t
        odd_top = score(first_at + 1, odd_ref)
        first = attend(first_at, even_ref, even_top)
        even_top = score(jnp.minimum(first_at + 2, BLK - 1), even_ref)
        second = attend(first_at + 1, odd_ref, odd_top)
        both = jnp.concatenate([first, second], axis=0)
        att_ref[span(t * BLOCK, BLOCK), :] = both.T.astype(BF16)
        return even_top

    lax.fori_loop(0, PAIRS // 2, pair, score(start, even_ref))


def middle_kernel(
    place_ref, x_pair, x_other, c_pair, c_other, a_pair, a_other, attt_ref, w_ref,
    out_ref, grad_out, gz_ref, dots_ref, owg_ref, wide_ref, pad_ref, grad_ref, sem,
):
    head = place_ref[0]
    rows = grad_ref.shape[0]
    grad_copy = pltpu.make_async_copy(grad_ref, grad_out, sem)
    own_w = w_ref[span(head * HD, HD), :]
    wide_ref[...] = jnp.zeros_like(wide_ref)
    for part in range(4):
        piece = w_ref[span((head ^ part) * HD, HD), :]
        at = (2 * part) * HD
        wide_ref[at : at + HD, :D] = piece
        wide_ref[at + HD : at + 2 * HD, D:] = piece
    pad_ref[:HD, :] = jnp.zeros((HD, D), BF16)
    pad_ref[HD:, :] = own_w
    a_refs = parts_of(a_pair, a_other)
    owg = jnp.zeros((HD, D), F32)
    pairs = rows // (2 * BLOCK)
    for part, (x_ref, c_ref) in enumerate(zip(parts_of(x_pair, x_other), parts_of(c_pair, c_other))):
        group = head ^ part
        at = span(group * (rows // 2), rows // 2)
        lhs = jnp.concatenate([a[at, :] for a in a_refs], axis=1)
        product = dot(lhs, wide_ref[...])
        lows = []
        for i in range(2 * pairs):
            local = slice(i * BLOCK, (i + 1) * BLOCK)
            pair, half = i // 2, i % 2
            summed = x_ref[local, :].astype(F32) + product[
                pair * BLOCK : (pair + 1) * BLOCK, half * D : (half + 1) * D
            ]
            inverse = lax.rsqrt(jnp.mean(summed * summed, axis=-1, keepdims=True) + 1e-06)
            normed = summed * inverse
            upstream = c_ref[local, :].astype(F32)
            grad = (upstream - normed * jnp.mean(upstream * normed, axis=-1, keepdims=True)) * inverse
            lows.append(grad.astype(BF16))
            if part == 0:
                out_ref[local, :] = normed.astype(BF16)
                grad_ref[local, :] = grad
        if part == 0:
            grad_copy.start()
        low = jnp.concatenate(lows, axis=0)
        at = span(group * rows, rows)
        gz_ref[at, :] = dot_last(low, pad_ref[...]).astype(BF16) * jnp.asarray(SCALE, BF16)
        turned = dot_last(own_w, low).astype(BF16).astype(F32)
        attended = attt_ref[:, at]
        sums = jnp.sum(turned * attended.astype(F32), axis=0, keepdims=True) * SCALE
        for i in range(2 * pairs):
            dots_ref[group * (2 * pairs) + i] = jnp.broadcast_to(
                sums[:, i * BLOCK : (i + 1) * BLOCK], (8, BLOCK)
            )
        owg += dot(attended, low)
    owg_ref[...] = owg
    grad_copy.wait()


def backward_kernel(
    count, place_ref, slot_ref, count_ref, qz_ref, gz_ref, table_ref, tablet_ref, top_ref, inv_ref, dots_ref, *refs
):
    own_ref, dqt_ref, refs = refs[0], refs[1], refs[2:]
    dq_refs, leave_refs = refs[:4], refs[4 : 4 + count]
    acc_ref, dq_ref, even_ref, odd_ref = refs[4 + count :]
    head, node = place_ref[0], place_ref[1]
    acc_ref[...] = jnp.zeros_like(acc_ref)

    def slots_of(i):
        return [slot_ref[i, j] for j in range(PER)]

    def rows_of(i):
        at = span(i * BLOCK, BLOCK)
        return jnp.concatenate([qz_ref[at, :], gz_ref[at, :]], axis=0)

    def score(i, both_ref):
        keys = jnp.concatenate([table_ref[s] for s in slots_of(i)], axis=0)
        both_ref[...] = dot_last(keys, rows_of(i))

    def spread(i, both_ref):
        slots = slots_of(i)
        live = count_ref[i]
        top = top_ref[i, :1, :]
        inverse = inv_ref[i, :1, :]
        dots = dots_ref[i, :1, :]
        weights, grads = [], []
        for j in range(PER):
            here = slice(j * BLOCK, (j + 1) * BLOCK)
            weight = jnp.exp2((both_ref[here, :BLOCK] - top) * SCALE_LOG2E) * inverse
            weight = jnp.where(j < live, weight, 0.0)
            weights.append(weight.astype(BF16))
            grads.append((weight * (both_ref[here, BLOCK:] - dots)).astype(BF16))
        score_grad = jnp.concatenate(grads, axis=0)
        low = jnp.concatenate(weights, axis=0)
        pair_grads = dot(jnp.concatenate([score_grad, low], axis=1), rows_of(i))
        for j in range(PER):
            acc_ref[slots[j]] += pair_grads[j * BLOCK : (j + 1) * BLOCK]
        turned = jnp.concatenate([tablet_ref[s, :HD, :] for s in slots], axis=1)
        result = dot(turned, score_grad)
        dqt_ref[:, span(i * BLOCK, BLOCK)] = result.astype(BF16)
        return result

    score(0, even_ref)

    @pl.loop(0, PAIRS)
    def _(t):
        score(2 * t + 1, odd_ref)
        first = spread(2 * t, even_ref)
        score(jnp.minimum(2 * t + 2, BLK - 1), even_ref)
        second = spread(2 * t + 1, odd_ref)
        both = jnp.concatenate([first, second], axis=0)
        dq_ref[span(t * BLOCK, BLOCK), :] = both.T.astype(BF16)

    lane = lax.broadcasted_iota(jnp.int32, (1, BLOCK), 1)
    unscale = jnp.where(lane < HD, 1.0, 1.0 / SCALE)
    own_ref[...] = acc_ref[:BLK] * unscale
    for m in range(count):
        for c in range(CAP):
            leave_refs[m][c] = (acc_ref[BLK + (node ^ m) * CAP + c] * unscale).astype(BF16)
    for part in range(4):
        size = dq_refs[part].shape[0]
        dq_refs[part][...] = dq_ref[span((head ^ part) * size, size), :]


def query_weight_kernel(place_ref, dqt_ref, pair_ref, other_ref, in_ref, out_ref, wkv_ref, wq_ref, k_ref, q_ref):
    head = place_ref[0]
    rows = pair_ref.shape[0] // 2
    total = jnp.zeros((HD, D), F32)
    for part, x_ref in enumerate(parts_of(pair_ref, other_ref)):
        total += dot(dqt_ref[:, span((head ^ part) * rows, rows)], x_ref[...])
    out_ref[...] = total
    blank = jnp.zeros((D, HD), BF16)
    for g in range(HEADS):
        at = g * 3 * HD
        query = in_ref[:, at : at + HD]
        k_ref[g] = in_ref[:, at + HD : at + 3 * HD]
        q_ref[g, :D] = jnp.concatenate([query, blank], axis=1)
        q_ref[g, D:] = jnp.concatenate([blank, query], axis=1)
    for part in range(4):
        lanes = slice(part * BLOCK, (part + 1) * BLOCK)
        wkv_ref[:, lanes] = k_ref[head ^ part]
        wq_ref[:, lanes] = q_ref[head ^ part]


def collect_kernel(count, place_ref, wanted_ref, own_ref, *refs):
    back_refs, dq_refs, refs = by_mask(refs[:count], back_order(count)), refs[count : count + 4], refs[count + 4 :]
    xt_ref, owg_ref, qwg_ref, refs = *refs[:3], refs[3:]
    send_refs, piece_refs, sum_ref = refs[:4], refs[4:8], refs[8]
    head, node = place_ref[0], place_ref[1]
    sum_ref[...] = own_ref[...]
    for m in range(count):
        for c in range(CAP):
            sum_ref[wanted_ref[node ^ m, 0, c]] += back_refs[m][c].astype(F32)
    for part in range(4):
        rows = 2 * dq_refs[part].shape[0]
        first = (head ^ part) * (rows // BLOCK)
        for i in range(rows // BLOCK):
            send_refs[part][i * BLOCK : (i + 1) * BLOCK, :] = sum_ref[first + i].astype(BF16)
        send_refs[part][rows:, :] = dq_refs[part][...]
    total = jnp.zeros((D, BLOCK), F32)
    for part in range(4):
        rows = 2 * dq_refs[part].shape[0]
        total += dot(xt_ref[:, span((head ^ part) * rows, rows)], send_refs[part][:rows, :])
    every = jnp.concatenate([owg_ref[...], qwg_ref[...], total.T], axis=0)
    split(every, group_of(node, top_shift(count)), piece_refs)


def finish_kernel(grad_from, s0, s3, s2, s1, wq_ref, wkv_ref, out_ref, done_ref, grad_ref, sem):
    done_ref[...] = jnp.zeros_like(done_ref)
    grad_copy = pltpu.make_async_copy(grad_from, grad_ref, sem)
    grad_copy.start()
    rows = out_ref.shape[0]
    s_refs = (s0, s1, s2, s3)
    kv = jnp.concatenate([s[:rows, :] for s in s_refs], axis=1)
    base = dot_last(kv, wkv_ref[...])
    lhs = jnp.concatenate([s[rows:, :] for s in s_refs], axis=1)
    product = dot_last(lhs, wq_ref[...])
    grad_copy.wait()
    for i in range(rows // BLOCK):
        at = slice(i * BLOCK, (i + 1) * BLOCK)
        pack = slice(i // 2 * BLOCK, (i // 2 + 1) * BLOCK)
        half = i % 2
        out_ref[at, :] = (
            grad_ref[at, :] + base[at] + product[pack, half * D : (half + 1) * D]
        ).astype(BF16)


def on_device(features, in_weight, out_weight, cotangent, key_slots, block_count, wanted):
    head_count = lax.axis_size("head")
    node_count = lax.axis_size("node")
    rows = features.shape[0]
    node_rows = rows * head_count
    total_nodes = node_rows * node_count
    table_size = BLK + node_count * CAP
    limit = (14 + table_size // 4) * MIB
    place = jnp.stack([lax.axis_index("head"), lax.axis_index("node")]).astype(jnp.int32)
    block_set = (CAP, BLOCK, BLOCK)

    def swap(value, axis, mask):
        size = lax.axis_size(axis)
        return lax.ppermute(value, axis, [(i, i ^ mask) for i in range(size)])

    def pair_up(values, after=()):
        rows, width = values[0].shape
        (pair,) = call(
            functools.partial(pair_kernel, len(values)),
            "pair",
            [((len(values) * rows, width), values[0].dtype)],
            [vmem()] * (len(values) + len(after)),
            4 * MIB,
        )(*values, *after)
        return pair, swap(pair, "head", 1)

    def exchange(pieces, axis, unit=1):
        moved = list(pieces)
        for mask in reversed(range(1, len(pieces))):
            moved[mask] = swap(pieces[mask], axis, mask * unit)
        return moved

    def add_nodes(pieces, shift, factor, after=()):
        moved = exchange(pieces, "node", 1 << shift)
        piece = (pieces[0].shape, F32)
        (total,) = call(
            functools.partial(sum_kernel, factor),
            "sum",
            [piece],
            [vmem()] * (4 + len(after)),
            4 * MIB,
        )(moved[0], *moved[:0:-1], *after)
        if shift == 1:
            total = total + swap(total, "node", 1)
        elif shift > 1:
            lower = call(
                functools.partial(split_kernel, shift - 2),
                "split",
                [((piece[0][0] // 4, D), F32)] * 4,
                [smem(), vmem()],
                limit,
            )(place, total)
            (total,) = call(
                functools.partial(join_kernel, shift - 2),
                "join",
                [piece],
                [smem()] + [vmem()] * 4,
                limit,
            )(place, *add_nodes(lower, shift - 2, 1.0))
        total = total.astype(pieces[0].dtype)
        return exchange([total] * 4, "node", 1 << shift)

    order = issue_order(node_count)
    across = swap(features, "head", 2)
    c_across = swap(cotangent, "head", 2)
    wants = lax.all_to_all(
        wanted.reshape(node_count, 1, CAP), "node", split_axis=0, concat_axis=0, tiled=True
    )
    xs = pair_up([features, across], [wants])
    qz, kv, *outgoing = call(
        functools.partial(project_kernel, node_count),
        "project",
        [((node_rows, BLOCK), BF16)] * 2 + [(block_set, BF16)] * node_count,
        [smem()] * 2 + [vmem()] * 2 + [hbm()],
        limit,
        flops=2 * node_rows * D * D,
        scratch=[
            pltpu.VMEM((D, D), BF16),
            pltpu.VMEM((D, 3 * D), BF16),
            pltpu.SemaphoreType.DMA,
        ],
    )(place, wants, *xs, in_weight)
    incoming = exchange(outgoing, "node")
    xt, kvt = call(
        prepare_kernel,
        "prepare",
        [((D, node_rows), BF16), ((BLK, BLOCK, BLOCK), BF16)],
        [smem()] * 3 + [vmem()] * 4,
        limit,
        flops=2 * node_rows * D * D,
    )(place, key_slots, block_count, *xs, kv, c_across)
    half = BLK // 2
    half_att = ((half * BLOCK // 2, BLOCK), BF16)
    early_att, early_attt, table, tablet, early_top, early_inv = call(
        functools.partial(early_forward_kernel, node_count),
        "early_forward",
        [
            half_att,
            ((HD, half * BLOCK), BF16),
            ((table_size, BLOCK, BLOCK), BF16),
            ((table_size, BLOCK, BLOCK), BF16),
            ((half, 8, BLOCK), F32),
            ((half, 8, BLOCK), F32),
        ],
        [smem()] * 3 + [vmem()] * (3 + node_count),
        limit,
        flops=2 * node_rows * PER * BLOCK * BLOCK,
        scratch=[pltpu.VMEM((PER * BLOCK, BLOCK), F32)] * 2,
    )(place, key_slots, block_count, qz, kv, kvt, *[incoming[m] for m in order])
    early_across = swap(early_att, "head", 2)
    late_att, attt, top, inv = call(
        late_forward_kernel,
        "late_forward",
        [
            half_att,
            ((HD, node_rows), BF16),
            ((BLK, 8, BLOCK), F32),
            ((BLK, 8, BLOCK), F32),
        ],
        [smem()] * 2 + [vmem()] * 6,
        limit,
        flops=2 * node_rows * PER * BLOCK * BLOCK,
        scratch=[pltpu.VMEM((PER * BLOCK, BLOCK), F32)] * 2,
    )(key_slots, block_count, qz, table, tablet, early_attt, early_top, early_inv)
    late_across = swap(late_att, "head", 2)
    parts = pair_up([early_att, late_att, early_across, late_across])
    cs = pair_up([cotangent, c_across], [top])
    output, norm_grad, gz, dots, owg = call(
        middle_kernel,
        "middle",
        [
            ((rows, D), BF16),
            ((rows, D), F32),
            ((node_rows, BLOCK), BF16),
            ((BLK, 8, BLOCK), F32),
            ((HD, D), F32),
        ],
        [smem()] + [vmem()] * 8,
        limit,
        flops=8 * node_rows * D * D,
        scratch=[
            pltpu.VMEM((2 * D, 2 * D), BF16),
            pltpu.VMEM((BLOCK, D), BF16),
            pltpu.VMEM((rows, D), F32),
            pltpu.SemaphoreType.DMA,
        ],
        out_specs=[vmem(), hbm()] + [vmem()] * 3,
    )(place, *xs, *cs, *parts, attt, out_weight)
    own, dqt, *rest = call(
        functools.partial(backward_kernel, node_count),
        "backward",
        [((BLK, BLOCK, BLOCK), F32), ((HD, node_rows), BF16)]
        + [((rows // 2, BLOCK), BF16)] * 4
        + [(block_set, BF16)] * node_count,
        [smem()] * 3 + [vmem()] * 7,
        limit,
        flops=10 * node_rows * PER * BLOCK * BLOCK,
        scratch=[
            pltpu.VMEM((table_size, BLOCK, BLOCK), F32),
            pltpu.VMEM((PAIRS * BLOCK, BLOCK), BF16),
            pltpu.VMEM((PER * BLOCK, 2 * BLOCK), F32),
            pltpu.VMEM((PER * BLOCK, 2 * BLOCK), F32),
        ],
    )(place, key_slots, block_count, qz, gz, table, tablet, top, inv, dots)
    returned = exchange(rest[4:], "node")
    query_wg, wkv, wq = call(
        query_weight_kernel,
        "query_weight",
        [((HD, D), F32), ((D, 2 * D), BF16), ((2 * D, 2 * D), BF16)],
        [smem()] + [vmem()] * 4,
        limit,
        flops=2 * node_rows * D * HD,
        scratch=[pltpu.VMEM((HEADS, D, BLOCK), BF16), pltpu.VMEM((HEADS, 2 * D, BLOCK), BF16)],
    )(place, dqt, *xs, in_weight)
    collected = call(
        functools.partial(collect_kernel, node_count),
        "collect",
        [((rows * 3 // 2, BLOCK), BF16)] * 4 + [((HD, D), BF16)] * 4,
        [smem()] * 2 + [vmem()] * (8 + node_count),
        limit,
        flops=2 * node_rows * D * BLOCK,
        scratch=[pltpu.VMEM((BLK, BLOCK, BLOCK), F32)],
    )(place, wants, own, *[returned[m] for m in back_order(node_count)], *rest[:4], xt, owg, query_wg)
    arrived = exchange(collected[:4], "head")
    shift = top_shift(node_count)
    factor = total_nodes ** (-0.5)
    late = add_nodes(collected[4:], shift, factor)
    feature_grad, finished = call(
        finish_kernel,
        "finish",
        [((rows, D), BF16), ((8, BLOCK), F32)],
        [hbm()] + [vmem()] * 6,
        limit,
        flops=4 * rows * 3 * D * D,
        scratch=[pltpu.VMEM((rows, D), F32), pltpu.SemaphoreType.DMA],
    )(norm_grad, arrived[0], *arrived[:0:-1], wq, wkv)
    in_grad, out_grad = call(
        functools.partial(result_kernel, shift),
        "result",
        [((3 * HD, D), F32), ((HD, D), F32)],
        [smem()] + [vmem()] * 5,
        limit,
    )(place, *late, finished)
    return (output, feature_grad, in_grad.T, out_grad)


def solution(mesh):
    placed = (
        P(("node", "head"), None),
        P(),
        P(),
        P(("node", "head"), None),
        P("node", None),
        P("node"),
        P("node", None, None),
    )
    return jax.shard_map(
        on_device,
        mesh=mesh,
        in_specs=placed,
        out_specs=(
            P(("node", "head"), None),
            P(("node", "head"), None),
            P(None, "head"),
            P("head", None),
        ),
        check_vma=False,
    )
```

```python
import functools
import math

import jax
import jax.numpy as jnp
from jax import lax
from jax.experimental import pallas as pl
from jax.experimental.pallas import tpu as pltpu
from jax.sharding import PartitionSpec as P

HEADS = 4
HD = 64
BLOCK = 128
BLK = 16
PER = 12
CAP = 2
D = 256
PAIRS = BLK // 2
SCALE = HD ** (-0.5)
SCALE_LOG2E = SCALE * math.log2(math.e)
BF16 = jnp.bfloat16
F32 = jnp.float32
MIB = 1 << 20
LAST = (((1,), (1,)), ((), ()))


def dot(a, b):
    return jnp.dot(a, b, preferred_element_type=F32)


def dot_last(a, b):
    return lax.dot_general(a, b, LAST, preferred_element_type=F32)


def span(start, size):
    return pl.ds(pl.multiple_of(start, size), size)


def smem():
    return pl.BlockSpec(memory_space=pltpu.SMEM)


def vmem():
    return pl.BlockSpec(memory_space=pltpu.VMEM)


def hbm():
    return pl.BlockSpec(memory_space=pltpu.HBM)


def call(kernel, name, outs, in_specs, limit, flops=0, scratch=(), out_specs=None):
    return pl.pallas_call(
        kernel,
        name=name,
        out_shape=tuple(jax.ShapeDtypeStruct(shape, kind) for shape, kind in outs),
        in_specs=in_specs,
        out_specs=tuple(out_specs or [vmem() for _ in outs]),
        scratch_shapes=scratch,
        compiler_params=pltpu.CompilerParams(vmem_limit_bytes=limit),
        cost_estimate=pl.CostEstimate(flops=flops, bytes_accessed=4 * MIB, transcendentals=0),
    )


def top_shift(count):
    return count.bit_length() - 3


def group_of(node, shift):
    return (node >> shift) & 3


def split(value, group, piece_refs):
    size = value.shape[0] // 4
    for g in range(4):
        for m in range(4):

            @pl.when((group ^ m) == g)
            def _():
                piece_refs[m][...] = value[g * size : (g + 1) * size, :].astype(piece_refs[m].dtype)


def split_kernel(shift, place_ref, value_ref, *piece_refs):
    split(value_ref[...], group_of(place_ref[1], shift), piece_refs)


def join(piece_refs, group, g):
    value = piece_refs[0][...]
    for m in range(1, 4):
        value = jnp.where((group ^ m) == g, piece_refs[m][...], value)
    return value


def join_kernel(shift, place_ref, p0, p1, p2, p3, out_ref):
    group = group_of(place_ref[1], shift)
    out_ref[...] = jnp.concatenate([join((p0, p1, p2, p3), group, g) for g in range(4)], axis=0)


def sum_kernel(factor, *refs):
    out_ref = refs[-1]
    values = [ref[...].astype(F32) for ref in refs[:4]]
    out_ref[...] = ((values[0] + values[1]) + (values[2] + values[3])) * factor


def result_kernel(shift, place_ref, l0, l1, l2, l3, after_ref, in_ref, out_ref):
    group = group_of(place_ref[1], shift)
    for m, piece_ref in enumerate((l0, l1, l2, l3)):
        at = group ^ m

        @pl.when(at == 0)
        def _():
            out_ref[...] = piece_ref[...].astype(F32)

        @pl.when(at > 0)
        def _():
            in_ref[span((at - 1) * HD, HD), :] = piece_ref[...].astype(F32)


def pair_kernel(count, *refs):
    out_ref = refs[-1]
    rows = refs[0].shape[0]
    for i in range(count):
        out_ref[i * rows : (i + 1) * rows, :] = refs[i][...]


def parts_of(pair_ref, other_ref):
    rows = pair_ref.shape[0] // 2
    return (pair_ref.at[:rows], other_ref.at[:rows], pair_ref.at[rows:], other_ref.at[rows:])


def step_masks(count):
    near, far = list(range(count // 2 - 1, 0, -1)), list(range(count - 1, count // 2 - 1, -1))
    return [0] + far + near, [0] + near + far


def mask_at(step, head, count):
    even, odd = step_masks(count)
    return jnp.where((head & 1) == 1, odd[step], even[step])


def project_kernel(count, place_ref, wanted_ref, pair_ref, other_ref, in_from, *refs):
    qz_ref, kv_ref, refs = refs[0], refs[1], refs[2:]
    out_refs, (wide_ref, in_ref, sem) = refs[:count], refs[count:]
    in_copy = pltpu.make_async_copy(in_from, in_ref, sem)
    in_copy.start()
    x_refs = parts_of(pair_ref, other_ref)
    head, node = place_ref[0], place_ref[1]
    rows = x_refs[0].shape[0]
    in_copy.wait()
    wide_ref[:, HD:BLOCK] = jnp.zeros((D, HD), BF16)
    for g in range(HEADS):

        @pl.when(head == g)
        def _():
            at = g * 3 * HD
            wide_ref[:, :HD] = in_ref[:, at : at + HD]
            wide_ref[:, BLOCK:] = in_ref[:, at + HD : at + 3 * HD]

    for part in range(4):
        at = span((head ^ part) * rows, rows)
        y = dot(x_refs[part][...], wide_ref[...]).astype(BF16)
        qz_ref[at, :] = y[:, :BLOCK]
        kv_ref[at, :] = y[:, BLOCK:]
    for step in range(count):
        other = node ^ mask_at(step, head, count)
        for c in range(CAP):
            block = wanted_ref[other, 0, c]
            out_refs[step][c] = kv_ref[span(block * BLOCK, BLOCK), :]


def prepare_kernel(place_ref, slot_ref, count_ref, pair_ref, other_ref, kv_ref, after_ref, xt_ref, kvt_ref):
    head = place_ref[0]
    rows = pair_ref.shape[0] // 2
    for part, x_ref in enumerate(parts_of(pair_ref, other_ref)):
        xt_ref[:, span((head ^ part) * rows, rows)] = x_ref[...].T
    for i in range(BLK):
        kvt_ref[i] = kv_ref[i * BLOCK : (i + 1) * BLOCK, :].T


def fill_table(place_ref, kv_ref, kvt_ref, in_refs, table_ref, tablet_ref):
    head, node = place_ref[0], place_ref[1]
    for i in range(BLK):
        table_ref[i] = kv_ref[i * BLOCK : (i + 1) * BLOCK, :]
        tablet_ref[i] = kvt_ref[i]
    for step, in_ref in enumerate(in_refs):
        other = node ^ mask_at(step, head, len(in_refs))
        for c in range(CAP):
            block = in_ref[c]
            at = BLK + other * CAP + c
            table_ref[at] = block
            tablet_ref[at] = block.T


def early_forward_kernel(count, place_ref, slot_ref, count_ref, qz_ref, kv_ref, kvt_ref, *refs):
    in_refs, refs = refs[:count], refs[count:]
    att_ref, attt_ref, table_ref, tablet_ref, top_ref, inv_ref, even_ref, odd_ref = refs
    fill_table(place_ref, kv_ref, kvt_ref, in_refs, table_ref, tablet_ref)
    attend_blocks(
        0, slot_ref, count_ref, qz_ref, table_ref, tablet_ref,
        att_ref, attt_ref, top_ref, inv_ref, even_ref, odd_ref,
    )


def late_forward_kernel(
    slot_ref, count_ref, qz_ref, table_ref, tablet_ref, early_attt_ref, early_top_ref, early_inv_ref,
    att_ref, attt_ref, top_ref, inv_ref, even_ref, odd_ref,
):
    half = BLK // 2
    attt_ref[:, : half * BLOCK] = early_attt_ref[...]
    top_ref[:half] = early_top_ref[...]
    inv_ref[:half] = early_inv_ref[...]
    attend_blocks(
        half, slot_ref, count_ref, qz_ref, table_ref, tablet_ref,
        att_ref, attt_ref, top_ref, inv_ref, even_ref, odd_ref,
    )


def attend_blocks(
    start, slot_ref, count_ref, qz_ref, table_ref, tablet_ref,
    att_ref, attt_ref, top_ref, inv_ref, even_ref, odd_ref,
):
    def slots_of(i):
        return [slot_ref[i, j] for j in range(PER)]

    def score(i, raw_ref):
        live = count_ref[i]
        keys = jnp.concatenate([table_ref[s] for s in slots_of(i)], axis=0)
        raw = dot_last(keys, qz_ref[span(i * BLOCK, BLOCK), :])
        top = None
        for j in range(PER):
            here = jnp.where(j < live, raw[j * BLOCK : (j + 1) * BLOCK], -1e30)
            raw_ref[j * BLOCK : (j + 1) * BLOCK, :] = here
            here = here.reshape(BLOCK // 8, 8, BLOCK)
            highest = jnp.max(here, axis=0)
            top = highest if top is None else jnp.maximum(top, highest)
        return jnp.max(top, axis=0, keepdims=True)

    def attend(i, raw_ref, top):
        total = None
        for j in range(PER):
            here = slice(j * BLOCK, (j + 1) * BLOCK)
            raised = jnp.exp2((raw_ref[here, :] - top) * SCALE_LOG2E)
            raw_ref[here, :] = raised
            part = jnp.sum(raised.reshape(BLOCK // 8, 8, BLOCK), axis=0)
            total = part if total is None else total + part
        inverse = 1.0 / jnp.sum(total, axis=0, keepdims=True)
        values = jnp.concatenate([tablet_ref[s, HD:, :] for s in slots_of(i)], axis=1)
        result = dot(values, (raw_ref[...] * inverse).astype(BF16))
        attt_ref[:, span(i * BLOCK, BLOCK)] = result.astype(BF16)
        top_ref[i] = jnp.broadcast_to(top, (8, BLOCK))
        inv_ref[i] = jnp.broadcast_to(inverse, (8, BLOCK))
        return result

    def pair(t, even_top):
        first_at = start + 2 * t
        odd_top = score(first_at + 1, odd_ref)
        first = attend(first_at, even_ref, even_top)
        even_top = score(jnp.minimum(first_at + 2, BLK - 1), even_ref)
        second = attend(first_at + 1, odd_ref, odd_top)
        both = jnp.concatenate([first, second], axis=0)
        att_ref[span(t * BLOCK, BLOCK), :] = both.T.astype(BF16)
        return even_top

    lax.fori_loop(0, PAIRS // 2, pair, score(start, even_ref))


def middle_kernel(
    place_ref, x_pair, x_other, c_pair, c_other, a_pair, a_other, attt_ref, w_ref,
    out_ref, grad_out, gz_ref, dots_ref, owg_ref, wide_ref, pad_ref, grad_ref, sem,
):
    head = place_ref[0]
    rows = grad_ref.shape[0]
    grad_copy = pltpu.make_async_copy(grad_ref, grad_out, sem)
    own_w = w_ref[span(head * HD, HD), :]
    wide_ref[...] = jnp.zeros_like(wide_ref)
    for part in range(4):
        piece = w_ref[span((head ^ part) * HD, HD), :]
        at = (2 * part) * HD
        wide_ref[at : at + HD, :D] = piece
        wide_ref[at + HD : at + 2 * HD, D:] = piece
    pad_ref[:HD, :] = jnp.zeros((HD, D), BF16)
    pad_ref[HD:, :] = own_w
    a_refs = parts_of(a_pair, a_other)
    owg = jnp.zeros((HD, D), F32)
    pairs = rows // (2 * BLOCK)
    for part, (x_ref, c_ref) in enumerate(zip(parts_of(x_pair, x_other), parts_of(c_pair, c_other))):
        group = head ^ part
        at = span(group * (rows // 2), rows // 2)
        lhs = jnp.concatenate([a[at, :] for a in a_refs], axis=1)
        product = dot(lhs, wide_ref[...])
        lows = []
        for i in range(2 * pairs):
            local = slice(i * BLOCK, (i + 1) * BLOCK)
            pair, half = i // 2, i % 2
            summed = x_ref[local, :].astype(F32) + product[
                pair * BLOCK : (pair + 1) * BLOCK, half * D : (half + 1) * D
            ]
            inverse = lax.rsqrt(jnp.mean(summed * summed, axis=-1, keepdims=True) + 1e-06)
            normed = summed * inverse
            upstream = c_ref[local, :].astype(F32)
            grad = (upstream - normed * jnp.mean(upstream * normed, axis=-1, keepdims=True)) * inverse
            lows.append(grad.astype(BF16))
            if part == 0:
                out_ref[local, :] = normed.astype(BF16)
                grad_ref[local, :] = grad
        if part == 0:
            grad_copy.start()
        low = jnp.concatenate(lows, axis=0)
        at = span(group * rows, rows)
        gz_ref[at, :] = dot_last(low, pad_ref[...]).astype(BF16) * jnp.asarray(SCALE, BF16)
        turned = dot_last(own_w, low).astype(BF16).astype(F32)
        attended = attt_ref[:, at]
        sums = jnp.sum(turned * attended.astype(F32), axis=0, keepdims=True) * SCALE
        for i in range(2 * pairs):
            dots_ref[group * (2 * pairs) + i] = jnp.broadcast_to(
                sums[:, i * BLOCK : (i + 1) * BLOCK], (8, BLOCK)
            )
        owg += dot(attended, low)
    owg_ref[...] = owg
    grad_copy.wait()


def backward_kernel(
    count, place_ref, slot_ref, count_ref, qz_ref, gz_ref, table_ref, tablet_ref, top_ref, inv_ref, dots_ref, *refs
):
    own_ref, dqt_ref, refs = refs[0], refs[1], refs[2:]
    dq_refs, leave_refs = refs[:4], refs[4 : 4 + count]
    acc_ref, dq_ref, even_ref, odd_ref = refs[4 + count :]
    head, node = place_ref[0], place_ref[1]
    acc_ref[...] = jnp.zeros_like(acc_ref)

    def slots_of(i):
        return [slot_ref[i, j] for j in range(PER)]

    def rows_of(i):
        at = span(i * BLOCK, BLOCK)
        return jnp.concatenate([qz_ref[at, :], gz_ref[at, :]], axis=0)

    def score(i, both_ref):
        keys = jnp.concatenate([table_ref[s] for s in slots_of(i)], axis=0)
        both_ref[...] = dot_last(keys, rows_of(i))

    def spread(i, both_ref):
        slots = slots_of(i)
        live = count_ref[i]
        top = top_ref[i, :1, :]
        inverse = inv_ref[i, :1, :]
        dots = dots_ref[i, :1, :]
        weights, grads = [], []
        for j in range(PER):
            here = slice(j * BLOCK, (j + 1) * BLOCK)
            weight = jnp.exp2((both_ref[here, :BLOCK] - top) * SCALE_LOG2E) * inverse
            weight = jnp.where(j < live, weight, 0.0)
            weights.append(weight.astype(BF16))
            grads.append((weight * (both_ref[here, BLOCK:] - dots)).astype(BF16))
        score_grad = jnp.concatenate(grads, axis=0)
        low = jnp.concatenate(weights, axis=0)
        pair_grads = dot(jnp.concatenate([score_grad, low], axis=1), rows_of(i))
        for j in range(PER):
            acc_ref[slots[j]] += pair_grads[j * BLOCK : (j + 1) * BLOCK]
        turned = jnp.concatenate([tablet_ref[s, :HD, :] for s in slots], axis=1)
        result = dot(turned, score_grad)
        dqt_ref[:, span(i * BLOCK, BLOCK)] = result.astype(BF16)
        return result

    score(0, even_ref)

    @pl.loop(0, PAIRS)
    def _(t):
        score(2 * t + 1, odd_ref)
        first = spread(2 * t, even_ref)
        score(jnp.minimum(2 * t + 2, BLK - 1), even_ref)
        second = spread(2 * t + 1, odd_ref)
        both = jnp.concatenate([first, second], axis=0)
        dq_ref[span(t * BLOCK, BLOCK), :] = both.T.astype(BF16)

    lane = lax.broadcasted_iota(jnp.int32, (1, BLOCK), 1)
    unscale = jnp.where(lane < HD, 1.0, 1.0 / SCALE)
    own_ref[...] = acc_ref[:BLK] * unscale
    for step in range(count):
        other = node ^ mask_at(step, head, count)
        for c in range(CAP):
            leave_refs[step][c] = (acc_ref[BLK + other * CAP + c] * unscale).astype(BF16)
    for part in range(4):
        size = dq_refs[part].shape[0]
        dq_refs[part][...] = dq_ref[span((head ^ part) * size, size), :]


def query_weight_kernel(place_ref, dqt_ref, pair_ref, other_ref, in_ref, out_ref, wkv_ref, wq_ref, k_ref, q_ref):
    head = place_ref[0]
    rows = pair_ref.shape[0] // 2
    total = jnp.zeros((HD, D), F32)
    for part, x_ref in enumerate(parts_of(pair_ref, other_ref)):
        total += dot(dqt_ref[:, span((head ^ part) * rows, rows)], x_ref[...])
    out_ref[...] = total
    blank = jnp.zeros((D, HD), BF16)
    for g in range(HEADS):
        at = g * 3 * HD
        query = in_ref[:, at : at + HD]
        k_ref[g] = in_ref[:, at + HD : at + 3 * HD]
        q_ref[g, :D] = jnp.concatenate([query, blank], axis=1)
        q_ref[g, D:] = jnp.concatenate([blank, query], axis=1)
    for part in range(4):
        lanes = slice(part * BLOCK, (part + 1) * BLOCK)
        wkv_ref[:, lanes] = k_ref[head ^ part]
        wq_ref[:, lanes] = q_ref[head ^ part]


def collect_kernel(count, place_ref, wanted_ref, own_ref, *refs):
    back_refs, dq_refs, refs = refs[:count], refs[count : count + 4], refs[count + 4 :]
    xt_ref, owg_ref, qwg_ref, refs = *refs[:3], refs[3:]
    own_send, beside_send, across_send, piece_refs, sum_ref = *refs[:3], refs[3:7], refs[7]
    size = own_send.shape[0]
    send_refs = (own_send, beside_send, across_send.at[:size], across_send.at[size:])
    head, node = place_ref[0], place_ref[1]
    sum_ref[...] = own_ref[...]
    for step in range(count):
        other = node ^ mask_at(step, head, count)
        for c in range(CAP):
            sum_ref[wanted_ref[other, 0, c]] += back_refs[step][c].astype(F32)
    for part in range(4):
        rows = 2 * dq_refs[part].shape[0]
        first = (head ^ part) * (rows // BLOCK)
        for i in range(rows // BLOCK):
            send_refs[part][i * BLOCK : (i + 1) * BLOCK, :] = sum_ref[first + i].astype(BF16)
        send_refs[part][rows:, :] = dq_refs[part][...]
    total = jnp.zeros((D, BLOCK), F32)
    for part in range(4):
        rows = 2 * dq_refs[part].shape[0]
        total += dot(xt_ref[:, span((head ^ part) * rows, rows)], send_refs[part][:rows, :])
    every = jnp.concatenate([owg_ref[...], qwg_ref[...], total.T], axis=0)
    split(every, group_of(node, top_shift(count)), piece_refs)


def relay_kernel(beside_ref, across_ref, after_ref, out_ref):
    size = beside_ref.shape[0]
    out_ref[:size, :] = beside_ref[...]
    out_ref[size:, :] = across_ref[size:, :]


def finish_kernel(grad_from, own_ref, beside_ref, across_ref, wq_ref, wkv_ref, out_ref, done_ref, grad_ref, sem):
    done_ref[...] = jnp.zeros_like(done_ref)
    grad_copy = pltpu.make_async_copy(grad_from, grad_ref, sem)
    grad_copy.start()
    rows = out_ref.shape[0]
    size = own_ref.shape[0]
    s_refs = (own_ref, beside_ref.at[:size], across_ref.at[:size], beside_ref.at[size:])
    kv = jnp.concatenate([s[:rows, :] for s in s_refs], axis=1)
    base = dot_last(kv, wkv_ref[...])
    lhs = jnp.concatenate([s[rows:, :] for s in s_refs], axis=1)
    product = dot_last(lhs, wq_ref[...])
    grad_copy.wait()
    for i in range(rows // BLOCK):
        at = slice(i * BLOCK, (i + 1) * BLOCK)
        pack = slice(i // 2 * BLOCK, (i // 2 + 1) * BLOCK)
        half = i % 2
        out_ref[at, :] = (
            grad_ref[at, :] + base[at] + product[pack, half * D : (half + 1) * D]
        ).astype(BF16)


def on_device(features, in_weight, out_weight, cotangent, key_slots, block_count, wanted):
    head_count = lax.axis_size("head")
    node_count = lax.axis_size("node")
    rows = features.shape[0]
    node_rows = rows * head_count
    total_nodes = node_rows * node_count
    table_size = BLK + node_count * CAP
    limit = (14 + table_size // 4) * MIB
    place = jnp.stack([lax.axis_index("head"), lax.axis_index("node")]).astype(jnp.int32)
    block_set = (CAP, BLOCK, BLOCK)

    def swap(value, axis, mask):
        size = lax.axis_size(axis)
        return lax.ppermute(value, axis, [(i, i ^ mask) for i in range(size)])

    def pair_up(values, after=()):
        rows, width = values[0].shape
        (pair,) = call(
            functools.partial(pair_kernel, len(values)),
            "pair",
            [((len(values) * rows, width), values[0].dtype)],
            [vmem()] * (len(values) + len(after)),
            4 * MIB,
        )(*values, *after)
        return pair, swap(pair, "head", 1)

    def exchange(pieces, axis, unit=1):
        moved = list(pieces)
        for mask in reversed(range(1, len(pieces))):
            moved[mask] = swap(pieces[mask], axis, mask * unit)
        return moved

    def add_nodes(pieces, shift, factor, after=()):
        moved = exchange(pieces, "node", 1 << shift)
        piece = (pieces[0].shape, F32)
        (total,) = call(
            functools.partial(sum_kernel, factor),
            "sum",
            [piece],
            [vmem()] * (4 + len(after)),
            4 * MIB,
        )(moved[0], *moved[:0:-1], *after)
        if shift == 1:
            total = total + swap(total, "node", 1)
        elif shift > 1:
            lower = call(
                functools.partial(split_kernel, shift - 2),
                "split",
                [((piece[0][0] // 4, D), F32)] * 4,
                [smem(), vmem()],
                limit,
            )(place, total)
            (total,) = call(
                functools.partial(join_kernel, shift - 2),
                "join",
                [piece],
                [smem()] + [vmem()] * 4,
                limit,
            )(place, *add_nodes(lower, shift - 2, 1.0)[0])
        total = total.astype(pieces[0].dtype)
        return exchange([total] * 4, "node", 1 << shift), total

    def exchange_nodes(pieces):
        moved = list(pieces)
        even, odd = step_masks(node_count)
        for step in range(1, node_count):
            perm = [
                (n * head_count + h, (n ^ (odd if h & 1 else even)[step]) * head_count + h)
                for n in range(node_count)
                for h in range(head_count)
            ]
            moved[step] = lax.ppermute(pieces[step], ("node", "head"), perm)
        return moved

    across = swap(features, "head", 2)
    c_across = swap(cotangent, "head", 2)
    wants = lax.all_to_all(
        wanted.reshape(node_count, 1, CAP), "node", split_axis=0, concat_axis=0, tiled=True
    )
    xs = pair_up([features, across], [wants])
    qz, kv, *outgoing = call(
        functools.partial(project_kernel, node_count),
        "project",
        [((node_rows, BLOCK), BF16)] * 2 + [(block_set, BF16)] * node_count,
        [smem()] * 2 + [vmem()] * 2 + [hbm()],
        limit,
        flops=2 * node_rows * D * D,
        scratch=[
            pltpu.VMEM((D, D), BF16),
            pltpu.VMEM((D, 3 * D), BF16),
            pltpu.SemaphoreType.DMA,
        ],
    )(place, wants, *xs, in_weight)
    incoming = exchange_nodes(outgoing)
    xt, kvt = call(
        prepare_kernel,
        "prepare",
        [((D, node_rows), BF16), ((BLK, BLOCK, BLOCK), BF16)],
        [smem()] * 3 + [vmem()] * 4,
        limit,
        flops=2 * node_rows * D * D,
    )(place, key_slots, block_count, *xs, kv, c_across)
    half = BLK // 2
    half_att = ((half * BLOCK // 2, BLOCK), BF16)
    early_att, early_attt, table, tablet, early_top, early_inv = call(
        functools.partial(early_forward_kernel, node_count),
        "early_forward",
        [
            half_att,
            ((HD, half * BLOCK), BF16),
            ((table_size, BLOCK, BLOCK), BF16),
            ((table_size, BLOCK, BLOCK), BF16),
            ((half, 8, BLOCK), F32),
            ((half, 8, BLOCK), F32),
        ],
        [smem()] * 3 + [vmem()] * (3 + node_count),
        limit,
        flops=2 * node_rows * PER * BLOCK * BLOCK,
        scratch=[pltpu.VMEM((PER * BLOCK, BLOCK), F32)] * 2,
    )(place, key_slots, block_count, qz, kv, kvt, *incoming)
    early_across = swap(early_att, "head", 2)
    late_att, attt, top, inv = call(
        late_forward_kernel,
        "late_forward",
        [
            half_att,
            ((HD, node_rows), BF16),
            ((BLK, 8, BLOCK), F32),
            ((BLK, 8, BLOCK), F32),
        ],
        [smem()] * 2 + [vmem()] * 6,
        limit,
        flops=2 * node_rows * PER * BLOCK * BLOCK,
        scratch=[pltpu.VMEM((PER * BLOCK, BLOCK), F32)] * 2,
    )(key_slots, block_count, qz, table, tablet, early_attt, early_top, early_inv)
    late_across = swap(late_att, "head", 2)
    parts = pair_up([early_att, late_att, early_across, late_across])
    cs = pair_up([cotangent, c_across], [top])
    output, norm_grad, gz, dots, owg = call(
        middle_kernel,
        "middle",
        [
            ((rows, D), BF16),
            ((rows, D), F32),
            ((node_rows, BLOCK), BF16),
            ((BLK, 8, BLOCK), F32),
            ((HD, D), F32),
        ],
        [smem()] + [vmem()] * 8,
        limit,
        flops=8 * node_rows * D * D,
        scratch=[
            pltpu.VMEM((2 * D, 2 * D), BF16),
            pltpu.VMEM((BLOCK, D), BF16),
            pltpu.VMEM((rows, D), F32),
            pltpu.SemaphoreType.DMA,
        ],
        out_specs=[vmem(), hbm()] + [vmem()] * 3,
    )(place, *xs, *cs, *parts, attt, out_weight)
    own, dqt, *rest = call(
        functools.partial(backward_kernel, node_count),
        "backward",
        [((BLK, BLOCK, BLOCK), F32), ((HD, node_rows), BF16)]
        + [((rows // 2, BLOCK), BF16)] * 4
        + [(block_set, BF16)] * node_count,
        [smem()] * 3 + [vmem()] * 7,
        limit,
        flops=10 * node_rows * PER * BLOCK * BLOCK,
        scratch=[
            pltpu.VMEM((table_size, BLOCK, BLOCK), F32),
            pltpu.VMEM((PAIRS * BLOCK, BLOCK), BF16),
            pltpu.VMEM((PER * BLOCK, 2 * BLOCK), F32),
            pltpu.VMEM((PER * BLOCK, 2 * BLOCK), F32),
        ],
    )(place, key_slots, block_count, qz, gz, table, tablet, top, inv, dots)
    returned = exchange_nodes(rest[4:])
    query_wg, wkv, wq = call(
        query_weight_kernel,
        "query_weight",
        [((HD, D), F32), ((D, 2 * D), BF16), ((2 * D, 2 * D), BF16)],
        [smem()] + [vmem()] * 4,
        limit,
        flops=2 * node_rows * D * HD,
        scratch=[pltpu.VMEM((HEADS, D, BLOCK), BF16), pltpu.VMEM((HEADS, 2 * D, BLOCK), BF16)],
    )(place, dqt, *xs, in_weight)
    sent = ((rows * 3 // 2, BLOCK), BF16)
    collected = call(
        functools.partial(collect_kernel, node_count),
        "collect",
        [sent, sent, ((rows * 3, BLOCK), BF16)] + [((HD, D), BF16)] * 4,
        [smem()] * 2 + [vmem()] * (8 + node_count),
        limit,
        flops=2 * node_rows * D * BLOCK,
        scratch=[pltpu.VMEM((BLK, BLOCK, BLOCK), F32)],
    )(place, wants, own, *returned, *rest[:4], xt, owg, query_wg)
    own_send, beside_send, across_send = collected[:3]
    across = swap(across_send, "head", 2)
    shift = top_shift(node_count)
    factor = total_nodes ** (-0.5)
    late, summed = add_nodes(collected[3:], shift, factor)
    (relay,) = call(
        relay_kernel, "relay", [((rows * 3, BLOCK), BF16)], [vmem()] * 3, 4 * MIB
    )(beside_send, across, summed)
    beside = swap(relay, "head", 1)
    feature_grad, finished = call(
        finish_kernel,
        "finish",
        [((rows, D), BF16), ((8, BLOCK), F32)],
        [hbm()] + [vmem()] * 5,
        limit,
        flops=4 * rows * 3 * D * D,
        scratch=[pltpu.VMEM((rows, D), F32), pltpu.SemaphoreType.DMA],
    )(norm_grad, own_send, beside, across, wq, wkv)
    in_grad, out_grad = call(
        functools.partial(result_kernel, shift),
        "result",
        [((3 * HD, D), F32), ((HD, D), F32)],
        [smem()] + [vmem()] * 5,
        limit,
    )(place, *late, finished)
    return (output, feature_grad, in_grad.T, out_grad)


def solution(mesh):
    placed = (
        P(("node", "head"), None),
        P(),
        P(),
        P(("node", "head"), None),
        P("node", None),
        P("node"),
        P("node", None, None),
    )
    return jax.shard_map(
        on_device,
        mesh=mesh,
        in_specs=placed,
        out_specs=(
            P(("node", "head"), None),
            P(("node", "head"), None),
            P(None, "head"),
            P("head", None),
        ),
        check_vma=False,
    )
```

```python
import functools
import math

import jax
import jax.numpy as jnp
from jax import lax
from jax.experimental import pallas as pl
from jax.experimental.pallas import tpu as pltpu
from jax.sharding import PartitionSpec as P

HEADS = 4
HD = 64
BLOCK = 128
BLK = 16
PER = 12
CAP = 2
D = 256
PAIRS = BLK // 2
SCALE = HD ** (-0.5)
SCALE_LOG2E = SCALE * math.log2(math.e)
BF16 = jnp.bfloat16
F32 = jnp.float32
MIB = 1 << 20
LAST = (((1,), (1,)), ((), ()))


def dot(a, b):
    return jnp.dot(a, b, preferred_element_type=F32)


def dot_last(a, b):
    return lax.dot_general(a, b, LAST, preferred_element_type=F32)


def span(start, size):
    return pl.ds(pl.multiple_of(start, size), size)


def smem():
    return pl.BlockSpec(memory_space=pltpu.SMEM)


def vmem():
    return pl.BlockSpec(memory_space=pltpu.VMEM)


def hbm():
    return pl.BlockSpec(memory_space=pltpu.HBM)


def call(kernel, name, outs, in_specs, limit, flops=0, scratch=(), out_specs=None):
    return pl.pallas_call(
        kernel,
        name=name,
        out_shape=tuple(jax.ShapeDtypeStruct(shape, kind) for shape, kind in outs),
        in_specs=in_specs,
        out_specs=tuple(out_specs or [vmem() for _ in outs]),
        scratch_shapes=scratch,
        compiler_params=pltpu.CompilerParams(vmem_limit_bytes=limit),
        cost_estimate=pl.CostEstimate(flops=flops, bytes_accessed=4 * MIB, transcendentals=0),
    )


def top_shift(count):
    return count.bit_length() - 3


def group_of(node, shift):
    return (node >> shift) & 3


PIECE_STEPS = ((0, 3, 2, 1), (0, 1, 2, 3))


def piece_at(group, step, head):
    return group ^ jnp.where((head & 1) == 1, PIECE_STEPS[1][step], PIECE_STEPS[0][step])


def split(value, group, head, piece_refs):
    size = value.shape[0] // 4
    for g in range(4):
        for step in range(4):

            @pl.when(piece_at(group, step, head) == g)
            def _():
                piece_refs[step][...] = value[g * size : (g + 1) * size, :].astype(piece_refs[step].dtype)


def split_kernel(shift, place_ref, value_ref, *piece_refs):
    split(value_ref[...], group_of(place_ref[1], shift), place_ref[0], piece_refs)


def join(piece_refs, group, head, g):
    value = piece_refs[0][...]
    for step in range(1, 4):
        value = jnp.where(piece_at(group, step, head) == g, piece_refs[step][...], value)
    return value


def join_kernel(shift, place_ref, p0, p1, p2, p3, out_ref):
    head, group = place_ref[0], group_of(place_ref[1], shift)
    out_ref[...] = jnp.concatenate([join((p0, p1, p2, p3), group, head, g) for g in range(4)], axis=0)


def sum_kernel(factor, *refs):
    out_ref = refs[-1]
    values = [ref[...].astype(F32) for ref in refs[:4]]
    out_ref[...] = ((values[0] + values[1]) + (values[2] + values[3])) * factor


def result_kernel(shift, place_ref, l0, l1, l2, l3, after_ref, in_ref, out_ref):
    head, group = place_ref[0], group_of(place_ref[1], shift)
    for step, piece_ref in enumerate((l0, l1, l2, l3)):
        at = piece_at(group, step, head)

        @pl.when(at == 0)
        def _():
            out_ref[...] = piece_ref[...].astype(F32)

        @pl.when(at > 0)
        def _():
            in_ref[span((at - 1) * HD, HD), :] = piece_ref[...].astype(F32)


def pair_kernel(count, *refs):
    out_ref = refs[-1]
    rows = refs[0].shape[0]
    for i in range(count):
        out_ref[i * rows : (i + 1) * rows, :] = refs[i][...]


def parts_of(pair_ref, other_ref):
    rows = pair_ref.shape[0] // 2
    return (pair_ref.at[:rows], other_ref.at[:rows], pair_ref.at[rows:], other_ref.at[rows:])


def step_masks(count):
    near, far = list(range(count // 2 - 1, 0, -1)), list(range(count - 1, count // 2 - 1, -1))
    return [0] + far + near, [0] + near + far


def mask_at(step, head, count):
    even, odd = step_masks(count)
    return jnp.where((head & 1) == 1, odd[step], even[step])


def project_kernel(count, place_ref, wanted_ref, pair_ref, other_ref, in_ref, *refs):
    qz_ref, kv_ref, refs = refs[0], refs[1], refs[2:]
    out_refs, wide_ref = refs[:count], refs[count]
    x_refs = parts_of(pair_ref, other_ref)
    head, node = place_ref[0], place_ref[1]
    rows = x_refs[0].shape[0]
    wide_ref[:, HD:BLOCK] = jnp.zeros((D, HD), BF16)
    for g in range(HEADS):

        @pl.when(head == g)
        def _():
            at = g * 3 * HD
            wide_ref[:, :HD] = in_ref[:, at : at + HD]
            wide_ref[:, BLOCK:] = in_ref[:, at + HD : at + 3 * HD]

    for part in range(4):
        at = span((head ^ part) * rows, rows)
        y = dot(x_refs[part][...], wide_ref[...]).astype(BF16)
        qz_ref[at, :] = y[:, :BLOCK]
        kv_ref[at, :] = y[:, BLOCK:]
    for step in range(count):
        other = node ^ mask_at(step, head, count)
        for c in range(CAP):
            block = wanted_ref[other, 0, c]
            out_refs[step][c] = kv_ref[span(block * BLOCK, BLOCK), :]


def prepare_kernel(place_ref, slot_ref, count_ref, pair_ref, other_ref, kv_ref, after_ref, xt_ref, kvt_ref):
    head = place_ref[0]
    rows = pair_ref.shape[0] // 2
    for part, x_ref in enumerate(parts_of(pair_ref, other_ref)):
        xt_ref[:, span((head ^ part) * rows, rows)] = x_ref[...].T
    for i in range(BLK):
        kvt_ref[i] = kv_ref[i * BLOCK : (i + 1) * BLOCK, :].T


def fill_table(place_ref, kv_ref, kvt_ref, in_refs, table_ref, tablet_ref):
    head, node = place_ref[0], place_ref[1]
    for i in range(BLK):
        table_ref[i] = kv_ref[i * BLOCK : (i + 1) * BLOCK, :]
        tablet_ref[i] = kvt_ref[i]
    for step, in_ref in enumerate(in_refs):
        other = node ^ mask_at(step, head, len(in_refs))
        for c in range(CAP):
            block = in_ref[c]
            at = BLK + other * CAP + c
            table_ref[at] = block
            tablet_ref[at] = block.T


def early_forward_kernel(count, place_ref, slot_ref, count_ref, qz_ref, kv_ref, kvt_ref, *refs):
    in_refs, refs = refs[:count], refs[count:]
    att_ref, attt_ref, table_ref, tablet_ref, top_ref, inv_ref, even_ref, odd_ref = refs
    fill_table(place_ref, kv_ref, kvt_ref, in_refs, table_ref, tablet_ref)
    attend_blocks(
        0, slot_ref, count_ref, qz_ref, table_ref, tablet_ref,
        att_ref, attt_ref, top_ref, inv_ref, even_ref, odd_ref,
    )


def late_forward_kernel(
    slot_ref, count_ref, qz_ref, table_ref, tablet_ref, early_attt_ref, early_top_ref, early_inv_ref,
    att_ref, attt_ref, top_ref, inv_ref, even_ref, odd_ref,
):
    half = BLK // 2
    attt_ref[:, : half * BLOCK] = early_attt_ref[...]
    top_ref[:half] = early_top_ref[...]
    inv_ref[:half] = early_inv_ref[...]
    attend_blocks(
        half, slot_ref, count_ref, qz_ref, table_ref, tablet_ref,
        att_ref, attt_ref, top_ref, inv_ref, even_ref, odd_ref,
    )


def attend_blocks(
    start, slot_ref, count_ref, qz_ref, table_ref, tablet_ref,
    att_ref, attt_ref, top_ref, inv_ref, even_ref, odd_ref,
):
    def slots_of(i):
        return [slot_ref[i, j] for j in range(PER)]

    def score(i, raw_ref):
        live = count_ref[i]
        keys = jnp.concatenate([table_ref[s] for s in slots_of(i)], axis=0)
        raw = dot_last(keys, qz_ref[span(i * BLOCK, BLOCK), :])
        top = None
        for j in range(PER):
            here = jnp.where(j < live, raw[j * BLOCK : (j + 1) * BLOCK], -1e30)
            raw_ref[j * BLOCK : (j + 1) * BLOCK, :] = here
            here = here.reshape(BLOCK // 8, 8, BLOCK)
            highest = jnp.max(here, axis=0)
            top = highest if top is None else jnp.maximum(top, highest)
        return jnp.max(top, axis=0, keepdims=True)

    def attend(i, raw_ref, top):
        total = None
        for j in range(PER):
            here = slice(j * BLOCK, (j + 1) * BLOCK)
            raised = jnp.exp2((raw_ref[here, :] - top) * SCALE_LOG2E)
            raw_ref[here, :] = raised
            part = jnp.sum(raised.reshape(BLOCK // 8, 8, BLOCK), axis=0)
            total = part if total is None else total + part
        inverse = 1.0 / jnp.sum(total, axis=0, keepdims=True)
        values = jnp.concatenate([tablet_ref[s, HD:, :] for s in slots_of(i)], axis=1)
        result = dot(values, (raw_ref[...] * inverse).astype(BF16))
        attt_ref[:, span(i * BLOCK, BLOCK)] = result.astype(BF16)
        top_ref[i] = jnp.broadcast_to(top, (8, BLOCK))
        inv_ref[i] = jnp.broadcast_to(inverse, (8, BLOCK))
        return result

    def pair(t, even_top):
        first_at = start + 2 * t
        odd_top = score(first_at + 1, odd_ref)
        first = attend(first_at, even_ref, even_top)
        even_top = score(jnp.minimum(first_at + 2, BLK - 1), even_ref)
        second = attend(first_at + 1, odd_ref, odd_top)
        both = jnp.concatenate([first, second], axis=0)
        att_ref[span(t * BLOCK, BLOCK), :] = both.T.astype(BF16)
        return even_top

    lax.fori_loop(0, PAIRS // 2, pair, score(start, even_ref))


def middle_kernel(
    place_ref, x_pair, x_other, c_pair, c_other, a_pair, a_other, attt_ref, w_ref,
    out_ref, grad_out, gz_ref, dots_ref, low_ref, wide_ref, pad_ref, grad_ref, sem,
):
    head = place_ref[0]
    rows = grad_ref.shape[0]
    grad_copy = pltpu.make_async_copy(grad_ref, grad_out, sem)
    own_w = w_ref[span(head * HD, HD), :]
    wide_ref[...] = jnp.zeros_like(wide_ref)
    for part in range(4):
        piece = w_ref[span((head ^ part) * HD, HD), :]
        at = (2 * part) * HD
        wide_ref[at : at + HD, :D] = piece
        wide_ref[at + HD : at + 2 * HD, D:] = piece
    pad_ref[:HD, :] = jnp.zeros((HD, D), BF16)
    pad_ref[HD:, :] = own_w
    a_refs = parts_of(a_pair, a_other)
    pairs = rows // (2 * BLOCK)
    for part, (x_ref, c_ref) in enumerate(zip(parts_of(x_pair, x_other), parts_of(c_pair, c_other))):
        group = head ^ part
        at = span(group * (rows // 2), rows // 2)
        lhs = jnp.concatenate([a[at, :] for a in a_refs], axis=1)
        product = dot(lhs, wide_ref[...])
        lows = []
        for i in range(2 * pairs):
            local = slice(i * BLOCK, (i + 1) * BLOCK)
            pair, half = i // 2, i % 2
            summed = x_ref[local, :].astype(F32) + product[
                pair * BLOCK : (pair + 1) * BLOCK, half * D : (half + 1) * D
            ]
            inverse = lax.rsqrt(jnp.mean(summed * summed, axis=-1, keepdims=True) + 1e-06)
            normed = summed * inverse
            upstream = c_ref[local, :].astype(F32)
            grad = (upstream - normed * jnp.mean(upstream * normed, axis=-1, keepdims=True)) * inverse
            lows.append(grad.astype(BF16))
            if part == 0:
                out_ref[local, :] = normed.astype(BF16)
                grad_ref[local, :] = grad
        if part == 0:
            grad_copy.start()
        low = jnp.concatenate(lows, axis=0)
        at = span(group * rows, rows)
        gz_ref[at, :] = dot_last(low, pad_ref[...]).astype(BF16) * jnp.asarray(SCALE, BF16)
        turned = dot_last(own_w, low).astype(BF16).astype(F32)
        attended = attt_ref[:, at]
        sums = jnp.sum(turned * attended.astype(F32), axis=0, keepdims=True) * SCALE
        for i in range(2 * pairs):
            dots_ref[group * (2 * pairs) + i] = jnp.broadcast_to(
                sums[:, i * BLOCK : (i + 1) * BLOCK], (8, BLOCK)
            )
        low_ref[at, :] = low
    grad_copy.wait()


def backward_kernel(
    count, place_ref, slot_ref, count_ref, qz_ref, gz_ref, table_ref, tablet_ref, top_ref, inv_ref, dots_ref, *refs
):
    own_ref, dqt_ref, refs = refs[0], refs[1], refs[2:]
    dq_refs, leave_refs = refs[:4], refs[4 : 4 + count]
    acc_ref, dq_ref, even_ref, odd_ref = refs[4 + count :]
    head, node = place_ref[0], place_ref[1]
    acc_ref[...] = jnp.zeros_like(acc_ref)

    def slots_of(i):
        return [slot_ref[i, j] for j in range(PER)]

    def rows_of(i):
        at = span(i * BLOCK, BLOCK)
        return jnp.concatenate([qz_ref[at, :], gz_ref[at, :]], axis=0)

    def score(i, both_ref):
        keys = jnp.concatenate([table_ref[s] for s in slots_of(i)], axis=0)
        both_ref[...] = dot_last(keys, rows_of(i))

    def spread(i, both_ref):
        slots = slots_of(i)
        live = count_ref[i]
        top = top_ref[i, :1, :]
        inverse = inv_ref[i, :1, :]
        dots = dots_ref[i, :1, :]
        weights, grads = [], []
        for j in range(PER):
            here = slice(j * BLOCK, (j + 1) * BLOCK)
            weight = jnp.exp2((both_ref[here, :BLOCK] - top) * SCALE_LOG2E) * inverse
            weight = jnp.where(j < live, weight, 0.0)
            weights.append(weight.astype(BF16))
            grads.append((weight * (both_ref[here, BLOCK:] - dots)).astype(BF16))
        score_grad = jnp.concatenate(grads, axis=0)
        low = jnp.concatenate(weights, axis=0)
        pair_grads = dot(jnp.concatenate([score_grad, low], axis=1), rows_of(i))
        for j in range(PER):
            acc_ref[slots[j]] += pair_grads[j * BLOCK : (j + 1) * BLOCK]
        turned = jnp.concatenate([tablet_ref[s, :HD, :] for s in slots], axis=1)
        result = dot(turned, score_grad)
        dqt_ref[:, span(i * BLOCK, BLOCK)] = result.astype(BF16)
        return result

    score(0, even_ref)

    @pl.loop(0, PAIRS)
    def _(t):
        score(2 * t + 1, odd_ref)
        first = spread(2 * t, even_ref)
        score(jnp.minimum(2 * t + 2, BLK - 1), even_ref)
        second = spread(2 * t + 1, odd_ref)
        both = jnp.concatenate([first, second], axis=0)
        dq_ref[span(t * BLOCK, BLOCK), :] = both.T.astype(BF16)

    lane = lax.broadcasted_iota(jnp.int32, (1, BLOCK), 1)
    unscale = jnp.where(lane < HD, 1.0, 1.0 / SCALE)
    own_ref[...] = acc_ref[:BLK] * unscale
    for step in range(count):
        other = node ^ mask_at(step, head, count)
        for c in range(CAP):
            leave_refs[step][c] = (acc_ref[BLK + other * CAP + c] * unscale).astype(BF16)
    for part in range(4):
        size = dq_refs[part].shape[0]
        dq_refs[part][...] = dq_ref[span((head ^ part) * size, size), :]


def query_weight_kernel(
    place_ref, dqt_ref, pair_ref, other_ref, in_ref, attt_ref, low_ref,
    out_ref, owg_ref, wkv_ref, wq_ref, k_ref, q_ref,
):
    owg_ref[...] = dot(attt_ref[...], low_ref[...])
    head = place_ref[0]
    rows = pair_ref.shape[0] // 2
    total = jnp.zeros((HD, D), F32)
    for part, x_ref in enumerate(parts_of(pair_ref, other_ref)):
        total += dot(dqt_ref[:, span((head ^ part) * rows, rows)], x_ref[...])
    out_ref[...] = total
    blank = jnp.zeros((D, HD), BF16)
    for g in range(HEADS):
        at = g * 3 * HD
        query = in_ref[:, at : at + HD]
        k_ref[g] = in_ref[:, at + HD : at + 3 * HD]
        q_ref[g, :D] = jnp.concatenate([query, blank], axis=1)
        q_ref[g, D:] = jnp.concatenate([blank, query], axis=1)
    for part in range(4):
        lanes = slice(part * BLOCK, (part + 1) * BLOCK)
        wkv_ref[:, lanes] = k_ref[head ^ part]
        wq_ref[:, lanes] = q_ref[head ^ part]


def collect_kernel(count, place_ref, wanted_ref, own_ref, *refs):
    back_refs, dq_refs, refs = refs[:count], refs[count : count + 4], refs[count + 4 :]
    xt_ref, owg_ref, qwg_ref, refs = *refs[:3], refs[3:]
    own_send, beside_send, across_send, piece_refs, sum_ref = *refs[:3], refs[3:7], refs[7]
    size = own_send.shape[0]
    send_refs = (own_send, beside_send, across_send.at[:size], across_send.at[size:])
    head, node = place_ref[0], place_ref[1]
    sum_ref[...] = own_ref[...]
    for step in range(count):
        other = node ^ mask_at(step, head, count)
        for c in range(CAP):
            sum_ref[wanted_ref[other, 0, c]] += back_refs[step][c].astype(F32)
    for part in range(4):
        rows = 2 * dq_refs[part].shape[0]
        first = (head ^ part) * (rows // BLOCK)
        for i in range(rows // BLOCK):
            send_refs[part][i * BLOCK : (i + 1) * BLOCK, :] = sum_ref[first + i].astype(BF16)
        send_refs[part][rows:, :] = dq_refs[part][...]
    total = jnp.zeros((D, BLOCK), F32)
    for part in range(4):
        rows = 2 * dq_refs[part].shape[0]
        total += dot(xt_ref[:, span((head ^ part) * rows, rows)], send_refs[part][:rows, :])
    every = jnp.concatenate([owg_ref[...], qwg_ref[...], total.T], axis=0)
    split(every, group_of(node, top_shift(count)), head, piece_refs)


def relay_kernel(beside_ref, across_ref, after_ref, out_ref):
    size = beside_ref.shape[0]
    out_ref[:size, :] = beside_ref[...]
    out_ref[size:, :] = across_ref[size:, :]


def finish_kernel(grad_from, own_ref, beside_ref, across_ref, wq_ref, wkv_ref, out_ref, done_ref, grad_ref, sem):
    done_ref[...] = jnp.zeros_like(done_ref)
    grad_copy = pltpu.make_async_copy(grad_from, grad_ref, sem)
    grad_copy.start()
    rows = out_ref.shape[0]
    size = own_ref.shape[0]
    s_refs = (own_ref, beside_ref.at[:size], across_ref.at[:size], beside_ref.at[size:])
    kv = jnp.concatenate([s[:rows, :] for s in s_refs], axis=1)
    base = dot_last(kv, wkv_ref[...])
    lhs = jnp.concatenate([s[rows:, :] for s in s_refs], axis=1)
    product = dot_last(lhs, wq_ref[...])
    grad_copy.wait()
    for i in range(rows // BLOCK):
        at = slice(i * BLOCK, (i + 1) * BLOCK)
        pack = slice(i // 2 * BLOCK, (i // 2 + 1) * BLOCK)
        half = i % 2
        out_ref[at, :] = (
            grad_ref[at, :] + base[at] + product[pack, half * D : (half + 1) * D]
        ).astype(BF16)


def on_device(features, in_weight, out_weight, cotangent, key_slots, block_count, wanted):
    head_count = lax.axis_size("head")
    node_count = lax.axis_size("node")
    rows = features.shape[0]
    node_rows = rows * head_count
    total_nodes = node_rows * node_count
    table_size = BLK + node_count * CAP
    limit = (14 + table_size // 4) * MIB
    place = jnp.stack([lax.axis_index("head"), lax.axis_index("node")]).astype(jnp.int32)
    block_set = (CAP, BLOCK, BLOCK)

    def swap(value, axis, mask):
        size = lax.axis_size(axis)
        return lax.ppermute(value, axis, [(i, i ^ mask) for i in range(size)])

    def pair_up(values, after=()):
        rows, width = values[0].shape
        (pair,) = call(
            functools.partial(pair_kernel, len(values)),
            "pair",
            [((len(values) * rows, width), values[0].dtype)],
            [vmem()] * (len(values) + len(after)),
            4 * MIB,
        )(*values, *after)
        return pair, swap(pair, "head", 1)

    def exchange_nodes(pieces, masks, unit=1):
        moved = list(pieces)
        for step in range(1, len(pieces)):
            perm = [
                (n * head_count + h, (n ^ (masks[h & 1][step] * unit)) * head_count + h)
                for n in range(node_count)
                for h in range(head_count)
            ]
            moved[step] = lax.ppermute(pieces[step], ("node", "head"), perm)
        return moved

    def add_nodes(pieces, shift, factor, after=()):
        moved = exchange_nodes(pieces, PIECE_STEPS, 1 << shift)
        piece = (pieces[0].shape, F32)
        (total,) = call(
            functools.partial(sum_kernel, factor),
            "sum",
            [piece],
            [vmem()] * (4 + len(after)),
            4 * MIB,
        )(*moved, *after)
        if shift == 1:
            total = total + swap(total, "node", 1)
        elif shift > 1:
            lower = call(
                functools.partial(split_kernel, shift - 2),
                "split",
                [((piece[0][0] // 4, D), F32)] * 4,
                [smem(), vmem()],
                limit,
            )(place, total)
            (total,) = call(
                functools.partial(join_kernel, shift - 2),
                "join",
                [piece],
                [smem()] + [vmem()] * 4,
                limit,
            )(place, *add_nodes(lower, shift - 2, 1.0)[0])
        total = total.astype(pieces[0].dtype)
        return exchange_nodes([total] * 4, PIECE_STEPS, 1 << shift), total

    across = swap(features, "head", 2)
    c_across = swap(cotangent, "head", 2)
    wants = lax.all_to_all(
        wanted.reshape(node_count, 1, CAP), "node", split_axis=0, concat_axis=0, tiled=True
    )
    xs = pair_up([features, across], [wants])
    qz, kv, *outgoing = call(
        functools.partial(project_kernel, node_count),
        "project",
        [((node_rows, BLOCK), BF16)] * 2 + [(block_set, BF16)] * node_count,
        [smem()] * 2 + [vmem()] * 3,
        limit,
        flops=2 * node_rows * D * D,
        scratch=[pltpu.VMEM((D, D), BF16)],
    )(place, wants, *xs, in_weight)
    incoming = exchange_nodes(outgoing, step_masks(node_count))
    xt, kvt = call(
        prepare_kernel,
        "prepare",
        [((D, node_rows), BF16), ((BLK, BLOCK, BLOCK), BF16)],
        [smem()] * 3 + [vmem()] * 4,
        limit,
        flops=2 * node_rows * D * D,
    )(place, key_slots, block_count, *xs, kv, c_across)
    half = BLK // 2
    half_att = ((half * BLOCK // 2, BLOCK), BF16)
    early_att, early_attt, table, tablet, early_top, early_inv = call(
        functools.partial(early_forward_kernel, node_count),
        "early_forward",
        [
            half_att,
            ((HD, half * BLOCK), BF16),
            ((table_size, BLOCK, BLOCK), BF16),
            ((table_size, BLOCK, BLOCK), BF16),
            ((half, 8, BLOCK), F32),
            ((half, 8, BLOCK), F32),
        ],
        [smem()] * 3 + [vmem()] * (3 + node_count),
        limit,
        flops=2 * node_rows * PER * BLOCK * BLOCK,
        scratch=[pltpu.VMEM((PER * BLOCK, BLOCK), F32)] * 2,
    )(place, key_slots, block_count, qz, kv, kvt, *incoming)
    early_across = swap(early_att, "head", 2)
    late_att, attt, top, inv = call(
        late_forward_kernel,
        "late_forward",
        [
            half_att,
            ((HD, node_rows), BF16),
            ((BLK, 8, BLOCK), F32),
            ((BLK, 8, BLOCK), F32),
        ],
        [smem()] * 2 + [vmem()] * 6,
        limit,
        flops=2 * node_rows * PER * BLOCK * BLOCK,
        scratch=[pltpu.VMEM((PER * BLOCK, BLOCK), F32)] * 2,
    )(key_slots, block_count, qz, table, tablet, early_attt, early_top, early_inv)
    late_across = swap(late_att, "head", 2)
    parts = pair_up([early_att, late_att, early_across, late_across])
    cs = pair_up([cotangent, c_across], [top])
    output, norm_grad, gz, dots, low = call(
        middle_kernel,
        "middle",
        [
            ((rows, D), BF16),
            ((rows, D), F32),
            ((node_rows, BLOCK), BF16),
            ((BLK, 8, BLOCK), F32),
            ((node_rows, D), BF16),
        ],
        [smem()] + [vmem()] * 8,
        limit,
        flops=8 * node_rows * D * D,
        scratch=[
            pltpu.VMEM((2 * D, 2 * D), BF16),
            pltpu.VMEM((BLOCK, D), BF16),
            pltpu.VMEM((rows, D), F32),
            pltpu.SemaphoreType.DMA,
        ],
        out_specs=[vmem(), hbm()] + [vmem()] * 3,
    )(place, *xs, *cs, *parts, attt, out_weight)
    own, dqt, *rest = call(
        functools.partial(backward_kernel, node_count),
        "backward",
        [((BLK, BLOCK, BLOCK), F32), ((HD, node_rows), BF16)]
        + [((rows // 2, BLOCK), BF16)] * 4
        + [(block_set, BF16)] * node_count,
        [smem()] * 3 + [vmem()] * 7,
        limit,
        flops=10 * node_rows * PER * BLOCK * BLOCK,
        scratch=[
            pltpu.VMEM((table_size, BLOCK, BLOCK), F32),
            pltpu.VMEM((PAIRS * BLOCK, BLOCK), BF16),
            pltpu.VMEM((PER * BLOCK, 2 * BLOCK), F32),
            pltpu.VMEM((PER * BLOCK, 2 * BLOCK), F32),
        ],
    )(place, key_slots, block_count, qz, gz, table, tablet, top, inv, dots)
    returned = exchange_nodes(rest[4:], step_masks(node_count))
    query_wg, owg, wkv, wq = call(
        query_weight_kernel,
        "query_weight",
        [((HD, D), F32)] * 2 + [((D, 2 * D), BF16), ((2 * D, 2 * D), BF16)],
        [smem()] + [vmem()] * 6,
        limit,
        flops=2 * node_rows * D * HD,
        scratch=[pltpu.VMEM((HEADS, D, BLOCK), BF16), pltpu.VMEM((HEADS, 2 * D, BLOCK), BF16)],
    )(place, dqt, *xs, in_weight, attt, low)
    sent = ((rows * 3 // 2, BLOCK), BF16)
    collected = call(
        functools.partial(collect_kernel, node_count),
        "collect",
        [sent, sent, ((rows * 3, BLOCK), BF16)] + [((HD, D), BF16)] * 4,
        [smem()] * 2 + [vmem()] * (8 + node_count),
        limit,
        flops=2 * node_rows * D * BLOCK,
        scratch=[pltpu.VMEM((BLK, BLOCK, BLOCK), F32)],
    )(place, wants, own, *returned, *rest[:4], xt, owg, query_wg)
    own_send, beside_send, across_send = collected[:3]
    across = swap(across_send, "head", 2)
    shift = top_shift(node_count)
    factor = total_nodes ** (-0.5)
    late, summed = add_nodes(collected[3:], shift, factor)
    (relay,) = call(
        relay_kernel, "relay", [((rows * 3, BLOCK), BF16)], [vmem()] * 3, 4 * MIB
    )(beside_send, across, summed)
    beside = swap(relay, "head", 1)
    feature_grad, finished = call(
        finish_kernel,
        "finish",
        [((rows, D), BF16), ((8, BLOCK), F32)],
        [hbm()] + [vmem()] * 5,
        limit,
        flops=4 * rows * 3 * D * D,
        scratch=[pltpu.VMEM((rows, D), F32), pltpu.SemaphoreType.DMA],
    )(norm_grad, own_send, beside, across, wq, wkv)
    in_grad, out_grad = call(
        functools.partial(result_kernel, shift),
        "result",
        [((3 * HD, D), F32), ((HD, D), F32)],
        [smem()] + [vmem()] * 5,
        limit,
    )(place, *late, finished)
    return (output, feature_grad, in_grad.T, out_grad)


def solution(mesh):
    placed = (
        P(("node", "head"), None),
        P(),
        P(),
        P(("node", "head"), None),
        P("node", None),
        P("node"),
        P("node", None, None),
    )
    return jax.shard_map(
        on_device,
        mesh=mesh,
        in_specs=placed,
        out_specs=(
            P(("node", "head"), None),
            P(("node", "head"), None),
            P(None, "head"),
            P("head", None),
        ),
        check_vma=False,
    )
```

```python
import functools
import math

import jax
import jax.numpy as jnp
from jax import lax
from jax.experimental import pallas as pl
from jax.experimental.pallas import tpu as pltpu
from jax.sharding import PartitionSpec as P

HEADS = 4
HD = 64
BLOCK = 128
BLK = 16
PER = 12
CAP = 2
D = 256
PAIRS = BLK // 2
SCALE = HD ** (-0.5)
SCALE_LOG2E = SCALE * math.log2(math.e)
BF16 = jnp.bfloat16
F32 = jnp.float32
MIB = 1 << 20
LAST = (((1,), (1,)), ((), ()))


def dot(a, b):
    return jnp.dot(a, b, preferred_element_type=F32)


def dot_last(a, b):
    return lax.dot_general(a, b, LAST, preferred_element_type=F32)


def span(start, size):
    return pl.ds(pl.multiple_of(start, size), size)


def smem():
    return pl.BlockSpec(memory_space=pltpu.SMEM)


def vmem():
    return pl.BlockSpec(memory_space=pltpu.VMEM)


def hbm():
    return pl.BlockSpec(memory_space=pltpu.HBM)


def call(kernel, name, outs, in_specs, limit, flops=0, scratch=(), out_specs=None):
    return pl.pallas_call(
        kernel,
        name=name,
        out_shape=tuple(jax.ShapeDtypeStruct(shape, kind) for shape, kind in outs),
        in_specs=in_specs,
        out_specs=tuple(out_specs or [vmem() for _ in outs]),
        scratch_shapes=scratch,
        compiler_params=pltpu.CompilerParams(vmem_limit_bytes=limit),
        cost_estimate=pl.CostEstimate(flops=flops, bytes_accessed=4 * MIB, transcendentals=0),
    )


def top_shift(count):
    return count.bit_length() - 3


def group_of(node, shift):
    return (node >> shift) & 3


PIECE_STEPS = ((0, 3, 2, 1), (0, 3, 2, 1))


def piece_at(group, step, head):
    return group ^ jnp.where((head & 1) == 1, PIECE_STEPS[1][step], PIECE_STEPS[0][step])


def split(value, group, head, piece_refs):
    size = value.shape[0] // 4
    for g in range(4):
        for step in range(4):

            @pl.when(piece_at(group, step, head) == g)
            def _():
                piece_refs[step][...] = value[g * size : (g + 1) * size, :].astype(piece_refs[step].dtype)


def split_kernel(shift, place_ref, value_ref, *piece_refs):
    split(value_ref[...], group_of(place_ref[1], shift), place_ref[0], piece_refs)


def join(piece_refs, group, head, g):
    value = piece_refs[0][...]
    for step in range(1, 4):
        value = jnp.where(piece_at(group, step, head) == g, piece_refs[step][...], value)
    return value


def join_kernel(shift, place_ref, p0, p1, p2, p3, out_ref):
    head, group = place_ref[0], group_of(place_ref[1], shift)
    out_ref[...] = jnp.concatenate([join((p0, p1, p2, p3), group, head, g) for g in range(4)], axis=0)


def sum_kernel(factor, *refs):
    out_ref = refs[-1]
    values = [ref[...].astype(F32) for ref in refs[:4]]
    out_ref[...] = ((values[0] + values[1]) + (values[2] + values[3])) * factor


def result_kernel(shift, place_ref, l0, l1, l2, l3, after_ref, in_ref, out_ref):
    head, group = place_ref[0], group_of(place_ref[1], shift)
    for step, piece_ref in enumerate((l0, l1, l2, l3)):
        at = piece_at(group, step, head)

        @pl.when(at == 0)
        def _():
            out_ref[...] = piece_ref[...].astype(F32)

        @pl.when(at > 0)
        def _():
            in_ref[span((at - 1) * HD, HD), :] = piece_ref[...].astype(F32)


def pair_kernel(count, *refs):
    out_ref = refs[-1]
    rows = refs[0].shape[0]
    for i in range(count):
        out_ref[i * rows : (i + 1) * rows, :] = refs[i][...]


def parts_of(pair_ref, other_ref):
    rows = pair_ref.shape[0] // 2
    return (pair_ref.at[:rows], other_ref.at[:rows], pair_ref.at[rows:], other_ref.at[rows:])


def step_masks(count):
    near, far = list(range(count // 2 - 1, 0, -1)), list(range(count - 1, count // 2 - 1, -1))
    return [0] + far + near, [0] + near + far


def mask_at(step, head, count):
    even, odd = step_masks(count)
    return jnp.where((head & 1) == 1, odd[step], even[step])


def project_kernel(count, place_ref, wanted_ref, pair_ref, other_ref, in_ref, *refs):
    qz_ref, kv_ref, refs = refs[0], refs[1], refs[2:]
    out_refs, wide_ref = refs[:count], refs[count]
    x_refs = parts_of(pair_ref, other_ref)
    head, node = place_ref[0], place_ref[1]
    rows = x_refs[0].shape[0]
    wide_ref[:, HD:BLOCK] = jnp.zeros((D, HD), BF16)
    for g in range(HEADS):

        @pl.when(head == g)
        def _():
            at = g * 3 * HD
            wide_ref[:, :HD] = in_ref[:, at : at + HD]
            wide_ref[:, BLOCK:] = in_ref[:, at + HD : at + 3 * HD]

    for part in range(4):
        at = span((head ^ part) * rows, rows)
        y = dot(x_refs[part][...], wide_ref[...]).astype(BF16)
        qz_ref[at, :] = y[:, :BLOCK]
        kv_ref[at, :] = y[:, BLOCK:]
    for step in range(count):
        other = node ^ mask_at(step, head, count)
        for c in range(CAP):
            block = wanted_ref[other, 0, c]
            out_refs[step][c] = kv_ref[span(block * BLOCK, BLOCK), :]


def prepare_kernel(place_ref, slot_ref, count_ref, pair_ref, other_ref, kv_ref, after_ref, xt_ref, kvt_ref):
    head = place_ref[0]
    rows = pair_ref.shape[0] // 2
    for part, x_ref in enumerate(parts_of(pair_ref, other_ref)):
        xt_ref[:, span((head ^ part) * rows, rows)] = x_ref[...].T
    for i in range(BLK):
        kvt_ref[i] = kv_ref[i * BLOCK : (i + 1) * BLOCK, :].T


def fill_table(place_ref, kv_ref, kvt_ref, in_refs, table_ref, tablet_ref):
    head, node = place_ref[0], place_ref[1]
    for i in range(BLK):
        table_ref[i] = kv_ref[i * BLOCK : (i + 1) * BLOCK, :]
        tablet_ref[i] = kvt_ref[i]
    for step, in_ref in enumerate(in_refs):
        other = node ^ mask_at(step, head, len(in_refs))
        for c in range(CAP):
            block = in_ref[c]
            at = BLK + other * CAP + c
            table_ref[at] = block
            tablet_ref[at] = block.T


def early_forward_kernel(count, place_ref, slot_ref, count_ref, qz_ref, kv_ref, kvt_ref, *refs):
    in_refs, refs = refs[:count], refs[count:]
    att_ref, attt_ref, table_ref, tablet_ref, top_ref, inv_ref, even_ref, odd_ref = refs
    fill_table(place_ref, kv_ref, kvt_ref, in_refs, table_ref, tablet_ref)
    attend_blocks(
        0, slot_ref, count_ref, qz_ref, table_ref, tablet_ref,
        att_ref, attt_ref, top_ref, inv_ref, even_ref, odd_ref,
    )


def late_forward_kernel(
    slot_ref, count_ref, qz_ref, table_ref, tablet_ref, early_attt_ref, early_top_ref, early_inv_ref,
    att_ref, attt_ref, top_ref, inv_ref, even_ref, odd_ref,
):
    half = BLK // 2
    attt_ref[:, : half * BLOCK] = early_attt_ref[...]
    top_ref[:half] = early_top_ref[...]
    inv_ref[:half] = early_inv_ref[...]
    attend_blocks(
        half, slot_ref, count_ref, qz_ref, table_ref, tablet_ref,
        att_ref, attt_ref, top_ref, inv_ref, even_ref, odd_ref,
    )


def attend_blocks(
    start, slot_ref, count_ref, qz_ref, table_ref, tablet_ref,
    att_ref, attt_ref, top_ref, inv_ref, even_ref, odd_ref,
):
    def slots_of(i):
        return [slot_ref[i, j] for j in range(PER)]

    def score(i, raw_ref):
        live = count_ref[i]
        keys = jnp.concatenate([table_ref[s] for s in slots_of(i)], axis=0)
        raw = dot_last(keys, qz_ref[span(i * BLOCK, BLOCK), :])
        top = None
        for j in range(PER):
            here = jnp.where(j < live, raw[j * BLOCK : (j + 1) * BLOCK], -1e30)
            raw_ref[j * BLOCK : (j + 1) * BLOCK, :] = here
            here = here.reshape(BLOCK // 8, 8, BLOCK)
            highest = jnp.max(here, axis=0)
            top = highest if top is None else jnp.maximum(top, highest)
        return jnp.max(top, axis=0, keepdims=True)

    def attend(i, raw_ref, top):
        total = None
        for j in range(PER):
            here = slice(j * BLOCK, (j + 1) * BLOCK)
            raised = jnp.exp2((raw_ref[here, :] - top) * SCALE_LOG2E)
            raw_ref[here, :] = raised
            part = jnp.sum(raised.reshape(BLOCK // 8, 8, BLOCK), axis=0)
            total = part if total is None else total + part
        inverse = 1.0 / jnp.sum(total, axis=0, keepdims=True)
        values = jnp.concatenate([tablet_ref[s, HD:, :] for s in slots_of(i)], axis=1)
        result = dot(values, (raw_ref[...] * inverse).astype(BF16))
        attt_ref[:, span(i * BLOCK, BLOCK)] = result.astype(BF16)
        top_ref[i] = jnp.broadcast_to(top, (8, BLOCK))
        inv_ref[i] = jnp.broadcast_to(inverse, (8, BLOCK))
        return result

    def pair(t, even_top):
        first_at = start + 2 * t
        odd_top = score(first_at + 1, odd_ref)
        first = attend(first_at, even_ref, even_top)
        even_top = score(jnp.minimum(first_at + 2, BLK - 1), even_ref)
        second = attend(first_at + 1, odd_ref, odd_top)
        both = jnp.concatenate([first, second], axis=0)
        att_ref[span(t * BLOCK, BLOCK), :] = both.T.astype(BF16)
        return even_top

    lax.fori_loop(0, PAIRS // 2, pair, score(start, even_ref))


def middle_kernel(
    place_ref, x_pair, x_other, c_pair, c_other, a_pair, a_other, attt_ref, w_ref,
    out_ref, grad_out, gz_ref, dots_ref, low_ref, wide_ref, pad_ref, grad_ref, sem,
):
    head = place_ref[0]
    rows = grad_ref.shape[0]
    grad_copy = pltpu.make_async_copy(grad_ref, grad_out, sem)
    own_w = w_ref[span(head * HD, HD), :]
    wide_ref[...] = jnp.zeros_like(wide_ref)
    for part in range(4):
        piece = w_ref[span((head ^ part) * HD, HD), :]
        at = (2 * part) * HD
        wide_ref[at : at + HD, :D] = piece
        wide_ref[at + HD : at + 2 * HD, D:] = piece
    pad_ref[:HD, :] = jnp.zeros((HD, D), BF16)
    pad_ref[HD:, :] = own_w
    a_refs = parts_of(a_pair, a_other)
    pairs = rows // (2 * BLOCK)
    for part, (x_ref, c_ref) in enumerate(zip(parts_of(x_pair, x_other), parts_of(c_pair, c_other))):
        group = head ^ part
        at = span(group * (rows // 2), rows // 2)
        lhs = jnp.concatenate([a[at, :] for a in a_refs], axis=1)
        product = dot(lhs, wide_ref[...])
        lows = []
        for i in range(2 * pairs):
            local = slice(i * BLOCK, (i + 1) * BLOCK)
            pair, half = i // 2, i % 2
            summed = x_ref[local, :].astype(F32) + product[
                pair * BLOCK : (pair + 1) * BLOCK, half * D : (half + 1) * D
            ]
            inverse = lax.rsqrt(jnp.mean(summed * summed, axis=-1, keepdims=True) + 1e-06)
            normed = summed * inverse
            upstream = c_ref[local, :].astype(F32)
            grad = (upstream - normed * jnp.mean(upstream * normed, axis=-1, keepdims=True)) * inverse
            lows.append(grad.astype(BF16))
            if part == 0:
                out_ref[local, :] = normed.astype(BF16)
                grad_ref[local, :] = grad
        if part == 0:
            grad_copy.start()
        low = jnp.concatenate(lows, axis=0)
        at = span(group * rows, rows)
        gz_ref[at, :] = dot_last(low, pad_ref[...]).astype(BF16) * jnp.asarray(SCALE, BF16)
        turned = dot_last(own_w, low).astype(BF16).astype(F32)
        attended = attt_ref[:, at]
        sums = jnp.sum(turned * attended.astype(F32), axis=0, keepdims=True) * SCALE
        for i in range(2 * pairs):
            dots_ref[group * (2 * pairs) + i] = jnp.broadcast_to(
                sums[:, i * BLOCK : (i + 1) * BLOCK], (8, BLOCK)
            )
        low_ref[at, :] = low
    grad_copy.wait()


def backward_kernel(
    count, place_ref, slot_ref, count_ref, qz_ref, gz_ref, table_ref, tablet_ref, top_ref, inv_ref, dots_ref, *refs
):
    own_ref, dqt_ref, refs = refs[0], refs[1], refs[2:]
    dq_refs, leave_refs = refs[:4], refs[4 : 4 + count]
    acc_ref, dq_ref, even_ref, odd_ref = refs[4 + count :]
    head, node = place_ref[0], place_ref[1]
    acc_ref[...] = jnp.zeros_like(acc_ref)

    def slots_of(i):
        return [slot_ref[i, j] for j in range(PER)]

    def rows_of(i):
        at = span(i * BLOCK, BLOCK)
        return jnp.concatenate([qz_ref[at, :], gz_ref[at, :]], axis=0)

    def score(i, both_ref):
        keys = jnp.concatenate([table_ref[s] for s in slots_of(i)], axis=0)
        both_ref[...] = dot_last(keys, rows_of(i))

    def spread(i, both_ref):
        slots = slots_of(i)
        live = count_ref[i]
        top = top_ref[i, :1, :]
        inverse = inv_ref[i, :1, :]
        dots = dots_ref[i, :1, :]
        weights, grads = [], []
        for j in range(PER):
            here = slice(j * BLOCK, (j + 1) * BLOCK)
            weight = jnp.exp2((both_ref[here, :BLOCK] - top) * SCALE_LOG2E) * inverse
            weight = jnp.where(j < live, weight, 0.0)
            weights.append(weight.astype(BF16))
            grads.append((weight * (both_ref[here, BLOCK:] - dots)).astype(BF16))
        score_grad = jnp.concatenate(grads, axis=0)
        low = jnp.concatenate(weights, axis=0)
        pair_grads = dot(jnp.concatenate([score_grad, low], axis=1), rows_of(i))
        for j in range(PER):
            acc_ref[slots[j]] += pair_grads[j * BLOCK : (j + 1) * BLOCK]
        turned = jnp.concatenate([tablet_ref[s, :HD, :] for s in slots], axis=1)
        result = dot(turned, score_grad)
        dqt_ref[:, span(i * BLOCK, BLOCK)] = result.astype(BF16)
        return result

    score(0, even_ref)

    @pl.loop(0, PAIRS)
    def _(t):
        score(2 * t + 1, odd_ref)
        first = spread(2 * t, even_ref)
        score(jnp.minimum(2 * t + 2, BLK - 1), even_ref)
        second = spread(2 * t + 1, odd_ref)
        both = jnp.concatenate([first, second], axis=0)
        dq_ref[span(t * BLOCK, BLOCK), :] = both.T.astype(BF16)

    lane = lax.broadcasted_iota(jnp.int32, (1, BLOCK), 1)
    unscale = jnp.where(lane < HD, 1.0, 1.0 / SCALE)
    own_ref[...] = acc_ref[:BLK] * unscale
    for step in range(count):
        other = node ^ mask_at(step, head, count)
        for c in range(CAP):
            leave_refs[step][c] = (acc_ref[BLK + other * CAP + c] * unscale).astype(BF16)
    for part in range(4):
        size = dq_refs[part].shape[0]
        dq_refs[part][...] = dq_ref[span((head ^ part) * size, size), :]


def query_weight_kernel(
    place_ref, dqt_ref, pair_ref, other_ref, in_ref, attt_ref, low_ref,
    out_ref, owg_ref, wkv_ref, wq_ref, k_ref, q_ref,
):
    owg_ref[...] = dot(attt_ref[...], low_ref[...])
    head = place_ref[0]
    rows = pair_ref.shape[0] // 2
    total = jnp.zeros((HD, D), F32)
    for part, x_ref in enumerate(parts_of(pair_ref, other_ref)):
        total += dot(dqt_ref[:, span((head ^ part) * rows, rows)], x_ref[...])
    out_ref[...] = total
    blank = jnp.zeros((D, HD), BF16)
    for g in range(HEADS):
        at = g * 3 * HD
        query = in_ref[:, at : at + HD]
        k_ref[g] = in_ref[:, at + HD : at + 3 * HD]
        q_ref[g, :D] = jnp.concatenate([query, blank], axis=1)
        q_ref[g, D:] = jnp.concatenate([blank, query], axis=1)
    for part in range(4):
        lanes = slice(part * BLOCK, (part + 1) * BLOCK)
        wkv_ref[:, lanes] = k_ref[head ^ part]
        wq_ref[:, lanes] = q_ref[head ^ part]


def collect_kernel(count, place_ref, wanted_ref, own_ref, *refs):
    back_refs, dq_refs, refs = refs[:count], refs[count : count + 4], refs[count + 4 :]
    xt_ref, owg_ref, qwg_ref, refs = *refs[:3], refs[3:]
    own_send, beside_send, across_send, piece_refs, sum_ref = *refs[:3], refs[3:7], refs[7]
    size = own_send.shape[0]
    send_refs = (own_send, beside_send, across_send.at[:size], across_send.at[size:])
    head, node = place_ref[0], place_ref[1]
    sum_ref[...] = own_ref[...]
    for step in range(count):
        other = node ^ mask_at(step, head, count)
        for c in range(CAP):
            sum_ref[wanted_ref[other, 0, c]] += back_refs[step][c].astype(F32)
    for part in range(4):
        rows = 2 * dq_refs[part].shape[0]
        first = (head ^ part) * (rows // BLOCK)
        for i in range(rows // BLOCK):
            send_refs[part][i * BLOCK : (i + 1) * BLOCK, :] = sum_ref[first + i].astype(BF16)
        send_refs[part][rows:, :] = dq_refs[part][...]
    total = jnp.zeros((D, BLOCK), F32)
    for part in range(4):
        rows = 2 * dq_refs[part].shape[0]
        total += dot(xt_ref[:, span((head ^ part) * rows, rows)], send_refs[part][:rows, :])
    every = jnp.concatenate([owg_ref[...], qwg_ref[...], total.T], axis=0)
    split(every, group_of(node, top_shift(count)), head, piece_refs)


def relay_kernel(beside_ref, across_ref, after_ref, out_ref):
    size = beside_ref.shape[0]
    out_ref[:size, :] = beside_ref[...]
    out_ref[size:, :] = across_ref[size:, :]


def finish_kernel(grad_from, own_ref, beside_ref, across_ref, wq_ref, wkv_ref, out_ref, done_ref, grad_ref, sem):
    done_ref[...] = jnp.zeros_like(done_ref)
    grad_copy = pltpu.make_async_copy(grad_from, grad_ref, sem)
    grad_copy.start()
    rows = out_ref.shape[0]
    size = own_ref.shape[0]
    s_refs = (own_ref, beside_ref.at[:size], across_ref.at[:size], beside_ref.at[size:])
    kv = jnp.concatenate([s[:rows, :] for s in s_refs], axis=1)
    base = dot_last(kv, wkv_ref[...])
    lhs = jnp.concatenate([s[rows:, :] for s in s_refs], axis=1)
    product = dot_last(lhs, wq_ref[...])
    grad_copy.wait()
    for i in range(rows // BLOCK):
        at = slice(i * BLOCK, (i + 1) * BLOCK)
        pack = slice(i // 2 * BLOCK, (i // 2 + 1) * BLOCK)
        half = i % 2
        out_ref[at, :] = (
            grad_ref[at, :] + base[at] + product[pack, half * D : (half + 1) * D]
        ).astype(BF16)


def on_device(features, in_weight, out_weight, cotangent, key_slots, block_count, wanted):
    head_count = lax.axis_size("head")
    node_count = lax.axis_size("node")
    rows = features.shape[0]
    node_rows = rows * head_count
    total_nodes = node_rows * node_count
    table_size = BLK + node_count * CAP
    limit = (14 + table_size // 4) * MIB
    place = jnp.stack([lax.axis_index("head"), lax.axis_index("node")]).astype(jnp.int32)
    block_set = (CAP, BLOCK, BLOCK)

    def swap(value, axis, mask):
        size = lax.axis_size(axis)
        return lax.ppermute(value, axis, [(i, i ^ mask) for i in range(size)])

    def pair_up(values, after=()):
        rows, width = values[0].shape
        (pair,) = call(
            functools.partial(pair_kernel, len(values)),
            "pair",
            [((len(values) * rows, width), values[0].dtype)],
            [vmem()] * (len(values) + len(after)),
            4 * MIB,
        )(*values, *after)
        return pair, swap(pair, "head", 1)

    def exchange_nodes(pieces, masks, unit=1):
        moved = list(pieces)
        for step in range(1, len(pieces)):
            perm = [
                (n * head_count + h, (n ^ (masks[h & 1][step] * unit)) * head_count + h)
                for n in range(node_count)
                for h in range(head_count)
            ]
            moved[step] = lax.ppermute(pieces[step], ("node", "head"), perm)
        return moved

    def add_nodes(pieces, shift, factor, after=()):
        moved = exchange_nodes(pieces, PIECE_STEPS, 1 << shift)
        piece = (pieces[0].shape, F32)
        (total,) = call(
            functools.partial(sum_kernel, factor),
            "sum",
            [piece],
            [vmem()] * (4 + len(after)),
            4 * MIB,
        )(*moved, *after)
        if shift == 1:
            total = total + swap(total, "node", 1)
        elif shift > 1:
            lower = call(
                functools.partial(split_kernel, shift - 2),
                "split",
                [((piece[0][0] // 4, D), F32)] * 4,
                [smem(), vmem()],
                limit,
            )(place, total)
            (total,) = call(
                functools.partial(join_kernel, shift - 2),
                "join",
                [piece],
                [smem()] + [vmem()] * 4,
                limit,
            )(place, *add_nodes(lower, shift - 2, 1.0)[0])
        total = total.astype(pieces[0].dtype)
        return exchange_nodes([total] * 4, PIECE_STEPS, 1 << shift), total

    across = swap(features, "head", 2)
    c_across = swap(cotangent, "head", 2)
    wants = lax.all_to_all(
        wanted.reshape(node_count, 1, CAP), "node", split_axis=0, concat_axis=0, tiled=True
    )
    xs = pair_up([features, across], [wants])
    qz, kv, *outgoing = call(
        functools.partial(project_kernel, node_count),
        "project",
        [((node_rows, BLOCK), BF16)] * 2 + [(block_set, BF16)] * node_count,
        [smem()] * 2 + [vmem()] * 3,
        limit,
        flops=2 * node_rows * D * D,
        scratch=[pltpu.VMEM((D, D), BF16)],
    )(place, wants, *xs, in_weight)
    incoming = exchange_nodes(outgoing, step_masks(node_count))
    xt, kvt = call(
        prepare_kernel,
        "prepare",
        [((D, node_rows), BF16), ((BLK, BLOCK, BLOCK), BF16)],
        [smem()] * 3 + [vmem()] * 4,
        limit,
        flops=2 * node_rows * D * D,
    )(place, key_slots, block_count, *xs, kv, c_across)
    half = BLK // 2
    half_att = ((half * BLOCK // 2, BLOCK), BF16)
    early_att, early_attt, table, tablet, early_top, early_inv = call(
        functools.partial(early_forward_kernel, node_count),
        "early_forward",
        [
            half_att,
            ((HD, half * BLOCK), BF16),
            ((table_size, BLOCK, BLOCK), BF16),
            ((table_size, BLOCK, BLOCK), BF16),
            ((half, 8, BLOCK), F32),
            ((half, 8, BLOCK), F32),
        ],
        [smem()] * 3 + [vmem()] * (3 + node_count),
        limit,
        flops=2 * node_rows * PER * BLOCK * BLOCK,
        scratch=[pltpu.VMEM((PER * BLOCK, BLOCK), F32)] * 2,
    )(place, key_slots, block_count, qz, kv, kvt, *incoming)
    early_across = swap(early_att, "head", 2)
    late_att, attt, top, inv = call(
        late_forward_kernel,
        "late_forward",
        [
            half_att,
            ((HD, node_rows), BF16),
            ((BLK, 8, BLOCK), F32),
            ((BLK, 8, BLOCK), F32),
        ],
        [smem()] * 2 + [vmem()] * 6,
        limit,
        flops=2 * node_rows * PER * BLOCK * BLOCK,
        scratch=[pltpu.VMEM((PER * BLOCK, BLOCK), F32)] * 2,
    )(key_slots, block_count, qz, table, tablet, early_attt, early_top, early_inv)
    late_across = swap(late_att, "head", 2)
    parts = pair_up([early_att, late_att, early_across, late_across])
    cs = pair_up([cotangent, c_across], [top])
    output, norm_grad, gz, dots, low = call(
        middle_kernel,
        "middle",
        [
            ((rows, D), BF16),
            ((rows, D), F32),
            ((node_rows, BLOCK), BF16),
            ((BLK, 8, BLOCK), F32),
            ((node_rows, D), BF16),
        ],
        [smem()] + [vmem()] * 8,
        limit,
        flops=8 * node_rows * D * D,
        scratch=[
            pltpu.VMEM((2 * D, 2 * D), BF16),
            pltpu.VMEM((BLOCK, D), BF16),
            pltpu.VMEM((rows, D), F32),
            pltpu.SemaphoreType.DMA,
        ],
        out_specs=[vmem(), hbm()] + [vmem()] * 3,
    )(place, *xs, *cs, *parts, attt, out_weight)
    own, dqt, *rest = call(
        functools.partial(backward_kernel, node_count),
        "backward",
        [((BLK, BLOCK, BLOCK), F32), ((HD, node_rows), BF16)]
        + [((rows // 2, BLOCK), BF16)] * 4
        + [(block_set, BF16)] * node_count,
        [smem()] * 3 + [vmem()] * 7,
        limit,
        flops=10 * node_rows * PER * BLOCK * BLOCK,
        scratch=[
            pltpu.VMEM((table_size, BLOCK, BLOCK), F32),
            pltpu.VMEM((PAIRS * BLOCK, BLOCK), BF16),
            pltpu.VMEM((PER * BLOCK, 2 * BLOCK), F32),
            pltpu.VMEM((PER * BLOCK, 2 * BLOCK), F32),
        ],
    )(place, key_slots, block_count, qz, gz, table, tablet, top, inv, dots)
    returned = exchange_nodes(rest[4:], step_masks(node_count))
    query_wg, owg, wkv, wq = call(
        query_weight_kernel,
        "query_weight",
        [((HD, D), F32)] * 2 + [((D, 2 * D), BF16), ((2 * D, 2 * D), BF16)],
        [smem()] + [vmem()] * 6,
        limit,
        flops=2 * node_rows * D * HD,
        scratch=[pltpu.VMEM((HEADS, D, BLOCK), BF16), pltpu.VMEM((HEADS, 2 * D, BLOCK), BF16)],
    )(place, dqt, *xs, in_weight, attt, low)
    sent = ((rows * 3 // 2, BLOCK), BF16)
    collected = call(
        functools.partial(collect_kernel, node_count),
        "collect",
        [sent, sent, ((rows * 3, BLOCK), BF16)] + [((HD, D), BF16)] * 4,
        [smem()] * 2 + [vmem()] * (8 + node_count),
        limit,
        flops=2 * node_rows * D * BLOCK,
        scratch=[pltpu.VMEM((BLK, BLOCK, BLOCK), F32)],
    )(place, wants, own, *returned, *rest[:4], xt, owg, query_wg)
    own_send, beside_send, across_send = collected[:3]
    across = swap(across_send, "head", 2)
    shift = top_shift(node_count)
    factor = total_nodes ** (-0.5)
    late, summed = add_nodes(collected[3:], shift, factor)
    (relay,) = call(
        relay_kernel, "relay", [((rows * 3, BLOCK), BF16)], [vmem()] * 3, 4 * MIB
    )(beside_send, across, summed)
    beside = swap(relay, "head", 1)
    feature_grad, finished = call(
        finish_kernel,
        "finish",
        [((rows, D), BF16), ((8, BLOCK), F32)],
        [hbm()] + [vmem()] * 5,
        limit,
        flops=4 * rows * 3 * D * D,
        scratch=[pltpu.VMEM((rows, D), F32), pltpu.SemaphoreType.DMA],
    )(norm_grad, own_send, beside, across, wq, wkv)
    in_grad, out_grad = call(
        functools.partial(result_kernel, shift),
        "result",
        [((3 * HD, D), F32), ((HD, D), F32)],
        [smem()] + [vmem()] * 5,
        limit,
    )(place, *late, finished)
    return (output, feature_grad, in_grad.T, out_grad)


def solution(mesh):
    placed = (
        P(("node", "head"), None),
        P(),
        P(),
        P(("node", "head"), None),
        P("node", None),
        P("node"),
        P("node", None, None),
    )
    return jax.shard_map(
        on_device,
        mesh=mesh,
        in_specs=placed,
        out_specs=(
            P(("node", "head"), None),
            P(("node", "head"), None),
            P(None, "head"),
            P("head", None),
        ),
        check_vma=False,
    )
```

```python
import functools
import math

import jax
import jax.numpy as jnp
from jax import lax
from jax.experimental import pallas as pl
from jax.experimental.pallas import tpu as pltpu
from jax.sharding import PartitionSpec as P

HEADS = 4
HD = 64
BLOCK = 128
BLK = 16
PER = 12
CAP = 2
D = 256
PAIRS = BLK // 2
SCALE = HD ** (-0.5)
SCALE_LOG2E = SCALE * math.log2(math.e)
BF16 = jnp.bfloat16
F32 = jnp.float32
MIB = 1 << 20
LAST = (((1,), (1,)), ((), ()))


def dot(a, b):
    return jnp.dot(a, b, preferred_element_type=F32)


def dot_last(a, b):
    return lax.dot_general(a, b, LAST, preferred_element_type=F32)


def span(start, size):
    return pl.ds(pl.multiple_of(start, size), size)


def smem():
    return pl.BlockSpec(memory_space=pltpu.SMEM)


def vmem():
    return pl.BlockSpec(memory_space=pltpu.VMEM)


def hbm():
    return pl.BlockSpec(memory_space=pltpu.HBM)


def call(kernel, name, outs, in_specs, limit, flops=0, scratch=(), out_specs=None):
    return pl.pallas_call(
        kernel,
        name=name,
        out_shape=tuple(jax.ShapeDtypeStruct(shape, kind) for shape, kind in outs),
        in_specs=in_specs,
        out_specs=tuple(out_specs or [vmem() for _ in outs]),
        scratch_shapes=scratch,
        compiler_params=pltpu.CompilerParams(vmem_limit_bytes=limit),
        cost_estimate=pl.CostEstimate(flops=flops, bytes_accessed=4 * MIB, transcendentals=0),
    )


def top_shift(count):
    return count.bit_length() - 3


def group_of(node, shift):
    return (node >> shift) & 3


PIECE_STEPS = ((0, 3, 2, 1), (0, 3, 2, 1))


def piece_at(group, step, head):
    return group ^ jnp.where((head & 1) == 1, PIECE_STEPS[1][step], PIECE_STEPS[0][step])


def split(value, group, head, piece_refs):
    size = value.shape[0] // 4
    for g in range(4):
        for step in range(4):

            @pl.when(piece_at(group, step, head) == g)
            def _():
                piece_refs[step][...] = value[g * size : (g + 1) * size, :].astype(piece_refs[step].dtype)


def split_kernel(shift, place_ref, value_ref, *piece_refs):
    split(value_ref[...], group_of(place_ref[1], shift), place_ref[0], piece_refs)


def join(piece_refs, group, head, g):
    value = piece_refs[0][...]
    for step in range(1, 4):
        value = jnp.where(piece_at(group, step, head) == g, piece_refs[step][...], value)
    return value


def join_kernel(shift, place_ref, p0, p1, p2, p3, out_ref):
    head, group = place_ref[0], group_of(place_ref[1], shift)
    out_ref[...] = jnp.concatenate([join((p0, p1, p2, p3), group, head, g) for g in range(4)], axis=0)


def sum_kernel(factor, *refs):
    out_ref = refs[-1]
    values = [ref[...].astype(F32) for ref in refs[:4]]
    out_ref[...] = ((values[0] + values[1]) + (values[2] + values[3])) * factor


def result_kernel(shift, place_ref, l0, l3, l2, l1, after_ref, in_ref, out_ref):
    head, group = place_ref[0], group_of(place_ref[1], shift)
    for step, piece_ref in enumerate((l0, l1, l2, l3)):
        at = piece_at(group, step, head)

        @pl.when(at == 0)
        def _():
            out_ref[...] = piece_ref[...].astype(F32)

        @pl.when(at > 0)
        def _():
            in_ref[span((at - 1) * HD, HD), :] = piece_ref[...].astype(F32)


def pair_kernel(count, *refs):
    out_ref = refs[-1]
    rows = refs[0].shape[0]
    for i in range(count):
        out_ref[i * rows : (i + 1) * rows, :] = refs[i][...]


def parts_of(pair_ref, other_ref):
    rows = pair_ref.shape[0] // 2
    return (pair_ref.at[:rows], other_ref.at[:rows], pair_ref.at[rows:], other_ref.at[rows:])


def step_masks(count):
    near, far = list(range(count // 2 - 1, 0, -1)), list(range(count - 1, count // 2 - 1, -1))
    return [0] + far + near, [0] + near + far


def mask_at(step, head, count):
    even, odd = step_masks(count)
    return jnp.where((head & 1) == 1, odd[step], even[step])


def project_kernel(count, place_ref, wanted_ref, pair_ref, other_ref, in_ref, *refs):
    qz_ref, kv_ref, refs = refs[0], refs[1], refs[2:]
    out_refs, wide_ref = refs[:count], refs[count]
    x_refs = parts_of(pair_ref, other_ref)
    head, node = place_ref[0], place_ref[1]
    rows = x_refs[0].shape[0]
    wide_ref[:, HD:BLOCK] = jnp.zeros((D, HD), BF16)
    for g in range(HEADS):

        @pl.when(head == g)
        def _():
            at = g * 3 * HD
            wide_ref[:, :HD] = in_ref[:, at : at + HD]
            wide_ref[:, BLOCK:] = in_ref[:, at + HD : at + 3 * HD]

    for part in range(4):
        at = span((head ^ part) * rows, rows)
        y = dot(x_refs[part][...], wide_ref[...]).astype(BF16)
        qz_ref[at, :] = y[:, :BLOCK]
        kv_ref[at, :] = y[:, BLOCK:]
    for step in range(count):
        other = node ^ mask_at(step, head, count)
        for c in range(CAP):
            block = wanted_ref[other, 0, c]
            out_refs[step][c] = kv_ref[span(block * BLOCK, BLOCK), :]


def prepare_kernel(place_ref, slot_ref, count_ref, pair_ref, other_ref, kv_ref, after_ref, xt_ref, kvt_ref):
    head = place_ref[0]
    rows = pair_ref.shape[0] // 2
    for part, x_ref in enumerate(parts_of(pair_ref, other_ref)):
        xt_ref[:, span((head ^ part) * rows, rows)] = x_ref[...].T
    for i in range(BLK):
        kvt_ref[i] = kv_ref[i * BLOCK : (i + 1) * BLOCK, :].T


def fill_table(place_ref, kv_ref, kvt_ref, in_refs, table_ref, tablet_ref):
    head, node = place_ref[0], place_ref[1]
    for i in range(BLK):
        table_ref[i] = kv_ref[i * BLOCK : (i + 1) * BLOCK, :]
        tablet_ref[i] = kvt_ref[i]
    for step, in_ref in enumerate(in_refs):
        other = node ^ mask_at(step, head, len(in_refs))
        for c in range(CAP):
            block = in_ref[c]
            at = BLK + other * CAP + c
            table_ref[at] = block
            tablet_ref[at] = block.T


def early_forward_kernel(count, place_ref, slot_ref, count_ref, qz_ref, kv_ref, kvt_ref, *refs):
    in_refs, refs = refs[:count], refs[count:]
    att_ref, attt_ref, table_ref, tablet_ref, top_ref, inv_ref, even_ref, odd_ref = refs
    fill_table(place_ref, kv_ref, kvt_ref, in_refs, table_ref, tablet_ref)
    attend_blocks(
        0, slot_ref, count_ref, qz_ref, table_ref, tablet_ref,
        att_ref, attt_ref, top_ref, inv_ref, even_ref, odd_ref,
    )


def late_forward_kernel(
    slot_ref, count_ref, qz_ref, table_ref, tablet_ref, early_attt_ref, early_top_ref, early_inv_ref,
    att_ref, attt_ref, top_ref, inv_ref, even_ref, odd_ref,
):
    half = BLK // 2
    attt_ref[:, : half * BLOCK] = early_attt_ref[...]
    top_ref[:half] = early_top_ref[...]
    inv_ref[:half] = early_inv_ref[...]
    attend_blocks(
        half, slot_ref, count_ref, qz_ref, table_ref, tablet_ref,
        att_ref, attt_ref, top_ref, inv_ref, even_ref, odd_ref,
    )


def attend_blocks(
    start, slot_ref, count_ref, qz_ref, table_ref, tablet_ref,
    att_ref, attt_ref, top_ref, inv_ref, even_ref, odd_ref,
):
    def slots_of(i):
        return [slot_ref[i, j] for j in range(PER)]

    def score(i, raw_ref):
        live = count_ref[i]
        keys = jnp.concatenate([table_ref[s] for s in slots_of(i)], axis=0)
        raw = dot_last(keys, qz_ref[span(i * BLOCK, BLOCK), :])
        top = None
        for j in range(PER):
            here = jnp.where(j < live, raw[j * BLOCK : (j + 1) * BLOCK], -1e30)
            raw_ref[j * BLOCK : (j + 1) * BLOCK, :] = here
            here = here.reshape(BLOCK // 8, 8, BLOCK)
            highest = jnp.max(here, axis=0)
            top = highest if top is None else jnp.maximum(top, highest)
        return jnp.max(top, axis=0, keepdims=True)

    def attend(i, raw_ref, top):
        total = None
        for j in range(PER):
            here = slice(j * BLOCK, (j + 1) * BLOCK)
            raised = jnp.exp2((raw_ref[here, :] - top) * SCALE_LOG2E)
            raw_ref[here, :] = raised
            part = jnp.sum(raised.reshape(BLOCK // 8, 8, BLOCK), axis=0)
            total = part if total is None else total + part
        inverse = 1.0 / jnp.sum(total, axis=0, keepdims=True)
        values = jnp.concatenate([tablet_ref[s, HD:, :] for s in slots_of(i)], axis=1)
        result = dot(values, (raw_ref[...] * inverse).astype(BF16))
        attt_ref[:, span(i * BLOCK, BLOCK)] = result.astype(BF16)
        top_ref[i] = jnp.broadcast_to(top, (8, BLOCK))
        inv_ref[i] = jnp.broadcast_to(inverse, (8, BLOCK))
        return result

    def pair(t, even_top):
        first_at = start + 2 * t
        odd_top = score(first_at + 1, odd_ref)
        first = attend(first_at, even_ref, even_top)
        even_top = score(jnp.minimum(first_at + 2, BLK - 1), even_ref)
        second = attend(first_at + 1, odd_ref, odd_top)
        both = jnp.concatenate([first, second], axis=0)
        att_ref[span(t * BLOCK, BLOCK), :] = both.T.astype(BF16)
        return even_top

    lax.fori_loop(0, PAIRS // 2, pair, score(start, even_ref))


def middle_kernel(
    place_ref, x_pair, x_other, c_pair, c_other, a_pair, a_other, attt_ref, w_ref,
    out_ref, grad_out, gz_ref, dots_ref, low_ref, wide_ref, pad_ref, grad_ref, sem,
):
    head = place_ref[0]
    rows = grad_ref.shape[0]
    grad_copy = pltpu.make_async_copy(grad_ref, grad_out, sem)
    own_w = w_ref[span(head * HD, HD), :]
    wide_ref[...] = jnp.zeros_like(wide_ref)
    for part in range(4):
        piece = w_ref[span((head ^ part) * HD, HD), :]
        at = (2 * part) * HD
        wide_ref[at : at + HD, :D] = piece
        wide_ref[at + HD : at + 2 * HD, D:] = piece
    pad_ref[:HD, :] = jnp.zeros((HD, D), BF16)
    pad_ref[HD:, :] = own_w
    a_refs = parts_of(a_pair, a_other)
    pairs = rows // (2 * BLOCK)
    for part, (x_ref, c_ref) in enumerate(zip(parts_of(x_pair, x_other), parts_of(c_pair, c_other))):
        group = head ^ part
        at = span(group * (rows // 2), rows // 2)
        lhs = jnp.concatenate([a[at, :] for a in a_refs], axis=1)
        product = dot(lhs, wide_ref[...])
        lows = []
        for i in range(2 * pairs):
            local = slice(i * BLOCK, (i + 1) * BLOCK)
            pair, half = i // 2, i % 2
            summed = x_ref[local, :].astype(F32) + product[
                pair * BLOCK : (pair + 1) * BLOCK, half * D : (half + 1) * D
            ]
            inverse = lax.rsqrt(jnp.mean(summed * summed, axis=-1, keepdims=True) + 1e-06)
            normed = summed * inverse
            upstream = c_ref[local, :].astype(F32)
            grad = (upstream - normed * jnp.mean(upstream * normed, axis=-1, keepdims=True)) * inverse
            lows.append(grad.astype(BF16))
            if part == 0:
                out_ref[local, :] = normed.astype(BF16)
                grad_ref[local, :] = grad
        if part == 0:
            grad_copy.start()
        low = jnp.concatenate(lows, axis=0)
        at = span(group * rows, rows)
        gz_ref[at, :] = dot_last(low, pad_ref[...]).astype(BF16) * jnp.asarray(SCALE, BF16)
        turned = dot_last(own_w, low).astype(BF16).astype(F32)
        attended = attt_ref[:, at]
        sums = jnp.sum(turned * attended.astype(F32), axis=0, keepdims=True) * SCALE
        for i in range(2 * pairs):
            dots_ref[group * (2 * pairs) + i] = jnp.broadcast_to(
                sums[:, i * BLOCK : (i + 1) * BLOCK], (8, BLOCK)
            )
        low_ref[at, :] = low
    grad_copy.wait()


def backward_kernel(
    count, place_ref, slot_ref, count_ref, qz_ref, gz_ref, table_ref, tablet_ref, top_ref, inv_ref, dots_ref, *refs
):
    own_ref, dqt_ref, refs = refs[0], refs[1], refs[2:]
    dq_refs, leave_refs = refs[:4], refs[4 : 4 + count]
    acc_ref, dq_ref, even_ref, odd_ref = refs[4 + count :]
    head, node = place_ref[0], place_ref[1]
    acc_ref[...] = jnp.zeros_like(acc_ref)

    def slots_of(i):
        return [slot_ref[i, j] for j in range(PER)]

    def rows_of(i):
        at = span(i * BLOCK, BLOCK)
        return jnp.concatenate([qz_ref[at, :], gz_ref[at, :]], axis=0)

    def score(i, both_ref):
        keys = jnp.concatenate([table_ref[s] for s in slots_of(i)], axis=0)
        both_ref[...] = dot_last(keys, rows_of(i))

    def spread(i, both_ref):
        slots = slots_of(i)
        live = count_ref[i]
        top = top_ref[i, :1, :]
        inverse = inv_ref[i, :1, :]
        dots = dots_ref[i, :1, :]
        weights, grads = [], []
        for j in range(PER):
            here = slice(j * BLOCK, (j + 1) * BLOCK)
            weight = jnp.exp2((both_ref[here, :BLOCK] - top) * SCALE_LOG2E) * inverse
            weight = jnp.where(j < live, weight, 0.0)
            weights.append(weight.astype(BF16))
            grads.append((weight * (both_ref[here, BLOCK:] - dots)).astype(BF16))
        score_grad = jnp.concatenate(grads, axis=0)
        low = jnp.concatenate(weights, axis=0)
        pair_grads = dot(jnp.concatenate([score_grad, low], axis=1), rows_of(i))
        for j in range(PER):
            acc_ref[slots[j]] += pair_grads[j * BLOCK : (j + 1) * BLOCK]
        turned = jnp.concatenate([tablet_ref[s, :HD, :] for s in slots], axis=1)
        result = dot(turned, score_grad)
        dqt_ref[:, span(i * BLOCK, BLOCK)] = result.astype(BF16)
        return result

    score(0, even_ref)

    @pl.loop(0, PAIRS)
    def _(t):
        score(2 * t + 1, odd_ref)
        first = spread(2 * t, even_ref)
        score(jnp.minimum(2 * t + 2, BLK - 1), even_ref)
        second = spread(2 * t + 1, odd_ref)
        both = jnp.concatenate([first, second], axis=0)
        dq_ref[span(t * BLOCK, BLOCK), :] = both.T.astype(BF16)

    lane = lax.broadcasted_iota(jnp.int32, (1, BLOCK), 1)
    unscale = jnp.where(lane < HD, 1.0, 1.0 / SCALE)
    own_ref[...] = acc_ref[:BLK] * unscale
    for step in range(count):
        other = node ^ mask_at(step, head, count)
        for c in range(CAP):
            leave_refs[step][c] = (acc_ref[BLK + other * CAP + c] * unscale).astype(BF16)
    for part in range(4):
        size = dq_refs[part].shape[0]
        dq_refs[part][...] = dq_ref[span((head ^ part) * size, size), :]


def query_weight_kernel(
    place_ref, dqt_ref, pair_ref, other_ref, in_ref, attt_ref, low_ref,
    out_ref, owg_ref, wkv_ref, wq_ref, k_ref, q_ref,
):
    owg_ref[...] = dot(attt_ref[...], low_ref[...])
    head = place_ref[0]
    rows = pair_ref.shape[0] // 2
    total = jnp.zeros((HD, D), F32)
    for part, x_ref in enumerate(parts_of(pair_ref, other_ref)):
        total += dot(dqt_ref[:, span((head ^ part) * rows, rows)], x_ref[...])
    out_ref[...] = total
    blank = jnp.zeros((D, HD), BF16)
    for g in range(HEADS):
        at = g * 3 * HD
        query = in_ref[:, at : at + HD]
        k_ref[g] = in_ref[:, at + HD : at + 3 * HD]
        q_ref[g, :D] = jnp.concatenate([query, blank], axis=1)
        q_ref[g, D:] = jnp.concatenate([blank, query], axis=1)
    for part in range(4):
        lanes = slice(part * BLOCK, (part + 1) * BLOCK)
        wkv_ref[:, lanes] = k_ref[head ^ part]
        wq_ref[:, lanes] = q_ref[head ^ part]


def collect_kernel(count, place_ref, wanted_ref, own_ref, *refs):
    back_refs, dq_refs, refs = refs[:count], refs[count : count + 4], refs[count + 4 :]
    xt_ref, owg_ref, qwg_ref, refs = *refs[:3], refs[3:]
    own_send, beside_send, across_send, piece_refs, sum_ref = *refs[:3], refs[3:7], refs[7]
    size = own_send.shape[0]
    send_refs = (own_send, beside_send, across_send.at[:size], across_send.at[size:])
    head, node = place_ref[0], place_ref[1]
    sum_ref[...] = own_ref[...]
    for step in range(count):
        other = node ^ mask_at(step, head, count)
        for c in range(CAP):
            sum_ref[wanted_ref[other, 0, c]] += back_refs[step][c].astype(F32)
    for part in range(4):
        rows = 2 * dq_refs[part].shape[0]
        first = (head ^ part) * (rows // BLOCK)
        for i in range(rows // BLOCK):
            send_refs[part][i * BLOCK : (i + 1) * BLOCK, :] = sum_ref[first + i].astype(BF16)
        send_refs[part][rows:, :] = dq_refs[part][...]
    total = jnp.zeros((D, BLOCK), F32)
    for part in range(4):
        rows = 2 * dq_refs[part].shape[0]
        total += dot(xt_ref[:, span((head ^ part) * rows, rows)], send_refs[part][:rows, :])
    every = jnp.concatenate([owg_ref[...], qwg_ref[...], total.T], axis=0)
    split(every, group_of(node, top_shift(count)), head, piece_refs)


def relay_kernel(beside_ref, across_ref, after_ref, out_ref):
    size = beside_ref.shape[0]
    out_ref[:size, :] = beside_ref[...]
    out_ref[size:, :] = across_ref[size:, :]


def finish_kernel(grad_from, own_ref, beside_ref, across_ref, wq_ref, wkv_ref, out_ref, done_ref, grad_ref, sem):
    done_ref[...] = jnp.zeros_like(done_ref)
    grad_copy = pltpu.make_async_copy(grad_from, grad_ref, sem)
    grad_copy.start()
    rows = out_ref.shape[0]
    size = own_ref.shape[0]
    s_refs = (own_ref, beside_ref.at[:size], across_ref.at[:size], beside_ref.at[size:])
    kv = jnp.concatenate([s[:rows, :] for s in s_refs], axis=1)
    base = dot_last(kv, wkv_ref[...])
    lhs = jnp.concatenate([s[rows:, :] for s in s_refs], axis=1)
    product = dot_last(lhs, wq_ref[...])
    grad_copy.wait()
    for i in range(rows // BLOCK):
        at = slice(i * BLOCK, (i + 1) * BLOCK)
        pack = slice(i // 2 * BLOCK, (i // 2 + 1) * BLOCK)
        half = i % 2
        out_ref[at, :] = (
            grad_ref[at, :] + base[at] + product[pack, half * D : (half + 1) * D]
        ).astype(BF16)


def on_device(features, in_weight, out_weight, cotangent, key_slots, block_count, wanted):
    head_count = lax.axis_size("head")
    node_count = lax.axis_size("node")
    rows = features.shape[0]
    node_rows = rows * head_count
    total_nodes = node_rows * node_count
    table_size = BLK + node_count * CAP
    limit = (14 + table_size // 4) * MIB
    place = jnp.stack([lax.axis_index("head"), lax.axis_index("node")]).astype(jnp.int32)
    block_set = (CAP, BLOCK, BLOCK)

    def swap(value, axis, mask):
        size = lax.axis_size(axis)
        return lax.ppermute(value, axis, [(i, i ^ mask) for i in range(size)])

    def pair_up(values, after=()):
        rows, width = values[0].shape
        (pair,) = call(
            functools.partial(pair_kernel, len(values)),
            "pair",
            [((len(values) * rows, width), values[0].dtype)],
            [vmem()] * (len(values) + len(after)),
            4 * MIB,
        )(*values, *after)
        return pair, swap(pair, "head", 1)

    def exchange_nodes(pieces, masks, unit=1):
        moved = list(pieces)
        for step in range(1, len(pieces)):
            perm = [
                (n * head_count + h, (n ^ (masks[h & 1][step] * unit)) * head_count + h)
                for n in range(node_count)
                for h in range(head_count)
            ]
            moved[step] = lax.ppermute(pieces[step], ("node", "head"), perm)
        return moved

    def add_nodes(pieces, shift, factor, after=()):
        moved = exchange_nodes(pieces, PIECE_STEPS, 1 << shift)
        piece = (pieces[0].shape, F32)
        (total,) = call(
            functools.partial(sum_kernel, factor),
            "sum",
            [piece],
            [vmem()] * (4 + len(after)),
            4 * MIB,
        )(*moved, *after)
        if shift == 1:
            total = total + swap(total, "node", 1)
        elif shift > 1:
            lower = call(
                functools.partial(split_kernel, shift - 2),
                "split",
                [((piece[0][0] // 4, D), F32)] * 4,
                [smem(), vmem()],
                limit,
            )(place, total)
            (total,) = call(
                functools.partial(join_kernel, shift - 2),
                "join",
                [piece],
                [smem()] + [vmem()] * 4,
                limit,
            )(place, *add_nodes(lower, shift - 2, 1.0)[0])
        total = total.astype(pieces[0].dtype)
        return exchange_nodes([total] * 4, PIECE_STEPS, 1 << shift), total

    across = swap(features, "head", 2)
    c_across = swap(cotangent, "head", 2)
    wants = lax.all_to_all(
        wanted.reshape(node_count, 1, CAP), "node", split_axis=0, concat_axis=0, tiled=True
    )
    xs = pair_up([features, across], [wants])
    qz, kv, *outgoing = call(
        functools.partial(project_kernel, node_count),
        "project",
        [((node_rows, BLOCK), BF16)] * 2 + [(block_set, BF16)] * node_count,
        [smem()] * 2 + [vmem()] * 3,
        limit,
        flops=2 * node_rows * D * D,
        scratch=[pltpu.VMEM((D, D), BF16)],
    )(place, wants, *xs, in_weight)
    incoming = exchange_nodes(outgoing, step_masks(node_count))
    xt, kvt = call(
        prepare_kernel,
        "prepare",
        [((D, node_rows), BF16), ((BLK, BLOCK, BLOCK), BF16)],
        [smem()] * 3 + [vmem()] * 4,
        limit,
        flops=2 * node_rows * D * D,
    )(place, key_slots, block_count, *xs, kv, c_across)
    half = BLK // 2
    half_att = ((half * BLOCK // 2, BLOCK), BF16)
    early_att, early_attt, table, tablet, early_top, early_inv = call(
        functools.partial(early_forward_kernel, node_count),
        "early_forward",
        [
            half_att,
            ((HD, half * BLOCK), BF16),
            ((table_size, BLOCK, BLOCK), BF16),
            ((table_size, BLOCK, BLOCK), BF16),
            ((half, 8, BLOCK), F32),
            ((half, 8, BLOCK), F32),
        ],
        [smem()] * 3 + [vmem()] * (3 + node_count),
        limit,
        flops=2 * node_rows * PER * BLOCK * BLOCK,
        scratch=[pltpu.VMEM((PER * BLOCK, BLOCK), F32)] * 2,
    )(place, key_slots, block_count, qz, kv, kvt, *incoming)
    early_across = swap(early_att, "head", 2)
    late_att, attt, top, inv = call(
        late_forward_kernel,
        "late_forward",
        [
            half_att,
            ((HD, node_rows), BF16),
            ((BLK, 8, BLOCK), F32),
            ((BLK, 8, BLOCK), F32),
        ],
        [smem()] * 2 + [vmem()] * 6,
        limit,
        flops=2 * node_rows * PER * BLOCK * BLOCK,
        scratch=[pltpu.VMEM((PER * BLOCK, BLOCK), F32)] * 2,
    )(key_slots, block_count, qz, table, tablet, early_attt, early_top, early_inv)
    late_across = swap(late_att, "head", 2)
    parts = pair_up([early_att, late_att, early_across, late_across])
    cs = pair_up([cotangent, c_across], [top])
    output, norm_grad, gz, dots, low = call(
        middle_kernel,
        "middle",
        [
            ((rows, D), BF16),
            ((rows, D), F32),
            ((node_rows, BLOCK), BF16),
            ((BLK, 8, BLOCK), F32),
            ((node_rows, D), BF16),
        ],
        [smem()] + [vmem()] * 8,
        limit,
        flops=8 * node_rows * D * D,
        scratch=[
            pltpu.VMEM((2 * D, 2 * D), BF16),
            pltpu.VMEM((BLOCK, D), BF16),
            pltpu.VMEM((rows, D), F32),
            pltpu.SemaphoreType.DMA,
        ],
        out_specs=[vmem(), hbm()] + [vmem()] * 3,
    )(place, *xs, *cs, *parts, attt, out_weight)
    own, dqt, *rest = call(
        functools.partial(backward_kernel, node_count),
        "backward",
        [((BLK, BLOCK, BLOCK), F32), ((HD, node_rows), BF16)]
        + [((rows // 2, BLOCK), BF16)] * 4
        + [(block_set, BF16)] * node_count,
        [smem()] * 3 + [vmem()] * 7,
        limit,
        flops=10 * node_rows * PER * BLOCK * BLOCK,
        scratch=[
            pltpu.VMEM((table_size, BLOCK, BLOCK), F32),
            pltpu.VMEM((PAIRS * BLOCK, BLOCK), BF16),
            pltpu.VMEM((PER * BLOCK, 2 * BLOCK), F32),
            pltpu.VMEM((PER * BLOCK, 2 * BLOCK), F32),
        ],
    )(place, key_slots, block_count, qz, gz, table, tablet, top, inv, dots)
    returned = exchange_nodes(rest[4:], step_masks(node_count))
    query_wg, owg, wkv, wq = call(
        query_weight_kernel,
        "query_weight",
        [((HD, D), F32)] * 2 + [((D, 2 * D), BF16), ((2 * D, 2 * D), BF16)],
        [smem()] + [vmem()] * 6,
        limit,
        flops=2 * node_rows * D * HD,
        scratch=[pltpu.VMEM((HEADS, D, BLOCK), BF16), pltpu.VMEM((HEADS, 2 * D, BLOCK), BF16)],
    )(place, dqt, *xs, in_weight, attt, low)
    sent = ((rows * 3 // 2, BLOCK), BF16)
    collected = call(
        functools.partial(collect_kernel, node_count),
        "collect",
        [sent, sent, ((rows * 3, BLOCK), BF16)] + [((HD, D), BF16)] * 4,
        [smem()] * 2 + [vmem()] * (8 + node_count),
        limit,
        flops=2 * node_rows * D * BLOCK,
        scratch=[pltpu.VMEM((BLK, BLOCK, BLOCK), F32)],
    )(place, wants, own, *returned, *rest[:4], xt, owg, query_wg)
    own_send, beside_send, across_send = collected[:3]
    across = swap(across_send, "head", 2)
    shift = top_shift(node_count)
    factor = total_nodes ** (-0.5)
    late, summed = add_nodes(collected[3:], shift, factor)
    (relay,) = call(
        relay_kernel, "relay", [((rows * 3, BLOCK), BF16)], [vmem()] * 3, 4 * MIB
    )(beside_send, across, summed)
    beside = swap(relay, "head", 1)
    feature_grad, finished = call(
        finish_kernel,
        "finish",
        [((rows, D), BF16), ((8, BLOCK), F32)],
        [hbm()] + [vmem()] * 5,
        limit,
        flops=4 * rows * 3 * D * D,
        scratch=[pltpu.VMEM((rows, D), F32), pltpu.SemaphoreType.DMA],
    )(norm_grad, own_send, beside, across, wq, wkv)
    in_grad, out_grad = call(
        functools.partial(result_kernel, shift),
        "result",
        [((3 * HD, D), F32), ((HD, D), F32)],
        [smem()] + [vmem()] * 5,
        limit,
    )(place, late[0], *late[:0:-1], finished)
    return (output, feature_grad, in_grad.T, out_grad)


def solution(mesh):
    placed = (
        P(("node", "head"), None),
        P(),
        P(),
        P(("node", "head"), None),
        P("node", None),
        P("node"),
        P("node", None, None),
    )
    return jax.shard_map(
        on_device,
        mesh=mesh,
        in_specs=placed,
        out_specs=(
            P(("node", "head"), None),
            P(("node", "head"), None),
            P(None, "head"),
            P("head", None),
        ),
        check_vma=False,
    )
```
